32 devices in a mesh: bucket: 4 (over z), batch: 8 (over y, x, core).
Axes of the slice: x: 2, y: 2, z: 4, core: 2. Of those that a mesh axis runs over, the one named last changes fastest.
Arguments:
- images: float32 [640, 3, 1024], P(('bucket', 'batch')), may hold values from -4 to 4
- pixel_mask: int32 [640, 1024], P(('bucket', 'batch')), may hold values from 0 to 1, as said below
- timesteps: int32 [640], P(('bucket', 'batch')), may hold values from 0 to 999, as said below
- noise_field: float32 [640, 3, 1024], P(('bucket', 'batch')), may hold values from -5 to 5
- matrices: float32 [5120, 256], P('bucket')
- matrix_moms: float32 [5120, 256], P('bucket'), may hold values from -0.004941059 to 0.004941059
- stem_weight: float32 [27, 128], replicated, may hold values from -1.25 to 1.25
- stem_moms: float32 [27, 128], replicated, may hold values from -0.004941059 to 0.004941059
- head_weight: float32 [3456, 12], replicated, may hold values from -0.109375 to 0.109375
- head_moms: float32 [3456, 12], replicated, may hold values from -0.004941059 to 0.004941059
- vectors: float32 [2956], replicated, may hold values from 0.25 to 1.75
- vector_firsts: float32 [2956], replicated, may hold values from -0.00049410586 to 0.00049410586
- vector_seconds: float32 [2956], replicated, may hold values from 1.5258789e-09 to 6.1035155e-09
Outputs:
- loss_sum: float32 [], replicated
- weight_sum: float32 [], replicated
- new_matrices: float32 [5120, 256], P('bucket')
- new_matrix_moms: float32 [5120, 256], P('bucket')
- matrix_copies: bfloat16 [5120, 256], P('bucket')
- new_stem: float32 [27, 128], replicated
- new_stem_moms: float32 [27, 128], replicated
- stem_copy: bfloat16 [27, 128], replicated
- new_head: float32 [3456, 12], replicated
- new_head_moms: float32 [3456, 12], replicated
- head_copy: bfloat16 [3456, 12], replicated
- new_vectors: float32 [2956], replicated
- new_firsts: float32 [2956], replicated
- new_seconds: float32 [2956], replicated
- vector_copy: bfloat16 [2956], replicated
The draws below stay inside these ranges and needn't reach their ends.
Inputs may be any that keep to these rules, and one draw needn't show every extreme that they name: `pixel_mask`: 0 or 1; the share of ones differs from image to image. `timesteps`: an image on index b of the bucket axis has a timestep in [b * 1000 / 4, (b + 1) * 1000 / 4).
All inputs are finite; a program needn't handle non-finite values.
Results may differ from the reference program's by a relative error of at most 0.007.
The reference program's roundings to bfloat16 on the way count: a program that leaves them out, or rounds other values in their place, can miss the bound.
Values may be sent and summed in bfloat16 or wider, within the bound.
A program may use at most 512 MiB of HBM per device.

```python
import math
import jax
import jax.numpy as jnp
from jax import lax

C1 = 128
CHANNELS_MID = 256
TEMB = 512
GROUPS = 32
S = 32
IMG_DEV = 20
TSTEPS = 1000
NS_STEPS = 5
STEP = 10
IMAGES = 640
MROWS = 5120
HROWS = 3456
PLEN = 2956
N_BUCKET = 4
N_BATCH = 8


def draw_pixel_mask(key, part):
    key = jax.random.fold_in(key, 11)
    image_key, pixel_key = jax.random.split(key)
    positions = jnp.arange(IMAGES, dtype=jnp.int32)
    batch_pos = positions // IMG_DEV % N_BATCH
    jitter = jax.random.randint(image_key, (IMAGES,), 0, 1000)
    thresholds = 150 + 700 * (batch_pos * 1000 + jitter) // (N_BATCH * 1000)
    rolls = jax.random.randint(pixel_key, (IMAGES, S * S), 0, 1000)
    return (rolls < thresholds[:, None]).astype(jnp.int32)


def draw_timesteps(key, part):
    key = jax.random.fold_in(key, 12)
    positions = jnp.arange(IMAGES, dtype=jnp.int32)
    bucket_span = TSTEPS // N_BUCKET
    owner_pos = positions // (IMG_DEV * N_BATCH)
    chosen = owner_pos * bucket_span + jax.random.randint(key, (IMAGES,), 0, bucket_span)
    chosen = chosen.at[0].set(0)
    return chosen.at[IMAGES - 1].set(TSTEPS - 1)


def draw_matrices(key, part):
    key = jax.random.fold_in(key, 13)
    seg_list = [9 * C1, 9 * CHANNELS_MID, C1, TEMB, CHANNELS_MID, CHANNELS_MID, CHANNELS_MID, CHANNELS_MID]
    factors = [1.0, 1.0, 1.0, 1.0, 1.4, 1.4, 1.0, 4.0]
    pieces = [jnp.full((seg_rows // N_BUCKET,), factor / math.sqrt(seg_rows), jnp.float32) for seg_rows, factor in zip(seg_list, factors)]
    row_scale = jnp.tile(jnp.concatenate(pieces), N_BUCKET)
    return jax.random.normal(key, (MROWS, CHANNELS_MID), jnp.float32) * row_scale[:, None]


def levels(rng, extent, cuts, smallest, high):
    level, own = 1.0, jax.random.fold_in(rng, 6)
    for position, blocks in cuts:
        steps = jnp.exp(jax.random.uniform(jax.random.fold_in(own, position), (blocks,), jnp.float32, smallest / len(cuts), high / len(cuts)))
        level = level * jnp.repeat(steps, extent[position] // blocks).reshape([-1 if axis == position else 1 for axis in range(len(extent))])
    return level


def gaussian(own_key, dims, scale, most, cuts=(), kind=jnp.bfloat16):
    values = jax.random.normal(own_key, dims, jnp.float32) * scale
    if len(cuts) > 0:
        values = levels(own_key, dims, cuts, -0.22, 0.18) * values
    return jnp.clip(values, min=-most, max=most).astype(kind)


def setup_inputs(seed: int = 0) -> dict:
    splits = jax.random.split(jax.random.key(seed), 14)
    images = gaussian(splits[0], (IMAGES, 3, S * S), 1.0, 4.0, ((0, 32),), jnp.float32)
    pixel_mask = draw_pixel_mask(jax.random.fold_in(splits[13], 71), 0)
    timesteps = draw_timesteps(jax.random.fold_in(splits[13], 71), 0)
    noise_field = gaussian(splits[3], (IMAGES, 3, S * S), 1.0, 5.0, ((0, 32),), jnp.float32)
    matrices = draw_matrices(jax.random.fold_in(splits[13], 71), 0)
    matrix_moms = gaussian(splits[5], (MROWS, CHANNELS_MID), (1.0 / (IMAGES * S * S) ** 0.5), 0.004941059, ((0, 4),), jnp.float32)
    stem_weight = gaussian(splits[6], (27, C1), 27 ** -0.5, 1.25, (), jnp.float32)
    stem_moms = gaussian(splits[7], (27, C1), (1.0 / (IMAGES * S * S) ** 0.5), 0.004941059, (), jnp.float32)
    head_weight = gaussian(splits[8], (HROWS, 12), HROWS ** -0.5, 0.109375, (), jnp.float32)
    head_moms = gaussian(splits[9], (HROWS, 12), (1.0 / (IMAGES * S * S) ** 0.5), 0.004941059, (), jnp.float32)
    vectors = jnp.clip(1.0 + 0.15 * jax.random.normal(splits[10], (PLEN,), jnp.float32), 0.25, 1.75)
    vector_firsts = gaussian(splits[11], (PLEN,), (0.1 / (IMAGES * S * S) ** 0.5), 0.00049410586, (), jnp.float32)
    vector_seconds = jnp.clip(jnp.exp(jax.random.uniform(splits[12], (PLEN,), jnp.float32, math.log(1.5258788677030566e-09), math.log(6.103515470812226e-09))), 1.5258788677030566e-09, 6.103515470812226e-09)
    return dict(images=images, pixel_mask=pixel_mask, timesteps=timesteps, noise_field=noise_field, matrices=matrices, matrix_moms=matrix_moms, stem_weight=stem_weight, stem_moms=stem_moms, head_weight=head_weight, head_moms=head_moms, vectors=vectors, vector_firsts=vector_firsts, vector_seconds=vector_seconds)


@jax.custom_vjp
def low(v):
    return lax.optimization_barrier(v.astype(jnp.bfloat16)).astype(jnp.float32)

@jax.custom_vjp
def reduced_backward(v):
    return v

def low_keep(v):
    return (low(v), None)

def low_pass(kept, grad):
    return (grad,)

def back_keep(v):
    return (v, None)

def back_low(kept, grad):
    return (low(grad),)
low.defvjp(low_keep, low_pass)
reduced_backward.defvjp(back_keep, back_low)
GN_EPS = 1e-05
NORM_EPS = 1e-12
MOMENTUM = 0.95
LR_MUON = 0.5
DECAY = 0.01
NS_A = 3.4445
NS_B = -4.775
NS_C = 2.0315
BETA_ONE = 0.9
BETA_TWO = 0.999
LR_ADAM = 0.5
ADAM_EPS = 1e-08
EXACT_PRECISION = lax.Precision.HIGHEST

def segment_rows():
    return [9 * C1, 9 * CHANNELS_MID, C1, TEMB, CHANNELS_MID, CHANNELS_MID, CHANNELS_MID, CHANNELS_MID]

def unpack(packed, owners):
    blocks = packed.reshape(owners, -1, packed.shape[1])
    pieces = []
    start = 0
    for seg_rows in segment_rows():
        share = seg_rows // owners
        pieces.append(blocks[:, start:start + share, :].reshape(seg_rows, packed.shape[1]))
        start += share
    return pieces

def pack(pieces, owners):
    blocks = [piece.reshape(owners, -1, piece.shape[1]) for piece in pieces]
    return jnp.concatenate(blocks, axis=1).reshape(-1, pieces[0].shape[1])

def split_vector(vectors):
    lengths = [C1, C1, C1] + [CHANNELS_MID] * 10 + [12]
    pieces = []
    start = 0
    for length in lengths:
        pieces.append(vectors[start:start + length])
        start += length
    return pieces

def plan(timesteps):
    frac_t = (timesteps.astype(jnp.float32) / TSTEPS + 0.008) / 1.008
    level = jnp.cos(frac_t * (math.pi / 2)) ** 2
    ratio = level / (1.0 - level)
    return (level, jnp.minimum(1.0, 5.0 / ratio))

def embed(timesteps):
    half_width = TEMB // 2
    freqs = jnp.exp(-math.log(10000.0) * jnp.arange(half_width, dtype=jnp.float32) / half_width)
    angles = timesteps.astype(jnp.float32)[:, None] * freqs[None, :]
    return jnp.concatenate([jnp.sin(angles), jnp.cos(angles)], axis=1)

def swish(values):
    return values * jax.nn.sigmoid(values)

def group_norm(values, gain_v, shift_v):
    samples, places, chans = values.shape
    grouped = values.reshape(samples, places, GROUPS, chans // GROUPS)
    centre = lax.optimization_barrier(jnp.mean(grouped, axis=(1, 3), keepdims=True))
    centered = grouped - centre
    spread = lax.optimization_barrier(jnp.mean(centered * centered, axis=(1, 3), keepdims=True))
    normed = (centered * lax.rsqrt(spread + GN_EPS)).reshape(samples, places, chans)
    return normed * gain_v + shift_v

def patches(grid):
    samples, height, across, chans = grid.shape
    padded = jnp.pad(grid, ((0, 0), (1, 1), (1, 1), (0, 0)))
    parts = [padded[:, shift_y:shift_y + height, shift_x:shift_x + across, :] for shift_y in range(3) for shift_x in range(3)]
    return jnp.concatenate(parts, axis=3).reshape(samples, height * across, 9 * chans)

def project(left, right):
    return jnp.einsum('bpk,kn->bpn', left, right, precision=EXACT_PRECISION)

def forward(params, images, pixel_mask, timesteps, noise_field):
    matrices, stem_weight, head_weight, vectors = params
    conv_one, conv_two, skip_w, temb_w, query_w, key_w, value_w, out_w = unpack(matrices, N_BUCKET)
    stem_b, gain_one, shift_one, conv_one_b, temb_b, gain_two, shift_two, conv_two_b, gain_att, shift_att, query_b, value_b, out_b, head_b = split_vector(vectors)
    samples = images.shape[0]
    half_side = S // 2
    level, weight = plan(timesteps)
    noisy = jnp.sqrt(level)[:, None, None] * images + jnp.sqrt(1.0 - level)[:, None, None] * noise_field
    grid = noisy.reshape(samples, 3, S, S).transpose(0, 2, 3, 1)
    stem_out = reduced_backward(project(patches(low(grid)), low(stem_weight))) + stem_b
    pooled = lax.optimization_barrier(jnp.mean(stem_out.reshape(samples, half_side, 2, half_side, 2, C1), axis=(2, 4))).reshape(samples, -1, C1)
    act_one = low(swish(group_norm(pooled, gain_one, shift_one)))
    time_in = low(swish(embed(timesteps)))
    time_proj = reduced_backward(jnp.dot(time_in, low(temb_w), precision=EXACT_PRECISION)) + temb_b
    conv_in = reduced_backward(project(patches(act_one.reshape(samples, half_side, half_side, C1)), low(conv_one)))
    hidden_one = conv_in + conv_one_b + time_proj[:, None, :]
    act_two = low(swish(group_norm(hidden_one, gain_two, shift_two)))
    hidden_two = reduced_backward(project(patches(act_two.reshape(samples, half_side, half_side, CHANNELS_MID)), low(conv_two))) + conv_two_b
    resid = reduced_backward(project(low(pooled), low(skip_w))) + hidden_two
    normed = low(group_norm(resid, gain_att, shift_att))
    proj_all = jnp.concatenate([query_w, key_w, value_w], axis=1)
    joined = reduced_backward(project(normed, low(proj_all)))
    query_rows = low(joined[:, :, :CHANNELS_MID] + query_b)
    key_rows_reduced = low(joined[:, :, CHANNELS_MID:2 * CHANNELS_MID])
    value_rows_reduced = low(joined[:, :, 2 * CHANNELS_MID:] + value_b)
    attention_logits = reduced_backward(jnp.einsum('upo,uwo->upw', query_rows, key_rows_reduced, precision=EXACT_PRECISION)) * CHANNELS_MID ** (-0.5)
    attention_probabilities = low(jax.nn.softmax(attention_logits, axis=-1))
    attention_output = reduced_backward(jnp.einsum('lap,lph->lah', attention_probabilities, value_rows_reduced, precision=EXACT_PRECISION))
    output = resid + reduced_backward(project(low(attention_output), low(out_w))) + out_b
    joined_skip = low(swish(jnp.concatenate([output, pooled], axis=2)))
    head_out = reduced_backward(project(patches(joined_skip.reshape(samples, half_side, half_side, CHANNELS_MID + C1)), low(head_weight))) + head_b
    predicted = head_out.reshape(samples, half_side, half_side, 2, 2, 3).transpose(0, 5, 1, 3, 2, 4).reshape(samples, 3, S * S)
    error = predicted - noise_field
    masked = pixel_mask.astype(jnp.float32)[:, None, :] * weight[:, None, None]
    return jnp.sum(masked * error * error)

def ns_update(iterate, gram):
    inner = NS_B * gram + NS_C * jnp.dot(gram, gram, precision=EXACT_PRECISION)
    return NS_A * iterate + jnp.dot(iterate, inner, precision=EXACT_PRECISION)

def muon(weight_m, moment, gradient):
    moment_new = MOMENTUM * moment + gradient
    direction = gradient + MOMENTUM * moment_new
    iterate = direction * lax.rsqrt(jnp.sum(direction * direction) + NORM_EPS)
    for step in range(NS_STEPS):
        iterate = ns_update(iterate, jnp.dot(iterate.T, iterate, precision=EXACT_PRECISION))
    return (weight_m * (1.0 - LR_MUON * DECAY) - LR_MUON * iterate, moment_new)

def reference(images, pixel_mask, timesteps, noise_field, matrices, matrix_moms, stem_weight, stem_moms, head_weight, head_moms, vectors, vector_firsts, vector_seconds):
    level, weight = plan(timesteps)
    counts = lax.optimization_barrier(jnp.sum(pixel_mask.astype(jnp.float32), axis=1))
    weight_sum = jnp.sum(3.0 * weight * counts)
    params = (matrices, stem_weight, head_weight, vectors)

    def one_group(carry, group):

        def cut(array):
            return lax.dynamic_slice_in_dim(array, (group * IMG_DEV).astype(jnp.int32), IMG_DEV, 0)

        def loss_of(inner):
            return forward(inner, cut(images), cut(pixel_mask), cut(timesteps), cut(noise_field))
        value, pullback = jax.vjp(loss_of, params)
        grads = pullback(jnp.ones((), value.dtype) / weight_sum)[0]
        return ((carry[0] + value, jax.tree.map(jnp.add, carry[1], grads)), None)
    start = (jnp.zeros((), jnp.float32), jax.tree.map(jnp.zeros_like, params))
    (loss_sum, grads), unused = lax.scan(one_group, start, jnp.arange(IMAGES // IMG_DEV, dtype=jnp.int32))
    grad_mats, grad_stem, grad_head, grad_vec = grads
    fresh_list, moment_list = ([], [])
    for weight_m, moment, gradient in zip(unpack(matrices, N_BUCKET), unpack(matrix_moms, N_BUCKET), unpack(grad_mats, N_BUCKET)):
        fresh, moment_new = muon(weight_m, moment, gradient)
        fresh_list.append(fresh)
        moment_list.append(moment_new)
    new_matrices = pack(fresh_list, N_BUCKET)
    new_matrix_moms = pack(moment_list, N_BUCKET)
    new_stem, new_stem_moms = muon(stem_weight, stem_moms, grad_stem)
    new_head, new_head_moms = muon(head_weight, head_moms, grad_head)
    new_firsts = BETA_ONE * vector_firsts + (1.0 - BETA_ONE) * grad_vec
    new_seconds = BETA_TWO * vector_seconds + (1.0 - BETA_TWO) * grad_vec * grad_vec
    step_dir = new_firsts / (1.0 - BETA_ONE ** STEP) / (jnp.sqrt(new_seconds / (1.0 - BETA_TWO ** STEP)) + ADAM_EPS)
    new_vectors = vectors - LR_ADAM * step_dir
    return (loss_sum, weight_sum, new_matrices, new_matrix_moms, new_matrices.astype(jnp.bfloat16), new_stem, new_stem_moms, new_stem.astype(jnp.bfloat16), new_head, new_head_moms, new_head.astype(jnp.bfloat16), new_vectors, new_firsts, new_seconds, new_vectors.astype(jnp.bfloat16))
```

```python
import math

import jax
import jax.numpy as jnp
from jax import lax
from jax.sharding import PartitionSpec as P

C1 = 128
CHANNELS_MID = 256
TEMB = 512
GROUPS = 32
S = 32
TSTEPS = 1000
NS_STEPS = 5
STEP = 10


GN_EPS = 1e-05
NORM_EPS = 1e-12
MOMENTUM = 0.95
LR_MUON = 0.5
DECAY = 0.01
NS_A = 3.4445
NS_B = -4.775
NS_C = 2.0315
BETA_ONE = 0.9
BETA_TWO = 0.999
LR_ADAM = 0.5
ADAM_EPS = 1e-08
EXACT_PRECISION = lax.Precision.HIGHEST
LOWTYPE = jnp.bfloat16


def for_sending(shard):
    return jax.tree.map(lambda a: a.astype(jnp.bfloat16) if a.dtype == jnp.float32 else a, shard)


def segment_rows():
    return [
        9 * C1,
        9 * CHANNELS_MID,
        C1,
        TEMB,
        CHANNELS_MID,
        CHANNELS_MID,
        CHANNELS_MID,
        CHANNELS_MID,
    ]


def unpack(packed, owners):
    blocks = packed.reshape(owners, -1, packed.shape[1])
    pieces = []
    start = 0
    for seg_rows in segment_rows():
        share = seg_rows // owners
        pieces.append(blocks[:, start : start + share, :].reshape(seg_rows, packed.shape[1]))
        start += share
    return pieces


def pack(pieces, owners):
    blocks = [piece.reshape(owners, -1, piece.shape[1]) for piece in pieces]
    return jnp.concatenate(blocks, axis=1).reshape(-1, pieces[0].shape[1])


def split_vector(vectors):
    lengths = [C1, C1, C1] + [CHANNELS_MID] * 10 + [12]
    pieces = []
    start = 0
    for length in lengths:
        pieces.append(vectors[start : start + length])
        start += length
    return pieces


def plan(timesteps):
    frac_t = (timesteps.astype(jnp.float32) / TSTEPS + 0.008) / 1.008
    level = jnp.cos(frac_t * (math.pi / 2)) ** 2
    ratio = level / (1.0 - level)
    return (level, jnp.minimum(1.0, 5.0 / ratio))


def embed(timesteps):
    half_width = TEMB // 2
    freqs = jnp.exp(-math.log(10000.0) * jnp.arange(half_width, dtype=jnp.float32) / half_width)
    angles = timesteps.astype(jnp.float32)[:, None] * freqs[None, :]
    return jnp.concatenate([jnp.sin(angles), jnp.cos(angles)], axis=1)


def swish(values):
    return values * jax.nn.sigmoid(values)


def group_norm(values, gain_v, shift_v):
    samples, places, chans = values.shape
    grouped = values.reshape(samples, places, GROUPS, chans // GROUPS)
    centre = jnp.mean(grouped, axis=(1, 3), keepdims=True)
    centered = grouped - centre
    spread = jnp.mean(centered * centered, axis=(1, 3), keepdims=True)
    normed = (centered * lax.rsqrt(spread + GN_EPS)).reshape(samples, places, chans)
    return normed * gain_v + shift_v


def norm_act(values, gain_v, shift_v):
    return swish(group_norm(values, gain_v, shift_v))


def join_act(output, pooled):
    return swish(jnp.concatenate([output, pooled], axis=2))


def patches(grid):
    samples, height, across, chans = grid.shape
    padded = jnp.pad(grid, ((0, 0), (1, 1), (1, 1), (0, 0)))
    parts = [
        padded[:, shift_y : shift_y + height, shift_x : shift_x + across, :]
        for shift_y in range(3)
        for shift_x in range(3)
    ]
    return jnp.concatenate(parts, axis=3).reshape(samples, height * across, 9 * chans)


def unpatch(grad_cols, height, chans):
    samples = grad_cols.shape[0]
    parts = grad_cols.reshape(samples, height, height, 9, chans)
    total = None
    for shift_y in range(3):
        for shift_x in range(3):
            placed = jnp.pad(
                parts[:, :, :, shift_y * 3 + shift_x, :],
                ((0, 0), (shift_y, 2 - shift_y), (shift_x, 2 - shift_x), (0, 0)),
            )
            total = placed if total is None else total + placed
    return total[:, 1:-1, 1:-1, :].reshape(samples, height * height, chans)


def mult(left, right):
    return jnp.einsum("bpk,kn->bpn", left, right, preferred_element_type=jnp.float32)


def back_mult(grad_out, right):
    return jnp.einsum("bpn,kn->bpk", grad_out, right, preferred_element_type=jnp.float32)


def weight_grad(left, grad_out):
    return jnp.einsum("bpk,bpn->kn", left, grad_out, preferred_element_type=jnp.float32)


def row_total(values):
    return jnp.sum(values, axis=(0, 1))


def ns_update(iterate, gram):
    inner = NS_B * gram + NS_C * jnp.dot(gram, gram, precision=EXACT_PRECISION)
    return NS_A * iterate + jnp.dot(iterate, inner, precision=EXACT_PRECISION)


def local_muon(weight_m, moment, gradient):
    moment_new = MOMENTUM * moment + gradient
    direction = gradient + MOMENTUM * moment_new
    iterate = direction * lax.rsqrt(jnp.sum(direction * direction) + NORM_EPS)
    for step in range(NS_STEPS):
        iterate = ns_update(iterate, jnp.dot(iterate.T, iterate, precision=EXACT_PRECISION))
    return (weight_m * (1.0 - LR_MUON * DECAY) - LR_MUON * iterate, moment_new)


def ns_product(gram):
    eye = jnp.eye(gram.shape[0], dtype=jnp.float32)
    product = None
    for step in range(NS_STEPS):
        square = jnp.dot(gram, gram, precision=EXACT_PRECISION)
        factor = NS_A * eye + NS_B * gram + NS_C * square
        product = (
            factor if product is None else jnp.dot(product, factor, precision=EXACT_PRECISION)
        )
        if step < NS_STEPS - 1:
            half = jnp.dot(gram, factor, precision=EXACT_PRECISION)
            gram = jnp.dot(factor, half, precision=EXACT_PRECISION)
    return product


def shards(
    images,
    pixel_mask,
    timesteps,
    noise_field,
    matrices,
    matrix_moms,
    stem_weight,
    stem_moms,
    head_weight,
    head_moms,
    vectors,
    vector_firsts,
    vector_seconds,
):
    owners = lax.axis_size("bucket")
    gathered = lax.all_gather(matrices.astype(LOWTYPE), "bucket", axis=0, tiled=True)
    conv_one, conv_two, skip_w, temb_w, query_w, key_w, value_w, out_w = unpack(gathered, owners)
    proj_all = jnp.concatenate([query_w, key_w, value_w], axis=1)
    stem_low = stem_weight.astype(LOWTYPE)
    head_low = head_weight.astype(LOWTYPE)
    (
        stem_b,
        gain_one,
        shift_one,
        conv_one_b,
        temb_b,
        gain_two,
        shift_two,
        conv_two_b,
        gain_att,
        shift_att,
        query_b,
        value_b,
        out_b,
        head_b,
    ) = split_vector(vectors)
    samples = images.shape[0]
    half_side = S // 2
    level, weight = plan(timesteps)
    counts = jnp.sum(pixel_mask.astype(jnp.float32), axis=1)
    weight_local = jnp.sum(3.0 * weight * counts)
    noisy = (
        jnp.sqrt(level)[:, None, None] * images + jnp.sqrt(1.0 - level)[:, None, None] * noise_field
    )
    grid = noisy.reshape(samples, 3, S, S).transpose(0, 2, 3, 1).astype(LOWTYPE)
    cols_stem = patches(grid)
    stem_out = mult(cols_stem, stem_low) + stem_b
    pooled = jnp.mean(
        stem_out.reshape(samples, half_side, 2, half_side, 2, C1), axis=(2, 4)
    ).reshape(samples, -1, C1)
    pooled_low = pooled.astype(LOWTYPE)
    act_one_f, pull_one = jax.vjp(norm_act, pooled, gain_one, shift_one)
    cols_one = patches(act_one_f.astype(LOWTYPE).reshape(samples, half_side, half_side, C1))
    time_in = swish(embed(timesteps)).astype(LOWTYPE)
    time_proj = jnp.dot(time_in, temb_w, preferred_element_type=jnp.float32) + temb_b
    hidden_one = mult(cols_one, conv_one) + conv_one_b + time_proj[:, None, :]
    act_two_f, pull_two = jax.vjp(norm_act, hidden_one, gain_two, shift_two)
    cols_two = patches(
        act_two_f.astype(LOWTYPE).reshape(samples, half_side, half_side, CHANNELS_MID)
    )
    resid = mult(pooled_low, skip_w) + mult(cols_two, conv_two) + conv_two_b
    normed_f, pull_att = jax.vjp(group_norm, resid, gain_att, shift_att)
    normed = normed_f.astype(LOWTYPE)
    joined = mult(normed, proj_all)
    query_rows = (joined[:, :, :CHANNELS_MID] + query_b).astype(LOWTYPE)
    key_rows_reduced = joined[:, :, CHANNELS_MID : 2 * CHANNELS_MID].astype(LOWTYPE)
    value_rows_reduced = (joined[:, :, 2 * CHANNELS_MID :] + value_b).astype(LOWTYPE)
    query_scale = CHANNELS_MID ** (-0.5)
    attention_logits = (
        jnp.einsum("upo,uwo->upw", query_rows, key_rows_reduced, preferred_element_type=jnp.float32)
        * query_scale
    )
    attn_f = jax.nn.softmax(attention_logits, axis=-1)
    attention_reduced = attn_f.astype(LOWTYPE)
    attention_output = jnp.einsum(
        "lap,lph->lah", attention_reduced, value_rows_reduced, preferred_element_type=jnp.float32
    ).astype(LOWTYPE)
    output = resid + mult(attention_output, out_w) + out_b
    joined_f, pull_join = jax.vjp(join_act, output, pooled)
    cols_head = patches(
        joined_f.astype(LOWTYPE).reshape(samples, half_side, half_side, CHANNELS_MID + C1)
    )
    head_out = mult(cols_head, head_low) + head_b
    predicted = (
        head_out.reshape(samples, half_side, half_side, 2, 2, 3)
        .transpose(0, 5, 1, 3, 2, 4)
        .reshape(samples, 3, S * S)
    )
    error = predicted - noise_field
    masked = pixel_mask.astype(jnp.float32)[:, None, :] * weight[:, None, None]
    loss_local = jnp.sum(masked * error * error)
    grad_pred = 2.0 * masked * error
    grad_head_out = (
        grad_pred.reshape(samples, 3, half_side, 2, half_side, 2)
        .transpose(0, 2, 4, 3, 5, 1)
        .reshape(samples, -1, 12)
    )
    g_head_b = row_total(grad_head_out)
    grad_head_low = grad_head_out.astype(LOWTYPE)
    g_head = weight_grad(cols_head, grad_head_low)
    grad_joined = unpatch(back_mult(grad_head_low, head_low), half_side, CHANNELS_MID + C1)
    grad_output, grad_pool_head = pull_join(grad_joined)
    g_out_b = row_total(grad_output)
    grad_out_low = grad_output.astype(LOWTYPE)
    g_out = weight_grad(attention_output, grad_out_low)
    attention_gradient = back_mult(grad_out_low, out_w).astype(LOWTYPE)
    grad_weights = jnp.einsum(
        "upo,uwo->upw", attention_gradient, value_rows_reduced, preferred_element_type=jnp.float32
    )
    value_gradient = jnp.einsum(
        "fep,fet->fpt", attention_reduced, attention_gradient, preferred_element_type=jnp.float32
    )
    grad_scores = attn_f * (grad_weights - jnp.sum(grad_weights * attn_f, axis=-1, keepdims=True))
    unscaled_gradient = (grad_scores * query_scale).astype(LOWTYPE)
    grad_queries = jnp.einsum(
        "lap,lph->lah", unscaled_gradient, key_rows_reduced, preferred_element_type=jnp.float32
    )
    key_gradient = jnp.einsum(
        "fep,fet->fpt", unscaled_gradient, query_rows, preferred_element_type=jnp.float32
    )
    g_query_b = row_total(grad_queries)
    g_value_b = row_total(value_gradient)
    grad_joined_low = jnp.concatenate([grad_queries, key_gradient, value_gradient], axis=2).astype(
        LOWTYPE
    )
    g_proj = weight_grad(normed, grad_joined_low)
    grad_normed = back_mult(grad_joined_low, proj_all)
    grad_resid_att, g_gain_att, g_shift_att = pull_att(grad_normed)
    grad_resid = grad_output + grad_resid_att
    grad_resid_low = grad_resid.astype(LOWTYPE)
    g_skip = weight_grad(pooled_low, grad_resid_low)
    grad_pool_skip = back_mult(grad_resid_low, skip_w)
    g_conv_two_b = row_total(grad_resid)
    g_conv_two = weight_grad(cols_two, grad_resid_low)
    grad_act_two = unpatch(back_mult(grad_resid_low, conv_two), half_side, CHANNELS_MID)
    grad_hidden, g_gain_two, g_shift_two = pull_two(grad_act_two)
    g_conv_one_b = row_total(grad_hidden)
    grad_time = jnp.sum(grad_hidden, axis=1)
    g_temb_b = jnp.sum(grad_time, axis=0)
    g_temb = jnp.dot(time_in.T, grad_time.astype(LOWTYPE), preferred_element_type=jnp.float32)
    grad_hidden_low = grad_hidden.astype(LOWTYPE)
    g_conv_one = weight_grad(cols_one, grad_hidden_low)
    grad_act_one = unpatch(back_mult(grad_hidden_low, conv_one), half_side, C1)
    grad_pool_one, g_gain_one, g_shift_one = pull_one(grad_act_one)
    grad_pooled = grad_pool_head + grad_pool_skip + grad_pool_one
    grad_stem_out = jnp.broadcast_to(
        grad_pooled.reshape(samples, half_side, 1, half_side, 1, C1) * 0.25,
        (samples, half_side, 2, half_side, 2, C1),
    ).reshape(samples, S * S, C1)
    g_stem_b = row_total(grad_stem_out)
    g_stem = weight_grad(cols_stem, grad_stem_out.astype(LOWTYPE))
    grad_pack = pack(
        [
            g_conv_one,
            g_conv_two,
            g_skip,
            g_temb,
            g_proj[:, :CHANNELS_MID],
            g_proj[:, CHANNELS_MID : 2 * CHANNELS_MID],
            g_proj[:, 2 * CHANNELS_MID :],
            g_out,
        ],
        owners,
    )
    grad_vec = jnp.concatenate(
        [
            g_stem_b,
            g_gain_one,
            g_shift_one,
            g_conv_one_b,
            g_temb_b,
            g_gain_two,
            g_shift_two,
            g_conv_two_b,
            g_gain_att,
            g_shift_att,
            g_query_b,
            g_value_b,
            g_out_b,
            g_head_b,
        ]
    )
    rows_dev = matrices.shape[0]
    summed, grad_stem, grad_headw, grad_vec, loss_sum, weight_sum = lax.psum(
        (grad_pack, g_stem, g_head, grad_vec, loss_local, weight_local), ("bucket", "batch")
    )
    inverse = 1.0 / weight_sum
    summed = summed * inverse
    grad_stem = grad_stem * inverse
    grad_headw = grad_headw * inverse
    grad_vec = grad_vec * inverse
    grad_mine = lax.dynamic_slice_in_dim(summed, lax.axis_index("bucket") * rows_dev, rows_dev, 0)
    shares = [seg_rows // owners for seg_rows in segment_rows()]
    weight_parts, moment_parts, grad_parts = ([], [], [])
    start = 0
    for share in shares:
        weight_parts.append(matrices[start : start + share])
        moment_parts.append(matrix_moms[start : start + share])
        grad_parts.append(grad_mine[start : start + share])
        start += share
    moments_new = [
        MOMENTUM * moment + gradient for moment, gradient in zip(moment_parts, grad_parts)
    ]
    directions = [gradient + MOMENTUM * moment for gradient, moment in zip(grad_parts, moments_new)]
    gram_sums = lax.psum(
        tuple(jnp.dot(d.T, d, precision=EXACT_PRECISION) for d in directions), "bucket"
    )
    iterates = []
    for direction, gram in zip(directions, gram_sums):
        scale = lax.rsqrt(jnp.trace(gram) + NORM_EPS)
        iterates.append(
            jnp.dot(direction * scale, ns_product(gram * (scale * scale)), precision=EXACT_PRECISION)
        )
    new_matrices = jnp.concatenate(
        [
            weight_m * (1.0 - LR_MUON * DECAY) - LR_MUON * iterate
            for weight_m, iterate in zip(weight_parts, iterates)
        ],
        axis=0,
    )
    new_matrix_moms = jnp.concatenate(moments_new, axis=0)
    new_stem, new_stem_moms = local_muon(stem_weight, stem_moms, grad_stem)
    new_head, new_head_moms = local_muon(head_weight, head_moms, grad_headw)
    new_firsts = BETA_ONE * vector_firsts + (1.0 - BETA_ONE) * grad_vec
    new_seconds = BETA_TWO * vector_seconds + (1.0 - BETA_TWO) * grad_vec * grad_vec
    step_dir = (
        new_firsts
        / (1.0 - BETA_ONE**STEP)
        / (jnp.sqrt(new_seconds / (1.0 - BETA_TWO**STEP)) + ADAM_EPS)
    )
    new_vectors = vectors - LR_ADAM * step_dir
    return (
        loss_sum,
        weight_sum,
        new_matrices,
        new_matrix_moms,
        new_matrices.astype(LOWTYPE),
        new_stem,
        new_stem_moms,
        new_stem.astype(LOWTYPE),
        new_head,
        new_head_moms,
        new_head.astype(LOWTYPE),
        new_vectors,
        new_firsts,
        new_seconds,
        new_vectors.astype(LOWTYPE),
    )


def solution(mesh):
    return jax.shard_map(
        shards,
        mesh=mesh,
        in_specs=(
            P(("bucket", "batch"), None, None),
            P(("bucket", "batch"), None),
            P(("bucket", "batch")),
            P(("bucket", "batch"), None, None),
            P("bucket", None),
            P("bucket", None),
            P(),
            P(),
            P(),
            P(),
            P(),
            P(),
            P(),
        ),
        out_specs=(
            P(),
            P(),
            P("bucket", None),
            P("bucket", None),
            P("bucket", None),
            P(),
            P(),
            P(),
            P(),
            P(),
            P(),
            P(),
            P(),
            P(),
            P(),
        ),
        check_vma=False,
    )
```

```python
import functools
import math

import jax
import jax.numpy as jnp
import numpy as np
from jax import lax
from jax.experimental import pallas as pl
from jax.experimental.pallas import tpu as pltpu
from jax.sharding import PartitionSpec as P

C1 = 128
CHANNELS_MID = 256
TEMB = 512
GROUPS = 32
S = 32
TSTEPS = 1000
NS_STEPS = 5
STEP = 10


GN_EPS = 1e-05
NORM_EPS = 1e-12
MOMENTUM = 0.95
LR_MUON = 0.5
DECAY = 0.01
NS_A = 3.4445
NS_B = -4.775
NS_C = 2.0315
BETA_ONE = 0.9
BETA_TWO = 0.999
LR_ADAM = 0.5
ADAM_EPS = 1e-08
EXACT_PRECISION = lax.Precision.HIGHEST
LOWTYPE = jnp.bfloat16


def segment_rows():
    return [
        9 * C1,
        9 * CHANNELS_MID,
        C1,
        TEMB,
        CHANNELS_MID,
        CHANNELS_MID,
        CHANNELS_MID,
        CHANNELS_MID,
    ]


def unpack(packed, owners):
    blocks = packed.reshape(owners, -1, packed.shape[1])
    pieces = []
    start = 0
    for seg_rows in segment_rows():
        share = seg_rows // owners
        pieces.append(blocks[:, start : start + share, :].reshape(seg_rows, packed.shape[1]))
        start += share
    return pieces


def pack(pieces, owners):
    blocks = [piece.reshape(owners, -1, piece.shape[1]) for piece in pieces]
    return jnp.concatenate(blocks, axis=1).reshape(-1, pieces[0].shape[1])


def plan(timesteps):
    frac_t = (timesteps.astype(jnp.float32) / TSTEPS + 0.008) / 1.008
    level = jnp.cos(frac_t * (math.pi / 2)) ** 2
    ratio = level / (1.0 - level)
    return (level, jnp.minimum(1.0, 5.0 / ratio))


def embed(timesteps):
    half_width = TEMB // 2
    freqs = jnp.exp(-math.log(10000.0) * jnp.arange(half_width, dtype=jnp.float32) / half_width)
    angles = timesteps.astype(jnp.float32)[:, None] * freqs[None, :]
    return jnp.concatenate([jnp.sin(angles), jnp.cos(angles)], axis=1)


def swish(values):
    return values * jax.nn.sigmoid(values)


F32 = jnp.float32
PLACES = 256
SIDE = 16
HALO = 288
TAPS = 9
ROWS12 = 16
CHUNK = 64
VMEM_BYTES = 56 * 1024 * 1024
SEG_OFF = (0, 1152, 3456, 3584, 4096, 4352, 4608, 4864, 5120)


def dot_nn(a, b, precision=None):
    return lax.dot_general(
        a, b, (((1,), (0,)), ((), ())), preferred_element_type=F32, precision=precision
    )


def dot_nt(a, b):
    return lax.dot_general(a, b, (((1,), (1,)), ((), ())), preferred_element_type=F32)


def dot_tn(a, b):
    return lax.dot_general(a, b, (((0,), (0,)), ((), ())), preferred_element_type=F32)


def sigmoid(v):
    return 1.0 / (1.0 + jnp.exp(-v))


def fold8(v):
    rows, chans = v.shape
    return jnp.sum(v.reshape(rows // 8, 8, chans), axis=0)


def shift_lanes(x, di, dj):
    lane = lax.broadcasted_iota(jnp.int32, x.shape, 1)
    row, col = lane // SIDE + di, lane % SIDE + dj
    offset = (-(SIDE * di + dj)) % PLACES
    moved = x if offset == 0 else pltpu.roll(x, offset, 1)
    valid = (row >= 0) & (row < SIDE) & (col >= 0) & (col < SIDE)
    return jnp.where(valid, moved, 0.0)


def tap_offsets():
    return [(di, dj) for di in (-1, 0, 1) for dj in (-1, 0, 1)]


def unet_body(
    group,
    steps,
    noisy_ref,
    noise_ref,
    maskw_ref,
    time_ref,
    stemw_ref,
    headw_ref,
    conv1_ref,
    conv1b_ref,
    conv2_ref,
    conv2b_ref,
    skip_ref,
    temb_ref,
    qkv_ref,
    outw_ref,
    vec_ref,
    headb_ref,
    same128_ref,
    same256_ref,
    acc_ref,
    gstem_ref,
    ghead_ref,
    gvec_ref,
    ghb_ref,
    loss_ref,
    x0,
    hid,
    res,
    outp,
    attn,
    a1,
    a2,
    normed,
    qkv,
    plow,
    attl,
    joined,
    patch,
    pad1,
    pad2,
    shiftf,
    dyf,
    dout,
    dq3,
    dpool,
    tproj,
    gtime,
):
    step = pl.program_id(0)
    mid = CHANNELS_MID
    chunks = range(0, PLACES, CHUNK)
    images = range(group)

    @pl.when(step == 0)
    def _():
        acc_ref[...] = jnp.zeros_like(acc_ref)
        gstem_ref[...] = jnp.zeros_like(gstem_ref)
        ghead_ref[...] = jnp.zeros_like(ghead_ref)
        gvec_ref[...] = jnp.zeros_like(gvec_ref)
        ghb_ref[...] = jnp.zeros_like(ghb_ref)
        loss_ref[...] = jnp.zeros_like(loss_ref)
        gtime[...] = jnp.zeros_like(gtime)
        for ref in (a1, a2, pad1, pad2):
            for g in images:
                ref[g, :SIDE, :] = jnp.zeros((SIDE, ref.shape[2]), ref.dtype)
                ref[g, HALO - SIDE :, :] = jnp.zeros((SIDE, ref.shape[2]), ref.dtype)
        shiftf[...] = jnp.zeros_like(shiftf)
        tproj[...] = dot_nn(time_ref[...], temb_ref[...])

    def vec(row, chans=mid):
        return vec_ref[row : row + 1, :chans]

    def add_vec(row, value):
        gvec_ref[row : row + 1, : value.shape[1]] += value

    def total(parts):
        return jnp.concatenate([jnp.sum(p, axis=0, keepdims=True) for p in parts], axis=0)

    def grouped(stats, chans):
        same = same128_ref if chans == C1 else same256_ref
        return dot_nn(stats, same[...], precision=EXACT_PRECISION)

    def gn_stats(ref, sums, chans):
        mean = grouped(sums, chans)
        parts = []
        for g in images:
            acc = jnp.zeros((8, chans), F32)
            for r in chunks:
                c = ref[g, r : r + CHUNK, :] - mean[g : g + 1]
                acc += fold8(c * c)
            parts.append(acc)
        return mean, lax.rsqrt(grouped(total(parts), chans) + GN_EPS)

    def edge(chans, left):
        col = lax.broadcasted_iota(jnp.int32, (CHUNK, chans), 0) % SIDE
        return (col > 0) if left else (col < SIDE - 1)

    def act_shift(ref, mean, rstd, gain, shift, dest, chans):
        for g in images:
            for r in chunks:
                y = (ref[g, r : r + CHUNK, :] - mean[g : g + 1]) * rstd[g : g + 1] * gain + shift
                a = y * sigmoid(y)
                shiftf[g, 8 + r : 8 + r + CHUNK, :chans] = a
                dest[g, SIDE + r : SIDE + r + CHUNK, chans : 2 * chans] = a.astype(LOWTYPE)
            for r in chunks:
                before = shiftf[g, 7 + r : 7 + r + CHUNK, :chans]
                after = shiftf[g, 9 + r : 9 + r + CHUNK, :chans]
                rows = slice(SIDE + r, SIDE + r + CHUNK)
                dest[g, rows, :chans] = jnp.where(edge(chans, True), before, 0.0).astype(LOWTYPE)
                dest[g, rows, 2 * chans :] = jnp.where(edge(chans, False), after, 0.0).astype(
                    LOWTYPE
                )

    def dy_cat(ref, g, order):
        return jnp.concatenate(
            [ref[g, SIDE * k : SIDE * k + PLACES, :] for k in order], axis=1
        )

    def stack(parts):
        return jnp.concatenate(parts, axis=0) if len(parts) > 1 else parts[0]

    for g in images:
        noisy = noisy_ref[g].astype(F32)
        for tap, (di, dj) in enumerate(tap_offsets()):
            patch[g, tap * ROWS12 : (tap + 1) * ROWS12, :] = shift_lanes(noisy, di, dj).astype(
                LOWTYPE
            )
    sums = []
    for g in images:
        wide = dot_tn(patch[g], stemw_ref[...])
        acc = jnp.zeros((8, C1), F32)
        for r in chunks:
            w = wide[r : r + CHUNK]
            v = (w[:, :C1] + w[:, C1 : 2 * C1]) + w[:, 2 * C1 :] + vec(0, C1)
            x0[g, r : r + CHUNK, :] = v
            acc += fold8(v)
        sums.append(acc)
    mean1, rstd1 = gn_stats(x0, total(sums), C1)
    gain1, shift1 = vec(1, C1), vec(2, C1)
    act_shift(x0, mean1, rstd1, gain1, shift1, a1, C1)

    wide = dot_nn(stack([dy_cat(a1, g, (0, 1, 2)) for g in images]), conv1_ref[...])
    sums = []
    for g in images:
        bias = vec(3) + vec(4) + tproj[pl.ds(step * group + g, 1), :]
        acc = jnp.zeros((8, mid), F32)
        for r in chunks:
            v = wide[g * PLACES + r : g * PLACES + r + CHUNK] + bias
            hid[g, r : r + CHUNK, :] = v
            acc += fold8(v)
        sums.append(acc)
    mean2, rstd2 = gn_stats(hid, total(sums), mid)
    gain2, shift2 = vec(5), vec(6)
    act_shift(hid, mean2, rstd2, gain2, shift2, a2, mid)

    wide = dot_nn(stack([dy_cat(a2, g, (0, 1, 2)) for g in images]), conv2_ref[...])
    low0 = stack([x0[g].astype(LOWTYPE) for g in images])
    wide = wide + dot_nn(low0, skip_ref[...])
    sums = []
    for g in images:
        acc = jnp.zeros((8, mid), F32)
        for r in chunks:
            v = wide[g * PLACES + r : g * PLACES + r + CHUNK] + vec(7)
            res[g, r : r + CHUNK, :] = v
            acc += fold8(v)
        sums.append(acc)
    mean3, rstd3 = gn_stats(res, total(sums), mid)
    gain3, shift3 = vec(8), vec(9)
    for g in images:
        for r in chunks:
            y = (res[g, r : r + CHUNK, :] - mean3[g : g + 1]) * rstd3[g : g + 1] * gain3 + shift3
            normed[g * PLACES + r : g * PLACES + r + CHUNK, :] = y.astype(LOWTYPE)

    wide = dot_nn(normed[...], qkv_ref[...])
    qkv[:, :mid] = (wide[:, :mid] + vec(10)).astype(LOWTYPE)
    qkv[:, mid : 2 * mid] = wide[:, mid : 2 * mid].astype(LOWTYPE)
    qkv[:, 2 * mid :] = (wide[:, 2 * mid :] + vec(11)).astype(LOWTYPE)
    scale = mid ** (-0.5)
    for g in images:
        rows = slice(g * PLACES, (g + 1) * PLACES)
        logits = dot_nt(qkv[rows, :mid], qkv[rows, mid : 2 * mid])
        for r in chunks:
            s = logits[r : r + CHUNK] * scale
            e = jnp.exp(s - jnp.max(s, axis=1, keepdims=True))
            p = e / jnp.sum(e, axis=1, keepdims=True)
            attn[g, r : r + CHUNK, :] = p
            plow[g, r : r + CHUNK, :] = p.astype(LOWTYPE)
        attl[rows, :] = dot_nn(plow[g], qkv[rows, 2 * mid :]).astype(LOWTYPE)
    wide = dot_nn(attl[...], outw_ref[...])
    for g in images:
        for r in chunks:
            rows = slice(g * PLACES + r, g * PLACES + r + CHUNK)
            o = res[g, r : r + CHUNK, :] + wide[rows] + vec(12)
            outp[g, r : r + CHUNK, :] = o
            joined[rows, :mid] = (o * sigmoid(o)).astype(LOWTYPE)
            x = x0[g, r : r + CHUNK, :]
            joined[rows, mid:] = (x * sigmoid(x)).astype(LOWTYPE)

    for g in images:
        rows = slice(g * PLACES, (g + 1) * PLACES)
        taps = dot_nt(headw_ref[...], joined[rows, :])
        head = headb_ref[:, :1] + jnp.zeros((ROWS12, PLACES), F32)
        for tap, (di, dj) in enumerate(tap_offsets()):
            head = head + shift_lanes(taps[tap * ROWS12 : (tap + 1) * ROWS12, :], di, dj)
        error = head - noise_ref[g]
        masked = maskw_ref[g] * error
        loss_ref[...] += masked * error
        grad = 2.0 * masked
        ghb_ref[...] += grad
        gradl = grad.astype(LOWTYPE).astype(F32)
        dtap = jnp.concatenate(
            [shift_lanes(gradl, -di, -dj).astype(LOWTYPE) for di, dj in tap_offsets()], axis=0
        )
        ghead_ref[...] += dot_nn(dtap, joined[rows, :])
        wide = dot_tn(dtap, headw_ref[...])
        acc = jnp.zeros((8, mid), F32)
        for r in chunks:
            o = outp[g, r : r + CHUNK, :]
            s = sigmoid(o)
            d = wide[r : r + CHUNK, :mid] * (s * (1.0 + o * (1.0 - s)))
            outp[g, r : r + CHUNK, :] = d
            dout[g * PLACES + r : g * PLACES + r + CHUNK, :] = d.astype(LOWTYPE)
            acc += fold8(d)
            x = x0[g, r : r + CHUNK, :]
            s = sigmoid(x)
            dpool[g, r : r + CHUNK, :] = wide[r : r + CHUNK, mid:] * (s * (1.0 + x * (1.0 - s)))
        add_vec(12, jnp.sum(acc, axis=0, keepdims=True))

    lowt = dout[...].T
    acc_ref[:, SEG_OFF[7] : SEG_OFF[8]] += dot_nn(lowt, attl[...])
    datt = dot_nt(dout[...], outw_ref[...]).astype(LOWTYPE)
    for g in images:
        rows = slice(g * PLACES, (g + 1) * PLACES)
        datt_g = datt[rows]
        gweights = dot_nt(datt_g, qkv[rows, 2 * mid :])
        dval = dot_tn(plow[g], datt_g)
        for r in chunks:
            p = attn[g, r : r + CHUNK, :]
            gw = gweights[r : r + CHUNK]
            ds = p * (gw - jnp.sum(gw * p, axis=1, keepdims=True))
            plow[g, r : r + CHUNK, :] = (ds * scale).astype(LOWTYPE)
        dqry = dot_nn(plow[g], qkv[rows, mid : 2 * mid])
        dkey = dot_tn(plow[g], qkv[rows, :mid])
        add_vec(10, jnp.sum(fold8(dqry), axis=0, keepdims=True))
        add_vec(11, jnp.sum(fold8(dval), axis=0, keepdims=True))
        dq3[rows, :mid] = dqry.astype(LOWTYPE)
        dq3[rows, mid : 2 * mid] = dkey.astype(LOWTYPE)
        dq3[rows, 2 * mid :] = dval.astype(LOWTYPE)
    for k in range(3):
        lowt = dq3[:, k * mid : (k + 1) * mid].T
        acc_ref[:, SEG_OFF[4 + k] : SEG_OFF[5 + k]] += dot_nn(lowt, normed[...])
    wide = dot_nt(dq3[...], qkv_ref[...])

    ones, twos = [], []
    for g in images:
        one, two = jnp.zeros((8, mid), F32), jnp.zeros((8, mid), F32)
        for r in chunks:
            xh = (res[g, r : r + CHUNK, :] - mean3[g : g + 1]) * rstd3[g : g + 1]
            d = wide[g * PLACES + r : g * PLACES + r + CHUNK]
            res[g, r : r + CHUNK, :] = xh
            dyf[g, r : r + CHUNK, :] = d
            one += fold8(d)
            two += fold8(d * xh)
        ones.append(one)
        twos.append(two)
    ones, twos = total(ones), total(twos)
    add_vec(9, jnp.sum(ones, axis=0, keepdims=True))
    add_vec(8, jnp.sum(twos, axis=0, keepdims=True))
    m1, m2 = grouped(ones * gain3, mid), grouped(twos * gain3, mid)
    for g in images:
        r1 = rstd3[g : g + 1]
        acc = jnp.zeros((8, mid), F32)
        for r in chunks:
            d = dyf[g, r : r + CHUNK, :] * (gain3 * r1)
            d = d - m1[g : g + 1] * r1 - res[g, r : r + CHUNK, :] * (m2[g : g + 1] * r1)
            d = d + outp[g, r : r + CHUNK, :]
            acc += fold8(d)
            pad2[g, SIDE + r : SIDE + r + CHUNK, :] = d.astype(LOWTYPE)
        add_vec(7, jnp.sum(acc, axis=0, keepdims=True))

    low = stack([pad2[g, SIDE : SIDE + PLACES, :] for g in images])
    lowt = low.T
    acc_ref[:, SEG_OFF[2] : SEG_OFF[3]] += dot_nn(lowt, low0)
    acc_ref[:, SEG_OFF[1] : SEG_OFF[2]] += dot_nn(
        lowt, stack([dy_cat(a2, g, (0, 1, 2)) for g in images])
    )
    dskip = dot_nt(low, skip_ref[...])
    for g in images:
        dpool[g] += dskip[g * PLACES : (g + 1) * PLACES]

    def conv_back(pad, weights, g, chans, apply):
        wide = dot_nt(dy_cat(pad, g, (2, 1, 0)), weights)
        shiftf[g, 8 : 8 + PLACES, :chans] = wide[:, :chans]
        dyf[g, :, :chans] = wide[:, chans : 2 * chans]
        for r in chunks:
            after = shiftf[g, 9 + r : 9 + r + CHUNK, :chans]
            dyf[g, r : r + CHUNK, :chans] += jnp.where(edge(chans, False), after, 0.0)
        shiftf[g, 8 : 8 + PLACES, :chans] = wide[:, 2 * chans :]
        for r in chunks:
            before = shiftf[g, 7 + r : 7 + r + CHUNK, :chans]
            apply(r, dyf[g, r : r + CHUNK, :chans] + jnp.where(edge(chans, True), before, 0.0))

    def norm_back(pad, weights, ref, mean, rstd, gain, shift, chans):
        ones, twos = [], []
        for g in images:
            sums = [jnp.zeros((8, chans), F32), jnp.zeros((8, chans), F32)]

            def apply(r, da, g=g, sums=sums):
                xh = (ref[g, r : r + CHUNK, :] - mean[g : g + 1]) * rstd[g : g + 1]
                y = xh * gain + shift
                s = sigmoid(y)
                d = da * (s * (1.0 + y * (1.0 - s)))
                ref[g, r : r + CHUNK, :] = xh
                dyf[g, r : r + CHUNK, :chans] = d
                sums[0] += fold8(d)
                sums[1] += fold8(d * xh)

            conv_back(pad, weights, g, chans, apply)
            ones.append(sums[0])
            twos.append(sums[1])
        ones, twos = total(ones), total(twos)
        m1, m2 = grouped(ones * gain, chans), grouped(twos * gain, chans)
        return jnp.sum(ones, axis=0, keepdims=True), jnp.sum(twos, axis=0, keepdims=True), m1, m2

    one, two, m1, m2 = norm_back(pad2, conv2b_ref[...], hid, mean2, rstd2, gain2, shift2, mid)
    add_vec(6, one)
    add_vec(5, two)
    for g in images:
        r1 = rstd2[g : g + 1]
        acc = jnp.zeros((8, mid), F32)
        for r in chunks:
            d = dyf[g, r : r + CHUNK, :] * (gain2 * r1)
            d = d - m1[g : g + 1] * r1 - hid[g, r : r + CHUNK, :] * (m2[g : g + 1] * r1)
            acc += fold8(d)
            pad1[g, SIDE + r : SIDE + r + CHUNK, :] = d.astype(LOWTYPE)
        acc = jnp.sum(acc, axis=0, keepdims=True)
        add_vec(3, acc)
        add_vec(4, acc)
        gtime[pl.ds(step * group + g, 1), :] = acc

    lowt = stack([pad1[g, SIDE : SIDE + PLACES, :] for g in images]).T
    acc_ref[:, SEG_OFF[0] : SEG_OFF[1]] += dot_nn(
        lowt, stack([dy_cat(a1, g, (0, 1, 2)) for g in images])
    )
    one, two, m1, m2 = norm_back(pad1, conv1b_ref[...], x0, mean1, rstd1, gain1, shift1, C1)
    add_vec(2, one)
    add_vec(1, two)
    for g in images:
        r1 = rstd1[g : g + 1]
        acc = jnp.zeros((8, C1), F32)
        lows = []
        for r in chunks:
            d = dyf[g, r : r + CHUNK, :C1] * (gain1 * r1)
            d = d - m1[g : g + 1] * r1 - x0[g, r : r + CHUNK, :] * (m2[g : g + 1] * r1)
            d = d + dpool[g, r : r + CHUNK, :]
            acc += fold8(d)
            lows.append(d.astype(LOWTYPE))
        add_vec(0, jnp.sum(acc, axis=0, keepdims=True))
        gstem_ref[...] += dot_nn(patch[g], stack(lows))

    @pl.when(step == steps - 1)
    def _():
        acc_ref[:, SEG_OFF[3] : SEG_OFF[4]] = dot_tn(gtime[...].astype(LOWTYPE), time_ref[...])


def unet_call(samples, operands):
    group = 2 if samples % 2 == 0 else 1
    steps = samples // group
    time_rows = operands[3].shape[0]
    mid = CHANNELS_MID
    places = group * PLACES

    def image_spec():
        return pl.BlockSpec((group, ROWS12, PLACES), lambda i: (i, 0, 0))

    def whole(shape):
        return pl.BlockSpec(shape, lambda i: (0,) * len(shape))

    out_shapes = [(mid, 5120), (TAPS * ROWS12, C1), (TAPS * ROWS12, mid + C1)] + [
        (ROWS12, mid)
    ] * 3
    scratch = [
        ((group, PLACES, C1), F32),
        ((group, PLACES, mid), F32),
        ((group, PLACES, mid), F32),
        ((group, PLACES, mid), F32),
        ((group, PLACES, mid), F32),
        ((group, HALO, 3 * C1), LOWTYPE),
        ((group, HALO, 3 * mid), LOWTYPE),
        ((places, mid), LOWTYPE),
        ((places, 3 * mid), LOWTYPE),
        ((group, PLACES, mid), LOWTYPE),
        ((places, mid), LOWTYPE),
        ((places, mid + C1), LOWTYPE),
        ((group, TAPS * ROWS12, PLACES), LOWTYPE),
        ((group, HALO, mid), LOWTYPE),
        ((group, HALO, mid), LOWTYPE),
        ((group, PLACES + 16, mid), F32),
        ((group, PLACES, mid), F32),
        ((places, mid), LOWTYPE),
        ((places, 3 * mid), LOWTYPE),
        ((group, PLACES, C1), F32),
        ((time_rows, mid), F32),
        ((time_rows, mid), F32),
    ]
    return pl.pallas_call(
        functools.partial(unet_body, group, steps),
        grid=(steps,),
        out_shape=[jax.ShapeDtypeStruct(shape, F32) for shape in out_shapes],
        in_specs=[image_spec()] * 3 + [whole(a.shape) for a in operands[3:]],
        out_specs=[whole(shape) for shape in out_shapes],
        scratch_shapes=[pltpu.VMEM(shape, kind) for shape, kind in scratch],
        compiler_params=pltpu.CompilerParams(vmem_limit_bytes=VMEM_BYTES),
    )(*operands)


def phase_order():
    pixel = np.arange(S * S)
    row, col = pixel // S, pixel % S
    lane = (row % 2 * 2 + col % 2) * PLACES + row // 2 * SIDE + col // 2
    return jnp.asarray(lane, jnp.int32)


def stem_spread():
    counts = np.zeros((3, 2, 3))
    for block in range(3):
        for inner in range(2):
            for sub in range(2):
                tap = 2 * (block - 1) + inner - sub + 1
                if 0 <= tap <= 2:
                    counts[block, inner, tap] += 1
    full = np.zeros((3, 3, 4, 4, 3, 3, 3))
    for c in range(3):
        both = np.einsum("ayt,bxu->abyxtu", counts, counts) * 0.25
        full[:, :, c, :, :, :, c] = both.reshape(3, 3, 4, 3, 3)
    return jnp.asarray(full.reshape(TAPS * ROWS12, 27), F32)


def split_three(values):
    first = lax.reduce_precision(values, 8, 7)
    second = lax.reduce_precision(values - first, 8, 7)
    third = values - first - second
    return jnp.concatenate([first, second, third], axis=1).astype(LOWTYPE)


def pad_rows(values, rows):
    return jnp.pad(values, [(0, 0)] * (values.ndim - 2) + [(0, rows - values.shape[-2]), (0, 0)])


def by_column(weights, chans):
    return weights.reshape(3, 3 * chans, CHANNELS_MID).transpose(1, 0, 2).reshape(3 * chans, -1)


def same_group(chans):
    group = np.arange(chans) // (chans // GROUPS)
    same = (group[:, None] == group[None, :]) / (PLACES * (chans // GROUPS))
    return jnp.asarray(same, F32)


def ns_update(iterate, gram):
    inner = NS_B * gram + NS_C * jnp.dot(gram, gram, precision=EXACT_PRECISION)
    return NS_A * iterate + jnp.dot(iterate, inner, precision=EXACT_PRECISION)


def local_muon(weight_m, moment, gradient):
    moment_new = MOMENTUM * moment + gradient
    direction = gradient + MOMENTUM * moment_new
    iterate = direction * lax.rsqrt(jnp.sum(direction * direction) + NORM_EPS)
    for step in range(NS_STEPS):
        iterate = ns_update(iterate, jnp.dot(iterate.T, iterate, precision=EXACT_PRECISION))
    return (weight_m * (1.0 - LR_MUON * DECAY) - LR_MUON * iterate, moment_new)


def ns_product(gram):
    eye = jnp.eye(gram.shape[0], dtype=jnp.float32)
    product = None
    for step in range(NS_STEPS):
        square = jnp.dot(gram, gram, precision=EXACT_PRECISION)
        factor = NS_A * eye + NS_B * gram + NS_C * square
        product = (
            factor if product is None else jnp.dot(product, factor, precision=EXACT_PRECISION)
        )
        if step < NS_STEPS - 1:
            half = jnp.dot(gram, factor, precision=EXACT_PRECISION)
            gram = jnp.dot(factor, half, precision=EXACT_PRECISION)
    return product


def shards(
    images,
    pixel_mask,
    timesteps,
    noise_field,
    matrices,
    matrix_moms,
    stem_weight,
    stem_moms,
    head_weight,
    head_moms,
    vectors,
    vector_firsts,
    vector_seconds,
):
    owners = lax.axis_size("bucket")
    gathered = lax.all_gather(matrices.astype(LOWTYPE), "bucket", axis=0, tiled=True)
    conv_one, conv_two, skip_w, temb_w, query_w, key_w, value_w, out_w = unpack(gathered, owners)
    samples = images.shape[0]
    level, weight = plan(timesteps)
    counts = jnp.sum(pixel_mask.astype(jnp.float32), axis=1)
    weight_local = jnp.sum(3.0 * weight * counts)
    noisy = (
        jnp.sqrt(level)[:, None, None] * images + jnp.sqrt(1.0 - level)[:, None, None] * noise_field
    )
    mask_weight = pixel_mask.astype(jnp.float32) * weight[:, None]
    rows = jnp.concatenate(
        [
            lax.reduce_precision(noisy, 8, 7).reshape(-1, S * S),
            noise_field.reshape(-1, S * S),
            mask_weight,
        ],
        axis=0,
    )
    order = (phase_order()[:, None] == jnp.arange(S * S, dtype=jnp.int32)[None, :]).astype(F32)
    phased = jnp.dot(rows, order, precision=EXACT_PRECISION)
    planes = 3 * samples
    noisy_low = pad_rows(phased[:planes].reshape(samples, 12, PLACES), ROWS12).astype(LOWTYPE)
    noise_planes = pad_rows(phased[planes : 2 * planes].reshape(samples, 12, PLACES), ROWS12)
    mask_planes = jnp.broadcast_to(
        phased[2 * planes :].reshape(samples, 1, 4, PLACES), (samples, 3, 4, PLACES)
    ).reshape(samples, 12, PLACES)
    mask_planes = pad_rows(mask_planes, ROWS12)
    time_in = pad_rows(swish(embed(timesteps)).astype(LOWTYPE), -(-samples // 16) * 16)
    spread = stem_spread()
    stem_blocks = split_three(
        jnp.dot(spread, lax.reduce_precision(stem_weight, 8, 7), precision=EXACT_PRECISION)
    )
    head_rows = head_weight.astype(LOWTYPE).reshape(TAPS, CHANNELS_MID + C1, 4, 3)
    head_rows = pad_rows(
        head_rows.transpose(0, 3, 2, 1).reshape(TAPS, 12, CHANNELS_MID + C1), ROWS12
    ).reshape(TAPS * ROWS12, -1)
    vec_rows = jnp.concatenate(
        [
            jnp.pad(vectors[: 3 * C1].reshape(3, C1), ((0, 0), (0, CHANNELS_MID - C1))),
            vectors[3 * C1 : -12].reshape(10, CHANNELS_MID),
        ],
        axis=0,
    )
    head_bias = jnp.broadcast_to(
        pad_rows(vectors[-12:].reshape(4, 3).T.reshape(12, 1), ROWS12), (ROWS12, C1)
    )
    acc, gstem_rows, ghead_rows, gvec, ghead_bias, loss_rows = unet_call(
        samples,
        [
            noisy_low,
            noise_planes,
            mask_planes,
            time_in,
            stem_blocks,
            head_rows,
            conv_one,
            by_column(conv_one, C1),
            conv_two,
            by_column(conv_two, CHANNELS_MID),
            skip_w,
            temb_w,
            jnp.concatenate([query_w, key_w, value_w], axis=1),
            out_w,
            pad_rows(vec_rows, ROWS12),
            head_bias,
            same_group(C1),
            same_group(CHANNELS_MID),
        ],
    )
    loss_local = jnp.sum(loss_rows)
    g_stem = jnp.dot(spread.T, gstem_rows, precision=EXACT_PRECISION)
    g_head = (
        ghead_rows.reshape(TAPS, ROWS12, -1)[:, :12]
        .reshape(TAPS, 3, 4, CHANNELS_MID + C1)
        .transpose(0, 3, 2, 1)
        .reshape(-1, 12)
    )
    grad_vec = jnp.concatenate(
        [
            gvec[:3, :C1].reshape(-1),
            gvec[3:13].reshape(-1),
            jnp.sum(ghead_bias[:12], axis=1).reshape(3, 4).T.reshape(-1),
        ]
    )
    natural = acc.T
    grad_pack = pack([natural[a:b] for a, b in zip(SEG_OFF[:-1], SEG_OFF[1:])], owners)
    rows_dev = matrices.shape[0]
    summed, grad_stem, grad_headw, grad_vec, loss_sum, weight_sum = lax.psum(
        (grad_pack, g_stem, g_head, grad_vec, loss_local, weight_local), ("bucket", "batch")
    )
    inverse = 1.0 / weight_sum
    summed = summed * inverse
    grad_stem = grad_stem * inverse
    grad_headw = grad_headw * inverse
    grad_vec = grad_vec * inverse
    grad_mine = lax.dynamic_slice_in_dim(summed, lax.axis_index("bucket") * rows_dev, rows_dev, 0)
    shares = [seg_rows // owners for seg_rows in segment_rows()]
    weight_parts, moment_parts, grad_parts = ([], [], [])
    start = 0
    for share in shares:
        weight_parts.append(matrices[start : start + share])
        moment_parts.append(matrix_moms[start : start + share])
        grad_parts.append(grad_mine[start : start + share])
        start += share
    moments_new = [
        MOMENTUM * moment + gradient for moment, gradient in zip(moment_parts, grad_parts)
    ]
    directions = [gradient + MOMENTUM * moment for gradient, moment in zip(grad_parts, moments_new)]
    gram_sums = lax.psum(
        tuple(jnp.dot(d.T, d, precision=EXACT_PRECISION) for d in directions), "bucket"
    )
    iterates = []
    for direction, gram in zip(directions, gram_sums):
        scale = lax.rsqrt(jnp.trace(gram) + NORM_EPS)
        iterates.append(
            jnp.dot(direction * scale, ns_product(gram * (scale * scale)), precision=EXACT_PRECISION)
        )
    new_matrices = jnp.concatenate(
        [
            weight_m * (1.0 - LR_MUON * DECAY) - LR_MUON * iterate
            for weight_m, iterate in zip(weight_parts, iterates)
        ],
        axis=0,
    )
    new_matrix_moms = jnp.concatenate(moments_new, axis=0)
    new_stem, new_stem_moms = local_muon(stem_weight, stem_moms, grad_stem)
    new_head, new_head_moms = local_muon(head_weight, head_moms, grad_headw)
    new_firsts = BETA_ONE * vector_firsts + (1.0 - BETA_ONE) * grad_vec
    new_seconds = BETA_TWO * vector_seconds + (1.0 - BETA_TWO) * grad_vec * grad_vec
    step_dir = (
        new_firsts
        / (1.0 - BETA_ONE**STEP)
        / (jnp.sqrt(new_seconds / (1.0 - BETA_TWO**STEP)) + ADAM_EPS)
    )
    new_vectors = vectors - LR_ADAM * step_dir
    return (
        loss_sum,
        weight_sum,
        new_matrices,
        new_matrix_moms,
        new_matrices.astype(LOWTYPE),
        new_stem,
        new_stem_moms,
        new_stem.astype(LOWTYPE),
        new_head,
        new_head_moms,
        new_head.astype(LOWTYPE),
        new_vectors,
        new_firsts,
        new_seconds,
        new_vectors.astype(LOWTYPE),
    )


def solution(mesh):
    return jax.shard_map(
        shards,
        mesh=mesh,
        in_specs=(
            P(("bucket", "batch"), None, None),
            P(("bucket", "batch"), None),
            P(("bucket", "batch")),
            P(("bucket", "batch"), None, None),
            P("bucket", None),
            P("bucket", None),
            P(),
            P(),
            P(),
            P(),
            P(),
            P(),
            P(),
        ),
        out_specs=(
            P(),
            P(),
            P("bucket", None),
            P("bucket", None),
            P("bucket", None),
            P(),
            P(),
            P(),
            P(),
            P(),
            P(),
            P(),
            P(),
            P(),
            P(),
        ),
        check_vma=False,
    )
```

```python
import functools
import math

import jax
import jax.numpy as jnp
import numpy as np
from jax import lax
from jax.experimental import pallas as pl
from jax.experimental.pallas import tpu as pltpu
from jax.sharding import PartitionSpec as P

C1 = 128
CHANNELS_MID = 256
TEMB = 512
GROUPS = 32
S = 32
TSTEPS = 1000
NS_STEPS = 5
STEP = 10


GN_EPS = 1e-05
NORM_EPS = 1e-12
MOMENTUM = 0.95
LR_MUON = 0.5
DECAY = 0.01
NS_A = 3.4445
NS_B = -4.775
NS_C = 2.0315
BETA_ONE = 0.9
BETA_TWO = 0.999
LR_ADAM = 0.5
ADAM_EPS = 1e-08
EXACT_PRECISION = lax.Precision.HIGHEST
LOWTYPE = jnp.bfloat16


def segment_rows():
    return [
        9 * C1,
        9 * CHANNELS_MID,
        C1,
        TEMB,
        CHANNELS_MID,
        CHANNELS_MID,
        CHANNELS_MID,
        CHANNELS_MID,
    ]


def unpack(packed, owners):
    blocks = packed.reshape(owners, -1, packed.shape[1])
    pieces = []
    start = 0
    for seg_rows in segment_rows():
        share = seg_rows // owners
        pieces.append(blocks[:, start : start + share, :].reshape(seg_rows, packed.shape[1]))
        start += share
    return pieces


def plan(timesteps):
    frac_t = (timesteps.astype(jnp.float32) / TSTEPS + 0.008) / 1.008
    level = jnp.cos(frac_t * (math.pi / 2)) ** 2
    ratio = level / (1.0 - level)
    return (level, jnp.minimum(1.0, 5.0 / ratio))


def embed(timesteps):
    half_width = TEMB // 2
    freqs = jnp.exp(-math.log(10000.0) * jnp.arange(half_width, dtype=jnp.float32) / half_width)
    angles = timesteps.astype(jnp.float32)[:, None] * freqs[None, :]
    return jnp.concatenate([jnp.sin(angles), jnp.cos(angles)], axis=1)


def swish(values):
    return values * jax.nn.sigmoid(values)


F32 = jnp.float32
PLACES = 256
SIDE = 16
HALO = 288
TAPS = 9
ROWS12 = 16
CHUNK = 64
SMALL_ROWS = 240
VMEM_BYTES = 56 * 1024 * 1024
SEG_OFF = (0, 1152, 3456, 3584, 4096, 4352, 4608, 4864, 5120)


def dot_nn(a, b, precision=None):
    return lax.dot_general(
        a, b, (((1,), (0,)), ((), ())), preferred_element_type=F32, precision=precision
    )


def dot_nt(a, b):
    return lax.dot_general(a, b, (((1,), (1,)), ((), ())), preferred_element_type=F32)


def dot_tn(a, b):
    return lax.dot_general(a, b, (((0,), (0,)), ((), ())), preferred_element_type=F32)


def sigmoid(v):
    return 1.0 / (1.0 + jnp.exp(-v))


def fold8(v):
    rows, chans = v.shape
    return jnp.sum(v.reshape(rows // 8, 8, chans), axis=0)


def shift_lanes(x, di, dj):
    lane = lax.broadcasted_iota(jnp.int32, x.shape, 1)
    row, col = lane // SIDE + di, lane % SIDE + dj
    offset = (-(SIDE * di + dj)) % PLACES
    moved = x if offset == 0 else pltpu.roll(x, offset, 1)
    valid = (row >= 0) & (row < SIDE) & (col >= 0) & (col < SIDE)
    return jnp.where(valid, moved, 0.0)


def tap_offsets():
    return [(di, dj) for di in (-1, 0, 1) for dj in (-1, 0, 1)]


def unet_body(
    group,
    steps,
    owners,
    peers,
    noisy_ref,
    noise_ref,
    maskw_ref,
    time_ref,
    stemw_ref,
    headw_ref,
    conv1_ref,
    conv1b_ref,
    conv2_ref,
    conv2b_ref,
    skip_ref,
    temb_ref,
    qkv_ref,
    outw_ref,
    vec_ref,
    headb_ref,
    same128_ref,
    same256_ref,
    spread_ref,
    rows_ref,
    misc_ref,
    acc_ref,
    gstem_ref,
    ghead_ref,
    gvec_ref,
    ghb_ref,
    loss_ref,
    wsum_ref,
    x0,
    hid,
    res,
    outp,
    attn,
    a1,
    a2,
    normed,
    qkv,
    plow,
    attl,
    joined,
    patch,
    pad1,
    pad2,
    shiftf,
    dyf,
    dout,
    dq3,
    dpool,
    tproj,
    gtime,
):
    step = pl.program_id(0)
    mid = CHANNELS_MID
    chunks = range(0, PLACES, CHUNK)
    images = range(group)

    @pl.when(step == 0)
    def _():
        acc_ref[...] = jnp.zeros_like(acc_ref)
        gstem_ref[...] = jnp.zeros_like(gstem_ref)
        ghead_ref[...] = jnp.zeros_like(ghead_ref)
        gvec_ref[...] = jnp.zeros_like(gvec_ref)
        ghb_ref[...] = jnp.zeros_like(ghb_ref)
        loss_ref[...] = jnp.zeros_like(loss_ref)
        wsum_ref[...] = jnp.zeros_like(wsum_ref)
        gtime[...] = jnp.zeros_like(gtime)
        for ref in (a1, a2, pad1, pad2):
            for g in images:
                ref[g, :SIDE, :] = jnp.zeros((SIDE, ref.shape[2]), ref.dtype)
                ref[g, HALO - SIDE :, :] = jnp.zeros((SIDE, ref.shape[2]), ref.dtype)
        shiftf[...] = jnp.zeros_like(shiftf)
        tproj[...] = dot_nn(time_ref[...], temb_ref[...])

    def vec(row, chans=mid):
        if chans == C1:
            return vec_ref[row : row + 1, :]
        row = 2 * row - 3
        return jnp.concatenate([vec_ref[row : row + 1, :], vec_ref[row + 1 : row + 2, :]], axis=1)

    def add_vec(row, value):
        gvec_ref[row : row + 1, : value.shape[1]] += value

    def total(parts):
        return jnp.concatenate([jnp.sum(p, axis=0, keepdims=True) for p in parts], axis=0)

    def grouped(stats, chans):
        same = same128_ref if chans == C1 else same256_ref
        return dot_nn(stats, same[...], precision=EXACT_PRECISION)

    def gn_stats(ref, sums, chans):
        mean = grouped(sums, chans)
        parts = []
        for g in images:
            acc = jnp.zeros((8, chans), F32)
            for r in chunks:
                c = ref[g, r : r + CHUNK, :] - mean[g : g + 1]
                acc += fold8(c * c)
            parts.append(acc)
        return mean, lax.rsqrt(grouped(total(parts), chans) + GN_EPS)

    def edge(chans, left):
        col = lax.broadcasted_iota(jnp.int32, (CHUNK, chans), 0) % SIDE
        return (col > 0) if left else (col < SIDE - 1)

    def act_shift(ref, mean, rstd, gain, shift, dest, chans):
        for g in images:
            for r in chunks:
                y = (ref[g, r : r + CHUNK, :] - mean[g : g + 1]) * rstd[g : g + 1] * gain + shift
                a = y * sigmoid(y)
                shiftf[g, 8 + r : 8 + r + CHUNK, :chans] = a
                dest[g, SIDE + r : SIDE + r + CHUNK, chans : 2 * chans] = a.astype(LOWTYPE)
            for r in chunks:
                before = shiftf[g, 7 + r : 7 + r + CHUNK, :chans]
                after = shiftf[g, 9 + r : 9 + r + CHUNK, :chans]
                rows = slice(SIDE + r, SIDE + r + CHUNK)
                dest[g, rows, :chans] = jnp.where(edge(chans, True), before, 0.0).astype(LOWTYPE)
                dest[g, rows, 2 * chans :] = jnp.where(edge(chans, False), after, 0.0).astype(
                    LOWTYPE
                )

    def dy_cat(ref, g, order):
        return jnp.concatenate(
            [ref[g, SIDE * k : SIDE * k + PLACES, :] for k in order], axis=1
        )

    def stack(parts):
        return jnp.concatenate(parts, axis=0) if len(parts) > 1 else parts[0]

    for g in images:
        noisy = noisy_ref[g].astype(F32)
        for tap, (di, dj) in enumerate(tap_offsets()):
            patch[g, tap * ROWS12 : (tap + 1) * ROWS12, :] = shift_lanes(noisy, di, dj).astype(
                LOWTYPE
            )
    sums = []
    for g in images:
        wide = dot_tn(patch[g], stemw_ref[...])
        acc = jnp.zeros((8, C1), F32)
        for r in chunks:
            w = wide[r : r + CHUNK]
            v = (w[:, :C1] + w[:, C1 : 2 * C1]) + w[:, 2 * C1 :] + vec(0, C1)
            x0[g, r : r + CHUNK, :] = v
            acc += fold8(v)
        sums.append(acc)
    mean1, rstd1 = gn_stats(x0, total(sums), C1)
    gain1, shift1 = vec(1, C1), vec(2, C1)
    act_shift(x0, mean1, rstd1, gain1, shift1, a1, C1)

    wide = dot_nn(stack([dy_cat(a1, g, (0, 1, 2)) for g in images]), conv1_ref[...])
    sums = []
    for g in images:
        bias = vec(3) + vec(4) + tproj[pl.ds(step * group + g, 1), :]
        acc = jnp.zeros((8, mid), F32)
        for r in chunks:
            v = wide[g * PLACES + r : g * PLACES + r + CHUNK] + bias
            hid[g, r : r + CHUNK, :] = v
            acc += fold8(v)
        sums.append(acc)
    mean2, rstd2 = gn_stats(hid, total(sums), mid)
    gain2, shift2 = vec(5), vec(6)
    act_shift(hid, mean2, rstd2, gain2, shift2, a2, mid)

    wide = dot_nn(stack([dy_cat(a2, g, (0, 1, 2)) for g in images]), conv2_ref[...])
    low0 = stack([x0[g].astype(LOWTYPE) for g in images])
    wide = wide + dot_nn(low0, skip_ref[...])
    sums = []
    for g in images:
        acc = jnp.zeros((8, mid), F32)
        for r in chunks:
            v = wide[g * PLACES + r : g * PLACES + r + CHUNK] + vec(7)
            res[g, r : r + CHUNK, :] = v
            acc += fold8(v)
        sums.append(acc)
    mean3, rstd3 = gn_stats(res, total(sums), mid)
    gain3, shift3 = vec(8), vec(9)
    for g in images:
        for r in chunks:
            y = (res[g, r : r + CHUNK, :] - mean3[g : g + 1]) * rstd3[g : g + 1] * gain3 + shift3
            normed[g * PLACES + r : g * PLACES + r + CHUNK, :] = y.astype(LOWTYPE)

    wide = dot_nn(normed[...], qkv_ref[...])
    qkv[:, :mid] = (wide[:, :mid] + vec(10)).astype(LOWTYPE)
    qkv[:, mid : 2 * mid] = wide[:, mid : 2 * mid].astype(LOWTYPE)
    qkv[:, 2 * mid :] = (wide[:, 2 * mid :] + vec(11)).astype(LOWTYPE)
    scale = mid ** (-0.5)
    for g in images:
        rows = slice(g * PLACES, (g + 1) * PLACES)
        logits = dot_nt(qkv[rows, :mid], qkv[rows, mid : 2 * mid])
        for r in chunks:
            s = logits[r : r + CHUNK] * scale
            e = jnp.exp(s - jnp.max(s, axis=1, keepdims=True))
            p = e / jnp.sum(e, axis=1, keepdims=True)
            attn[g, r : r + CHUNK, :] = p
            plow[g, r : r + CHUNK, :] = p.astype(LOWTYPE)
        attl[rows, :] = dot_nn(plow[g], qkv[rows, 2 * mid :]).astype(LOWTYPE)
    wide = dot_nn(attl[...], outw_ref[...])
    for g in images:
        for r in chunks:
            rows = slice(g * PLACES + r, g * PLACES + r + CHUNK)
            o = res[g, r : r + CHUNK, :] + wide[rows] + vec(12)
            outp[g, r : r + CHUNK, :] = o
            joined[rows, :mid] = (o * sigmoid(o)).astype(LOWTYPE)
            x = x0[g, r : r + CHUNK, :]
            joined[rows, mid:] = (x * sigmoid(x)).astype(LOWTYPE)

    for g in images:
        rows = slice(g * PLACES, (g + 1) * PLACES)
        taps = dot_nt(headw_ref[...], joined[rows, :])
        head = headb_ref[:, :1] + jnp.zeros((ROWS12, PLACES), F32)
        for tap, (di, dj) in enumerate(tap_offsets()):
            head = head + shift_lanes(taps[tap * ROWS12 : (tap + 1) * ROWS12, :], di, dj)
        error = head - noise_ref[g]
        masked = maskw_ref[g] * error
        loss_ref[...] += masked * error
        wsum_ref[...] += maskw_ref[g]
        grad = 2.0 * masked
        ghb_ref[...] += grad
        gradl = grad.astype(LOWTYPE).astype(F32)
        dtap = jnp.concatenate(
            [shift_lanes(gradl, -di, -dj).astype(LOWTYPE) for di, dj in tap_offsets()], axis=0
        )
        ghead_ref[...] += dot_nn(dtap, joined[rows, :])
        wide = dot_tn(dtap, headw_ref[...])
        acc = jnp.zeros((8, mid), F32)
        for r in chunks:
            o = outp[g, r : r + CHUNK, :]
            s = sigmoid(o)
            d = wide[r : r + CHUNK, :mid] * (s * (1.0 + o * (1.0 - s)))
            outp[g, r : r + CHUNK, :] = d
            dout[g * PLACES + r : g * PLACES + r + CHUNK, :] = d.astype(LOWTYPE)
            acc += fold8(d)
            x = x0[g, r : r + CHUNK, :]
            s = sigmoid(x)
            dpool[g, r : r + CHUNK, :] = wide[r : r + CHUNK, mid:] * (s * (1.0 + x * (1.0 - s)))
        add_vec(12, jnp.sum(acc, axis=0, keepdims=True))

    lowt = dout[...].T
    acc_ref[:, SEG_OFF[7] : SEG_OFF[8]] += dot_nn(lowt, attl[...])
    datt = dot_nt(dout[...], outw_ref[...]).astype(LOWTYPE)
    for g in images:
        rows = slice(g * PLACES, (g + 1) * PLACES)
        datt_g = datt[rows]
        gweights = dot_nt(datt_g, qkv[rows, 2 * mid :])
        dval = dot_tn(plow[g], datt_g)
        for r in chunks:
            p = attn[g, r : r + CHUNK, :]
            gw = gweights[r : r + CHUNK]
            ds = p * (gw - jnp.sum(gw * p, axis=1, keepdims=True))
            plow[g, r : r + CHUNK, :] = (ds * scale).astype(LOWTYPE)
        dqry = dot_nn(plow[g], qkv[rows, mid : 2 * mid])
        dkey = dot_tn(plow[g], qkv[rows, :mid])
        add_vec(10, jnp.sum(fold8(dqry), axis=0, keepdims=True))
        add_vec(11, jnp.sum(fold8(dval), axis=0, keepdims=True))
        dq3[rows, :mid] = dqry.astype(LOWTYPE)
        dq3[rows, mid : 2 * mid] = dkey.astype(LOWTYPE)
        dq3[rows, 2 * mid :] = dval.astype(LOWTYPE)
    for k in range(3):
        lowt = dq3[:, k * mid : (k + 1) * mid].T
        acc_ref[:, SEG_OFF[4 + k] : SEG_OFF[5 + k]] += dot_nn(lowt, normed[...])
    wide = dot_nt(dq3[...], qkv_ref[...])

    ones, twos = [], []
    for g in images:
        one, two = jnp.zeros((8, mid), F32), jnp.zeros((8, mid), F32)
        for r in chunks:
            xh = (res[g, r : r + CHUNK, :] - mean3[g : g + 1]) * rstd3[g : g + 1]
            d = wide[g * PLACES + r : g * PLACES + r + CHUNK]
            res[g, r : r + CHUNK, :] = xh
            dyf[g, r : r + CHUNK, :] = d
            one += fold8(d)
            two += fold8(d * xh)
        ones.append(one)
        twos.append(two)
    ones, twos = total(ones), total(twos)
    add_vec(9, jnp.sum(ones, axis=0, keepdims=True))
    add_vec(8, jnp.sum(twos, axis=0, keepdims=True))
    m1, m2 = grouped(ones * gain3, mid), grouped(twos * gain3, mid)
    for g in images:
        r1 = rstd3[g : g + 1]
        acc = jnp.zeros((8, mid), F32)
        for r in chunks:
            d = dyf[g, r : r + CHUNK, :] * (gain3 * r1)
            d = d - m1[g : g + 1] * r1 - res[g, r : r + CHUNK, :] * (m2[g : g + 1] * r1)
            d = d + outp[g, r : r + CHUNK, :]
            acc += fold8(d)
            pad2[g, SIDE + r : SIDE + r + CHUNK, :] = d.astype(LOWTYPE)
        add_vec(7, jnp.sum(acc, axis=0, keepdims=True))

    low = stack([pad2[g, SIDE : SIDE + PLACES, :] for g in images])
    lowt = low.T
    acc_ref[:, SEG_OFF[2] : SEG_OFF[3]] += dot_nn(lowt, low0)
    acc_ref[:, SEG_OFF[1] : SEG_OFF[2]] += dot_nn(
        lowt, stack([dy_cat(a2, g, (0, 1, 2)) for g in images])
    )
    dskip = dot_nt(low, skip_ref[...])
    for g in images:
        dpool[g] += dskip[g * PLACES : (g + 1) * PLACES]

    def conv_back(pad, weights, g, chans, apply):
        wide = dot_nt(dy_cat(pad, g, (2, 1, 0)), weights)
        shiftf[g, 8 : 8 + PLACES, :chans] = wide[:, :chans]
        dyf[g, :, :chans] = wide[:, chans : 2 * chans]
        for r in chunks:
            after = shiftf[g, 9 + r : 9 + r + CHUNK, :chans]
            dyf[g, r : r + CHUNK, :chans] += jnp.where(edge(chans, False), after, 0.0)
        shiftf[g, 8 : 8 + PLACES, :chans] = wide[:, 2 * chans :]
        for r in chunks:
            before = shiftf[g, 7 + r : 7 + r + CHUNK, :chans]
            apply(r, dyf[g, r : r + CHUNK, :chans] + jnp.where(edge(chans, True), before, 0.0))

    def norm_back(pad, weights, ref, mean, rstd, gain, shift, chans):
        ones, twos = [], []
        for g in images:
            sums = [jnp.zeros((8, chans), F32), jnp.zeros((8, chans), F32)]

            def apply(r, da, g=g, sums=sums):
                xh = (ref[g, r : r + CHUNK, :] - mean[g : g + 1]) * rstd[g : g + 1]
                y = xh * gain + shift
                s = sigmoid(y)
                d = da * (s * (1.0 + y * (1.0 - s)))
                ref[g, r : r + CHUNK, :] = xh
                dyf[g, r : r + CHUNK, :chans] = d
                sums[0] += fold8(d)
                sums[1] += fold8(d * xh)

            conv_back(pad, weights, g, chans, apply)
            ones.append(sums[0])
            twos.append(sums[1])
        ones, twos = total(ones), total(twos)
        m1, m2 = grouped(ones * gain, chans), grouped(twos * gain, chans)
        return jnp.sum(ones, axis=0, keepdims=True), jnp.sum(twos, axis=0, keepdims=True), m1, m2

    one, two, m1, m2 = norm_back(pad2, conv2b_ref[...], hid, mean2, rstd2, gain2, shift2, mid)
    add_vec(6, one)
    add_vec(5, two)
    for g in images:
        r1 = rstd2[g : g + 1]
        acc = jnp.zeros((8, mid), F32)
        for r in chunks:
            d = dyf[g, r : r + CHUNK, :] * (gain2 * r1)
            d = d - m1[g : g + 1] * r1 - hid[g, r : r + CHUNK, :] * (m2[g : g + 1] * r1)
            acc += fold8(d)
            pad1[g, SIDE + r : SIDE + r + CHUNK, :] = d.astype(LOWTYPE)
        acc = jnp.sum(acc, axis=0, keepdims=True)
        add_vec(3, acc)
        add_vec(4, acc)
        gtime[pl.ds(step * group + g, 1), :] = acc

    lowt = stack([pad1[g, SIDE : SIDE + PLACES, :] for g in images]).T
    acc_ref[:, SEG_OFF[0] : SEG_OFF[1]] += dot_nn(
        lowt, stack([dy_cat(a1, g, (0, 1, 2)) for g in images])
    )
    one, two, m1, m2 = norm_back(pad1, conv1b_ref[...], x0, mean1, rstd1, gain1, shift1, C1)
    add_vec(2, one)
    add_vec(1, two)
    for g in images:
        r1 = rstd1[g : g + 1]
        acc = jnp.zeros((8, C1), F32)
        lows = []
        for r in chunks:
            d = dyf[g, r : r + CHUNK, :C1] * (gain1 * r1)
            d = d - m1[g : g + 1] * r1 - x0[g, r : r + CHUNK, :] * (m2[g : g + 1] * r1)
            d = d + dpool[g, r : r + CHUNK, :]
            acc += fold8(d)
            lows.append(d.astype(LOWTYPE))
        add_vec(0, jnp.sum(acc, axis=0, keepdims=True))
        gstem_ref[...] += dot_nn(patch[g], stack(lows))

    @pl.when(step == steps - 1)
    def _():
        acc_ref[:, SEG_OFF[3] : SEG_OFF[4]] = dot_tn(gtime[...].astype(LOWTYPE), time_ref[...])
        if rows_ref.shape[0] > 5120 + SMALL_ROWS:
            rows_ref[...] = jnp.zeros_like(rows_ref)
        pieces = gradient_pieces(owners, peers)
        for block in range(0, 5120, C1):
            turned = acc_ref[:, block : block + C1].T
            for source, size, target in pieces:
                low, high = max(source, block), min(source + size, block + C1)
                if low < high:
                    start = target + low - source
                    rows_ref[start : start + high - low, :] = turned[low - block : high - block]
        stem = lax.dot_general(
            spread_ref[...],
            gstem_ref[...],
            (((0,), (0,)), ((), ())),
            preferred_element_type=F32,
            precision=EXACT_PRECISION,
        )
        head = ghead_ref[...]
        none = jnp.zeros((ROWS12, C1), F32)
        tiles = [head[k : k + 16, :mid] for k in range(0, 144, 16)]
        for k in range(0, 80, 16):
            other = head[80 + k : 96 + k, mid:] if k < 64 else none
            tiles.append(jnp.concatenate([head[k : k + 16, mid:], other], axis=1))
        tiles.append(jnp.concatenate([stem[:16], stem[16:]], axis=1))
        for tile, (start, _) in zip(tiles, small_tiles(owners, peers)):
            rows_ref[start : start + 16, :] = tile
        misc_ref[:, :mid] = gvec_ref[...]
        misc_ref[13:14, :mid] = jnp.sum(loss_ref[...], axis=0, keepdims=True)
        misc_ref[14:15, :mid] = jnp.sum(wsum_ref[...], axis=0, keepdims=True)
        misc_ref[:, mid:] = ghb_ref[:, :C1] + ghb_ref[:, C1:]


def chunk_rows(owners, peers):
    share = -(-5120 // (owners * peers))
    return -(-share // 16) * 16, -(-(-(-SMALL_ROWS // peers)) // 16) * 16


def block_rows(owners, peers):
    chunk, small = chunk_rows(owners, peers)
    return owners * chunk + small


def slot_of(peer, peers):
    return peer % 2 * (peers // 2) + peer // 2


def gradient_pieces(owners, peers):
    chunk, _ = chunk_rows(owners, peers)
    block = block_rows(owners, peers)
    pieces = []
    for owner in range(owners):
        packed = 0
        for seg, seg_rows in enumerate(segment_rows()):
            share = seg_rows // owners
            done = 0
            while done < share:
                row = packed + done
                size = min(share - done, chunk - row % chunk)
                target = slot_of(row // chunk, peers) * block + owner * chunk + row % chunk
                pieces.append((SEG_OFF[seg] + owner * share + done, size, target))
                done += size
            packed += share
    return pieces


def small_tiles(owners, peers):
    chunk, small = chunk_rows(owners, peers)
    tiles = []
    for row in range(0, SMALL_ROWS, 16):
        slot = slot_of(row // small, peers)
        tiles.append((slot * block_rows(owners, peers) + owners * chunk + row % small, slot))
    return tiles


def unet_call(samples, owners, peers, operands):
    group = 2 if samples % 2 == 0 else 1
    steps = samples // group
    time_rows = operands[3].shape[0]
    mid = CHANNELS_MID
    places = group * PLACES

    def image_spec():
        return pl.BlockSpec((group, ROWS12, PLACES), lambda i: (i, 0, 0))

    def whole(shape):
        return pl.BlockSpec(shape, lambda i: (0,) * len(shape))

    out_shapes = [(peers * block_rows(owners, peers), mid), (ROWS12, mid + C1)]
    scratch = [
        ((mid, 5120), F32),
        ((TAPS * ROWS12, C1), F32),
        ((TAPS * ROWS12, mid + C1), F32),
        ((ROWS12, mid), F32),
        ((ROWS12, mid), F32),
        ((ROWS12, mid), F32),
        ((ROWS12, mid), F32),
        ((group, PLACES, C1), F32),
        ((group, PLACES, mid), F32),
        ((group, PLACES, mid), F32),
        ((group, PLACES, mid), F32),
        ((group, PLACES, mid), F32),
        ((group, HALO, 3 * C1), LOWTYPE),
        ((group, HALO, 3 * mid), LOWTYPE),
        ((places, mid), LOWTYPE),
        ((places, 3 * mid), LOWTYPE),
        ((group, PLACES, mid), LOWTYPE),
        ((places, mid), LOWTYPE),
        ((places, mid + C1), LOWTYPE),
        ((group, TAPS * ROWS12, PLACES), LOWTYPE),
        ((group, HALO, mid), LOWTYPE),
        ((group, HALO, mid), LOWTYPE),
        ((group, PLACES + 16, mid), F32),
        ((group, PLACES, mid), F32),
        ((places, mid), LOWTYPE),
        ((places, 3 * mid), LOWTYPE),
        ((group, PLACES, C1), F32),
        ((time_rows, mid), F32),
        ((time_rows, mid), F32),
    ]
    return pl.pallas_call(
        functools.partial(unet_body, group, steps, owners, peers),
        grid=(steps,),
        out_shape=[jax.ShapeDtypeStruct(shape, F32) for shape in out_shapes],
        in_specs=[image_spec()] * 3 + [whole(a.shape) for a in operands[3:]],
        out_specs=[whole(shape) for shape in out_shapes],
        scratch_shapes=[pltpu.VMEM(shape, kind) for shape, kind in scratch],
        compiler_params=pltpu.CompilerParams(vmem_limit_bytes=VMEM_BYTES),
    )(*operands)


TASKS = ((1, 0), (0, 0), (0, 1), (2, 0), (1, 1), (2, 1), (3, 0), (3, 1))
MESH = pl.DeviceIdType.MESH
SMALL_LANES = 9 * (CHANNELS_MID + C1)


def ns_chain(gram, eye):
    product = None
    for step in range(NS_STEPS):
        square = dot_nn(gram, gram, EXACT_PRECISION)
        factor = NS_A * eye + NS_B * gram + NS_C * square
        product = factor if product is None else dot_nn(product, factor, EXACT_PRECISION)
        if step < NS_STEPS - 1:
            gram = dot_nn(factor, dot_nn(gram, factor, EXACT_PRECISION), EXACT_PRECISION)
    return product


def identity(size):
    rows = lax.broadcasted_iota(jnp.int32, (size, size), 0)
    cols = lax.broadcasted_iota(jnp.int32, (size, size), 1)
    return (rows == cols).astype(F32)


def muon_body(
    owners,
    peers,
    rows_ref,
    misc_ref,
    weight_ref,
    moment_ref,
    stem_ref,
    stemm_ref,
    head_ref,
    headm_ref,
    vec_ref,
    first_ref,
    second_ref,
    new_ref,
    newm_ref,
    copy_ref,
    nstem_ref,
    nstemm_ref,
    nhead_ref,
    nheadm_ref,
    nvec_ref,
    nfirst_ref,
    nsecond_ref,
    sums_ref,
    recv1,
    own2,
    send2,
    recv2,
    send3,
    recv3,
    recvs3,
    gathered,
    misc1,
    misc2,
    misc3,
    direction,
    mine_u,
    gram_part,
    gram_recv,
    gram_all,
    small,
    x_zero,
    x_one,
    sem1,
    sem2,
    sem3,
    sems3,
    sema,
    semb,
    semg,
    semh,
    semx,
    semy,
    semm1,
    semm2,
    semm3,
):
    mid = CHANNELS_MID
    chips = peers // 2
    chunk, small_chunk = chunk_rows(owners, peers)
    block = block_rows(owners, peers)
    held = chunk + small_chunk
    own_rows = weight_ref.shape[0]
    z = lax.axis_index("bucket")
    peer = lax.axis_index("batch")
    chip, core = peer // 2, peer % 2
    partner = {"batch": chip * 2 + 1 - core}
    started = []

    def same_core(k):
        return {"batch": lax.rem(chip + k, chips) * 2 + core}

    def along(k):
        return {"bucket": lax.rem(z + k, owners)}

    def send(source, target, sems, slot, device, begin=True):
        copy = pltpu.make_async_remote_copy(
            src_ref=source,
            dst_ref=target,
            send_sem=sems.at[0, slot],
            recv_sem=sems.at[1, slot],
            device_id=device,
            device_id_type=MESH,
        )
        copy.start()
        if begin:
            started.append(copy)
        return copy

    barrier = pltpu.get_barrier_semaphore()
    friends = [partner] + [same_core(k) for k in range(1, chips)]
    friends += [along(k) for k in range(1, owners)]
    for friend in friends:
        pl.semaphore_signal(barrier, inc=1, device_id=friend, device_id_type=MESH)
    pl.semaphore_wait(barrier, len(friends))

    misc_copy = send(misc_ref, misc1, semm1, 0, partner)
    first = []
    order = list(range(1, chips)) + [0]
    for k in order:
        other = lax.rem(chip + k, chips)
        start = pl.multiple_of(((1 - core) * chips + other) * block, 16)
        first.append(send(rows_ref.at[pl.ds(start, block), :], recv1.at[k], sem1, k, partner))

    misc_copy.wait_recv()
    misc2[chip] = misc_ref[...] + misc1[...]
    misc_copies = [
        send(misc2.at[chip], misc2.at[chip], semm2, k - 1, same_core(k)) for k in range(1, chips)
    ]
    second = []
    for k, copy in zip(order, first):
        copy.wait_recv()
        other = lax.rem(chip + k, chips)
        start = pl.multiple_of((core * chips + other) * block, 16)
        total = rows_ref[pl.ds(start, block), :] + recv1[k]
        if k == 0:
            own2[...] = total
        else:
            send2[k - 1] = total
            second.append(send(send2.at[k - 1], recv2.at[k - 1], sem2, k - 1, same_core(k)))

    for copy in misc_copies:
        copy.wait_recv()
    misc3[z] = sum([misc2[k] for k in range(1, chips)], misc2[0])
    misc_copies = [
        send(misc3.at[z], misc3.at[z], semm3, k - 1, along(k)) for k in range(1, owners)
    ]
    for copy in second:
        copy.wait_recv()
    third = []
    for k in list(range(1, owners)) + [0]:
        start = pl.multiple_of(lax.rem(z + k, owners) * chunk, 16)
        rows = pl.ds(start, chunk)
        total = own2[rows, :]
        for other in range(chips - 1):
            total = total + recv2[other, rows, :]
        if k == 0:
            own2[rows, :] = total
        else:
            send3[k - 1] = total
            third.append(send(send3.at[k - 1], recv3.at[k - 1], sem3, k - 1, along(k)))
    tail = slice(owners * chunk, block)
    total = own2[tail, :]
    for other in range(chips - 1):
        total = total + recv2[other, tail, :]
    recvs3[z] = total
    third += [
        send(recvs3.at[z], recvs3.at[z], sems3, k - 1, along(k)) for k in range(1, owners)
    ]
    for copy in third:
        copy.wait_recv()
    total = own2[pl.ds(pl.multiple_of(z * chunk, 16), chunk), :]
    for other in range(owners - 1):
        total = total + recv3[other]
    slot = core * chips + chip
    gathered[slot, :chunk, :] = total
    total = recvs3[0]
    for other in range(1, owners):
        total = total + recvs3[other]
    gathered[slot, chunk:, :] = total

    here = gathered.at[slot]
    plane = [send(here, here, sema, k - 1, same_core(k)) for k in range(1, chips)]
    cross = [send(here, here, semb, 0, partner)]

    for copy in misc_copies:
        copy.wait_recv()
    misc = sum([misc3[k] for k in range(1, owners)], misc3[0])
    weight_sum = jnp.sum(misc[14:15, :mid], axis=1, keepdims=True)
    inverse = 1.0 / weight_sum
    loss_sum = jnp.sum(misc[13:14, :mid], axis=1, keepdims=True)
    lane = lax.broadcasted_iota(jnp.int32, (8, C1), 1)
    sums_ref[...] = jnp.where(lane == 0, loss_sum, weight_sum)
    head_bias = jnp.sum(misc[:, mid:].T, axis=0, keepdims=True)
    nvec_ref[...] = jnp.zeros_like(nvec_ref)
    nvec_ref[:3, :] = misc[:3, :C1]
    for row in range(3, 13):
        nvec_ref[2 * row - 3 : 2 * row - 2, :] = misc[row : row + 1, :C1]
        nvec_ref[2 * row - 2 : 2 * row - 1, :] = misc[row : row + 1, C1:mid]
    nvec_ref[23:24, :ROWS12] = head_bias
    grad = nvec_ref[...] * inverse
    firsts = BETA_ONE * first_ref[...] + (1.0 - BETA_ONE) * grad
    seconds = BETA_TWO * second_ref[...] + (1.0 - BETA_TWO) * grad * grad
    nfirst_ref[...] = firsts
    nsecond_ref[...] = seconds
    change = (
        firsts
        / (1.0 - BETA_ONE**STEP)
        / (jnp.sqrt(seconds / (1.0 - BETA_TWO**STEP)) + ADAM_EPS)
    )
    nvec_ref[...] = vec_ref[...] - LR_ADAM * change

    for k, copy in zip(range(1, chips), plane):
        copy.wait_recv()
        other = gathered.at[core * chips + lax.rem(chip + chips - k, chips)]
        cross.append(send(other, other, semb, k, partner))
    for copy in cross:
        copy.wait_recv()

    for owner_peer in range(peers):
        start = owner_peer * chunk
        size = min(chunk, own_rows - start)
        if size > 0:
            grad = gathered[slot_of(owner_peer, peers), :size, :] * inverse
            rows = slice(start, start + size)
            moment = MOMENTUM * moment_ref[rows, :] + grad
            newm_ref[rows, :] = moment
            direction[rows, :] = grad + MOMENTUM * moment
    shares = [rows // owners for rows in segment_rows()]
    starts = [sum(shares[:k]) for k in range(len(shares))]
    for (task_chip, task_core), share, start in zip(TASKS, shares, starts):

        @pl.when((lax.rem(chip, 4) == task_chip) & (core == task_core))
        def _(share=share, start=start):
            mine_u[:share, :] = direction[start : start + share, :]
            if share < mine_u.shape[0]:
                mine_u[share:, :] = jnp.zeros((mine_u.shape[0] - share, mid), F32)

    mine = mine_u[...]
    gram_part[...] = lax.dot_general(
        mine,
        mine,
        (((0,), (0,)), ((), ())),
        preferred_element_type=F32,
        precision=EXACT_PRECISION,
    )
    part = mid // owners
    copies = []
    for k in range(1, owners):
        start = pl.multiple_of(lax.rem(z + k, owners) * part, 8)
        copies.append(send(gram_part.at[pl.ds(start, part), :], gram_recv.at[z], semg, k - 1, along(k)))
    own_part = pl.ds(pl.multiple_of(z * part, 8), part)
    gram_recv[z] = gram_part[own_part, :]

    chunk_s = small_chunk
    tiles = []
    for tile in range(SMALL_ROWS // 16):
        row = tile * 16
        at = chunk + row % chunk_s
        tiles.append(gathered[slot_of(row // chunk_s, peers), at : at + 16, :] * inverse)
    for tap in range(TAPS):
        lanes = slice(tap * (mid + C1), tap * (mid + C1) + mid)
        nheadm_ref[:, lanes] = tiles[tap]
        lanes = slice(tap * (mid + C1) + mid, (tap + 1) * (mid + C1))
        if tap < 5:
            nheadm_ref[:, lanes] = tiles[9 + tap][:, :C1]
        else:
            nheadm_ref[:, lanes] = tiles[9 + tap - 5][:, C1:]
    grad = nheadm_ref[...]
    moment = MOMENTUM * headm_ref[...] + grad
    nheadm_ref[...] = moment
    turn = grad + MOMENTUM * moment
    small[...] = jnp.zeros_like(small)
    small[:16, :SMALL_LANES] = turn * lax.rsqrt(
        jnp.sum(jnp.sum(turn * turn, axis=1, keepdims=True), axis=0, keepdims=True) + NORM_EPS
    )
    grad = jnp.concatenate([tiles[14][:, :C1], tiles[14][:, C1:]], axis=0)
    moment = MOMENTUM * stemm_ref[...] + grad
    nstemm_ref[...] = moment
    turn = grad + MOMENTUM * moment
    small[32:, SMALL_LANES:] = turn * lax.rsqrt(
        jnp.sum(jnp.sum(turn * turn, axis=1, keepdims=True), axis=0, keepdims=True) + NORM_EPS
    )
    gram = lax.dot_general(
        small[...],
        small[...],
        (((1,), (1,)), ((), ())),
        preferred_element_type=F32,
        precision=EXACT_PRECISION,
    )
    product = ns_chain(gram, identity(64))
    turned = dot_nn(product, small[...], EXACT_PRECISION)
    keep = 1.0 - LR_MUON * DECAY
    nhead_ref[...] = head_ref[...] * keep - LR_MUON * turned[:16, :SMALL_LANES]
    nstem_ref[...] = stem_ref[...] * keep - LR_MUON * turned[32:, SMALL_LANES:]

    for copy in copies:
        copy.wait_recv()
    gram_all[own_part, :] = sum([gram_recv[k] for k in range(1, owners)], gram_recv[0])
    copies = [
        send(gram_all.at[own_part, :], gram_all.at[own_part, :], semh, k - 1, along(k))
        for k in range(1, owners)
    ]
    for copy in copies:
        copy.wait_recv()
    gram = gram_all[...]
    eye = identity(mid)
    trace = jnp.sum(jnp.sum(gram * eye, axis=1, keepdims=True), axis=0, keepdims=True)
    scale = lax.rsqrt(trace + NORM_EPS)
    product = ns_chain(gram * (scale * scale), eye) * scale
    turned = dot_nn(mine_u[...], product, EXACT_PRECISION)

    place = lax.rem(chip, 4)
    base = chip - place

    def in_group(k):
        return {"batch": (base + lax.rem(place + k, 4)) * 2 + core}

    for task_core, buffer in ((0, x_zero), (1, x_one)):

        @pl.when(core == task_core)
        def _(buffer=buffer, other_buffer=(x_one, x_zero)[task_core]):
            size = buffer.shape[1]
            buffer[place] = turned[:size].astype(LOWTYPE)
            here = buffer.at[place]
            plane = [send(here, here, semx, k - 1, in_group(k), False) for k in range(1, 4)]
            cross = [send(here, here, semy, 0, partner, False)]
            for k in range(1, 4):
                plane[k - 1].wait_recv()
                other = buffer.at[lax.rem(place + 4 - k, 4)]
                cross.append(send(other, other, semy, k, partner, False))
            for k in range(4):
                there = other_buffer.at[lax.rem(place + 4 - k, 4)]
                pltpu.make_async_remote_copy(
                    src_ref=there,
                    dst_ref=there,
                    send_sem=semy.at[0, k],
                    recv_sem=semy.at[1, k],
                    device_id=partner,
                    device_id_type=MESH,
                ).wait_recv()
            for copy in plane + cross:
                copy.wait_send()

    for (task_chip, task_core), share, start in zip(TASKS, shares, starts):
        buffer = (x_zero, x_one)[task_core]
        rows = slice(start, start + share)
        fresh = weight_ref[rows, :] * keep - LR_MUON * buffer[task_chip, :share, :].astype(F32)
        new_ref[rows, :] = fresh
        copy_ref[rows, :] = fresh.astype(LOWTYPE)
    for copy in started:
        copy.wait_send()


def muon_call(owners, peers, operands):
    mid = CHANNELS_MID
    chips = peers // 2
    chunk, small_chunk = chunk_rows(owners, peers)
    block = block_rows(owners, peers)
    rows = operands[2].shape[0]
    part = mid // owners
    shares = [seg_rows // owners for seg_rows in segment_rows()]
    most = [max(s for s, t in zip(shares, TASKS) if t[1] == core) for core in (0, 1)]
    out_shapes = [
        ((rows, mid), F32),
        ((rows, mid), F32),
        ((rows, mid), LOWTYPE),
        (operands[4].shape, F32),
        (operands[4].shape, F32),
        (operands[6].shape, F32),
        (operands[6].shape, F32),
        (operands[8].shape, F32),
        (operands[8].shape, F32),
        (operands[8].shape, F32),
        ((8, C1), F32),
    ]
    scratch = [
        ((chips, block, mid), F32),
        ((block, mid), F32),
        ((chips - 1, block, mid), F32),
        ((chips - 1, block, mid), F32),
        ((owners - 1, chunk, mid), F32),
        ((owners - 1, chunk, mid), F32),
        ((owners, small_chunk, mid), F32),
        ((peers, chunk + small_chunk, mid), F32),
        (operands[1].shape, F32),
        ((chips,) + operands[1].shape, F32),
        ((owners,) + operands[1].shape, F32),
        ((rows, mid), F32),
        ((max(most), mid), F32),
        ((mid, mid), F32),
        ((owners, part, mid), F32),
        ((mid, mid), F32),
        ((64, SMALL_LANES + C1), F32),
        ((4, most[0], mid), LOWTYPE),
        ((4, most[1], mid), LOWTYPE),
    ]
    sems = [
        chips,
        chips - 1,
        owners - 1,
        owners - 1,
        chips - 1,
        chips,
        owners - 1,
        owners - 1,
        3,
        4,
        1,
        chips - 1,
        owners - 1,
    ]
    vmem = pl.BlockSpec(memory_space=pltpu.VMEM)
    return pl.pallas_call(
        functools.partial(muon_body, owners, peers),
        out_shape=[jax.ShapeDtypeStruct(shape, kind) for shape, kind in out_shapes],
        in_specs=[vmem] * len(operands),
        out_specs=[vmem] * len(out_shapes),
        scratch_shapes=[pltpu.VMEM(shape, kind) for shape, kind in scratch]
        + [pltpu.SemaphoreType.DMA((2, count)) for count in sems],
        compiler_params=pltpu.CompilerParams(
            vmem_limit_bytes=VMEM_BYTES, collective_id=0, has_side_effects=True
        ),
    )(*operands)


def phase_order():
    pixel = np.arange(S * S)
    row, col = pixel // S, pixel % S
    lane = (row % 2 * 2 + col % 2) * PLACES + row // 2 * SIDE + col // 2
    return jnp.asarray(lane, jnp.int32)


def stem_spread():
    counts = np.zeros((3, 2, 3))
    for block in range(3):
        for inner in range(2):
            for sub in range(2):
                tap = 2 * (block - 1) + inner - sub + 1
                if 0 <= tap <= 2:
                    counts[block, inner, tap] += 1
    full = np.zeros((3, 3, ROWS12, 3, 3, 3))
    both = (np.einsum("ayt,bxu->abyxtu", counts, counts) * 0.25).reshape(3, 3, 4, 3, 3)
    for c in range(3):
        full[:, :, c:12:3, :, :, c] = both
    return jnp.asarray(full.reshape(TAPS * ROWS12, 27), F32)


def split_three(values):
    first = lax.reduce_precision(values, 8, 7)
    second = lax.reduce_precision(values - first, 8, 7)
    third = values - first - second
    return jnp.concatenate([first, second, third], axis=1).astype(LOWTYPE)


def pad_rows(values, rows):
    return jnp.pad(values, [(0, 0)] * (values.ndim - 2) + [(0, rows - values.shape[-2]), (0, 0)])


def lanes_of(vector):
    rows = -(-vector.shape[0] // (8 * C1)) * 8
    return jnp.pad(vector, (0, rows * C1 - vector.shape[0]), constant_values=1.0).reshape(rows, C1)


def by_column(weights, chans):
    return weights.reshape(3, 3 * chans, CHANNELS_MID).transpose(1, 0, 2).reshape(3 * chans, -1)


def same_group(chans):
    group = np.arange(chans) // (chans // GROUPS)
    same = (group[:, None] == group[None, :]) / (PLACES * (chans // GROUPS))
    return jnp.asarray(same, F32)


def shards(
    images,
    pixel_mask,
    timesteps,
    noise_field,
    matrices,
    matrix_moms,
    stem_weight,
    stem_moms,
    head_weight,
    head_moms,
    vectors,
    vector_firsts,
    vector_seconds,
):
    owners, peers = lax.axis_size("bucket"), lax.axis_size("batch")
    gathered = lax.all_gather(matrices.astype(LOWTYPE), "bucket", axis=0, tiled=True)
    conv_one, conv_two, skip_w, temb_w, query_w, key_w, value_w, out_w = unpack(gathered, owners)
    samples = images.shape[0]
    level, weight = plan(timesteps)
    noisy = (
        jnp.sqrt(level)[:, None, None] * images + jnp.sqrt(1.0 - level)[:, None, None] * noise_field
    )
    mask_weight = pixel_mask.astype(jnp.float32) * weight[:, None]
    rows = jnp.concatenate(
        [
            lax.reduce_precision(noisy, 8, 7).reshape(-1, S * S),
            noise_field.reshape(-1, S * S),
            mask_weight,
        ],
        axis=0,
    )
    order = (phase_order()[:, None] == jnp.arange(S * S, dtype=jnp.int32)[None, :]).astype(F32)
    phased = jnp.dot(rows, order, precision=EXACT_PRECISION)
    planes = 3 * samples
    pictures = phased[: 2 * planes].reshape(2, samples, 3, 4, PLACES).transpose(0, 1, 3, 2, 4)
    pictures = pad_rows(pictures.reshape(2, samples, 12, PLACES), ROWS12)
    noisy_low = pictures[0].astype(LOWTYPE)
    noise_planes = pictures[1]
    mask_planes = jnp.broadcast_to(
        phased[2 * planes :].reshape(samples, 4, 1, PLACES), (samples, 4, 3, PLACES)
    ).reshape(samples, 12, PLACES)
    mask_planes = pad_rows(mask_planes, ROWS12)
    time_in = pad_rows(swish(embed(timesteps)).astype(LOWTYPE), -(-samples // 16) * 16)
    spread = stem_spread()
    stem_blocks = split_three(
        jnp.dot(spread, lax.reduce_precision(stem_weight, 8, 7), precision=EXACT_PRECISION)
    )
    head_turned = head_weight.T
    head_rows = head_turned.astype(LOWTYPE).reshape(12, TAPS, CHANNELS_MID + C1)
    head_rows = pad_rows(head_rows.transpose(1, 0, 2), ROWS12).reshape(TAPS * ROWS12, -1)
    vec_rows = lanes_of(vectors)
    head_bias = jnp.broadcast_to(pad_rows(vectors[-12:].reshape(12, 1), ROWS12), (ROWS12, C1))
    rows_out, misc = unet_call(
        samples,
        owners,
        peers,
        [
            noisy_low,
            noise_planes,
            mask_planes,
            time_in,
            stem_blocks,
            head_rows,
            conv_one,
            by_column(conv_one, C1),
            conv_two,
            by_column(conv_two, CHANNELS_MID),
            skip_w,
            temb_w,
            jnp.concatenate([query_w, key_w, value_w], axis=1),
            out_w,
            vec_rows,
            head_bias,
            same_group(C1),
            same_group(CHANNELS_MID),
            jnp.pad(spread, ((0, 0), (0, 5))),
        ],
    )
    (
        new_matrices,
        new_matrix_moms,
        matrix_copies,
        new_stem,
        new_stem_moms,
        new_head,
        new_head_moms,
        new_vec,
        new_first,
        new_second,
        sums,
    ) = muon_call(
        owners,
        peers,
        [
            rows_out,
            misc,
            matrices,
            matrix_moms,
            pad_rows(stem_weight, 32),
            pad_rows(stem_moms, 32),
            pad_rows(head_turned, ROWS12),
            pad_rows(head_moms.T, ROWS12),
            vec_rows,
            lanes_of(vector_firsts),
            lanes_of(vector_seconds),
        ],
    )
    count = vectors.shape[0]
    new_stem, new_stem_moms = new_stem[:27], new_stem_moms[:27]
    new_head, new_head_moms = new_head[:12].T, new_head_moms[:12].T
    new_vectors = new_vec.reshape(-1)[:count]
    new_firsts = new_first.reshape(-1)[:count]
    new_seconds = new_second.reshape(-1)[:count]
    loss_sum, weight_sum = sums[0, 0], sums[0, 1]
    return (
        loss_sum,
        weight_sum,
        new_matrices,
        new_matrix_moms,
        matrix_copies,
        new_stem,
        new_stem_moms,
        new_stem.astype(LOWTYPE),
        new_head,
        new_head_moms,
        new_head.astype(LOWTYPE),
        new_vectors,
        new_firsts,
        new_seconds,
        new_vectors.astype(LOWTYPE),
    )


def solution(mesh):
    return jax.shard_map(
        shards,
        mesh=mesh,
        in_specs=(
            P(("bucket", "batch"), None, None),
            P(("bucket", "batch"), None),
            P(("bucket", "batch")),
            P(("bucket", "batch"), None, None),
            P("bucket", None),
            P("bucket", None),
            P(),
            P(),
            P(),
            P(),
            P(),
            P(),
            P(),
        ),
        out_specs=(
            P(),
            P(),
            P("bucket", None),
            P("bucket", None),
            P("bucket", None),
            P(),
            P(),
            P(),
            P(),
            P(),
            P(),
            P(),
            P(),
            P(),
            P(),
        ),
        check_vma=False,
    )
```

```python
import functools
import math

import jax
import jax.numpy as jnp
import numpy as np
from jax import lax
from jax.experimental import pallas as pl
from jax.experimental.pallas import tpu as pltpu
from jax.sharding import PartitionSpec as P

C1 = 128
CHANNELS_MID = 256
TEMB = 512
GROUPS = 32
S = 32
TSTEPS = 1000
NS_STEPS = 5
STEP = 10


GN_EPS = 1e-05
NORM_EPS = 1e-12
MOMENTUM = 0.95
LR_MUON = 0.5
DECAY = 0.01
NS_A = 3.4445
NS_B = -4.775
NS_C = 2.0315
BETA_ONE = 0.9
BETA_TWO = 0.999
LR_ADAM = 0.5
ADAM_EPS = 1e-08
EXACT_PRECISION = lax.Precision.HIGHEST
LOWTYPE = jnp.bfloat16


def segment_rows():
    return [
        9 * C1,
        9 * CHANNELS_MID,
        C1,
        TEMB,
        CHANNELS_MID,
        CHANNELS_MID,
        CHANNELS_MID,
        CHANNELS_MID,
    ]


def unpack(packed, owners):
    blocks = packed.reshape(owners, -1, packed.shape[1])
    pieces = []
    start = 0
    for seg_rows in segment_rows():
        share = seg_rows // owners
        pieces.append(blocks[:, start : start + share, :].reshape(seg_rows, packed.shape[1]))
        start += share
    return pieces


def plan(timesteps):
    frac_t = (timesteps.astype(jnp.float32) / TSTEPS + 0.008) / 1.008
    level = jnp.cos(frac_t * (math.pi / 2)) ** 2
    ratio = level / (1.0 - level)
    return (level, jnp.minimum(1.0, 5.0 / ratio))


def embed(timesteps):
    half_width = TEMB // 2
    freqs = jnp.exp(-math.log(10000.0) * jnp.arange(half_width, dtype=jnp.float32) / half_width)
    angles = timesteps.astype(jnp.float32)[:, None] * freqs[None, :]
    return jnp.concatenate([jnp.sin(angles), jnp.cos(angles)], axis=1)


def swish(values):
    return values * jax.nn.sigmoid(values)


F32 = jnp.float32
PLACES = 256
SIDE = 16
HALO = 288
TAPS = 9
ROWS12 = 16
CHUNK = 64
SMALL_ROWS = 240
VMEM_BYTES = 56 * 1024 * 1024
SEG_OFF = (0, 1152, 3456, 3584, 4096, 4352, 4608, 4864, 5120)


def dot_nn(a, b, precision=None):
    return lax.dot_general(
        a, b, (((1,), (0,)), ((), ())), preferred_element_type=F32, precision=precision
    )


def dot_nt(a, b):
    return lax.dot_general(a, b, (((1,), (1,)), ((), ())), preferred_element_type=F32)


def dot_tn(a, b):
    return lax.dot_general(a, b, (((0,), (0,)), ((), ())), preferred_element_type=F32)


def sigmoid(v):
    return 1.0 / (1.0 + jnp.exp(-v))


def fold8(v):
    rows, chans = v.shape
    return jnp.sum(v.reshape(rows // 8, 8, chans), axis=0)


def shift_lanes(x, di, dj):
    lane = lax.broadcasted_iota(jnp.int32, x.shape, 1)
    row, col = lane // SIDE + di, lane % SIDE + dj
    offset = (-(SIDE * di + dj)) % PLACES
    moved = x if offset == 0 else pltpu.roll(x, offset, 1)
    valid = (row >= 0) & (row < SIDE) & (col >= 0) & (col < SIDE)
    return jnp.where(valid, moved, 0.0)


def tap_offsets():
    return [(di, dj) for di in (-1, 0, 1) for dj in (-1, 0, 1)]


def unet_body(
    group,
    steps,
    owners,
    peers,
    noisy_ref,
    noise_ref,
    maskw_ref,
    time_ref,
    stemw_ref,
    headw_ref,
    conv1_ref,
    conv1b_ref,
    conv2_ref,
    conv2b_ref,
    skip_ref,
    temb_ref,
    qkv_ref,
    outw_ref,
    vec_ref,
    headb_ref,
    same128_ref,
    same256_ref,
    spread_ref,
    rows_ref,
    misc_ref,
    acc_ref,
    gstem_ref,
    ghead_ref,
    gvec_ref,
    ghb_ref,
    loss_ref,
    wsum_ref,
    x0,
    hid,
    res,
    outp,
    attn,
    a1,
    a2,
    normed,
    qkv,
    plow,
    attl,
    low0,
    joined,
    patch,
    pad1,
    pad2,
    shiftf,
    dyf,
    dout,
    dq3,
    dpool,
    tproj,
    gtime,
    dtap,
    datt,
    dscore,
    dpool_low,
):
    step = pl.program_id(0)
    mid = CHANNELS_MID
    chunks = range(0, PLACES, CHUNK)
    images = range(group)

    @pl.when(step == 0)
    def _():
        acc_ref[...] = jnp.zeros_like(acc_ref)
        gstem_ref[...] = jnp.zeros_like(gstem_ref)
        ghead_ref[...] = jnp.zeros_like(ghead_ref)
        gvec_ref[...] = jnp.zeros_like(gvec_ref)
        ghb_ref[...] = jnp.zeros_like(ghb_ref)
        loss_ref[...] = jnp.zeros_like(loss_ref)
        wsum_ref[...] = jnp.zeros_like(wsum_ref)
        gtime[...] = jnp.zeros_like(gtime)
        for ref in (a1, a2, pad1, pad2):
            for g in images:
                ref[g, :SIDE, :] = jnp.zeros((SIDE, ref.shape[2]), ref.dtype)
                ref[g, HALO - SIDE :, :] = jnp.zeros((SIDE, ref.shape[2]), ref.dtype)
        shiftf[...] = jnp.zeros_like(shiftf)
        tproj[...] = dot_nn(time_ref[...], temb_ref[...])

    def vec(row, chans=mid):
        if chans == C1:
            return vec_ref[row : row + 1, :]
        row = 2 * row - 3
        return jnp.concatenate([vec_ref[row : row + 1, :], vec_ref[row + 1 : row + 2, :]], axis=1)

    def add_vec(row, value):
        gvec_ref[row : row + 1, : value.shape[1]] += value

    def total(parts):
        return jnp.concatenate([jnp.sum(p, axis=0, keepdims=True) for p in parts], axis=0)

    def grouped(stats, chans):
        same = same128_ref if chans == C1 else same256_ref
        first = stats.astype(LOWTYPE).astype(F32)
        second = (stats - first).astype(LOWTYPE).astype(F32)
        third = stats - first - second
        sums = dot_nn(jnp.concatenate([first, second, third], axis=0).astype(LOWTYPE), same[...])
        return sums[:group] + sums[group : 2 * group] + sums[2 * group :]

    def gn_stats(ref, sums, chans):
        mean = grouped(sums, chans)
        parts = []
        for g in images:
            acc = jnp.zeros((8, chans), F32)
            for r in chunks:
                c = ref[g, r : r + CHUNK, :] - mean[g : g + 1]
                acc += fold8(c * c)
            parts.append(acc)
        return mean, lax.rsqrt(grouped(total(parts), chans) + GN_EPS)

    def edge(chans, left):
        col = lax.broadcasted_iota(jnp.int32, (CHUNK, chans), 0) % SIDE
        return (col > 0) if left else (col < SIDE - 1)

    def act_shift(ref, g, mean, rstd, gain, shift, dest, chans):
        for r in chunks:
            y = (ref[g, r : r + CHUNK, :] - mean[g : g + 1]) * rstd[g : g + 1] * gain + shift
            a = y * sigmoid(y)
            shiftf[g, 8 + r : 8 + r + CHUNK, :chans] = a
            dest[g, SIDE + r : SIDE + r + CHUNK, chans : 2 * chans] = a.astype(LOWTYPE)
        for r in chunks:
            before = shiftf[g, 7 + r : 7 + r + CHUNK, :chans]
            after = shiftf[g, 9 + r : 9 + r + CHUNK, :chans]
            rows = slice(SIDE + r, SIDE + r + CHUNK)
            dest[g, rows, :chans] = jnp.where(edge(chans, True), before, 0.0).astype(LOWTYPE)
            dest[g, rows, 2 * chans :] = jnp.where(edge(chans, False), after, 0.0).astype(LOWTYPE)

    def dy_cat(ref, g, order):
        return jnp.concatenate(
            [ref[g, SIDE * k : SIDE * k + PLACES, :] for k in order], axis=1
        )

    def stack(parts):
        return jnp.concatenate(parts, axis=0) if len(parts) > 1 else parts[0]

    def staged(stages, fillers=()):
        fillers = list(fillers)
        for stage in stages:
            for g in images:
                stage(g)
            if fillers:
                fillers.pop(0)()
        for filler in fillers:
            filler()

    def rows_of(g):
        return slice(g * PLACES, (g + 1) * PLACES)

    sums1 = [None] * group

    def stem_patch(g):
        noisy = noisy_ref[g].astype(F32)
        for tap, (di, dj) in enumerate(tap_offsets()):
            patch[g, tap * ROWS12 : (tap + 1) * ROWS12, :] = shift_lanes(noisy, di, dj).astype(
                LOWTYPE
            )

    def stem_pool(g):
        wide = dot_tn(patch[g], stemw_ref[...])
        acc = jnp.zeros((8, C1), F32)
        for r in chunks:
            w = wide[r : r + CHUNK]
            v = (w[:, :C1] + w[:, C1 : 2 * C1]) + w[:, 2 * C1 :] + vec(0, C1)
            x0[g, r : r + CHUNK, :] = v
            low0[g * PLACES + r : g * PLACES + r + CHUNK, :] = v.astype(LOWTYPE)
            acc += fold8(v)
        sums1[g] = acc

    staged([stem_patch, stem_pool])
    mean1, rstd1 = gn_stats(x0, total(sums1), C1)
    gain1, shift1 = vec(1, C1), vec(2, C1)

    sums2 = [None] * group

    def act_one(g):
        act_shift(x0, g, mean1, rstd1, gain1, shift1, a1, C1)

    def conv_one(g):
        wide = dot_nn(dy_cat(a1, g, (0, 1, 2)), conv1_ref[...])
        bias = vec(3) + vec(4) + tproj[pl.ds(step * group + g, 1), :]
        acc = jnp.zeros((8, mid), F32)
        for r in chunks:
            v = wide[r : r + CHUNK] + bias
            hid[g, r : r + CHUNK, :] = v
            acc += fold8(v)
        sums2[g] = acc

    staged([act_one, conv_one])
    mean2, rstd2 = gn_stats(hid, total(sums2), mid)
    gain2, shift2 = vec(5), vec(6)

    sums3 = [None] * group

    def act_two(g):
        act_shift(hid, g, mean2, rstd2, gain2, shift2, a2, mid)

    def conv_two(g):
        wide = dot_nn(dy_cat(a2, g, (0, 1, 2)), conv2_ref[...])
        wide = wide + dot_nn(low0[rows_of(g), :], skip_ref[...])
        acc = jnp.zeros((8, mid), F32)
        for r in chunks:
            v = wide[r : r + CHUNK] + vec(7)
            res[g, r : r + CHUNK, :] = v
            acc += fold8(v)
        sums3[g] = acc

    staged([act_two, conv_two])
    mean3, rstd3 = gn_stats(res, total(sums3), mid)
    gain3, shift3 = vec(8), vec(9)
    scale = mid ** (-0.5)
    ones3, twos3 = [None] * group, [None] * group

    def norm_three(g):
        for r in chunks:
            xh = (res[g, r : r + CHUNK, :] - mean3[g : g + 1]) * rstd3[g : g + 1]
            y = xh * gain3 + shift3
            normed[g * PLACES + r : g * PLACES + r + CHUNK, :] = y.astype(LOWTYPE)

    def project(g):
        rows = rows_of(g)
        wide = dot_nn(normed[rows, :], qkv_ref[...])
        qkv[rows, :mid] = (wide[:, :mid] + vec(10)).astype(LOWTYPE)
        qkv[rows, mid : 2 * mid] = wide[:, mid : 2 * mid].astype(LOWTYPE)
        qkv[rows, 2 * mid :] = (wide[:, 2 * mid :] + vec(11)).astype(LOWTYPE)

    def weigh(g):
        rows = rows_of(g)
        logits = dot_nt(qkv[rows, :mid], qkv[rows, mid : 2 * mid])
        for r in chunks:
            s = logits[r : r + CHUNK] * scale
            e = jnp.exp(s - jnp.max(s, axis=1, keepdims=True))
            p = e * (1.0 / jnp.sum(e, axis=1, keepdims=True))
            attn[g, r : r + CHUNK, :] = p
            plow[g, r : r + CHUNK, :] = p.astype(LOWTYPE)

    def attend(g):
        attl[rows_of(g), :] = dot_nn(plow[g], qkv[rows_of(g), 2 * mid :]).astype(LOWTYPE)

    def join(g):
        wide = dot_nn(attl[rows_of(g), :], outw_ref[...])
        for r in chunks:
            rows = slice(g * PLACES + r, g * PLACES + r + CHUNK)
            o = res[g, r : r + CHUNK, :] + wide[r : r + CHUNK] + vec(12)
            outp[g, r : r + CHUNK, :] = o
            joined[rows, :mid] = (o * sigmoid(o)).astype(LOWTYPE)
            x = x0[g, r : r + CHUNK, :]
            joined[rows, mid:] = (x * sigmoid(x)).astype(LOWTYPE)

    def head(g):
        taps = dot_nt(headw_ref[...], joined[rows_of(g), :])
        value = headb_ref[:, :1] + jnp.zeros((ROWS12, PLACES), F32)
        for tap, (di, dj) in enumerate(tap_offsets()):
            value = value + shift_lanes(taps[tap * ROWS12 : (tap + 1) * ROWS12, :], di, dj)
        error = value - noise_ref[g]
        masked = maskw_ref[g] * error
        loss_ref[...] += masked * error
        wsum_ref[...] += maskw_ref[g]
        grad = 2.0 * masked
        ghb_ref[...] += grad
        gradl = grad.astype(LOWTYPE).astype(F32)
        for tap, (di, dj) in enumerate(tap_offsets()):
            dtap[g, tap * ROWS12 : (tap + 1) * ROWS12, :] = shift_lanes(gradl, -di, -dj).astype(
                LOWTYPE
            )

    def head_back(g):
        wide = dot_tn(dtap[g], headw_ref[...])
        acc = jnp.zeros((8, mid), F32)
        for r in chunks:
            o = outp[g, r : r + CHUNK, :]
            s = sigmoid(o)
            d = wide[r : r + CHUNK, :mid] * (s * (1.0 + o * (1.0 - s)))
            outp[g, r : r + CHUNK, :] = d
            dout[g * PLACES + r : g * PLACES + r + CHUNK, :] = d.astype(LOWTYPE)
            acc += fold8(d)
            x = x0[g, r : r + CHUNK, :]
            s = sigmoid(x)
            dpool[g, r : r + CHUNK, :] = wide[r : r + CHUNK, mid:] * (s * (1.0 + x * (1.0 - s)))
        add_vec(12, jnp.sum(acc, axis=0, keepdims=True))

    def attend_back(g):
        datt[rows_of(g), :] = dot_nt(dout[rows_of(g), :], outw_ref[...]).astype(LOWTYPE)

    def weigh_back(g):
        rows = rows_of(g)
        gweights = dot_nt(datt[rows, :], qkv[rows, 2 * mid :])
        dval = dot_tn(plow[g], datt[rows, :])
        add_vec(11, jnp.sum(fold8(dval), axis=0, keepdims=True))
        dq3[rows, 2 * mid :] = dval.astype(LOWTYPE)
        for r in chunks:
            p = attn[g, r : r + CHUNK, :]
            gw = gweights[r : r + CHUNK]
            ds = p * (gw - jnp.sum(gw * p, axis=1, keepdims=True))
            dscore[g, r : r + CHUNK, :] = (ds * scale).astype(LOWTYPE)

    def query_back(g):
        rows = rows_of(g)
        dqry = dot_nn(dscore[g], qkv[rows, mid : 2 * mid])
        dkey = dot_tn(dscore[g], qkv[rows, :mid])
        add_vec(10, jnp.sum(fold8(dqry), axis=0, keepdims=True))
        dq3[rows, :mid] = dqry.astype(LOWTYPE)
        dq3[rows, mid : 2 * mid] = dkey.astype(LOWTYPE)

    def project_back(g):
        one, two = jnp.zeros((8, mid), F32), jnp.zeros((8, mid), F32)
        wide = dot_nt(dq3[rows_of(g), :], qkv_ref[...])
        for r in chunks:
            xh = (res[g, r : r + CHUNK, :] - mean3[g : g + 1]) * rstd3[g : g + 1]
            d = wide[r : r + CHUNK]
            res[g, r : r + CHUNK, :] = xh
            dyf[g, r : r + CHUNK, :] = d
            one += fold8(d)
            two += fold8(d * xh)
        ones3[g], twos3[g] = one, two

    staged(
        [
            norm_three,
            project,
            weigh,
            attend,
            join,
            head,
            head_back,
            attend_back,
            weigh_back,
            query_back,
            project_back,
        ]
    )

    ones, twos = total(ones3), total(twos3)
    add_vec(9, jnp.sum(ones, axis=0, keepdims=True))
    add_vec(8, jnp.sum(twos, axis=0, keepdims=True))

    def finish(ref, dest, rstd, gain, m1, m2, chans, extra, g, row):
        r1 = rstd[g : g + 1]
        acc = jnp.zeros((8, chans), F32)
        for r in chunks:
            d = dyf[g, r : r + CHUNK, :chans] * (gain * r1)
            d = d - m1[g : g + 1] * r1 - ref[g, r : r + CHUNK, :] * (m2[g : g + 1] * r1)
            if extra is not None:
                d = d + extra[g, r : r + CHUNK, :]
            acc += fold8(d)
            dest(g, r, d.astype(LOWTYPE))
        acc = jnp.sum(acc, axis=0, keepdims=True)
        add_vec(row, acc)
        return acc

    def to_pad(pad):
        def put(g, r, low):
            pad[g, SIDE + r : SIDE + r + CHUNK, :] = low

        return put

    def turned(parts):
        return stack(parts).T

    def pad_turned(pad):
        return turned([pad[g, SIDE : SIDE + PLACES, :] for g in images])

    def conv_back(pad, weights, g, chans, apply):
        wide = dot_nt(dy_cat(pad, g, (2, 1, 0)), weights)
        shiftf[g, 8 : 8 + PLACES, :chans] = wide[:, :chans]
        dyf[g, :, :chans] = wide[:, chans : 2 * chans]
        for r in chunks:
            after = shiftf[g, 9 + r : 9 + r + CHUNK, :chans]
            dyf[g, r : r + CHUNK, :chans] += jnp.where(edge(chans, False), after, 0.0)
        shiftf[g, 8 : 8 + PLACES, :chans] = wide[:, 2 * chans :]
        for r in chunks:
            before = shiftf[g, 7 + r : 7 + r + CHUNK, :chans]
            apply(r, dyf[g, r : r + CHUNK, :chans] + jnp.where(edge(chans, True), before, 0.0))

    def norm_back(pad, weights, ref, mean, rstd, gain, shift, chans, ones, twos, g):
        sums = [jnp.zeros((8, chans), F32), jnp.zeros((8, chans), F32)]

        def apply(r, da):
            xh = (ref[g, r : r + CHUNK, :] - mean[g : g + 1]) * rstd[g : g + 1]
            y = xh * gain + shift
            s = sigmoid(y)
            d = da * (s * (1.0 + y * (1.0 - s)))
            ref[g, r : r + CHUNK, :] = xh
            dyf[g, r : r + CHUNK, :chans] = d
            sums[0] += fold8(d)
            sums[1] += fold8(d * xh)

        conv_back(pad, weights[...], g, chans, apply)
        ones[g], twos[g] = sums

    def add_product(first, last, left, right):
        acc_ref[:, first:last] += dot_nn(left(), right())

    m1, m2 = grouped(ones * gain3, mid), grouped(twos * gain3, mid)
    ones2, twos2 = [None] * group, [None] * group

    def grad_out():
        add_product(SEG_OFF[7], SEG_OFF[8], lambda: dout[...].T, lambda: attl[...])

    def grad_project(k):
        add_product(
            SEG_OFF[4 + k],
            SEG_OFF[5 + k],
            lambda: dq3[:, k * mid : (k + 1) * mid].T,
            lambda: normed[...],
        )

    def grad_head():
        for g in images:
            ghead_ref[...] += dot_nn(dtap[g], joined[rows_of(g), :])

    staged(
        [
            lambda g: finish(res, to_pad(pad2), rstd3, gain3, m1, m2, mid, outp, g, 7),
            lambda g: norm_back(
                pad2, conv2b_ref, hid, mean2, rstd2, gain2, shift2, mid, ones2, twos2, g
            ),
        ],
        [grad_out, grad_head] + [functools.partial(grad_project, k) for k in range(3)],
    )
    ones, twos = total(ones2), total(twos2)
    add_vec(6, jnp.sum(ones, axis=0, keepdims=True))
    add_vec(5, jnp.sum(twos, axis=0, keepdims=True))

    n1, n2 = grouped(ones * gain2, mid), grouped(twos * gain2, mid)
    ones1, twos1 = [None] * group, [None] * group
    lowt2 = pad_turned(pad2)

    def finish_two(g):
        acc = finish(hid, to_pad(pad1), rstd2, gain2, n1, n2, mid, None, g, 3)
        add_vec(4, acc)
        gtime[pl.ds(step * group + g, 1), :] = acc

    def grad_conv(lowt, act, offset, k):
        width = act.shape[2]
        first = offset + k * width
        add_product(
            first,
            first + width,
            lambda: lowt,
            lambda: stack([act[g, SIDE * k : SIDE * k + PLACES, :] for g in images]),
        )

    def grad_skip():
        add_product(SEG_OFF[2], SEG_OFF[3], lambda: lowt2, lambda: low0[...])
        for g in images:
            dpool[g] += dot_nt(pad2[g, SIDE : SIDE + PLACES, :], skip_ref[...])

    staged(
        [
            finish_two,
            lambda g: norm_back(
                pad1, conv1b_ref, x0, mean1, rstd1, gain1, shift1, C1, ones1, twos1, g
            ),
        ],
        [functools.partial(grad_conv, lowt2, a2, SEG_OFF[1], k) for k in range(3)] + [grad_skip],
    )
    ones, twos = total(ones1), total(twos1)
    add_vec(2, jnp.sum(ones, axis=0, keepdims=True))
    add_vec(1, jnp.sum(twos, axis=0, keepdims=True))

    p1, p2 = grouped(ones * gain1, C1), grouped(twos * gain1, C1)
    lowt1 = pad_turned(pad1)

    def to_pool(g, r, low):
        dpool_low[g, r : r + CHUNK, :] = low

    def grad_stem(g):
        gstem_ref[...] += dot_nn(patch[g], dpool_low[g])

    staged(
        [lambda g: finish(x0, to_pool, rstd1, gain1, p1, p2, C1, dpool, g, 0), grad_stem],
        [functools.partial(grad_conv, lowt1, a1, SEG_OFF[0], k) for k in range(3)],
    )

    @pl.when(step == steps - 1)
    def _():
        acc_ref[:, SEG_OFF[3] : SEG_OFF[4]] = dot_tn(gtime[...].astype(LOWTYPE), time_ref[...])
        if rows_ref.shape[0] > 5120 + SMALL_ROWS:
            rows_ref[...] = jnp.zeros_like(rows_ref)
        pieces = gradient_pieces(owners, peers)
        for block in range(0, 5120, C1):
            turned = acc_ref[:, block : block + C1].T
            for source, size, target in pieces:
                low, high = max(source, block), min(source + size, block + C1)
                if low < high:
                    start = target + low - source
                    rows_ref[start : start + high - low, :] = turned[low - block : high - block]
        stem = lax.dot_general(
            spread_ref[...],
            gstem_ref[...],
            (((0,), (0,)), ((), ())),
            preferred_element_type=F32,
            precision=EXACT_PRECISION,
        )
        head = ghead_ref[...]
        none = jnp.zeros((ROWS12, C1), F32)
        tiles = [head[k : k + 16, :mid] for k in range(0, 144, 16)]
        for k in range(0, 80, 16):
            other = head[80 + k : 96 + k, mid:] if k < 64 else none
            tiles.append(jnp.concatenate([head[k : k + 16, mid:], other], axis=1))
        tiles.append(jnp.concatenate([stem[:16], stem[16:]], axis=1))
        for tile, (start, _) in zip(tiles, small_tiles(owners, peers)):
            rows_ref[start : start + 16, :] = tile
        misc_ref[:, :mid] = gvec_ref[...]
        misc_ref[13:14, :mid] = jnp.sum(loss_ref[...], axis=0, keepdims=True)
        misc_ref[14:15, :mid] = jnp.sum(wsum_ref[...], axis=0, keepdims=True)
        misc_ref[:, mid:] = ghb_ref[:, :C1] + ghb_ref[:, C1:]


def chunk_rows(owners, peers):
    share = -(-5120 // (owners * peers))
    return -(-share // 16) * 16, -(-(-(-SMALL_ROWS // peers)) // 16) * 16


def block_rows(owners, peers):
    chunk, small = chunk_rows(owners, peers)
    return owners * chunk + small


def slot_of(peer, peers):
    return peer % 2 * (peers // 2) + peer // 2


def gradient_pieces(owners, peers):
    chunk, _ = chunk_rows(owners, peers)
    block = block_rows(owners, peers)
    pieces = []
    for owner in range(owners):
        packed = 0
        for seg, seg_rows in enumerate(segment_rows()):
            share = seg_rows // owners
            done = 0
            while done < share:
                row = packed + done
                size = min(share - done, chunk - row % chunk)
                target = slot_of(row // chunk, peers) * block + owner * chunk + row % chunk
                pieces.append((SEG_OFF[seg] + owner * share + done, size, target))
                done += size
            packed += share
    return pieces


def small_tiles(owners, peers):
    chunk, small = chunk_rows(owners, peers)
    tiles = []
    for row in range(0, SMALL_ROWS, 16):
        slot = slot_of(row // small, peers)
        tiles.append((slot * block_rows(owners, peers) + owners * chunk + row % small, slot))
    return tiles


def unet_call(samples, owners, peers, operands):
    group = max(k for k in (1, 2, 4) if samples % k == 0)
    steps = samples // group
    time_rows = operands[3].shape[0]
    mid = CHANNELS_MID
    places = group * PLACES

    def image_spec():
        return pl.BlockSpec((group, ROWS12, PLACES), lambda i: (i, 0, 0))

    def whole(shape):
        return pl.BlockSpec(shape, lambda i: (0,) * len(shape))

    out_shapes = [(peers * block_rows(owners, peers), mid), (ROWS12, mid + C1)]
    scratch = [
        ((mid, 5120), F32),
        ((TAPS * ROWS12, C1), F32),
        ((TAPS * ROWS12, mid + C1), F32),
        ((ROWS12, mid), F32),
        ((ROWS12, mid), F32),
        ((ROWS12, mid), F32),
        ((ROWS12, mid), F32),
        ((group, PLACES, C1), F32),
        ((group, PLACES, mid), F32),
        ((group, PLACES, mid), F32),
        ((group, PLACES, mid), F32),
        ((group, PLACES, mid), F32),
        ((group, HALO, 3 * C1), LOWTYPE),
        ((group, HALO, 3 * mid), LOWTYPE),
        ((places, mid), LOWTYPE),
        ((places, 3 * mid), LOWTYPE),
        ((group, PLACES, mid), LOWTYPE),
        ((places, mid), LOWTYPE),
        ((places, C1), LOWTYPE),
        ((places, mid + C1), LOWTYPE),
        ((group, TAPS * ROWS12, PLACES), LOWTYPE),
        ((group, HALO, mid), LOWTYPE),
        ((group, HALO, mid), LOWTYPE),
        ((group, PLACES + 16, mid), F32),
        ((group, PLACES, mid), F32),
        ((places, mid), LOWTYPE),
        ((places, 3 * mid), LOWTYPE),
        ((group, PLACES, C1), F32),
        ((time_rows, mid), F32),
        ((time_rows, mid), F32),
        ((group, TAPS * ROWS12, PLACES), LOWTYPE),
        ((places, mid), LOWTYPE),
        ((group, PLACES, mid), LOWTYPE),
        ((group, PLACES, C1), LOWTYPE),
    ]
    return pl.pallas_call(
        functools.partial(unet_body, group, steps, owners, peers),
        grid=(steps,),
        out_shape=[jax.ShapeDtypeStruct(shape, F32) for shape in out_shapes],
        in_specs=[image_spec()] * 3 + [whole(a.shape) for a in operands[3:]],
        out_specs=[whole(shape) for shape in out_shapes],
        scratch_shapes=[pltpu.VMEM(shape, kind) for shape, kind in scratch],
        compiler_params=pltpu.CompilerParams(vmem_limit_bytes=VMEM_BYTES),
    )(*operands)


TASKS = ((1, 0), (0, 0), (0, 1), (2, 0), (1, 1), (2, 1), (3, 0), (3, 1))
MESH = pl.DeviceIdType.MESH
SMALL_LANES = 9 * (CHANNELS_MID + C1)


def ns_chain(gram, eye):
    product = None
    for step in range(NS_STEPS):
        square = dot_nn(gram, gram, EXACT_PRECISION)
        factor = NS_A * eye + NS_B * gram + NS_C * square
        product = factor if product is None else dot_nn(product, factor, EXACT_PRECISION)
        if step < NS_STEPS - 1:
            gram = dot_nn(factor, dot_nn(gram, factor, EXACT_PRECISION), EXACT_PRECISION)
    return product


def identity(size):
    rows = lax.broadcasted_iota(jnp.int32, (size, size), 0)
    cols = lax.broadcasted_iota(jnp.int32, (size, size), 1)
    return (rows == cols).astype(F32)


def muon_body(
    owners,
    peers,
    rows_ref,
    misc_ref,
    weight_ref,
    moment_ref,
    stem_ref,
    stemm_ref,
    head_ref,
    headm_ref,
    vec_ref,
    first_ref,
    second_ref,
    new_ref,
    newm_ref,
    copy_ref,
    nstem_ref,
    nstemm_ref,
    nhead_ref,
    nheadm_ref,
    nvec_ref,
    nfirst_ref,
    nsecond_ref,
    sums_ref,
    recv1,
    own2,
    send2,
    recv2,
    send3,
    recv3,
    recvs3,
    gathered,
    misc1,
    misc2,
    misc3,
    direction,
    mine_u,
    gram_part,
    gram_recv,
    gram_all,
    small,
    x_zero,
    x_one,
    sem1,
    sem2,
    sem3,
    sems3,
    sema,
    semb,
    semg,
    semh,
    semx,
    semy,
    semm1,
    semm2,
    semm3,
):
    mid = CHANNELS_MID
    chips = peers // 2
    chunk, small_chunk = chunk_rows(owners, peers)
    block = block_rows(owners, peers)
    held = chunk + small_chunk
    own_rows = weight_ref.shape[0]
    z = lax.axis_index("bucket")
    peer = lax.axis_index("batch")
    chip, core = peer // 2, peer % 2
    partner = {"batch": chip * 2 + 1 - core}
    started = []

    def same_core(k):
        return {"batch": lax.rem(chip + k, chips) * 2 + core}

    def along(k):
        return {"bucket": lax.rem(z + k, owners)}

    def send(source, target, sems, slot, device, begin=True):
        copy = pltpu.make_async_remote_copy(
            src_ref=source,
            dst_ref=target,
            send_sem=sems.at[0, slot],
            recv_sem=sems.at[1, slot],
            device_id=device,
            device_id_type=MESH,
        )
        copy.start()
        if begin:
            started.append(copy)
        return copy

    barrier = pltpu.get_barrier_semaphore()
    friends = [partner] + [same_core(k) for k in range(1, chips)]
    friends += [along(k) for k in range(1, owners)]
    for friend in friends:
        pl.semaphore_signal(barrier, inc=1, device_id=friend, device_id_type=MESH)
    pl.semaphore_wait(barrier, len(friends))

    misc_copy = send(misc_ref, misc1, semm1, 0, partner)
    first = []
    order = list(range(1, chips)) + [0]
    for k in order:
        other = lax.rem(chip + k, chips)
        start = pl.multiple_of(((1 - core) * chips + other) * block, 16)
        first.append(send(rows_ref.at[pl.ds(start, block), :], recv1.at[k], sem1, k, partner))

    misc_copy.wait_recv()
    misc2[chip] = misc_ref[...] + misc1[...]
    misc_copies = [
        send(misc2.at[chip], misc2.at[chip], semm2, k - 1, same_core(k)) for k in range(1, chips)
    ]
    second = []
    for k, copy in zip(order, first):
        copy.wait_recv()
        other = lax.rem(chip + k, chips)
        start = pl.multiple_of((core * chips + other) * block, 16)
        total = rows_ref[pl.ds(start, block), :] + recv1[k]
        if k == 0:
            own2[...] = total
        else:
            send2[k - 1] = total
            second.append(send(send2.at[k - 1], recv2.at[k - 1], sem2, k - 1, same_core(k)))

    for copy in misc_copies:
        copy.wait_recv()
    misc3[z] = sum([misc2[k] for k in range(1, chips)], misc2[0])
    misc_copies = [
        send(misc3.at[z], misc3.at[z], semm3, k - 1, along(k)) for k in range(1, owners)
    ]
    for copy in second:
        copy.wait_recv()
    third = []
    for k in list(range(1, owners)) + [0]:
        start = pl.multiple_of(lax.rem(z + k, owners) * chunk, 16)
        rows = pl.ds(start, chunk)
        total = own2[rows, :]
        for other in range(chips - 1):
            total = total + recv2[other, rows, :]
        if k == 0:
            own2[rows, :] = total
        else:
            send3[k - 1] = total
            third.append(send(send3.at[k - 1], recv3.at[k - 1], sem3, k - 1, along(k)))
    tail = slice(owners * chunk, block)
    total = own2[tail, :]
    for other in range(chips - 1):
        total = total + recv2[other, tail, :]
    recvs3[z] = total
    third += [
        send(recvs3.at[z], recvs3.at[z], sems3, k - 1, along(k)) for k in range(1, owners)
    ]
    for copy in third:
        copy.wait_recv()
    total = own2[pl.ds(pl.multiple_of(z * chunk, 16), chunk), :]
    for other in range(owners - 1):
        total = total + recv3[other]
    slot = core * chips + chip
    gathered[slot, :chunk, :] = total
    total = recvs3[0]
    for other in range(1, owners):
        total = total + recvs3[other]
    gathered[slot, chunk:, :] = total

    here = gathered.at[slot]
    plane = [send(here, here, sema, k - 1, same_core(k)) for k in range(1, chips)]
    cross = [send(here, here, semb, 0, partner)]

    for copy in misc_copies:
        copy.wait_recv()
    misc = sum([misc3[k] for k in range(1, owners)], misc3[0])
    weight_sum = jnp.sum(misc[14:15, :mid], axis=1, keepdims=True)
    inverse = 1.0 / weight_sum
    loss_sum = jnp.sum(misc[13:14, :mid], axis=1, keepdims=True)
    lane = lax.broadcasted_iota(jnp.int32, (8, C1), 1)
    sums_ref[...] = jnp.where(lane == 0, loss_sum, weight_sum)
    head_bias = jnp.sum(misc[:, mid:].T, axis=0, keepdims=True)
    nvec_ref[...] = jnp.zeros_like(nvec_ref)
    nvec_ref[:3, :] = misc[:3, :C1]
    for row in range(3, 13):
        nvec_ref[2 * row - 3 : 2 * row - 2, :] = misc[row : row + 1, :C1]
        nvec_ref[2 * row - 2 : 2 * row - 1, :] = misc[row : row + 1, C1:mid]
    nvec_ref[23:24, :ROWS12] = head_bias
    grad = nvec_ref[...] * inverse
    firsts = BETA_ONE * first_ref[...] + (1.0 - BETA_ONE) * grad
    seconds = BETA_TWO * second_ref[...] + (1.0 - BETA_TWO) * grad * grad
    nfirst_ref[...] = firsts
    nsecond_ref[...] = seconds
    change = (
        firsts
        / (1.0 - BETA_ONE**STEP)
        / (jnp.sqrt(seconds / (1.0 - BETA_TWO**STEP)) + ADAM_EPS)
    )
    nvec_ref[...] = vec_ref[...] - LR_ADAM * change

    for k, copy in zip(range(1, chips), plane):
        copy.wait_recv()
        other = gathered.at[core * chips + lax.rem(chip + chips - k, chips)]
        cross.append(send(other, other, semb, k, partner))
    for copy in cross:
        copy.wait_recv()

    for owner_peer in range(peers):
        start = owner_peer * chunk
        size = min(chunk, own_rows - start)
        if size > 0:
            grad = gathered[slot_of(owner_peer, peers), :size, :] * inverse
            rows = slice(start, start + size)
            moment = MOMENTUM * moment_ref[rows, :] + grad
            newm_ref[rows, :] = moment
            direction[rows, :] = grad + MOMENTUM * moment
    shares = [rows // owners for rows in segment_rows()]
    starts = [sum(shares[:k]) for k in range(len(shares))]
    for (task_chip, task_core), share, start in zip(TASKS, shares, starts):

        @pl.when((lax.rem(chip, 4) == task_chip) & (core == task_core))
        def _(share=share, start=start):
            mine_u[:share, :] = direction[start : start + share, :]
            if share < mine_u.shape[0]:
                mine_u[share:, :] = jnp.zeros((mine_u.shape[0] - share, mid), F32)

    mine = mine_u[...]
    gram_part[...] = lax.dot_general(
        mine,
        mine,
        (((0,), (0,)), ((), ())),
        preferred_element_type=F32,
        precision=EXACT_PRECISION,
    )
    part = mid // owners
    copies = []
    for k in range(1, owners):
        start = pl.multiple_of(lax.rem(z + k, owners) * part, 8)
        copies.append(send(gram_part.at[pl.ds(start, part), :], gram_recv.at[z], semg, k - 1, along(k)))
    own_part = pl.ds(pl.multiple_of(z * part, 8), part)
    gram_recv[z] = gram_part[own_part, :]

    chunk_s = small_chunk
    tiles = []
    for tile in range(SMALL_ROWS // 16):
        row = tile * 16
        at = chunk + row % chunk_s
        tiles.append(gathered[slot_of(row // chunk_s, peers), at : at + 16, :] * inverse)
    for tap in range(TAPS):
        lanes = slice(tap * (mid + C1), tap * (mid + C1) + mid)
        nheadm_ref[:, lanes] = tiles[tap]
        lanes = slice(tap * (mid + C1) + mid, (tap + 1) * (mid + C1))
        if tap < 5:
            nheadm_ref[:, lanes] = tiles[9 + tap][:, :C1]
        else:
            nheadm_ref[:, lanes] = tiles[9 + tap - 5][:, C1:]
    grad = nheadm_ref[...]
    moment = MOMENTUM * headm_ref[...] + grad
    nheadm_ref[...] = moment
    turn = grad + MOMENTUM * moment
    small[...] = jnp.zeros_like(small)
    small[:16, :SMALL_LANES] = turn * lax.rsqrt(
        jnp.sum(jnp.sum(turn * turn, axis=1, keepdims=True), axis=0, keepdims=True) + NORM_EPS
    )
    grad = jnp.concatenate([tiles[14][:, :C1], tiles[14][:, C1:]], axis=0)
    moment = MOMENTUM * stemm_ref[...] + grad
    nstemm_ref[...] = moment
    turn = grad + MOMENTUM * moment
    small[32:, SMALL_LANES:] = turn * lax.rsqrt(
        jnp.sum(jnp.sum(turn * turn, axis=1, keepdims=True), axis=0, keepdims=True) + NORM_EPS
    )
    gram = lax.dot_general(
        small[...],
        small[...],
        (((1,), (1,)), ((), ())),
        preferred_element_type=F32,
        precision=EXACT_PRECISION,
    )
    product = ns_chain(gram, identity(64))
    turned = dot_nn(product, small[...], EXACT_PRECISION)
    keep = 1.0 - LR_MUON * DECAY
    nhead_ref[...] = head_ref[...] * keep - LR_MUON * turned[:16, :SMALL_LANES]
    nstem_ref[...] = stem_ref[...] * keep - LR_MUON * turned[32:, SMALL_LANES:]

    for copy in copies:
        copy.wait_recv()
    gram_all[own_part, :] = sum([gram_recv[k] for k in range(1, owners)], gram_recv[0])
    copies = [
        send(gram_all.at[own_part, :], gram_all.at[own_part, :], semh, k - 1, along(k))
        for k in range(1, owners)
    ]
    for copy in copies:
        copy.wait_recv()
    gram = gram_all[...]
    eye = identity(mid)
    trace = jnp.sum(jnp.sum(gram * eye, axis=1, keepdims=True), axis=0, keepdims=True)
    scale = lax.rsqrt(trace + NORM_EPS)
    product = ns_chain(gram * (scale * scale), eye) * scale
    turned = dot_nn(mine_u[...], product, EXACT_PRECISION)

    place = lax.rem(chip, 4)
    base = chip - place

    def in_group(k):
        return {"batch": (base + lax.rem(place + k, 4)) * 2 + core}

    for task_core, buffer in ((0, x_zero), (1, x_one)):

        @pl.when(core == task_core)
        def _(buffer=buffer, other_buffer=(x_one, x_zero)[task_core]):
            size = buffer.shape[1]
            buffer[place] = turned[:size].astype(LOWTYPE)
            here = buffer.at[place]
            plane = [send(here, here, semx, k - 1, in_group(k), False) for k in range(1, 4)]
            cross = [send(here, here, semy, 0, partner, False)]
            for k in range(1, 4):
                plane[k - 1].wait_recv()
                other = buffer.at[lax.rem(place + 4 - k, 4)]
                cross.append(send(other, other, semy, k, partner, False))
            for k in range(4):
                there = other_buffer.at[lax.rem(place + 4 - k, 4)]
                pltpu.make_async_remote_copy(
                    src_ref=there,
                    dst_ref=there,
                    send_sem=semy.at[0, k],
                    recv_sem=semy.at[1, k],
                    device_id=partner,
                    device_id_type=MESH,
                ).wait_recv()
            for copy in plane + cross:
                copy.wait_send()

    for (task_chip, task_core), share, start in zip(TASKS, shares, starts):
        buffer = (x_zero, x_one)[task_core]
        rows = slice(start, start + share)
        fresh = weight_ref[rows, :] * keep - LR_MUON * buffer[task_chip, :share, :].astype(F32)
        new_ref[rows, :] = fresh
        copy_ref[rows, :] = fresh.astype(LOWTYPE)
    for copy in started:
        copy.wait_send()


def muon_call(owners, peers, operands):
    mid = CHANNELS_MID
    chips = peers // 2
    chunk, small_chunk = chunk_rows(owners, peers)
    block = block_rows(owners, peers)
    rows = operands[2].shape[0]
    part = mid // owners
    shares = [seg_rows // owners for seg_rows in segment_rows()]
    most = [max(s for s, t in zip(shares, TASKS) if t[1] == core) for core in (0, 1)]
    out_shapes = [
        ((rows, mid), F32),
        ((rows, mid), F32),
        ((rows, mid), LOWTYPE),
        (operands[4].shape, F32),
        (operands[4].shape, F32),
        (operands[6].shape, F32),
        (operands[6].shape, F32),
        (operands[8].shape, F32),
        (operands[8].shape, F32),
        (operands[8].shape, F32),
        ((8, C1), F32),
    ]
    scratch = [
        ((chips, block, mid), F32),
        ((block, mid), F32),
        ((chips - 1, block, mid), F32),
        ((chips - 1, block, mid), F32),
        ((owners - 1, chunk, mid), F32),
        ((owners - 1, chunk, mid), F32),
        ((owners, small_chunk, mid), F32),
        ((peers, chunk + small_chunk, mid), F32),
        (operands[1].shape, F32),
        ((chips,) + operands[1].shape, F32),
        ((owners,) + operands[1].shape, F32),
        ((rows, mid), F32),
        ((max(most), mid), F32),
        ((mid, mid), F32),
        ((owners, part, mid), F32),
        ((mid, mid), F32),
        ((64, SMALL_LANES + C1), F32),
        ((4, most[0], mid), LOWTYPE),
        ((4, most[1], mid), LOWTYPE),
    ]
    sems = [
        chips,
        chips - 1,
        owners - 1,
        owners - 1,
        chips - 1,
        chips,
        owners - 1,
        owners - 1,
        3,
        4,
        1,
        chips - 1,
        owners - 1,
    ]
    vmem = pl.BlockSpec(memory_space=pltpu.VMEM)
    return pl.pallas_call(
        functools.partial(muon_body, owners, peers),
        out_shape=[jax.ShapeDtypeStruct(shape, kind) for shape, kind in out_shapes],
        in_specs=[vmem] * len(operands),
        out_specs=[vmem] * len(out_shapes),
        scratch_shapes=[pltpu.VMEM(shape, kind) for shape, kind in scratch]
        + [pltpu.SemaphoreType.DMA((2, count)) for count in sems],
        compiler_params=pltpu.CompilerParams(
            vmem_limit_bytes=VMEM_BYTES, collective_id=0, has_side_effects=True
        ),
    )(*operands)


def phase_order():
    pixel = np.arange(S * S)
    row, col = pixel // S, pixel % S
    lane = (row % 2 * 2 + col % 2) * PLACES + row // 2 * SIDE + col // 2
    return jnp.asarray(lane, jnp.int32)


def stem_spread():
    counts = np.zeros((3, 2, 3))
    for block in range(3):
        for inner in range(2):
            for sub in range(2):
                tap = 2 * (block - 1) + inner - sub + 1
                if 0 <= tap <= 2:
                    counts[block, inner, tap] += 1
    full = np.zeros((3, 3, ROWS12, 3, 3, 3))
    both = (np.einsum("ayt,bxu->abyxtu", counts, counts) * 0.25).reshape(3, 3, 4, 3, 3)
    for c in range(3):
        full[:, :, c:12:3, :, :, c] = both
    return jnp.asarray(full.reshape(TAPS * ROWS12, 27), F32)


def split_three(values):
    first = lax.reduce_precision(values, 8, 7)
    second = lax.reduce_precision(values - first, 8, 7)
    third = values - first - second
    return jnp.concatenate([first, second, third], axis=1).astype(LOWTYPE)


def pad_rows(values, rows):
    return jnp.pad(values, [(0, 0)] * (values.ndim - 2) + [(0, rows - values.shape[-2]), (0, 0)])


def lanes_of(vector):
    rows = -(-vector.shape[0] // (8 * C1)) * 8
    return jnp.pad(vector, (0, rows * C1 - vector.shape[0]), constant_values=1.0).reshape(rows, C1)


def by_column(weights, chans):
    return weights.reshape(3, 3 * chans, CHANNELS_MID).transpose(1, 0, 2).reshape(3 * chans, -1)


def same_group(chans):
    group = np.arange(chans) // (chans // GROUPS)
    same = (group[:, None] == group[None, :]) / (PLACES * (chans // GROUPS))
    return jnp.asarray(same, LOWTYPE)


def shards(
    images,
    pixel_mask,
    timesteps,
    noise_field,
    matrices,
    matrix_moms,
    stem_weight,
    stem_moms,
    head_weight,
    head_moms,
    vectors,
    vector_firsts,
    vector_seconds,
):
    owners, peers = lax.axis_size("bucket"), lax.axis_size("batch")
    gathered = lax.all_gather(matrices.astype(LOWTYPE), "bucket", axis=0, tiled=True)
    conv_one, conv_two, skip_w, temb_w, query_w, key_w, value_w, out_w = unpack(gathered, owners)
    samples = images.shape[0]
    level, weight = plan(timesteps)
    noisy = (
        jnp.sqrt(level)[:, None, None] * images + jnp.sqrt(1.0 - level)[:, None, None] * noise_field
    )
    mask_weight = pixel_mask.astype(jnp.float32) * weight[:, None]
    rows = jnp.concatenate(
        [
            lax.reduce_precision(noisy, 8, 7).reshape(-1, S * S),
            noise_field.reshape(-1, S * S),
            mask_weight,
        ],
        axis=0,
    )
    order = (phase_order()[:, None] == jnp.arange(S * S, dtype=jnp.int32)[None, :]).astype(F32)
    phased = jnp.dot(rows, order, precision=EXACT_PRECISION)
    planes = 3 * samples
    pictures = phased[: 2 * planes].reshape(2, samples, 3, 4, PLACES).transpose(0, 1, 3, 2, 4)
    pictures = pad_rows(pictures.reshape(2, samples, 12, PLACES), ROWS12)
    noisy_low = pictures[0].astype(LOWTYPE)
    noise_planes = pictures[1]
    mask_planes = jnp.broadcast_to(
        phased[2 * planes :].reshape(samples, 4, 1, PLACES), (samples, 4, 3, PLACES)
    ).reshape(samples, 12, PLACES)
    mask_planes = pad_rows(mask_planes, ROWS12)
    time_in = pad_rows(swish(embed(timesteps)).astype(LOWTYPE), -(-samples // 16) * 16)
    spread = stem_spread()
    stem_blocks = split_three(
        jnp.dot(spread, lax.reduce_precision(stem_weight, 8, 7), precision=EXACT_PRECISION)
    )
    head_turned = head_weight.T
    head_rows = head_turned.astype(LOWTYPE).reshape(12, TAPS, CHANNELS_MID + C1)
    head_rows = pad_rows(head_rows.transpose(1, 0, 2), ROWS12).reshape(TAPS * ROWS12, -1)
    vec_rows = lanes_of(vectors)
    head_bias = jnp.broadcast_to(pad_rows(vectors[-12:].reshape(12, 1), ROWS12), (ROWS12, C1))
    rows_out, misc = unet_call(
        samples,
        owners,
        peers,
        [
            noisy_low,
            noise_planes,
            mask_planes,
            time_in,
            stem_blocks,
            head_rows,
            conv_one,
            by_column(conv_one, C1),
            conv_two,
            by_column(conv_two, CHANNELS_MID),
            skip_w,
            temb_w,
            jnp.concatenate([query_w, key_w, value_w], axis=1),
            out_w,
            vec_rows,
            head_bias,
            same_group(C1),
            same_group(CHANNELS_MID),
            jnp.pad(spread, ((0, 0), (0, 5))),
        ],
    )
    (
        new_matrices,
        new_matrix_moms,
        matrix_copies,
        new_stem,
        new_stem_moms,
        new_head,
        new_head_moms,
        new_vec,
        new_first,
        new_second,
        sums,
    ) = muon_call(
        owners,
        peers,
        [
            rows_out,
            misc,
            matrices,
            matrix_moms,
            pad_rows(stem_weight, 32),
            pad_rows(stem_moms, 32),
            pad_rows(head_turned, ROWS12),
            pad_rows(head_moms.T, ROWS12),
            vec_rows,
            lanes_of(vector_firsts),
            lanes_of(vector_seconds),
        ],
    )
    count = vectors.shape[0]
    new_stem, new_stem_moms = new_stem[:27], new_stem_moms[:27]
    new_head, new_head_moms = new_head[:12].T, new_head_moms[:12].T
    new_vectors = new_vec.reshape(-1)[:count]
    new_firsts = new_first.reshape(-1)[:count]
    new_seconds = new_second.reshape(-1)[:count]
    loss_sum, weight_sum = sums[0, 0], sums[0, 1]
    return (
        loss_sum,
        weight_sum,
        new_matrices,
        new_matrix_moms,
        matrix_copies,
        new_stem,
        new_stem_moms,
        new_stem.astype(LOWTYPE),
        new_head,
        new_head_moms,
        new_head.astype(LOWTYPE),
        new_vectors,
        new_firsts,
        new_seconds,
        new_vectors.astype(LOWTYPE),
    )


def solution(mesh):
    return jax.shard_map(
        shards,
        mesh=mesh,
        in_specs=(
            P(("bucket", "batch"), None, None),
            P(("bucket", "batch"), None),
            P(("bucket", "batch")),
            P(("bucket", "batch"), None, None),
            P("bucket", None),
            P("bucket", None),
            P(),
            P(),
            P(),
            P(),
            P(),
            P(),
            P(),
        ),
        out_specs=(
            P(),
            P(),
            P("bucket", None),
            P("bucket", None),
            P("bucket", None),
            P(),
            P(),
            P(),
            P(),
            P(),
            P(),
            P(),
            P(),
            P(),
            P(),
        ),
        check_vma=False,
    )
```

```python
import functools
import math

import jax
import jax.numpy as jnp
import numpy as np
from jax import lax
from jax.experimental import pallas as pl
from jax.experimental.pallas import tpu as pltpu
from jax.sharding import PartitionSpec as P

C1 = 128
CHANNELS_MID = 256
TEMB = 512
GROUPS = 32
S = 32
TSTEPS = 1000
NS_STEPS = 5
STEP = 10


GN_EPS = 1e-05
NORM_EPS = 1e-12
MOMENTUM = 0.95
LR_MUON = 0.5
DECAY = 0.01
NS_A = 3.4445
NS_B = -4.775
NS_C = 2.0315
BETA_ONE = 0.9
BETA_TWO = 0.999
LR_ADAM = 0.5
ADAM_EPS = 1e-08
EXACT_PRECISION = lax.Precision.HIGHEST
LOWTYPE = jnp.bfloat16


def segment_rows():
    return [
        9 * C1,
        9 * CHANNELS_MID,
        C1,
        TEMB,
        CHANNELS_MID,
        CHANNELS_MID,
        CHANNELS_MID,
        CHANNELS_MID,
    ]


def plan(timesteps):
    frac_t = (timesteps.astype(jnp.float32) / TSTEPS + 0.008) / 1.008
    level = jnp.cos(frac_t * (math.pi / 2)) ** 2
    ratio = level / (1.0 - level)
    return (level, jnp.minimum(1.0, 5.0 / ratio))


def embed(timesteps):
    half_width = TEMB // 2
    freqs = jnp.exp(-math.log(10000.0) * jnp.arange(half_width, dtype=jnp.float32) / half_width)
    angles = timesteps.astype(jnp.float32)[:, None] * freqs[None, :]
    return jnp.concatenate([jnp.sin(angles), jnp.cos(angles)], axis=1)


def swish(values):
    return values * jax.nn.sigmoid(values)


F32 = jnp.float32
PLACES = 256
SIDE = 16
HALO = 288
TAPS = 9
ROWS12 = 16
CHUNK = 64
SMALL_ROWS = 240
VMEM_BYTES = 56 * 1024 * 1024
SEG_OFF = (0, 1152, 3456, 3584, 4096, 4352, 4608, 4864, 5120)


def dot_nn(a, b, precision=None):
    return lax.dot_general(
        a, b, (((1,), (0,)), ((), ())), preferred_element_type=F32, precision=precision
    )


def dot_nt(a, b):
    return lax.dot_general(a, b, (((1,), (1,)), ((), ())), preferred_element_type=F32)


def dot_tn(a, b):
    return lax.dot_general(a, b, (((0,), (0,)), ((), ())), preferred_element_type=F32)


def sigmoid(v):
    return 1.0 / (1.0 + jnp.exp(-v))


def fold8(v):
    rows, chans = v.shape
    return jnp.sum(v.reshape(rows // 8, 8, chans), axis=0)


def shift_lanes(x, di, dj):
    lane = lax.broadcasted_iota(jnp.int32, x.shape, 1)
    row, col = lane // SIDE + di, lane % SIDE + dj
    offset = (-(SIDE * di + dj)) % PLACES
    moved = x if offset == 0 else pltpu.roll(x, offset, 1)
    valid = (row >= 0) & (row < SIDE) & (col >= 0) & (col < SIDE)
    return jnp.where(valid, moved, 0.0)


def tap_offsets():
    return [(di, dj) for di in (-1, 0, 1) for dj in (-1, 0, 1)]


def unet_body(
    group,
    steps,
    owners,
    peers,
    noisy_ref,
    noise_ref,
    maskw_ref,
    time_ref,
    stemw_ref,
    headw_ref,
    conv1_ref,
    conv1b_ref,
    conv2_ref,
    conv2b_ref,
    skip_ref,
    temb_ref,
    qkv_ref,
    outw_ref,
    vec_ref,
    headb_ref,
    same128_ref,
    same256_ref,
    spread_ref,
    rows_ref,
    misc_ref,
    acc_ref,
    gstem_ref,
    ghead_ref,
    gvec_ref,
    ghb_ref,
    loss_ref,
    wsum_ref,
    x0,
    hid,
    res,
    outp,
    attn,
    a1,
    a2,
    normed,
    qkv,
    plow,
    attl,
    low0,
    joined,
    patch,
    pad1,
    pad2,
    shiftf,
    dyf,
    dout,
    dq3,
    dpool,
    tproj,
    gtime,
    dtap,
    datt,
    dscore,
    dpool_low,
):
    step = pl.program_id(0)
    mid = CHANNELS_MID
    chunks = range(0, PLACES, CHUNK)
    images = range(group)

    @pl.when(step == 0)
    def _():
        acc_ref[...] = jnp.zeros_like(acc_ref)
        gstem_ref[...] = jnp.zeros_like(gstem_ref)
        ghead_ref[...] = jnp.zeros_like(ghead_ref)
        gvec_ref[...] = jnp.zeros_like(gvec_ref)
        ghb_ref[...] = jnp.zeros_like(ghb_ref)
        loss_ref[...] = jnp.zeros_like(loss_ref)
        wsum_ref[...] = jnp.zeros_like(wsum_ref)
        gtime[...] = jnp.zeros_like(gtime)
        for ref in (a1, a2, pad1, pad2):
            for g in images:
                ref[g, :SIDE, :] = jnp.zeros((SIDE, ref.shape[2]), ref.dtype)
                ref[g, HALO - SIDE :, :] = jnp.zeros((SIDE, ref.shape[2]), ref.dtype)
        shiftf[...] = jnp.zeros_like(shiftf)
        tproj[...] = dot_nn(time_ref[...], temb_ref[...])

    def vec(row, chans=mid):
        if chans == C1:
            return vec_ref[row : row + 1, :]
        row = 2 * row - 3
        return jnp.concatenate([vec_ref[row : row + 1, :], vec_ref[row + 1 : row + 2, :]], axis=1)

    def add_vec(row, value):
        gvec_ref[row : row + 1, : value.shape[1]] += value

    def total(parts):
        return jnp.concatenate([jnp.sum(p, axis=0, keepdims=True) for p in parts], axis=0)

    def grouped(stats, chans):
        same = same128_ref if chans == C1 else same256_ref
        first = stats.astype(LOWTYPE).astype(F32)
        second = (stats - first).astype(LOWTYPE).astype(F32)
        third = stats - first - second
        sums = dot_nn(jnp.concatenate([first, second, third], axis=0).astype(LOWTYPE), same[...])
        return sums[:group] + sums[group : 2 * group] + sums[2 * group :]

    def gn_stats(ref, sums, chans):
        mean = grouped(sums, chans)
        parts = []
        for g in images:
            acc = jnp.zeros((8, chans), F32)
            for r in chunks:
                c = ref[g, r : r + CHUNK, :] - mean[g : g + 1]
                acc += fold8(c * c)
            parts.append(acc)
        return mean, lax.rsqrt(grouped(total(parts), chans) + GN_EPS)

    def edge(chans, left):
        col = lax.broadcasted_iota(jnp.int32, (CHUNK, chans), 0) % SIDE
        return (col > 0) if left else (col < SIDE - 1)

    def act_shift(ref, g, mean, rstd, gain, shift, dest, chans):
        for r in chunks:
            y = (ref[g, r : r + CHUNK, :] - mean[g : g + 1]) * rstd[g : g + 1] * gain + shift
            a = y * sigmoid(y)
            shiftf[g, 8 + r : 8 + r + CHUNK, :chans] = a
            dest[g, SIDE + r : SIDE + r + CHUNK, chans : 2 * chans] = a.astype(LOWTYPE)
        for r in chunks:
            before = shiftf[g, 7 + r : 7 + r + CHUNK, :chans]
            after = shiftf[g, 9 + r : 9 + r + CHUNK, :chans]
            rows = slice(SIDE + r, SIDE + r + CHUNK)
            dest[g, rows, :chans] = jnp.where(edge(chans, True), before, 0.0).astype(LOWTYPE)
            dest[g, rows, 2 * chans :] = jnp.where(edge(chans, False), after, 0.0).astype(LOWTYPE)

    def dy_cat(ref, g, order):
        return jnp.concatenate(
            [ref[g, SIDE * k : SIDE * k + PLACES, :] for k in order], axis=1
        )

    def stack(parts):
        return jnp.concatenate(parts, axis=0) if len(parts) > 1 else parts[0]

    def staged(stages, fillers=()):
        fillers = list(fillers)
        for stage in stages:
            for g in images:
                stage(g)
            if fillers:
                fillers.pop(0)()
        for filler in fillers:
            filler()

    def rows_of(g):
        return slice(g * PLACES, (g + 1) * PLACES)

    sums1 = [None] * group

    def stem_patch(g):
        noisy = noisy_ref[g]
        for tap, (di, dj) in enumerate(tap_offsets()):
            patch[g, tap * ROWS12 : (tap + 1) * ROWS12, :] = shift_lanes(noisy, di, dj).astype(
                LOWTYPE
            )

    def stem_pool(g):
        wide = dot_tn(patch[g], stemw_ref[...])
        acc = jnp.zeros((8, C1), F32)
        for r in chunks:
            w = wide[r : r + CHUNK]
            v = (w[:, :C1] + w[:, C1 : 2 * C1]) + w[:, 2 * C1 :] + vec(0, C1)
            x0[g, r : r + CHUNK, :] = v
            low0[g * PLACES + r : g * PLACES + r + CHUNK, :] = v.astype(LOWTYPE)
            acc += fold8(v)
        sums1[g] = acc

    staged([stem_patch, stem_pool])
    mean1, rstd1 = gn_stats(x0, total(sums1), C1)
    gain1, shift1 = vec(1, C1), vec(2, C1)

    sums2 = [None] * group

    def act_one(g):
        act_shift(x0, g, mean1, rstd1, gain1, shift1, a1, C1)

    def conv_one(g):
        wide = dot_nn(dy_cat(a1, g, (0, 1, 2)), conv1_ref[...])
        bias = vec(3) + vec(4) + tproj[pl.ds(step * group + g, 1), :]
        acc = jnp.zeros((8, mid), F32)
        for r in chunks:
            v = wide[r : r + CHUNK] + bias
            hid[g, r : r + CHUNK, :] = v
            acc += fold8(v)
        sums2[g] = acc

    staged([act_one, conv_one])
    mean2, rstd2 = gn_stats(hid, total(sums2), mid)
    gain2, shift2 = vec(5), vec(6)

    sums3 = [None] * group

    def act_two(g):
        act_shift(hid, g, mean2, rstd2, gain2, shift2, a2, mid)

    def conv_two(g):
        wide = dot_nn(dy_cat(a2, g, (0, 1, 2)), conv2_ref[...])
        wide = wide + dot_nn(low0[rows_of(g), :], skip_ref[...])
        acc = jnp.zeros((8, mid), F32)
        for r in chunks:
            v = wide[r : r + CHUNK] + vec(7)
            res[g, r : r + CHUNK, :] = v
            acc += fold8(v)
        sums3[g] = acc

    staged([act_two, conv_two])
    mean3, rstd3 = gn_stats(res, total(sums3), mid)
    gain3, shift3 = vec(8), vec(9)
    scale = mid ** (-0.5)
    ones3, twos3 = [None] * group, [None] * group

    def norm_three(g):
        for r in chunks:
            xh = (res[g, r : r + CHUNK, :] - mean3[g : g + 1]) * rstd3[g : g + 1]
            y = xh * gain3 + shift3
            normed[g * PLACES + r : g * PLACES + r + CHUNK, :] = y.astype(LOWTYPE)

    def project(g):
        rows = rows_of(g)
        wide = dot_nn(normed[rows, :], qkv_ref[...])
        qkv[rows, :mid] = (wide[:, :mid] + vec(10)).astype(LOWTYPE)
        qkv[rows, mid : 2 * mid] = wide[:, mid : 2 * mid].astype(LOWTYPE)
        qkv[rows, 2 * mid :] = (wide[:, 2 * mid :] + vec(11)).astype(LOWTYPE)

    def weigh(g):
        rows = rows_of(g)
        logits = dot_nt(qkv[rows, :mid], qkv[rows, mid : 2 * mid])
        for r in chunks:
            s = logits[r : r + CHUNK] * scale
            e = jnp.exp(s - jnp.max(s, axis=1, keepdims=True))
            p = e * (1.0 / jnp.sum(e, axis=1, keepdims=True))
            attn[g, r : r + CHUNK, :] = p
            plow[g, r : r + CHUNK, :] = p.astype(LOWTYPE)

    def attend(g):
        attl[rows_of(g), :] = dot_nn(plow[g], qkv[rows_of(g), 2 * mid :]).astype(LOWTYPE)

    def join(g):
        wide = dot_nn(attl[rows_of(g), :], outw_ref[...])
        for r in chunks:
            rows = slice(g * PLACES + r, g * PLACES + r + CHUNK)
            o = res[g, r : r + CHUNK, :] + wide[r : r + CHUNK] + vec(12)
            outp[g, r : r + CHUNK, :] = o
            joined[rows, :mid] = (o * sigmoid(o)).astype(LOWTYPE)
            x = x0[g, r : r + CHUNK, :]
            joined[rows, mid:] = (x * sigmoid(x)).astype(LOWTYPE)

    def head(g):
        taps = dot_nt(headw_ref[...], joined[rows_of(g), :])
        value = headb_ref[:, :1] + jnp.zeros((ROWS12, PLACES), F32)
        for tap, (di, dj) in enumerate(tap_offsets()):
            value = value + shift_lanes(taps[tap * ROWS12 : (tap + 1) * ROWS12, :], di, dj)
        error = value - noise_ref[g]
        masked = maskw_ref[g] * error
        loss_ref[...] += masked * error
        wsum_ref[...] += maskw_ref[g]
        grad = 2.0 * masked
        ghb_ref[...] += grad
        gradl = grad.astype(LOWTYPE).astype(F32)
        for tap, (di, dj) in enumerate(tap_offsets()):
            dtap[g, tap * ROWS12 : (tap + 1) * ROWS12, :] = shift_lanes(gradl, -di, -dj).astype(
                LOWTYPE
            )

    def head_back(g):
        wide = dot_tn(dtap[g], headw_ref[...])
        acc = jnp.zeros((8, mid), F32)
        for r in chunks:
            o = outp[g, r : r + CHUNK, :]
            s = sigmoid(o)
            d = wide[r : r + CHUNK, :mid] * (s * (1.0 + o * (1.0 - s)))
            outp[g, r : r + CHUNK, :] = d
            dout[g * PLACES + r : g * PLACES + r + CHUNK, :] = d.astype(LOWTYPE)
            acc += fold8(d)
            x = x0[g, r : r + CHUNK, :]
            s = sigmoid(x)
            dpool[g, r : r + CHUNK, :] = wide[r : r + CHUNK, mid:] * (s * (1.0 + x * (1.0 - s)))
        add_vec(12, jnp.sum(acc, axis=0, keepdims=True))

    def attend_back(g):
        datt[rows_of(g), :] = dot_nt(dout[rows_of(g), :], outw_ref[...]).astype(LOWTYPE)

    def weigh_back(g):
        rows = rows_of(g)
        gweights = dot_nt(datt[rows, :], qkv[rows, 2 * mid :])
        dval = dot_tn(plow[g], datt[rows, :])
        add_vec(11, jnp.sum(fold8(dval), axis=0, keepdims=True))
        dq3[rows, 2 * mid :] = dval.astype(LOWTYPE)
        for r in chunks:
            p = attn[g, r : r + CHUNK, :]
            gw = gweights[r : r + CHUNK]
            ds = p * (gw - jnp.sum(gw * p, axis=1, keepdims=True))
            dscore[g, r : r + CHUNK, :] = (ds * scale).astype(LOWTYPE)

    def query_back(g):
        rows = rows_of(g)
        dqry = dot_nn(dscore[g], qkv[rows, mid : 2 * mid])
        dkey = dot_tn(dscore[g], qkv[rows, :mid])
        add_vec(10, jnp.sum(fold8(dqry), axis=0, keepdims=True))
        dq3[rows, :mid] = dqry.astype(LOWTYPE)
        dq3[rows, mid : 2 * mid] = dkey.astype(LOWTYPE)

    def project_back(g):
        one, two = jnp.zeros((8, mid), F32), jnp.zeros((8, mid), F32)
        wide = dot_nt(dq3[rows_of(g), :], qkv_ref[...])
        for r in chunks:
            xh = (res[g, r : r + CHUNK, :] - mean3[g : g + 1]) * rstd3[g : g + 1]
            d = wide[r : r + CHUNK]
            res[g, r : r + CHUNK, :] = xh
            dyf[g, r : r + CHUNK, :] = d
            one += fold8(d)
            two += fold8(d * xh)
        ones3[g], twos3[g] = one, two

    staged(
        [
            norm_three,
            project,
            weigh,
            attend,
            join,
            head,
            head_back,
            attend_back,
            weigh_back,
            query_back,
            project_back,
        ]
    )

    ones, twos = total(ones3), total(twos3)
    add_vec(9, jnp.sum(ones, axis=0, keepdims=True))
    add_vec(8, jnp.sum(twos, axis=0, keepdims=True))

    def finish(ref, dest, rstd, gain, m1, m2, chans, extra, g, row):
        r1 = rstd[g : g + 1]
        acc = jnp.zeros((8, chans), F32)
        for r in chunks:
            d = dyf[g, r : r + CHUNK, :chans] * (gain * r1)
            d = d - m1[g : g + 1] * r1 - ref[g, r : r + CHUNK, :] * (m2[g : g + 1] * r1)
            if extra is not None:
                d = d + extra[g, r : r + CHUNK, :]
            acc += fold8(d)
            dest(g, r, d.astype(LOWTYPE))
        acc = jnp.sum(acc, axis=0, keepdims=True)
        add_vec(row, acc)
        return acc

    def to_pad(pad):
        def put(g, r, low):
            pad[g, SIDE + r : SIDE + r + CHUNK, :] = low

        return put

    def turned(parts):
        return stack(parts).T

    def pad_turned(pad):
        return turned([pad[g, SIDE : SIDE + PLACES, :] for g in images])

    def conv_back(pad, weights, g, chans, apply):
        wide = dot_nt(dy_cat(pad, g, (2, 1, 0)), weights)
        shiftf[g, 8 : 8 + PLACES, :chans] = wide[:, :chans]
        dyf[g, :, :chans] = wide[:, chans : 2 * chans]
        for r in chunks:
            after = shiftf[g, 9 + r : 9 + r + CHUNK, :chans]
            dyf[g, r : r + CHUNK, :chans] += jnp.where(edge(chans, False), after, 0.0)
        shiftf[g, 8 : 8 + PLACES, :chans] = wide[:, 2 * chans :]
        for r in chunks:
            before = shiftf[g, 7 + r : 7 + r + CHUNK, :chans]
            apply(r, dyf[g, r : r + CHUNK, :chans] + jnp.where(edge(chans, True), before, 0.0))

    def norm_back(pad, weights, ref, mean, rstd, gain, shift, chans, ones, twos, g):
        sums = [jnp.zeros((8, chans), F32), jnp.zeros((8, chans), F32)]

        def apply(r, da):
            xh = (ref[g, r : r + CHUNK, :] - mean[g : g + 1]) * rstd[g : g + 1]
            y = xh * gain + shift
            s = sigmoid(y)
            d = da * (s * (1.0 + y * (1.0 - s)))
            ref[g, r : r + CHUNK, :] = xh
            dyf[g, r : r + CHUNK, :chans] = d
            sums[0] += fold8(d)
            sums[1] += fold8(d * xh)

        conv_back(pad, weights[...], g, chans, apply)
        ones[g], twos[g] = sums

    def add_product(first, last, left, right):
        acc_ref[:, first:last] += dot_nn(left(), right())

    m1, m2 = grouped(ones * gain3, mid), grouped(twos * gain3, mid)
    ones2, twos2 = [None] * group, [None] * group

    def grad_out():
        add_product(SEG_OFF[7], SEG_OFF[8], lambda: dout[...].T, lambda: attl[...])

    def grad_project(k):
        add_product(
            SEG_OFF[4 + k],
            SEG_OFF[5 + k],
            lambda: dq3[:, k * mid : (k + 1) * mid].T,
            lambda: normed[...],
        )

    def grad_head():
        for g in images:
            ghead_ref[...] += dot_nn(dtap[g], joined[rows_of(g), :])

    staged(
        [
            lambda g: finish(res, to_pad(pad2), rstd3, gain3, m1, m2, mid, outp, g, 7),
            lambda g: norm_back(
                pad2, conv2b_ref, hid, mean2, rstd2, gain2, shift2, mid, ones2, twos2, g
            ),
        ],
        [grad_out, grad_head] + [functools.partial(grad_project, k) for k in range(3)],
    )
    ones, twos = total(ones2), total(twos2)
    add_vec(6, jnp.sum(ones, axis=0, keepdims=True))
    add_vec(5, jnp.sum(twos, axis=0, keepdims=True))

    n1, n2 = grouped(ones * gain2, mid), grouped(twos * gain2, mid)
    ones1, twos1 = [None] * group, [None] * group
    lowt2 = pad_turned(pad2)

    def finish_two(g):
        acc = finish(hid, to_pad(pad1), rstd2, gain2, n1, n2, mid, None, g, 3)
        add_vec(4, acc)
        gtime[pl.ds(step * group + g, 1), :] = acc

    def grad_conv(lowt, act, offset, k):
        width = act.shape[2]
        first = offset + k * width
        add_product(
            first,
            first + width,
            lambda: lowt,
            lambda: stack([act[g, SIDE * k : SIDE * k + PLACES, :] for g in images]),
        )

    def grad_skip():
        add_product(SEG_OFF[2], SEG_OFF[3], lambda: lowt2, lambda: low0[...])
        for g in images:
            dpool[g] += dot_nt(pad2[g, SIDE : SIDE + PLACES, :], skip_ref[...])

    staged(
        [
            finish_two,
            lambda g: norm_back(
                pad1, conv1b_ref, x0, mean1, rstd1, gain1, shift1, C1, ones1, twos1, g
            ),
        ],
        [functools.partial(grad_conv, lowt2, a2, SEG_OFF[1], k) for k in range(3)] + [grad_skip],
    )
    ones, twos = total(ones1), total(twos1)
    add_vec(2, jnp.sum(ones, axis=0, keepdims=True))
    add_vec(1, jnp.sum(twos, axis=0, keepdims=True))

    p1, p2 = grouped(ones * gain1, C1), grouped(twos * gain1, C1)
    lowt1 = pad_turned(pad1)

    def to_pool(g, r, low):
        dpool_low[g, r : r + CHUNK, :] = low

    def grad_stem(g):
        gstem_ref[...] += dot_nn(patch[g], dpool_low[g])

    staged(
        [lambda g: finish(x0, to_pool, rstd1, gain1, p1, p2, C1, dpool, g, 0), grad_stem],
        [functools.partial(grad_conv, lowt1, a1, SEG_OFF[0], k) for k in range(3)],
    )

    @pl.when(step == steps - 1)
    def _():
        acc_ref[:, SEG_OFF[3] : SEG_OFF[4]] = dot_tn(gtime[...].astype(LOWTYPE), time_ref[...])
        if rows_ref.shape[0] > 5120 + SMALL_ROWS:
            rows_ref[...] = jnp.zeros_like(rows_ref)
        pieces = gradient_pieces(owners, peers)
        for block in range(0, 5120, C1):
            turned = acc_ref[:, block : block + C1].T
            for source, size, target in pieces:
                low, high = max(source, block), min(source + size, block + C1)
                if low < high:
                    start = target + low - source
                    rows_ref[start : start + high - low, :] = turned[low - block : high - block]
        stem = lax.dot_general(
            spread_ref[...],
            gstem_ref[...],
            (((0,), (0,)), ((), ())),
            preferred_element_type=F32,
            precision=EXACT_PRECISION,
        )
        head = ghead_ref[...]
        none = jnp.zeros((ROWS12, C1), F32)
        tiles = [head[k : k + 16, :mid] for k in range(0, 144, 16)]
        for k in range(0, 80, 16):
            other = head[80 + k : 96 + k, mid:] if k < 64 else none
            tiles.append(jnp.concatenate([head[k : k + 16, mid:], other], axis=1))
        tiles.append(jnp.concatenate([stem[:16], stem[16:]], axis=1))
        for tile, (start, _) in zip(tiles, small_tiles(owners, peers)):
            rows_ref[start : start + 16, :] = tile
        misc_ref[:, :mid] = gvec_ref[...]
        misc_ref[13:14, :mid] = jnp.sum(loss_ref[...], axis=0, keepdims=True)
        misc_ref[14:15, :mid] = jnp.sum(wsum_ref[...], axis=0, keepdims=True)
        misc_ref[:, mid:] = ghb_ref[:, :C1] + ghb_ref[:, C1:]


def chunk_rows(owners, peers):
    share = -(-5120 // (owners * peers))
    return -(-share // 16) * 16, -(-(-(-SMALL_ROWS // peers)) // 16) * 16


def block_rows(owners, peers):
    chunk, small = chunk_rows(owners, peers)
    return owners * chunk + small


def slot_of(peer, peers):
    return peer % 2 * (peers // 2) + peer // 2


def gradient_pieces(owners, peers):
    chunk, _ = chunk_rows(owners, peers)
    block = block_rows(owners, peers)
    pieces = []
    for owner in range(owners):
        packed = 0
        for seg, seg_rows in enumerate(segment_rows()):
            share = seg_rows // owners
            done = 0
            while done < share:
                row = packed + done
                size = min(share - done, chunk - row % chunk)
                target = slot_of(row // chunk, peers) * block + owner * chunk + row % chunk
                pieces.append((SEG_OFF[seg] + owner * share + done, size, target))
                done += size
            packed += share
    return pieces


def small_tiles(owners, peers):
    chunk, small = chunk_rows(owners, peers)
    tiles = []
    for row in range(0, SMALL_ROWS, 16):
        slot = slot_of(row // small, peers)
        tiles.append((slot * block_rows(owners, peers) + owners * chunk + row % small, slot))
    return tiles


def unet_call(samples, owners, peers, operands):
    group = max(k for k in (1, 2, 4) if samples % k == 0)
    steps = samples // group
    time_rows = operands[3].shape[0]
    mid = CHANNELS_MID
    places = group * PLACES

    def image_spec():
        return pl.BlockSpec((group, ROWS12, PLACES), lambda i: (i, 0, 0))

    def whole(shape):
        return pl.BlockSpec(shape, lambda i: (0,) * len(shape))

    out_shapes = [(peers * block_rows(owners, peers), mid), (ROWS12, mid + C1)]
    scratch = [
        ((mid, 5120), F32),
        ((TAPS * ROWS12, C1), F32),
        ((TAPS * ROWS12, mid + C1), F32),
        ((ROWS12, mid), F32),
        ((ROWS12, mid), F32),
        ((ROWS12, mid), F32),
        ((ROWS12, mid), F32),
        ((group, PLACES, C1), F32),
        ((group, PLACES, mid), F32),
        ((group, PLACES, mid), F32),
        ((group, PLACES, mid), F32),
        ((group, PLACES, mid), F32),
        ((group, HALO, 3 * C1), LOWTYPE),
        ((group, HALO, 3 * mid), LOWTYPE),
        ((places, mid), LOWTYPE),
        ((places, 3 * mid), LOWTYPE),
        ((group, PLACES, mid), LOWTYPE),
        ((places, mid), LOWTYPE),
        ((places, C1), LOWTYPE),
        ((places, mid + C1), LOWTYPE),
        ((group, TAPS * ROWS12, PLACES), LOWTYPE),
        ((group, HALO, mid), LOWTYPE),
        ((group, HALO, mid), LOWTYPE),
        ((group, PLACES + 16, mid), F32),
        ((group, PLACES, mid), F32),
        ((places, mid), LOWTYPE),
        ((places, 3 * mid), LOWTYPE),
        ((group, PLACES, C1), F32),
        ((time_rows, mid), F32),
        ((time_rows, mid), F32),
        ((group, TAPS * ROWS12, PLACES), LOWTYPE),
        ((places, mid), LOWTYPE),
        ((group, PLACES, mid), LOWTYPE),
        ((group, PLACES, C1), LOWTYPE),
    ]
    return pl.pallas_call(
        functools.partial(unet_body, group, steps, owners, peers),
        grid=(steps,),
        out_shape=[jax.ShapeDtypeStruct(shape, F32) for shape in out_shapes],
        in_specs=[image_spec()] * 3 + [whole(a.shape) for a in operands[3:]],
        out_specs=[whole(shape) for shape in out_shapes],
        scratch_shapes=[pltpu.VMEM(shape, kind) for shape, kind in scratch],
        compiler_params=pltpu.CompilerParams(vmem_limit_bytes=VMEM_BYTES),
    )(*operands)


TASKS = ((1, 0), (0, 0), (0, 1), (2, 0), (1, 1), (2, 1), (3, 0), (3, 1))
MESH = pl.DeviceIdType.MESH
SMALL_LANES = 9 * (CHANNELS_MID + C1)


def ns_chain(gram, eye):
    product = None
    for step in range(NS_STEPS):
        square = dot_nn(gram, gram, EXACT_PRECISION)
        factor = NS_A * eye + NS_B * gram + NS_C * square
        product = factor if product is None else dot_nn(product, factor, EXACT_PRECISION)
        if step < NS_STEPS - 1:
            gram = dot_nn(factor, dot_nn(gram, factor, EXACT_PRECISION), EXACT_PRECISION)
    return product


def identity(size):
    rows = lax.broadcasted_iota(jnp.int32, (size, size), 0)
    cols = lax.broadcasted_iota(jnp.int32, (size, size), 1)
    return (rows == cols).astype(F32)


def muon_body(
    owners,
    peers,
    rows_ref,
    misc_ref,
    weight_ref,
    moment_ref,
    stem_ref,
    stemm_ref,
    head_ref,
    headm_ref,
    vec_ref,
    first_ref,
    second_ref,
    new_ref,
    newm_ref,
    copy_ref,
    nstem_ref,
    nstemm_ref,
    nhead_ref,
    nheadm_ref,
    nvec_ref,
    nfirst_ref,
    nsecond_ref,
    sums_ref,
    recv1,
    own2,
    send2,
    recv2,
    send3,
    recv3,
    recvs3,
    gathered,
    misc1,
    misc2,
    misc3,
    direction,
    mine_u,
    gram_part,
    gram_recv,
    gram_all,
    small,
    x_zero,
    x_one,
    sem1,
    sem2,
    sem3,
    sems3,
    sema,
    semb,
    semg,
    semh,
    semx,
    semy,
    semm1,
    semm2,
    semm3,
):
    mid = CHANNELS_MID
    chips = peers // 2
    chunk, small_chunk = chunk_rows(owners, peers)
    block = block_rows(owners, peers)
    held = chunk + small_chunk
    own_rows = weight_ref.shape[0]
    z = lax.axis_index("bucket")
    peer = lax.axis_index("batch")
    chip, core = peer // 2, peer % 2
    partner = {"batch": chip * 2 + 1 - core}
    started = []

    def same_core(k):
        return {"batch": lax.rem(chip + k, chips) * 2 + core}

    def along(k):
        return {"bucket": lax.rem(z + k, owners)}

    def send(source, target, sems, slot, device, begin=True):
        copy = pltpu.make_async_remote_copy(
            src_ref=source,
            dst_ref=target,
            send_sem=sems.at[0, slot],
            recv_sem=sems.at[1, slot],
            device_id=device,
            device_id_type=MESH,
        )
        copy.start()
        if begin:
            started.append(copy)
        return copy

    barrier = pltpu.get_barrier_semaphore()
    friends = [partner] + [same_core(k) for k in range(1, chips)]
    friends += [along(k) for k in range(1, owners)]
    for friend in friends:
        pl.semaphore_signal(barrier, inc=1, device_id=friend, device_id_type=MESH)
    pl.semaphore_wait(barrier, len(friends))

    misc_copy = send(misc_ref, misc1, semm1, 0, partner)
    first = []
    order = list(range(1, chips)) + [0]
    for k in order:
        other = lax.rem(chip + k, chips)
        start = pl.multiple_of(((1 - core) * chips + other) * block, 16)
        first.append(send(rows_ref.at[pl.ds(start, block), :], recv1.at[k], sem1, k, partner))

    misc_copy.wait_recv()
    misc2[chip] = misc_ref[...] + misc1[...]
    misc_copies = [
        send(misc2.at[chip], misc2.at[chip], semm2, k - 1, same_core(k)) for k in range(1, chips)
    ]
    second = []
    for k, copy in zip(order, first):
        copy.wait_recv()
        other = lax.rem(chip + k, chips)
        start = pl.multiple_of((core * chips + other) * block, 16)
        total = rows_ref[pl.ds(start, block), :] + recv1[k]
        if k == 0:
            own2[...] = total
        else:
            send2[k - 1] = total
            second.append(send(send2.at[k - 1], recv2.at[k - 1], sem2, k - 1, same_core(k)))

    for copy in misc_copies:
        copy.wait_recv()
    misc3[z] = sum([misc2[k] for k in range(1, chips)], misc2[0])
    misc_copies = [
        send(misc3.at[z], misc3.at[z], semm3, k - 1, along(k)) for k in range(1, owners)
    ]
    for copy in second:
        copy.wait_recv()
    third = []
    for k in list(range(1, owners)) + [0]:
        start = pl.multiple_of(lax.rem(z + k, owners) * chunk, 16)
        rows = pl.ds(start, chunk)
        total = own2[rows, :]
        for other in range(chips - 1):
            total = total + recv2[other, rows, :]
        if k == 0:
            own2[rows, :] = total
        else:
            send3[k - 1] = total
            third.append(send(send3.at[k - 1], recv3.at[k - 1], sem3, k - 1, along(k)))
    tail = slice(owners * chunk, block)
    total = own2[tail, :]
    for other in range(chips - 1):
        total = total + recv2[other, tail, :]
    recvs3[z] = total
    third += [
        send(recvs3.at[z], recvs3.at[z], sems3, k - 1, along(k)) for k in range(1, owners)
    ]
    for copy in third:
        copy.wait_recv()
    total = own2[pl.ds(pl.multiple_of(z * chunk, 16), chunk), :]
    for other in range(owners - 1):
        total = total + recv3[other]
    slot = core * chips + chip
    gathered[slot, :chunk, :] = total
    total = recvs3[0]
    for other in range(1, owners):
        total = total + recvs3[other]
    gathered[slot, chunk:, :] = total

    here = gathered.at[slot]
    plane = [send(here, here, sema, k - 1, same_core(k)) for k in range(1, chips)]
    cross = [send(here, here, semb, 0, partner)]

    for copy in misc_copies:
        copy.wait_recv()
    misc = sum([misc3[k] for k in range(1, owners)], misc3[0])
    weight_sum = jnp.sum(misc[14:15, :mid], axis=1, keepdims=True)
    inverse = 1.0 / weight_sum
    loss_sum = jnp.sum(misc[13:14, :mid], axis=1, keepdims=True)
    lane = lax.broadcasted_iota(jnp.int32, (8, C1), 1)
    sums_ref[...] = jnp.where(lane == 0, loss_sum, weight_sum)
    head_bias = jnp.sum(misc[:, mid:].T, axis=0, keepdims=True)
    nvec_ref[...] = jnp.zeros_like(nvec_ref)
    nvec_ref[:3, :] = misc[:3, :C1]
    for row in range(3, 13):
        nvec_ref[2 * row - 3 : 2 * row - 2, :] = misc[row : row + 1, :C1]
        nvec_ref[2 * row - 2 : 2 * row - 1, :] = misc[row : row + 1, C1:mid]
    nvec_ref[23:24, :ROWS12] = head_bias
    grad = nvec_ref[...] * inverse
    firsts = BETA_ONE * first_ref[...] + (1.0 - BETA_ONE) * grad
    seconds = BETA_TWO * second_ref[...] + (1.0 - BETA_TWO) * grad * grad
    nfirst_ref[...] = firsts
    nsecond_ref[...] = seconds
    change = (
        firsts
        / (1.0 - BETA_ONE**STEP)
        / (jnp.sqrt(seconds / (1.0 - BETA_TWO**STEP)) + ADAM_EPS)
    )
    nvec_ref[...] = vec_ref[...] - LR_ADAM * change

    for k, copy in zip(range(1, chips), plane):
        copy.wait_recv()
        other = gathered.at[core * chips + lax.rem(chip + chips - k, chips)]
        cross.append(send(other, other, semb, k, partner))
    for copy in cross:
        copy.wait_recv()

    for owner_peer in range(peers):
        start = owner_peer * chunk
        size = min(chunk, own_rows - start)
        if size > 0:
            grad = gathered[slot_of(owner_peer, peers), :size, :] * inverse
            rows = slice(start, start + size)
            moment = MOMENTUM * moment_ref[rows, :] + grad
            newm_ref[rows, :] = moment
            direction[rows, :] = grad + MOMENTUM * moment
    shares = [rows // owners for rows in segment_rows()]
    starts = [sum(shares[:k]) for k in range(len(shares))]
    for (task_chip, task_core), share, start in zip(TASKS, shares, starts):

        @pl.when((lax.rem(chip, 4) == task_chip) & (core == task_core))
        def _(share=share, start=start):
            mine_u[:share, :] = direction[start : start + share, :]
            if share < mine_u.shape[0]:
                mine_u[share:, :] = jnp.zeros((mine_u.shape[0] - share, mid), F32)

    mine = mine_u[...]
    gram_part[...] = lax.dot_general(
        mine,
        mine,
        (((0,), (0,)), ((), ())),
        preferred_element_type=F32,
        precision=EXACT_PRECISION,
    )
    part = mid // owners
    copies = []
    for k in range(1, owners):
        start = pl.multiple_of(lax.rem(z + k, owners) * part, 8)
        copies.append(send(gram_part.at[pl.ds(start, part), :], gram_recv.at[z], semg, k - 1, along(k)))
    own_part = pl.ds(pl.multiple_of(z * part, 8), part)
    gram_recv[z] = gram_part[own_part, :]

    chunk_s = small_chunk
    tiles = []
    for tile in range(SMALL_ROWS // 16):
        row = tile * 16
        at = chunk + row % chunk_s
        tiles.append(gathered[slot_of(row // chunk_s, peers), at : at + 16, :] * inverse)
    for tap in range(TAPS):
        lanes = slice(tap * (mid + C1), tap * (mid + C1) + mid)
        nheadm_ref[:, lanes] = tiles[tap]
        lanes = slice(tap * (mid + C1) + mid, (tap + 1) * (mid + C1))
        if tap < 5:
            nheadm_ref[:, lanes] = tiles[9 + tap][:, :C1]
        else:
            nheadm_ref[:, lanes] = tiles[9 + tap - 5][:, C1:]
    grad = nheadm_ref[...]
    moment = MOMENTUM * headm_ref[...] + grad
    nheadm_ref[...] = moment
    turn = grad + MOMENTUM * moment
    small[...] = jnp.zeros_like(small)
    small[:16, :SMALL_LANES] = turn * lax.rsqrt(
        jnp.sum(jnp.sum(turn * turn, axis=1, keepdims=True), axis=0, keepdims=True) + NORM_EPS
    )
    grad = jnp.concatenate([tiles[14][:, :C1], tiles[14][:, C1:]], axis=0)
    moment = MOMENTUM * stemm_ref[...] + grad
    nstemm_ref[...] = moment
    turn = grad + MOMENTUM * moment
    small[32:, SMALL_LANES:] = turn * lax.rsqrt(
        jnp.sum(jnp.sum(turn * turn, axis=1, keepdims=True), axis=0, keepdims=True) + NORM_EPS
    )
    gram = lax.dot_general(
        small[...],
        small[...],
        (((1,), (1,)), ((), ())),
        preferred_element_type=F32,
        precision=EXACT_PRECISION,
    )
    product = ns_chain(gram, identity(64))
    turned = dot_nn(product, small[...], EXACT_PRECISION)
    keep = 1.0 - LR_MUON * DECAY
    nhead_ref[...] = head_ref[...] * keep - LR_MUON * turned[:16, :SMALL_LANES]
    nstem_ref[...] = stem_ref[...] * keep - LR_MUON * turned[32:, SMALL_LANES:]

    for copy in copies:
        copy.wait_recv()
    gram_all[own_part, :] = sum([gram_recv[k] for k in range(1, owners)], gram_recv[0])
    copies = [
        send(gram_all.at[own_part, :], gram_all.at[own_part, :], semh, k - 1, along(k))
        for k in range(1, owners)
    ]
    for copy in copies:
        copy.wait_recv()
    gram = gram_all[...]
    eye = identity(mid)
    trace = jnp.sum(jnp.sum(gram * eye, axis=1, keepdims=True), axis=0, keepdims=True)
    scale = lax.rsqrt(trace + NORM_EPS)
    product = ns_chain(gram * (scale * scale), eye) * scale
    turned = dot_nn(mine_u[...], product, EXACT_PRECISION)

    place = lax.rem(chip, 4)
    base = chip - place

    def in_group(k):
        return {"batch": (base + lax.rem(place + k, 4)) * 2 + core}

    for task_core, buffer in ((0, x_zero), (1, x_one)):

        @pl.when(core == task_core)
        def _(buffer=buffer, other_buffer=(x_one, x_zero)[task_core]):
            size = buffer.shape[1]
            buffer[place] = turned[:size].astype(LOWTYPE)
            here = buffer.at[place]
            plane = [send(here, here, semx, k - 1, in_group(k), False) for k in range(1, 4)]
            cross = [send(here, here, semy, 0, partner, False)]
            for k in range(1, 4):
                plane[k - 1].wait_recv()
                other = buffer.at[lax.rem(place + 4 - k, 4)]
                cross.append(send(other, other, semy, k, partner, False))
            for k in range(4):
                there = other_buffer.at[lax.rem(place + 4 - k, 4)]
                pltpu.make_async_remote_copy(
                    src_ref=there,
                    dst_ref=there,
                    send_sem=semy.at[0, k],
                    recv_sem=semy.at[1, k],
                    device_id=partner,
                    device_id_type=MESH,
                ).wait_recv()
            for copy in plane + cross:
                copy.wait_send()

    for (task_chip, task_core), share, start in zip(TASKS, shares, starts):
        buffer = (x_zero, x_one)[task_core]
        rows = slice(start, start + share)
        fresh = weight_ref[rows, :] * keep - LR_MUON * buffer[task_chip, :share, :].astype(F32)
        new_ref[rows, :] = fresh
        copy_ref[rows, :] = fresh.astype(LOWTYPE)
    for copy in started:
        copy.wait_send()


def muon_call(owners, peers, operands):
    mid = CHANNELS_MID
    chips = peers // 2
    chunk, small_chunk = chunk_rows(owners, peers)
    block = block_rows(owners, peers)
    rows = operands[2].shape[0]
    part = mid // owners
    shares = [seg_rows // owners for seg_rows in segment_rows()]
    most = [max(s for s, t in zip(shares, TASKS) if t[1] == core) for core in (0, 1)]
    out_shapes = [
        ((rows, mid), F32),
        ((rows, mid), F32),
        ((rows, mid), LOWTYPE),
        (operands[4].shape, F32),
        (operands[4].shape, F32),
        (operands[6].shape, F32),
        (operands[6].shape, F32),
        (operands[8].shape, F32),
        (operands[8].shape, F32),
        (operands[8].shape, F32),
        ((8, C1), F32),
    ]
    scratch = [
        ((chips, block, mid), F32),
        ((block, mid), F32),
        ((chips - 1, block, mid), F32),
        ((chips - 1, block, mid), F32),
        ((owners - 1, chunk, mid), F32),
        ((owners - 1, chunk, mid), F32),
        ((owners, small_chunk, mid), F32),
        ((peers, chunk + small_chunk, mid), F32),
        (operands[1].shape, F32),
        ((chips,) + operands[1].shape, F32),
        ((owners,) + operands[1].shape, F32),
        ((rows, mid), F32),
        ((max(most), mid), F32),
        ((mid, mid), F32),
        ((owners, part, mid), F32),
        ((mid, mid), F32),
        ((64, SMALL_LANES + C1), F32),
        ((4, most[0], mid), LOWTYPE),
        ((4, most[1], mid), LOWTYPE),
    ]
    sems = [
        chips,
        chips - 1,
        owners - 1,
        owners - 1,
        chips - 1,
        chips,
        owners - 1,
        owners - 1,
        3,
        4,
        1,
        chips - 1,
        owners - 1,
    ]
    vmem = pl.BlockSpec(memory_space=pltpu.VMEM)
    return pl.pallas_call(
        functools.partial(muon_body, owners, peers),
        out_shape=[jax.ShapeDtypeStruct(shape, kind) for shape, kind in out_shapes],
        in_specs=[vmem] * len(operands),
        out_specs=[vmem] * len(out_shapes),
        scratch_shapes=[pltpu.VMEM(shape, kind) for shape, kind in scratch]
        + [pltpu.SemaphoreType.DMA((2, count)) for count in sems],
        compiler_params=pltpu.CompilerParams(
            vmem_limit_bytes=VMEM_BYTES, collective_id=0, has_side_effects=True
        ),
    )(*operands)


def open_body(
    owners,
    peers,
    weight_ref,
    images_ref,
    noise_ref,
    mask_ref,
    image_ref,
    conv1_ref,
    conv1b_ref,
    conv2_ref,
    conv2b_ref,
    skip_ref,
    temb_ref,
    qkv_ref,
    outw_ref,
    noisy_ref,
    planes_ref,
    maskw_ref,
    held,
    left,
    sema,
    semb,
    semc,
):
    mid = CHANNELS_MID
    chips = peers // 2
    chunk, _ = chunk_rows(owners, peers)
    own_rows = weight_ref.shape[0]
    z = lax.axis_index("bucket")
    peer = lax.axis_index("batch")
    chip, core = peer // 2, peer % 2
    partner = {"batch": chip * 2 + 1 - core}
    slot = core * chips + chip
    started = []

    def same_core(k):
        return {"batch": lax.rem(chip + k, chips) * 2 + core}

    def along(k):
        return {"bucket": lax.rem(z + k, owners)}

    def send(source, target, sems, index, device):
        copy = pltpu.make_async_remote_copy(
            src_ref=source,
            dst_ref=target,
            send_sem=sems.at[0, index],
            recv_sem=sems.at[1, index],
            device_id=device,
            device_id_type=MESH,
        )
        copy.start()
        started.append(copy)
        return copy

    barrier = pltpu.get_barrier_semaphore()
    friends = [partner] + [same_core(k) for k in range(1, chips)]
    friends += [along(k) for k in range(1, owners)]
    for friend in friends:
        pl.semaphore_signal(barrier, inc=1, device_id=friend, device_id_type=MESH)

    for other in range(peers):
        start = other * chunk
        size = min(chunk, own_rows - start)
        if size > 0:
            held[z, slot_of(other, peers), :size, :] = weight_ref[start : start + size, :].astype(
                LOWTYPE
            )
        if size < chunk:
            held[z, slot_of(other, peers), max(size, 0) :, :] = jnp.zeros(
                (chunk - max(size, 0), mid), LOWTYPE
            )
    pl.semaphore_wait(barrier, len(friends))

    here = held.at[z, slot]
    first = [send(here, here, sema, k - 1, along(k)) for k in range(1, owners)]

    samples = mask_ref.shape[0]
    left[...] = jnp.zeros_like(left)
    for c in range(3):
        noise = noise_ref[c]
        noisy = image_ref[:, 0:1] * images_ref[c] + image_ref[:, 1:2] * noise
        left[c, :samples, :] = noisy.astype(LOWTYPE)
        one = noise.astype(LOWTYPE)
        rest = noise - one.astype(F32)
        two = rest.astype(LOWTYPE)
        left[3 + c, :samples, :] = one
        left[6 + c, :samples, :] = two
        left[9 + c, :samples, :] = (rest - two.astype(F32)).astype(LOWTYPE)
    left[12, :samples, :] = mask_ref[...].astype(F32).astype(LOWTYPE)
    for ref in (noisy_ref, planes_ref, maskw_ref):
        ref[:, 12:, :] = jnp.zeros((samples, ROWS12 - 12, PLACES), F32)

    def picture(quarter):
        pixel = lax.broadcasted_iota(jnp.int32, (S * S, PLACES), 0)
        lane = lax.broadcasted_iota(jnp.int32, (S * S, PLACES), 1)
        wanted = (
            (lane // SIDE * 2 + quarter // 2) * S + lane % SIDE * 2 + quarter % 2
        )
        pick = jnp.where(pixel == wanted, 1.0, 0.0).astype(LOWTYPE)
        rows = left.shape[1]
        moved = dot_nn(left[...].reshape(13 * rows, S * S), pick)
        maskw = moved[12 * rows : 12 * rows + samples] * image_ref[:, 2:3]
        for c in range(3):
            k = quarter * 3 + c
            noisy_ref[:, k, :] = moved[c * rows : c * rows + samples]
            planes_ref[:, k, :] = sum(
                [moved[(p + c) * rows : (p + c) * rows + samples] for p in (6, 9)],
                moved[(3 + c) * rows : (3 + c) * rows + samples],
            )
            maskw_ref[:, k, :] = maskw

    picture(0)
    second = []
    for k, copy in zip(range(1, owners), first):
        copy.wait_recv()
        there = held.at[lax.rem(z + owners - k, owners), slot]
        second.append(
            [
                send(there, there, semb, (k - 1) * (chips - 1) + j - 1, same_core(j))
                for j in range(1, chips)
            ]
        )
        if k < 4:
            picture(k)
    for k in range(owners, 4):
        picture(k)
    third = []
    for k, copies in zip(range(1, owners), second):
        for copy in copies:
            copy.wait_recv()
        mine = held.at[lax.rem(z + owners - k, owners), pl.ds(core * chips, chips)]
        third.append(send(mine, mine, semc, k - 1, partner))
    for copy in third:
        copy.wait_recv()

    def place(seg, row, values):
        size = values.shape[0]
        if seg < 2:
            whole, side = ((conv1_ref, conv1b_ref), (conv2_ref, conv2b_ref))[seg]
            whole[row : row + size, :] = values
            height = side.shape[0]
            done = 0
            while done < size:
                offset, inner = (row + done) // height, (row + done) % height
                part = min(size - done, height - inner)
                side[inner : inner + part, offset * mid : (offset + 1) * mid] = values[
                    done : done + part
                ]
                done += part
        elif seg in (4, 5, 6):
            qkv_ref[row : row + size, (seg - 4) * mid : (seg - 3) * mid] = values
        else:
            {2: skip_ref, 3: temb_ref, 7: outw_ref}[seg][row : row + size, :] = values

    for owner in range(owners):
        packed = 0
        for seg, seg_rows in enumerate(segment_rows()):
            share = seg_rows // owners
            done = 0
            while done < share:
                row = packed + done
                size = min(share - done, chunk - row % chunk)
                inner = row % chunk
                place(
                    seg,
                    owner * share + done,
                    held[owner, slot_of(row // chunk, peers), inner : inner + size, :],
                )
                done += size
            packed += share
    for copy in started:
        copy.wait_send()


def open_call(owners, peers, operands):
    mid = CHANNELS_MID
    chips = peers // 2
    chunk, _ = chunk_rows(owners, peers)
    samples = operands[3].shape[0]
    rows = -(-samples // 16) * 16
    out_shapes = [
        ((9 * C1, mid), LOWTYPE),
        ((3 * C1, 3 * mid), LOWTYPE),
        ((9 * mid, mid), LOWTYPE),
        ((3 * mid, 3 * mid), LOWTYPE),
        ((C1, mid), LOWTYPE),
        ((TEMB, mid), LOWTYPE),
        ((mid, 3 * mid), LOWTYPE),
        ((mid, mid), LOWTYPE),
        ((samples, ROWS12, PLACES), F32),
        ((samples, ROWS12, PLACES), F32),
        ((samples, ROWS12, PLACES), F32),
    ]
    vmem = pl.BlockSpec(memory_space=pltpu.VMEM)
    return pl.pallas_call(
        functools.partial(open_body, owners, peers),
        out_shape=[jax.ShapeDtypeStruct(shape, kind) for shape, kind in out_shapes],
        in_specs=[vmem] * len(operands),
        out_specs=[vmem] * len(out_shapes),
        scratch_shapes=[
            pltpu.VMEM((owners, peers, chunk, mid), LOWTYPE),
            pltpu.VMEM((13, rows, S * S), LOWTYPE),
            pltpu.SemaphoreType.DMA((2, owners - 1)),
            pltpu.SemaphoreType.DMA((2, (owners - 1) * (chips - 1))),
            pltpu.SemaphoreType.DMA((2, owners - 1)),
        ],
        compiler_params=pltpu.CompilerParams(
            vmem_limit_bytes=VMEM_BYTES, collective_id=1, has_side_effects=True
        ),
    )(*operands)


def stem_spread():
    counts = np.zeros((3, 2, 3))
    for block in range(3):
        for inner in range(2):
            for sub in range(2):
                tap = 2 * (block - 1) + inner - sub + 1
                if 0 <= tap <= 2:
                    counts[block, inner, tap] += 1
    full = np.zeros((3, 3, ROWS12, 3, 3, 3))
    both = (np.einsum("ayt,bxu->abyxtu", counts, counts) * 0.25).reshape(3, 3, 4, 3, 3)
    for c in range(3):
        full[:, :, c:12:3, :, :, c] = both
    return jnp.asarray(full.reshape(TAPS * ROWS12, 27), F32)


def split_three(values):
    first = lax.reduce_precision(values, 8, 7)
    second = lax.reduce_precision(values - first, 8, 7)
    third = values - first - second
    return jnp.concatenate([first, second, third], axis=1).astype(LOWTYPE)


def pad_rows(values, rows):
    return jnp.pad(values, [(0, 0)] * (values.ndim - 2) + [(0, rows - values.shape[-2]), (0, 0)])


def lanes_of(vector):
    rows = -(-vector.shape[0] // (8 * C1)) * 8
    return jnp.pad(vector, (0, rows * C1 - vector.shape[0]), constant_values=1.0).reshape(rows, C1)


def same_group(chans):
    group = np.arange(chans) // (chans // GROUPS)
    same = (group[:, None] == group[None, :]) / (PLACES * (chans // GROUPS))
    return jnp.asarray(same, LOWTYPE)


def shards(
    images,
    pixel_mask,
    timesteps,
    noise_field,
    matrices,
    matrix_moms,
    stem_weight,
    stem_moms,
    head_weight,
    head_moms,
    vectors,
    vector_firsts,
    vector_seconds,
):
    owners, peers = lax.axis_size("bucket"), lax.axis_size("batch")
    samples = images.shape[0]
    level, weight = plan(timesteps)
    per_image = jnp.stack([jnp.sqrt(level), jnp.sqrt(1.0 - level), weight], axis=1)
    conv1, conv1b, conv2, conv2b, skip, temb, qkv, outw, noisy, noise, mask_weight = open_call(
        owners,
        peers,
        [
            matrices,
            images.transpose(1, 0, 2),
            noise_field.transpose(1, 0, 2),
            pixel_mask,
            per_image,
        ],
    )
    time_in = pad_rows(swish(embed(timesteps)).astype(LOWTYPE), -(-samples // 16) * 16)
    spread = stem_spread()
    stem_blocks = split_three(
        jnp.dot(spread, lax.reduce_precision(stem_weight, 8, 7), precision=EXACT_PRECISION)
    )
    head_turned = head_weight.T
    head_rows = head_turned.astype(LOWTYPE).reshape(12, TAPS, CHANNELS_MID + C1)
    head_rows = pad_rows(head_rows.transpose(1, 0, 2), ROWS12).reshape(TAPS * ROWS12, -1)
    vec_rows = lanes_of(vectors)
    head_bias = jnp.broadcast_to(pad_rows(vectors[-12:].reshape(12, 1), ROWS12), (ROWS12, C1))
    rows_out, misc = unet_call(
        samples,
        owners,
        peers,
        [
            noisy,
            noise,
            mask_weight,
            time_in,
            stem_blocks,
            head_rows,
            conv1,
            conv1b,
            conv2,
            conv2b,
            skip,
            temb,
            qkv,
            outw,
            vec_rows,
            head_bias,
            same_group(C1),
            same_group(CHANNELS_MID),
            jnp.pad(spread, ((0, 0), (0, 5))),
        ],
    )
    (
        new_matrices,
        new_matrix_moms,
        matrix_copies,
        new_stem,
        new_stem_moms,
        new_head,
        new_head_moms,
        new_vec,
        new_first,
        new_second,
        sums,
    ) = muon_call(
        owners,
        peers,
        [
            rows_out,
            misc,
            matrices,
            matrix_moms,
            pad_rows(stem_weight, 32),
            pad_rows(stem_moms, 32),
            pad_rows(head_turned, ROWS12),
            pad_rows(head_moms.T, ROWS12),
            vec_rows,
            lanes_of(vector_firsts),
            lanes_of(vector_seconds),
        ],
    )
    count = vectors.shape[0]
    new_stem, new_stem_moms = new_stem[:27], new_stem_moms[:27]
    new_head, new_head_moms = new_head[:12].T, new_head_moms[:12].T
    new_vectors = new_vec.reshape(-1)[:count]
    new_firsts = new_first.reshape(-1)[:count]
    new_seconds = new_second.reshape(-1)[:count]
    loss_sum, weight_sum = sums[0, 0], sums[0, 1]
    return (
        loss_sum,
        weight_sum,
        new_matrices,
        new_matrix_moms,
        matrix_copies,
        new_stem,
        new_stem_moms,
        new_stem.astype(LOWTYPE),
        new_head,
        new_head_moms,
        new_head.astype(LOWTYPE),
        new_vectors,
        new_firsts,
        new_seconds,
        new_vectors.astype(LOWTYPE),
    )


def solution(mesh):
    return jax.shard_map(
        shards,
        mesh=mesh,
        in_specs=(
            P(("bucket", "batch"), None, None),
            P(("bucket", "batch"), None),
            P(("bucket", "batch")),
            P(("bucket", "batch"), None, None),
            P("bucket", None),
            P("bucket", None),
            P(),
            P(),
            P(),
            P(),
            P(),
            P(),
            P(),
        ),
        out_specs=(
            P(),
            P(),
            P("bucket", None),
            P("bucket", None),
            P("bucket", None),
            P(),
            P(),
            P(),
            P(),
            P(),
            P(),
            P(),
            P(),
            P(),
            P(),
        ),
        check_vma=False,
    )
```

```python
import functools
import math

import jax
import jax.numpy as jnp
import numpy as np
from jax import lax
from jax.experimental import pallas as pl
from jax.experimental.pallas import tpu as pltpu
from jax.sharding import PartitionSpec as P

C1 = 128
CHANNELS_MID = 256
TEMB = 512
GROUPS = 32
S = 32
TSTEPS = 1000
NS_STEPS = 5
STEP = 10


GN_EPS = 1e-05
NORM_EPS = 1e-12
MOMENTUM = 0.95
LR_MUON = 0.5
DECAY = 0.01
NS_A = 3.4445
NS_B = -4.775
NS_C = 2.0315
BETA_ONE = 0.9
BETA_TWO = 0.999
LR_ADAM = 0.5
ADAM_EPS = 1e-08
EXACT_PRECISION = lax.Precision.HIGHEST
LOWTYPE = jnp.bfloat16


def segment_rows():
    return [
        9 * C1,
        9 * CHANNELS_MID,
        C1,
        TEMB,
        CHANNELS_MID,
        CHANNELS_MID,
        CHANNELS_MID,
        CHANNELS_MID,
    ]


def plan(timesteps):
    frac_t = (timesteps.astype(jnp.float32) / TSTEPS + 0.008) / 1.008
    level = jnp.cos(frac_t * (math.pi / 2)) ** 2
    ratio = level / (1.0 - level)
    return (level, jnp.minimum(1.0, 5.0 / ratio))


def embed(timesteps):
    half_width = TEMB // 2
    freqs = jnp.exp(-math.log(10000.0) * jnp.arange(half_width, dtype=jnp.float32) / half_width)
    angles = timesteps.astype(jnp.float32)[:, None] * freqs[None, :]
    return jnp.concatenate([jnp.sin(angles), jnp.cos(angles)], axis=1)


def swish(values):
    return values * jax.nn.sigmoid(values)


F32 = jnp.float32
PLACES = 256
SIDE = 16
HALO = 288
TAPS = 9
ROWS12 = 16
CHUNK = 64
SMALL_ROWS = 240
VMEM_BYTES = 56 * 1024 * 1024
SEG_OFF = (0, 1152, 3456, 3584, 4096, 4352, 4608, 4864, 5120)


def dot_nn(a, b, precision=None):
    return lax.dot_general(
        a, b, (((1,), (0,)), ((), ())), preferred_element_type=F32, precision=precision
    )


def dot_nt(a, b):
    return lax.dot_general(a, b, (((1,), (1,)), ((), ())), preferred_element_type=F32)


def dot_tn(a, b):
    return lax.dot_general(a, b, (((0,), (0,)), ((), ())), preferred_element_type=F32)


def sigmoid(v):
    return 1.0 / (1.0 + jnp.exp(-v))


def fold8(v):
    rows, chans = v.shape
    return jnp.sum(v.reshape(rows // 8, 8, chans), axis=0)


def shift_lanes(x, di, dj):
    lane = lax.broadcasted_iota(jnp.int32, x.shape, 1)
    row, col = lane // SIDE + di, lane % SIDE + dj
    offset = (-(SIDE * di + dj)) % PLACES
    moved = x if offset == 0 else pltpu.roll(x, offset, 1)
    valid = (row >= 0) & (row < SIDE) & (col >= 0) & (col < SIDE)
    return jnp.where(valid, moved, 0.0)


def tap_offsets():
    return [(di, dj) for di in (-1, 0, 1) for dj in (-1, 0, 1)]


def unet_body(
    group,
    steps,
    owners,
    peers,
    noisy_ref,
    noise_ref,
    maskw_ref,
    time_ref,
    stemw_ref,
    headw_ref,
    conv1_ref,
    conv1b_ref,
    conv2_ref,
    conv2b_ref,
    skip_ref,
    temb_ref,
    qkv_ref,
    outw_ref,
    vec_ref,
    headb_ref,
    same128_ref,
    same256_ref,
    spread_ref,
    rows_ref,
    misc_ref,
    acc_ref,
    gstem_ref,
    ghead_ref,
    gvec_ref,
    ghb_ref,
    loss_ref,
    wsum_ref,
    x0,
    hid,
    res,
    outp,
    attn,
    a1,
    a2,
    normed,
    qkv,
    plow,
    attl,
    low0,
    joined,
    patch,
    pad1,
    pad2,
    shiftf,
    dyf,
    dout,
    dq3,
    dpool,
    tproj,
    gtime,
    dtap,
    datt,
    dscore,
    dpool_low,
):
    step = pl.program_id(0)
    mid = CHANNELS_MID
    chunks = range(0, PLACES, CHUNK)
    images = range(group)

    @pl.when(step == 0)
    def _():
        acc_ref[...] = jnp.zeros_like(acc_ref)
        gstem_ref[...] = jnp.zeros_like(gstem_ref)
        ghead_ref[...] = jnp.zeros_like(ghead_ref)
        gvec_ref[...] = jnp.zeros_like(gvec_ref)
        ghb_ref[...] = jnp.zeros_like(ghb_ref)
        loss_ref[...] = jnp.zeros_like(loss_ref)
        wsum_ref[...] = jnp.zeros_like(wsum_ref)
        gtime[...] = jnp.zeros_like(gtime)
        for ref in (a1, a2, pad1, pad2):
            for g in images:
                ref[g, :SIDE, :] = jnp.zeros((SIDE, ref.shape[2]), ref.dtype)
                ref[g, HALO - SIDE :, :] = jnp.zeros((SIDE, ref.shape[2]), ref.dtype)
        shiftf[...] = jnp.zeros_like(shiftf)
        tproj[...] = dot_nn(time_ref[...], temb_ref[...])

    def vec(row, chans=mid):
        if chans == C1:
            return vec_ref[row : row + 1, :]
        row = 2 * row - 3
        return jnp.concatenate([vec_ref[row : row + 1, :], vec_ref[row + 1 : row + 2, :]], axis=1)

    def add_vec(row, value):
        gvec_ref[row : row + 1, : value.shape[1]] += value

    def total(parts):
        return jnp.concatenate([jnp.sum(p, axis=0, keepdims=True) for p in parts], axis=0)

    def grouped(stats, chans):
        same = same128_ref if chans == C1 else same256_ref
        first = stats.astype(LOWTYPE).astype(F32)
        second = (stats - first).astype(LOWTYPE).astype(F32)
        third = stats - first - second
        sums = dot_nn(jnp.concatenate([first, second, third], axis=0).astype(LOWTYPE), same[...])
        return sums[:group] + sums[group : 2 * group] + sums[2 * group :]

    def gn_stats(ref, sums, chans):
        mean = grouped(sums, chans)
        parts = []
        for g in images:
            acc = jnp.zeros((8, chans), F32)
            for r in chunks:
                c = ref[g, r : r + CHUNK, :] - mean[g : g + 1]
                acc += fold8(c * c)
            parts.append(acc)
        return mean, lax.rsqrt(grouped(total(parts), chans) + GN_EPS)

    def edge(chans, left):
        col = lax.broadcasted_iota(jnp.int32, (CHUNK, chans), 0) % SIDE
        return (col > 0) if left else (col < SIDE - 1)

    def act_shift(ref, g, mean, rstd, gain, shift, dest, chans):
        for r in chunks:
            y = (ref[g, r : r + CHUNK, :] - mean[g : g + 1]) * rstd[g : g + 1] * gain + shift
            a = y * sigmoid(y)
            shiftf[g, 8 + r : 8 + r + CHUNK, :chans] = a
            dest[g, SIDE + r : SIDE + r + CHUNK, chans : 2 * chans] = a.astype(LOWTYPE)
        for r in chunks:
            before = shiftf[g, 7 + r : 7 + r + CHUNK, :chans]
            after = shiftf[g, 9 + r : 9 + r + CHUNK, :chans]
            rows = slice(SIDE + r, SIDE + r + CHUNK)
            dest[g, rows, :chans] = jnp.where(edge(chans, True), before, 0.0).astype(LOWTYPE)
            dest[g, rows, 2 * chans :] = jnp.where(edge(chans, False), after, 0.0).astype(LOWTYPE)

    def dy_cat(ref, g, order):
        return jnp.concatenate(
            [ref[g, SIDE * k : SIDE * k + PLACES, :] for k in order], axis=1
        )

    def stack(parts):
        return jnp.concatenate(parts, axis=0) if len(parts) > 1 else parts[0]

    def staged(stages, fillers=()):
        fillers = list(fillers)
        for stage in stages:
            for g in images:
                stage(g)
            if fillers:
                fillers.pop(0)()
        for filler in fillers:
            filler()

    def rows_of(g):
        return slice(g * PLACES, (g + 1) * PLACES)

    sums1 = [None] * group

    def stem_patch(g):
        noisy = noisy_ref[g]
        for tap, (di, dj) in enumerate(tap_offsets()):
            patch[g, tap * ROWS12 : (tap + 1) * ROWS12, :] = shift_lanes(noisy, di, dj).astype(
                LOWTYPE
            )

    def stem_pool(g):
        wide = dot_tn(patch[g], stemw_ref[...])
        acc = jnp.zeros((8, C1), F32)
        for r in chunks:
            w = wide[r : r + CHUNK]
            v = (w[:, :C1] + w[:, C1 : 2 * C1]) + w[:, 2 * C1 :] + vec(0, C1)
            x0[g, r : r + CHUNK, :] = v
            low0[g * PLACES + r : g * PLACES + r + CHUNK, :] = v.astype(LOWTYPE)
            acc += fold8(v)
        sums1[g] = acc

    staged([stem_patch, stem_pool])
    mean1, rstd1 = gn_stats(x0, total(sums1), C1)
    gain1, shift1 = vec(1, C1), vec(2, C1)

    sums2 = [None] * group

    def act_one(g):
        act_shift(x0, g, mean1, rstd1, gain1, shift1, a1, C1)

    def conv_one(g):
        wide = dot_nn(dy_cat(a1, g, (0, 1, 2)), conv1_ref[...])
        bias = vec(3) + vec(4) + tproj[pl.ds(step * group + g, 1), :]
        acc = jnp.zeros((8, mid), F32)
        for r in chunks:
            v = wide[r : r + CHUNK] + bias
            hid[g, r : r + CHUNK, :] = v
            acc += fold8(v)
        sums2[g] = acc

    staged([act_one, conv_one])
    mean2, rstd2 = gn_stats(hid, total(sums2), mid)
    gain2, shift2 = vec(5), vec(6)

    sums3 = [None] * group

    def act_two(g):
        act_shift(hid, g, mean2, rstd2, gain2, shift2, a2, mid)

    def conv_two(g):
        wide = dot_nn(dy_cat(a2, g, (0, 1, 2)), conv2_ref[...])
        wide = wide + dot_nn(low0[rows_of(g), :], skip_ref[...])
        acc = jnp.zeros((8, mid), F32)
        for r in chunks:
            v = wide[r : r + CHUNK] + vec(7)
            res[g, r : r + CHUNK, :] = v
            acc += fold8(v)
        sums3[g] = acc

    staged([act_two, conv_two])
    mean3, rstd3 = gn_stats(res, total(sums3), mid)
    gain3, shift3 = vec(8), vec(9)
    scale = mid ** (-0.5)
    ones3, twos3 = [None] * group, [None] * group

    def norm_three(g):
        for r in chunks:
            xh = (res[g, r : r + CHUNK, :] - mean3[g : g + 1]) * rstd3[g : g + 1]
            y = xh * gain3 + shift3
            normed[g * PLACES + r : g * PLACES + r + CHUNK, :] = y.astype(LOWTYPE)

    def project(g):
        rows = rows_of(g)
        wide = dot_nn(normed[rows, :], qkv_ref[...])
        qkv[rows, :mid] = (wide[:, :mid] + vec(10)).astype(LOWTYPE)
        qkv[rows, mid : 2 * mid] = wide[:, mid : 2 * mid].astype(LOWTYPE)
        qkv[rows, 2 * mid :] = (wide[:, 2 * mid :] + vec(11)).astype(LOWTYPE)

    def weigh(g):
        rows = rows_of(g)
        logits = dot_nt(qkv[rows, :mid], qkv[rows, mid : 2 * mid])
        for r in chunks:
            s = logits[r : r + CHUNK] * scale
            e = jnp.exp(s - jnp.max(s, axis=1, keepdims=True))
            p = e * (1.0 / jnp.sum(e, axis=1, keepdims=True))
            attn[g, r : r + CHUNK, :] = p
            plow[g, r : r + CHUNK, :] = p.astype(LOWTYPE)

    def attend(g):
        attl[rows_of(g), :] = dot_nn(plow[g], qkv[rows_of(g), 2 * mid :]).astype(LOWTYPE)

    def join(g):
        wide = dot_nn(attl[rows_of(g), :], outw_ref[...])
        for r in chunks:
            rows = slice(g * PLACES + r, g * PLACES + r + CHUNK)
            o = res[g, r : r + CHUNK, :] + wide[r : r + CHUNK] + vec(12)
            outp[g, r : r + CHUNK, :] = o
            joined[rows, :mid] = (o * sigmoid(o)).astype(LOWTYPE)
            x = x0[g, r : r + CHUNK, :]
            joined[rows, mid:] = (x * sigmoid(x)).astype(LOWTYPE)

    def head(g):
        taps = dot_nt(headw_ref[...], joined[rows_of(g), :])
        value = headb_ref[:, :1] + jnp.zeros((ROWS12, PLACES), F32)
        for tap, (di, dj) in enumerate(tap_offsets()):
            value = value + shift_lanes(taps[tap * ROWS12 : (tap + 1) * ROWS12, :], di, dj)
        error = value - noise_ref[g]
        masked = maskw_ref[g] * error
        loss_ref[...] += masked * error
        wsum_ref[...] += maskw_ref[g]
        grad = 2.0 * masked
        ghb_ref[...] += grad
        gradl = grad.astype(LOWTYPE).astype(F32)
        for tap, (di, dj) in enumerate(tap_offsets()):
            dtap[g, tap * ROWS12 : (tap + 1) * ROWS12, :] = shift_lanes(gradl, -di, -dj).astype(
                LOWTYPE
            )

    def head_back(g):
        wide = dot_tn(dtap[g], headw_ref[...])
        acc = jnp.zeros((8, mid), F32)
        for r in chunks:
            o = outp[g, r : r + CHUNK, :]
            s = sigmoid(o)
            d = wide[r : r + CHUNK, :mid] * (s * (1.0 + o * (1.0 - s)))
            outp[g, r : r + CHUNK, :] = d
            dout[g * PLACES + r : g * PLACES + r + CHUNK, :] = d.astype(LOWTYPE)
            acc += fold8(d)
            x = x0[g, r : r + CHUNK, :]
            s = sigmoid(x)
            dpool[g, r : r + CHUNK, :] = wide[r : r + CHUNK, mid:] * (s * (1.0 + x * (1.0 - s)))
        add_vec(12, jnp.sum(acc, axis=0, keepdims=True))

    def attend_back(g):
        datt[rows_of(g), :] = dot_nt(dout[rows_of(g), :], outw_ref[...]).astype(LOWTYPE)

    def weigh_back(g):
        rows = rows_of(g)
        gweights = dot_nt(datt[rows, :], qkv[rows, 2 * mid :])
        dval = dot_tn(plow[g], datt[rows, :])
        add_vec(11, jnp.sum(fold8(dval), axis=0, keepdims=True))
        dq3[rows, 2 * mid :] = dval.astype(LOWTYPE)
        for r in chunks:
            p = attn[g, r : r + CHUNK, :]
            gw = gweights[r : r + CHUNK]
            ds = p * (gw - jnp.sum(gw * p, axis=1, keepdims=True))
            dscore[g, r : r + CHUNK, :] = (ds * scale).astype(LOWTYPE)

    def query_back(g):
        rows = rows_of(g)
        dqry = dot_nn(dscore[g], qkv[rows, mid : 2 * mid])
        dkey = dot_tn(dscore[g], qkv[rows, :mid])
        add_vec(10, jnp.sum(fold8(dqry), axis=0, keepdims=True))
        dq3[rows, :mid] = dqry.astype(LOWTYPE)
        dq3[rows, mid : 2 * mid] = dkey.astype(LOWTYPE)

    def project_back(g):
        one, two = jnp.zeros((8, mid), F32), jnp.zeros((8, mid), F32)
        wide = dot_nt(dq3[rows_of(g), :], qkv_ref[...])
        for r in chunks:
            xh = (res[g, r : r + CHUNK, :] - mean3[g : g + 1]) * rstd3[g : g + 1]
            d = wide[r : r + CHUNK]
            res[g, r : r + CHUNK, :] = xh
            dyf[g, r : r + CHUNK, :] = d
            one += fold8(d)
            two += fold8(d * xh)
        ones3[g], twos3[g] = one, two

    staged(
        [
            norm_three,
            project,
            weigh,
            attend,
            join,
            head,
            head_back,
            attend_back,
            weigh_back,
            query_back,
            project_back,
        ]
    )

    ones, twos = total(ones3), total(twos3)
    add_vec(9, jnp.sum(ones, axis=0, keepdims=True))
    add_vec(8, jnp.sum(twos, axis=0, keepdims=True))

    def finish(ref, dest, rstd, gain, m1, m2, chans, extra, g, row):
        r1 = rstd[g : g + 1]
        acc = jnp.zeros((8, chans), F32)
        for r in chunks:
            d = dyf[g, r : r + CHUNK, :chans] * (gain * r1)
            d = d - m1[g : g + 1] * r1 - ref[g, r : r + CHUNK, :] * (m2[g : g + 1] * r1)
            if extra is not None:
                d = d + extra[g, r : r + CHUNK, :]
            acc += fold8(d)
            dest(g, r, d.astype(LOWTYPE))
        acc = jnp.sum(acc, axis=0, keepdims=True)
        add_vec(row, acc)
        return acc

    def to_pad(pad):
        def put(g, r, low):
            pad[g, SIDE + r : SIDE + r + CHUNK, :] = low

        return put

    def turned(parts):
        return stack(parts).T

    def pad_turned(pad):
        return turned([pad[g, SIDE : SIDE + PLACES, :] for g in images])

    def conv_back(pad, weights, g, chans, apply):
        wide = dot_nt(dy_cat(pad, g, (2, 1, 0)), weights)
        shiftf[g, 8 : 8 + PLACES, :chans] = wide[:, :chans]
        dyf[g, :, :chans] = wide[:, chans : 2 * chans]
        for r in chunks:
            after = shiftf[g, 9 + r : 9 + r + CHUNK, :chans]
            dyf[g, r : r + CHUNK, :chans] += jnp.where(edge(chans, False), after, 0.0)
        shiftf[g, 8 : 8 + PLACES, :chans] = wide[:, 2 * chans :]
        for r in chunks:
            before = shiftf[g, 7 + r : 7 + r + CHUNK, :chans]
            apply(r, dyf[g, r : r + CHUNK, :chans] + jnp.where(edge(chans, True), before, 0.0))

    def norm_back(pad, weights, ref, mean, rstd, gain, shift, chans, ones, twos, g):
        sums = [jnp.zeros((8, chans), F32), jnp.zeros((8, chans), F32)]

        def apply(r, da):
            xh = (ref[g, r : r + CHUNK, :] - mean[g : g + 1]) * rstd[g : g + 1]
            y = xh * gain + shift
            s = sigmoid(y)
            d = da * (s * (1.0 + y * (1.0 - s)))
            ref[g, r : r + CHUNK, :] = xh
            dyf[g, r : r + CHUNK, :chans] = d
            sums[0] += fold8(d)
            sums[1] += fold8(d * xh)

        conv_back(pad, weights[...], g, chans, apply)
        ones[g], twos[g] = sums

    def add_product(first, last, left, right):
        acc_ref[:, first:last] += dot_nn(left(), right())

    m1, m2 = grouped(ones * gain3, mid), grouped(twos * gain3, mid)
    ones2, twos2 = [None] * group, [None] * group

    def grad_out():
        add_product(SEG_OFF[7], SEG_OFF[8], lambda: dout[...].T, lambda: attl[...])

    def grad_project(k):
        add_product(
            SEG_OFF[4 + k],
            SEG_OFF[5 + k],
            lambda: dq3[:, k * mid : (k + 1) * mid].T,
            lambda: normed[...],
        )

    def grad_head():
        for g in images:
            ghead_ref[...] += dot_nn(dtap[g], joined[rows_of(g), :])

    staged(
        [
            lambda g: finish(res, to_pad(pad2), rstd3, gain3, m1, m2, mid, outp, g, 7),
            lambda g: norm_back(
                pad2, conv2b_ref, hid, mean2, rstd2, gain2, shift2, mid, ones2, twos2, g
            ),
        ],
        [grad_out, grad_head] + [functools.partial(grad_project, k) for k in range(3)],
    )
    ones, twos = total(ones2), total(twos2)
    add_vec(6, jnp.sum(ones, axis=0, keepdims=True))
    add_vec(5, jnp.sum(twos, axis=0, keepdims=True))

    n1, n2 = grouped(ones * gain2, mid), grouped(twos * gain2, mid)
    ones1, twos1 = [None] * group, [None] * group
    lowt2 = pad_turned(pad2)

    def finish_two(g):
        acc = finish(hid, to_pad(pad1), rstd2, gain2, n1, n2, mid, None, g, 3)
        add_vec(4, acc)
        gtime[pl.ds(step * group + g, 1), :] = acc

    def grad_conv(lowt, act, offset, k):
        width = act.shape[2]
        first = offset + k * width
        add_product(
            first,
            first + width,
            lambda: lowt,
            lambda: stack([act[g, SIDE * k : SIDE * k + PLACES, :] for g in images]),
        )

    def grad_skip():
        add_product(SEG_OFF[2], SEG_OFF[3], lambda: lowt2, lambda: low0[...])
        for g in images:
            dpool[g] += dot_nt(pad2[g, SIDE : SIDE + PLACES, :], skip_ref[...])

    staged(
        [
            finish_two,
            lambda g: norm_back(
                pad1, conv1b_ref, x0, mean1, rstd1, gain1, shift1, C1, ones1, twos1, g
            ),
        ],
        [functools.partial(grad_conv, lowt2, a2, SEG_OFF[1], k) for k in range(3)] + [grad_skip],
    )
    ones, twos = total(ones1), total(twos1)
    add_vec(2, jnp.sum(ones, axis=0, keepdims=True))
    add_vec(1, jnp.sum(twos, axis=0, keepdims=True))

    p1, p2 = grouped(ones * gain1, C1), grouped(twos * gain1, C1)
    lowt1 = pad_turned(pad1)

    def to_pool(g, r, low):
        dpool_low[g, r : r + CHUNK, :] = low

    def grad_stem(g):
        gstem_ref[...] += dot_nn(patch[g], dpool_low[g])

    staged(
        [lambda g: finish(x0, to_pool, rstd1, gain1, p1, p2, C1, dpool, g, 0), grad_stem],
        [functools.partial(grad_conv, lowt1, a1, SEG_OFF[0], k) for k in range(3)],
    )

    @pl.when(step == steps - 1)
    def _():
        acc_ref[:, SEG_OFF[3] : SEG_OFF[4]] = dot_tn(gtime[...].astype(LOWTYPE), time_ref[...])
        if rows_ref.shape[0] > 5120 + SMALL_ROWS:
            rows_ref[...] = jnp.zeros_like(rows_ref)
        pieces = gradient_pieces(owners, peers)
        for block in range(0, 5120, C1):
            turned = acc_ref[:, block : block + C1].T
            for source, size, target in pieces:
                low, high = max(source, block), min(source + size, block + C1)
                if low < high:
                    start = target + low - source
                    rows_ref[start : start + high - low, :] = turned[low - block : high - block]
        stem = lax.dot_general(
            spread_ref[...],
            gstem_ref[...],
            (((0,), (0,)), ((), ())),
            preferred_element_type=F32,
            precision=EXACT_PRECISION,
        )
        head = ghead_ref[...]
        none = jnp.zeros((ROWS12, C1), F32)
        tiles = [head[k : k + 16, :mid] for k in range(0, 144, 16)]
        for k in range(0, 80, 16):
            other = head[80 + k : 96 + k, mid:] if k < 64 else none
            tiles.append(jnp.concatenate([head[k : k + 16, mid:], other], axis=1))
        tiles.append(jnp.concatenate([stem[:16], stem[16:]], axis=1))
        for tile, (start, _) in zip(tiles, small_tiles(owners, peers)):
            rows_ref[start : start + 16, :] = tile
        misc_ref[:, :mid] = gvec_ref[...]
        misc_ref[13:14, :mid] = jnp.sum(loss_ref[...], axis=0, keepdims=True)
        misc_ref[14:15, :mid] = jnp.sum(wsum_ref[...], axis=0, keepdims=True)
        misc_ref[:, mid:] = ghb_ref[:, :C1] + ghb_ref[:, C1:]


def chunk_rows(owners, peers):
    share = -(-5120 // (owners * peers))
    return -(-share // 16) * 16, -(-(-(-SMALL_ROWS // peers)) // 16) * 16


def block_rows(owners, peers):
    chunk, small = chunk_rows(owners, peers)
    return owners * chunk + small


def slot_of(peer, peers):
    return peer % 2 * (peers // 2) + peer // 2


def gradient_pieces(owners, peers):
    chunk, _ = chunk_rows(owners, peers)
    block = block_rows(owners, peers)
    pieces = []
    for owner in range(owners):
        packed = 0
        for seg, seg_rows in enumerate(segment_rows()):
            share = seg_rows // owners
            done = 0
            while done < share:
                row = packed + done
                size = min(share - done, chunk - row % chunk)
                target = slot_of(row // chunk, peers) * block + owner * chunk + row % chunk
                pieces.append((SEG_OFF[seg] + owner * share + done, size, target))
                done += size
            packed += share
    return pieces


def small_tiles(owners, peers):
    chunk, small = chunk_rows(owners, peers)
    tiles = []
    for row in range(0, SMALL_ROWS, 16):
        slot = slot_of(row // small, peers)
        tiles.append((slot * block_rows(owners, peers) + owners * chunk + row % small, slot))
    return tiles


def unet_call(samples, owners, peers, operands):
    group = max(k for k in (1, 2, 4) if samples % k == 0)
    steps = samples // group
    time_rows = operands[3].shape[0]
    mid = CHANNELS_MID
    places = group * PLACES

    def image_spec():
        return pl.BlockSpec((group, ROWS12, PLACES), lambda i: (i, 0, 0))

    def whole(shape):
        return pl.BlockSpec(shape, lambda i: (0,) * len(shape))

    out_shapes = [(peers * block_rows(owners, peers), mid), (ROWS12, mid + C1)]
    scratch = [
        ((mid, 5120), F32),
        ((TAPS * ROWS12, C1), F32),
        ((TAPS * ROWS12, mid + C1), F32),
        ((ROWS12, mid), F32),
        ((ROWS12, mid), F32),
        ((ROWS12, mid), F32),
        ((ROWS12, mid), F32),
        ((group, PLACES, C1), F32),
        ((group, PLACES, mid), F32),
        ((group, PLACES, mid), F32),
        ((group, PLACES, mid), F32),
        ((group, PLACES, mid), F32),
        ((group, HALO, 3 * C1), LOWTYPE),
        ((group, HALO, 3 * mid), LOWTYPE),
        ((places, mid), LOWTYPE),
        ((places, 3 * mid), LOWTYPE),
        ((group, PLACES, mid), LOWTYPE),
        ((places, mid), LOWTYPE),
        ((places, C1), LOWTYPE),
        ((places, mid + C1), LOWTYPE),
        ((group, TAPS * ROWS12, PLACES), LOWTYPE),
        ((group, HALO, mid), LOWTYPE),
        ((group, HALO, mid), LOWTYPE),
        ((group, PLACES + 16, mid), F32),
        ((group, PLACES, mid), F32),
        ((places, mid), LOWTYPE),
        ((places, 3 * mid), LOWTYPE),
        ((group, PLACES, C1), F32),
        ((time_rows, mid), F32),
        ((time_rows, mid), F32),
        ((group, TAPS * ROWS12, PLACES), LOWTYPE),
        ((places, mid), LOWTYPE),
        ((group, PLACES, mid), LOWTYPE),
        ((group, PLACES, C1), LOWTYPE),
    ]
    return pl.pallas_call(
        functools.partial(unet_body, group, steps, owners, peers),
        grid=(steps,),
        out_shape=[jax.ShapeDtypeStruct(shape, F32) for shape in out_shapes],
        in_specs=[image_spec()] * 3 + [whole(a.shape) for a in operands[3:]],
        out_specs=[whole(shape) for shape in out_shapes],
        scratch_shapes=[pltpu.VMEM(shape, kind) for shape, kind in scratch],
        compiler_params=pltpu.CompilerParams(vmem_limit_bytes=VMEM_BYTES),
    )(*operands)


TASKS = ((1, 0), (0, 0), (0, 1), (2, 0), (1, 1), (2, 1), (3, 0), (3, 1))
MESH = pl.DeviceIdType.MESH
SMALL_LANES = 9 * (CHANNELS_MID + C1)


def ns_chain(gram, eye):
    product = None
    for step in range(NS_STEPS):
        square = dot_nn(gram, gram, EXACT_PRECISION)
        factor = NS_A * eye + NS_B * gram + NS_C * square
        product = factor if product is None else dot_nn(product, factor, EXACT_PRECISION)
        if step < NS_STEPS - 1:
            gram = dot_nn(factor, dot_nn(gram, factor, EXACT_PRECISION), EXACT_PRECISION)
    return product


def identity(size):
    rows = lax.broadcasted_iota(jnp.int32, (size, size), 0)
    cols = lax.broadcasted_iota(jnp.int32, (size, size), 1)
    return (rows == cols).astype(F32)


def muon_body(
    owners,
    peers,
    rows_ref,
    misc_ref,
    weight_ref,
    moment_ref,
    stem_ref,
    stemm_ref,
    head_ref,
    headm_ref,
    vec_ref,
    first_ref,
    second_ref,
    new_ref,
    newm_ref,
    copy_ref,
    nstem_ref,
    nstemm_ref,
    nhead_ref,
    nheadm_ref,
    nvec_ref,
    nfirst_ref,
    nsecond_ref,
    sums_ref,
    recv1,
    own2,
    send2,
    recv2,
    send3,
    recv3,
    recvs3,
    gathered,
    misc1,
    misc2,
    misc3,
    direction,
    mine_u,
    gram_part,
    gram_recv,
    gram_all,
    small,
    x_zero,
    x_one,
    sem1,
    sem2,
    sem3,
    sems3,
    sema,
    semb,
    semg,
    semh,
    semx,
    semy,
    semm1,
    semm2,
    semm3,
):
    mid = CHANNELS_MID
    chips = peers // 2
    chunk, small_chunk = chunk_rows(owners, peers)
    block = block_rows(owners, peers)
    held = chunk + small_chunk
    own_rows = weight_ref.shape[0]
    z = lax.axis_index("bucket")
    peer = lax.axis_index("batch")
    chip, core = peer // 2, peer % 2
    partner = {"batch": chip * 2 + 1 - core}
    started = []

    def same_core(k):
        return {"batch": lax.rem(chip + k, chips) * 2 + core}

    def along(k):
        return {"bucket": lax.rem(z + k, owners)}

    def send(source, target, sems, slot, device, begin=True):
        copy = pltpu.make_async_remote_copy(
            src_ref=source,
            dst_ref=target,
            send_sem=sems.at[0, slot],
            recv_sem=sems.at[1, slot],
            device_id=device,
            device_id_type=MESH,
        )
        copy.start()
        if begin:
            started.append(copy)
        return copy

    barrier = pltpu.get_barrier_semaphore()
    friends = [partner] + [same_core(k) for k in range(1, chips)]
    friends += [along(k) for k in range(1, owners)]
    for friend in friends:
        pl.semaphore_signal(barrier, inc=1, device_id=friend, device_id_type=MESH)
    pl.semaphore_wait(barrier, len(friends))

    parts = [None] + list(range(1, owners)) + [0]

    def part_rows(part, base=0):
        if part is None:
            return pl.ds(pl.multiple_of(base + owners * chunk, 16), small_chunk)
        start = base + lax.rem(z + part, owners) * chunk
        return pl.ds(pl.multiple_of(start, 16), chunk)

    def base_of(k, other_core):
        owner_core = 1 - core if other_core else core
        return (owner_core * chips + lax.rem(chip + k, chips)) * block

    misc_copy = send(misc_ref, misc1, semm1, 0, partner)
    order = list(range(1, chips)) + [0]
    first = {}
    for number, part in enumerate(parts):
        for k in order:
            first[part, k] = send(
                rows_ref.at[part_rows(part, base_of(k, True)), :],
                recv1.at[k, part_rows(part), :],
                sem1,
                number * chips + k,
                partner,
            )

    misc_copy.wait_recv()
    misc2[chip] = misc_ref[...] + misc1[...]
    misc_copies = [
        send(misc2.at[chip], misc2.at[chip], semm2, k - 1, same_core(k)) for k in range(1, chips)
    ]
    second = {}
    for number, part in enumerate(parts):
        rows = part_rows(part)
        for k in order:
            first[part, k].wait_recv()
            total = rows_ref[part_rows(part, base_of(k, False)), :] + recv1[k, rows, :]
            if k == 0:
                own2[rows, :] = total
            else:
                send2[k - 1, rows, :] = total
                second[part, k] = send(
                    send2.at[k - 1, rows, :],
                    recv2.at[k - 1, rows, :],
                    sem2,
                    number * (chips - 1) + k - 1,
                    same_core(k),
                )

    for copy in misc_copies:
        copy.wait_recv()
    misc3[z] = sum([misc2[k] for k in range(1, chips)], misc2[0])
    misc_copies = [
        send(misc3.at[z], misc3.at[z], semm3, k - 1, along(k)) for k in range(1, owners)
    ]
    third = []
    for part in parts:
        for k in range(1, chips):
            second[part, k].wait_recv()
        rows = part_rows(part)
        total = own2[rows, :]
        for other in range(chips - 1):
            total = total + recv2[other, rows, :]
        if part is None:
            recvs3[z] = total
            third += [
                send(recvs3.at[z], recvs3.at[z], sems3, k - 1, along(k)) for k in range(1, owners)
            ]
        elif part == 0:
            own2[rows, :] = total
        else:
            send3[part - 1] = total
            third.append(
                send(send3.at[part - 1], recv3.at[part - 1], sem3, part - 1, along(part))
            )
    for copy in third:
        copy.wait_recv()
    total = own2[pl.ds(pl.multiple_of(z * chunk, 16), chunk), :]
    for other in range(owners - 1):
        total = total + recv3[other]
    slot = core * chips + chip
    gathered[slot, :chunk, :] = total
    total = recvs3[0]
    for other in range(1, owners):
        total = total + recvs3[other]
    gathered[slot, chunk:, :] = total

    here = gathered.at[slot]
    plane = [send(here, here, sema, k - 1, same_core(k)) for k in range(1, chips)]
    cross = [send(here, here, semb, 0, partner)]

    for copy in misc_copies:
        copy.wait_recv()
    misc = sum([misc3[k] for k in range(1, owners)], misc3[0])
    weight_sum = jnp.sum(misc[14:15, :mid], axis=1, keepdims=True)
    inverse = 1.0 / weight_sum
    loss_sum = jnp.sum(misc[13:14, :mid], axis=1, keepdims=True)
    lane = lax.broadcasted_iota(jnp.int32, (8, C1), 1)
    sums_ref[...] = jnp.where(lane == 0, loss_sum, weight_sum)
    head_bias = jnp.sum(misc[:, mid:].T, axis=0, keepdims=True)
    nvec_ref[...] = jnp.zeros_like(nvec_ref)
    nvec_ref[:3, :] = misc[:3, :C1]
    for row in range(3, 13):
        nvec_ref[2 * row - 3 : 2 * row - 2, :] = misc[row : row + 1, :C1]
        nvec_ref[2 * row - 2 : 2 * row - 1, :] = misc[row : row + 1, C1:mid]
    nvec_ref[23:24, :ROWS12] = head_bias
    grad = nvec_ref[...] * inverse
    firsts = BETA_ONE * first_ref[...] + (1.0 - BETA_ONE) * grad
    seconds = BETA_TWO * second_ref[...] + (1.0 - BETA_TWO) * grad * grad
    nfirst_ref[...] = firsts
    nsecond_ref[...] = seconds
    change = (
        firsts
        / (1.0 - BETA_ONE**STEP)
        / (jnp.sqrt(seconds / (1.0 - BETA_TWO**STEP)) + ADAM_EPS)
    )
    nvec_ref[...] = vec_ref[...] - LR_ADAM * change

    for k, copy in zip(range(1, chips), plane):
        copy.wait_recv()
        other = gathered.at[core * chips + lax.rem(chip + chips - k, chips)]
        cross.append(send(other, other, semb, k, partner))
    for copy in cross:
        copy.wait_recv()

    for owner_peer in range(peers):
        start = owner_peer * chunk
        size = min(chunk, own_rows - start)
        if size > 0:
            grad = gathered[slot_of(owner_peer, peers), :size, :] * inverse
            rows = slice(start, start + size)
            moment = MOMENTUM * moment_ref[rows, :] + grad
            newm_ref[rows, :] = moment
            direction[rows, :] = grad + MOMENTUM * moment
    shares = [rows // owners for rows in segment_rows()]
    starts = [sum(shares[:k]) for k in range(len(shares))]
    for (task_chip, task_core), share, start in zip(TASKS, shares, starts):

        @pl.when((lax.rem(chip, 4) == task_chip) & (core == task_core))
        def _(share=share, start=start):
            mine_u[:share, :] = direction[start : start + share, :]
            if share < mine_u.shape[0]:
                mine_u[share:, :] = jnp.zeros((mine_u.shape[0] - share, mid), F32)

    mine = mine_u[...]
    gram_part[...] = lax.dot_general(
        mine,
        mine,
        (((0,), (0,)), ((), ())),
        preferred_element_type=F32,
        precision=EXACT_PRECISION,
    )
    part = mid // owners
    copies = []
    for k in range(1, owners):
        start = pl.multiple_of(lax.rem(z + k, owners) * part, 8)
        copies.append(send(gram_part.at[pl.ds(start, part), :], gram_recv.at[z], semg, k - 1, along(k)))
    own_part = pl.ds(pl.multiple_of(z * part, 8), part)
    gram_recv[z] = gram_part[own_part, :]

    chunk_s = small_chunk
    tiles = []
    for tile in range(SMALL_ROWS // 16):
        row = tile * 16
        at = chunk + row % chunk_s
        tiles.append(gathered[slot_of(row // chunk_s, peers), at : at + 16, :] * inverse)
    for tap in range(TAPS):
        lanes = slice(tap * (mid + C1), tap * (mid + C1) + mid)
        nheadm_ref[:, lanes] = tiles[tap]
        lanes = slice(tap * (mid + C1) + mid, (tap + 1) * (mid + C1))
        if tap < 5:
            nheadm_ref[:, lanes] = tiles[9 + tap][:, :C1]
        else:
            nheadm_ref[:, lanes] = tiles[9 + tap - 5][:, C1:]
    grad = nheadm_ref[...]
    moment = MOMENTUM * headm_ref[...] + grad
    nheadm_ref[...] = moment
    turn = grad + MOMENTUM * moment
    small[...] = jnp.zeros_like(small)
    small[:16, :SMALL_LANES] = turn * lax.rsqrt(
        jnp.sum(jnp.sum(turn * turn, axis=1, keepdims=True), axis=0, keepdims=True) + NORM_EPS
    )
    grad = jnp.concatenate([tiles[14][:, :C1], tiles[14][:, C1:]], axis=0)
    moment = MOMENTUM * stemm_ref[...] + grad
    nstemm_ref[...] = moment
    turn = grad + MOMENTUM * moment
    small[32:, SMALL_LANES:] = turn * lax.rsqrt(
        jnp.sum(jnp.sum(turn * turn, axis=1, keepdims=True), axis=0, keepdims=True) + NORM_EPS
    )
    gram = lax.dot_general(
        small[...],
        small[...],
        (((1,), (1,)), ((), ())),
        preferred_element_type=F32,
        precision=EXACT_PRECISION,
    )
    product = ns_chain(gram, identity(64))
    turned = dot_nn(product, small[...], EXACT_PRECISION)
    keep = 1.0 - LR_MUON * DECAY
    nhead_ref[...] = head_ref[...] * keep - LR_MUON * turned[:16, :SMALL_LANES]
    nstem_ref[...] = stem_ref[...] * keep - LR_MUON * turned[32:, SMALL_LANES:]

    for copy in copies:
        copy.wait_recv()
    gram_all[own_part, :] = sum([gram_recv[k] for k in range(1, owners)], gram_recv[0])
    copies = [
        send(gram_all.at[own_part, :], gram_all.at[own_part, :], semh, k - 1, along(k))
        for k in range(1, owners)
    ]
    for copy in copies:
        copy.wait_recv()
    gram = gram_all[...]
    eye = identity(mid)
    trace = jnp.sum(jnp.sum(gram * eye, axis=1, keepdims=True), axis=0, keepdims=True)
    scale = lax.rsqrt(trace + NORM_EPS)
    product = ns_chain(gram * (scale * scale), eye) * scale
    turned = dot_nn(mine_u[...], product, EXACT_PRECISION)

    place = lax.rem(chip, 4)
    base = chip - place

    def in_group(k):
        return {"batch": (base + lax.rem(place + k, 4)) * 2 + core}

    for task_core, buffer in ((0, x_zero), (1, x_one)):

        @pl.when(core == task_core)
        def _(buffer=buffer, other_buffer=(x_one, x_zero)[task_core]):
            size = buffer.shape[1]
            buffer[place] = turned[:size].astype(LOWTYPE)
            here = buffer.at[place]
            plane = [send(here, here, semx, k - 1, in_group(k), False) for k in range(1, 4)]
            cross = [send(here, here, semy, 0, partner, False)]
            for k in range(1, 4):
                plane[k - 1].wait_recv()
                other = buffer.at[lax.rem(place + 4 - k, 4)]
                cross.append(send(other, other, semy, k, partner, False))
            for k in range(4):
                there = other_buffer.at[lax.rem(place + 4 - k, 4)]
                pltpu.make_async_remote_copy(
                    src_ref=there,
                    dst_ref=there,
                    send_sem=semy.at[0, k],
                    recv_sem=semy.at[1, k],
                    device_id=partner,
                    device_id_type=MESH,
                ).wait_recv()
            for copy in plane + cross:
                copy.wait_send()

    for (task_chip, task_core), share, start in zip(TASKS, shares, starts):
        buffer = (x_zero, x_one)[task_core]
        rows = slice(start, start + share)
        fresh = weight_ref[rows, :] * keep - LR_MUON * buffer[task_chip, :share, :].astype(F32)
        new_ref[rows, :] = fresh
        copy_ref[rows, :] = fresh.astype(LOWTYPE)
    for copy in started:
        copy.wait_send()


def muon_call(owners, peers, operands):
    mid = CHANNELS_MID
    chips = peers // 2
    chunk, small_chunk = chunk_rows(owners, peers)
    block = block_rows(owners, peers)
    rows = operands[2].shape[0]
    part = mid // owners
    shares = [seg_rows // owners for seg_rows in segment_rows()]
    most = [max(s for s, t in zip(shares, TASKS) if t[1] == core) for core in (0, 1)]
    out_shapes = [
        ((rows, mid), F32),
        ((rows, mid), F32),
        ((rows, mid), LOWTYPE),
        (operands[4].shape, F32),
        (operands[4].shape, F32),
        (operands[6].shape, F32),
        (operands[6].shape, F32),
        (operands[8].shape, F32),
        (operands[8].shape, F32),
        (operands[8].shape, F32),
        ((8, C1), F32),
    ]
    scratch = [
        ((chips, block, mid), F32),
        ((block, mid), F32),
        ((chips - 1, block, mid), F32),
        ((chips - 1, block, mid), F32),
        ((owners - 1, chunk, mid), F32),
        ((owners - 1, chunk, mid), F32),
        ((owners, small_chunk, mid), F32),
        ((peers, chunk + small_chunk, mid), F32),
        (operands[1].shape, F32),
        ((chips,) + operands[1].shape, F32),
        ((owners,) + operands[1].shape, F32),
        ((rows, mid), F32),
        ((max(most), mid), F32),
        ((mid, mid), F32),
        ((owners, part, mid), F32),
        ((mid, mid), F32),
        ((64, SMALL_LANES + C1), F32),
        ((4, most[0], mid), LOWTYPE),
        ((4, most[1], mid), LOWTYPE),
    ]
    sems = [
        (owners + 1) * chips,
        (owners + 1) * (chips - 1),
        owners - 1,
        owners - 1,
        chips - 1,
        chips,
        owners - 1,
        owners - 1,
        3,
        4,
        1,
        chips - 1,
        owners - 1,
    ]
    vmem = pl.BlockSpec(memory_space=pltpu.VMEM)
    return pl.pallas_call(
        functools.partial(muon_body, owners, peers),
        out_shape=[jax.ShapeDtypeStruct(shape, kind) for shape, kind in out_shapes],
        in_specs=[vmem] * len(operands),
        out_specs=[vmem] * len(out_shapes),
        scratch_shapes=[pltpu.VMEM(shape, kind) for shape, kind in scratch]
        + [pltpu.SemaphoreType.DMA((2, count)) for count in sems],
        compiler_params=pltpu.CompilerParams(
            vmem_limit_bytes=VMEM_BYTES, collective_id=0, has_side_effects=True
        ),
    )(*operands)


def open_body(
    owners,
    peers,
    weight_ref,
    images_ref,
    noise_ref,
    mask_ref,
    image_ref,
    conv1_ref,
    conv1b_ref,
    conv2_ref,
    conv2b_ref,
    skip_ref,
    temb_ref,
    qkv_ref,
    outw_ref,
    noisy_ref,
    planes_ref,
    maskw_ref,
    held,
    left,
    sema,
    semb,
    semc,
):
    mid = CHANNELS_MID
    chips = peers // 2
    chunk, _ = chunk_rows(owners, peers)
    own_rows = weight_ref.shape[0]
    z = lax.axis_index("bucket")
    peer = lax.axis_index("batch")
    chip, core = peer // 2, peer % 2
    partner = {"batch": chip * 2 + 1 - core}
    slot = core * chips + chip
    started = []

    def same_core(k):
        return {"batch": lax.rem(chip + k, chips) * 2 + core}

    def along(k):
        return {"bucket": lax.rem(z + k, owners)}

    def send(source, target, sems, index, device):
        copy = pltpu.make_async_remote_copy(
            src_ref=source,
            dst_ref=target,
            send_sem=sems.at[0, index],
            recv_sem=sems.at[1, index],
            device_id=device,
            device_id_type=MESH,
        )
        copy.start()
        started.append(copy)
        return copy

    barrier = pltpu.get_barrier_semaphore()
    friends = [partner] + [same_core(k) for k in range(1, chips)]
    friends += [along(k) for k in range(1, owners)]
    for friend in friends:
        pl.semaphore_signal(barrier, inc=1, device_id=friend, device_id_type=MESH)

    for other in range(peers):
        start = other * chunk
        size = min(chunk, own_rows - start)
        if size > 0:
            held[z, slot_of(other, peers), :size, :] = weight_ref[start : start + size, :].astype(
                LOWTYPE
            )
        if size < chunk:
            held[z, slot_of(other, peers), max(size, 0) :, :] = jnp.zeros(
                (chunk - max(size, 0), mid), LOWTYPE
            )
    pl.semaphore_wait(barrier, len(friends))

    here = held.at[z, slot]
    first = [send(here, here, sema, k - 1, along(k)) for k in range(1, owners)]

    samples = mask_ref.shape[0]
    left[...] = jnp.zeros_like(left)
    for c in range(3):
        noise = noise_ref[c]
        noisy = image_ref[:, 0:1] * images_ref[c] + image_ref[:, 1:2] * noise
        left[c, :samples, :] = noisy.astype(LOWTYPE)
        one = noise.astype(LOWTYPE)
        rest = noise - one.astype(F32)
        two = rest.astype(LOWTYPE)
        left[3 + c, :samples, :] = one
        left[6 + c, :samples, :] = two
        left[9 + c, :samples, :] = (rest - two.astype(F32)).astype(LOWTYPE)
    left[12, :samples, :] = mask_ref[...].astype(F32).astype(LOWTYPE)
    for ref in (noisy_ref, planes_ref, maskw_ref):
        ref[:, 12:, :] = jnp.zeros((samples, ROWS12 - 12, PLACES), F32)

    def picture(quarter):
        pixel = lax.broadcasted_iota(jnp.int32, (S * S, PLACES), 0)
        lane = lax.broadcasted_iota(jnp.int32, (S * S, PLACES), 1)
        wanted = (
            (lane // SIDE * 2 + quarter // 2) * S + lane % SIDE * 2 + quarter % 2
        )
        pick = jnp.where(pixel == wanted, 1.0, 0.0).astype(LOWTYPE)
        rows = left.shape[1]
        moved = dot_nn(left[...].reshape(13 * rows, S * S), pick)
        maskw = moved[12 * rows : 12 * rows + samples] * image_ref[:, 2:3]
        for c in range(3):
            k = quarter * 3 + c
            noisy_ref[:, k, :] = moved[c * rows : c * rows + samples]
            planes_ref[:, k, :] = sum(
                [moved[(p + c) * rows : (p + c) * rows + samples] for p in (6, 9)],
                moved[(3 + c) * rows : (3 + c) * rows + samples],
            )
            maskw_ref[:, k, :] = maskw

    picture(0)
    second = []
    for k, copy in zip(range(1, owners), first):
        copy.wait_recv()
        there = held.at[lax.rem(z + owners - k, owners), slot]
        second.append(
            [
                send(there, there, semb, (k - 1) * (chips - 1) + j - 1, same_core(j))
                for j in range(1, chips)
            ]
        )
        if k < 4:
            picture(k)
    for k in range(owners, 4):
        picture(k)
    third = []
    for k, copies in zip(range(1, owners), second):
        for copy in copies:
            copy.wait_recv()
        mine = held.at[lax.rem(z + owners - k, owners), pl.ds(core * chips, chips)]
        third.append(send(mine, mine, semc, k - 1, partner))
    for copy in third:
        copy.wait_recv()

    def place(seg, row, values):
        size = values.shape[0]
        if seg < 2:
            whole, side = ((conv1_ref, conv1b_ref), (conv2_ref, conv2b_ref))[seg]
            whole[row : row + size, :] = values
            height = side.shape[0]
            done = 0
            while done < size:
                offset, inner = (row + done) // height, (row + done) % height
                part = min(size - done, height - inner)
                side[inner : inner + part, offset * mid : (offset + 1) * mid] = values[
                    done : done + part
                ]
                done += part
        elif seg in (4, 5, 6):
            qkv_ref[row : row + size, (seg - 4) * mid : (seg - 3) * mid] = values
        else:
            {2: skip_ref, 3: temb_ref, 7: outw_ref}[seg][row : row + size, :] = values

    for owner in range(owners):
        packed = 0
        for seg, seg_rows in enumerate(segment_rows()):
            share = seg_rows // owners
            done = 0
            while done < share:
                row = packed + done
                size = min(share - done, chunk - row % chunk)
                inner = row % chunk
                place(
                    seg,
                    owner * share + done,
                    held[owner, slot_of(row // chunk, peers), inner : inner + size, :],
                )
                done += size
            packed += share
    for copy in started:
        copy.wait_send()


def open_call(owners, peers, operands):
    mid = CHANNELS_MID
    chips = peers // 2
    chunk, _ = chunk_rows(owners, peers)
    samples = operands[3].shape[0]
    rows = -(-samples // 16) * 16
    out_shapes = [
        ((9 * C1, mid), LOWTYPE),
        ((3 * C1, 3 * mid), LOWTYPE),
        ((9 * mid, mid), LOWTYPE),
        ((3 * mid, 3 * mid), LOWTYPE),
        ((C1, mid), LOWTYPE),
        ((TEMB, mid), LOWTYPE),
        ((mid, 3 * mid), LOWTYPE),
        ((mid, mid), LOWTYPE),
        ((samples, ROWS12, PLACES), F32),
        ((samples, ROWS12, PLACES), F32),
        ((samples, ROWS12, PLACES), F32),
    ]
    vmem = pl.BlockSpec(memory_space=pltpu.VMEM)
    return pl.pallas_call(
        functools.partial(open_body, owners, peers),
        out_shape=[jax.ShapeDtypeStruct(shape, kind) for shape, kind in out_shapes],
        in_specs=[vmem] * len(operands),
        out_specs=[vmem] * len(out_shapes),
        scratch_shapes=[
            pltpu.VMEM((owners, peers, chunk, mid), LOWTYPE),
            pltpu.VMEM((13, rows, S * S), LOWTYPE),
            pltpu.SemaphoreType.DMA((2, owners - 1)),
            pltpu.SemaphoreType.DMA((2, (owners - 1) * (chips - 1))),
            pltpu.SemaphoreType.DMA((2, owners - 1)),
        ],
        compiler_params=pltpu.CompilerParams(
            vmem_limit_bytes=VMEM_BYTES, collective_id=1, has_side_effects=True
        ),
    )(*operands)


def stem_spread():
    counts = np.zeros((3, 2, 3))
    for block in range(3):
        for inner in range(2):
            for sub in range(2):
                tap = 2 * (block - 1) + inner - sub + 1
                if 0 <= tap <= 2:
                    counts[block, inner, tap] += 1
    full = np.zeros((3, 3, ROWS12, 3, 3, 3))
    both = (np.einsum("ayt,bxu->abyxtu", counts, counts) * 0.25).reshape(3, 3, 4, 3, 3)
    for c in range(3):
        full[:, :, c:12:3, :, :, c] = both
    return jnp.asarray(full.reshape(TAPS * ROWS12, 27), F32)


def split_three(values):
    first = lax.reduce_precision(values, 8, 7)
    second = lax.reduce_precision(values - first, 8, 7)
    third = values - first - second
    return jnp.concatenate([first, second, third], axis=1).astype(LOWTYPE)


def pad_rows(values, rows):
    return jnp.pad(values, [(0, 0)] * (values.ndim - 2) + [(0, rows - values.shape[-2]), (0, 0)])


def lanes_of(vector):
    rows = -(-vector.shape[0] // (8 * C1)) * 8
    return jnp.pad(vector, (0, rows * C1 - vector.shape[0]), constant_values=1.0).reshape(rows, C1)


def same_group(chans):
    group = np.arange(chans) // (chans // GROUPS)
    same = (group[:, None] == group[None, :]) / (PLACES * (chans // GROUPS))
    return jnp.asarray(same, LOWTYPE)


def shards(
    images,
    pixel_mask,
    timesteps,
    noise_field,
    matrices,
    matrix_moms,
    stem_weight,
    stem_moms,
    head_weight,
    head_moms,
    vectors,
    vector_firsts,
    vector_seconds,
):
    owners, peers = lax.axis_size("bucket"), lax.axis_size("batch")
    samples = images.shape[0]
    level, weight = plan(timesteps)
    per_image = jnp.stack([jnp.sqrt(level), jnp.sqrt(1.0 - level), weight], axis=1)
    conv1, conv1b, conv2, conv2b, skip, temb, qkv, outw, noisy, noise, mask_weight = open_call(
        owners,
        peers,
        [
            matrices,
            images.transpose(1, 0, 2),
            noise_field.transpose(1, 0, 2),
            pixel_mask,
            per_image,
        ],
    )
    time_in = pad_rows(swish(embed(timesteps)).astype(LOWTYPE), -(-samples // 16) * 16)
    spread = stem_spread()
    stem_blocks = split_three(
        jnp.dot(spread, lax.reduce_precision(stem_weight, 8, 7), precision=EXACT_PRECISION)
    )
    head_turned = head_weight.T
    head_rows = head_turned.astype(LOWTYPE).reshape(12, TAPS, CHANNELS_MID + C1)
    head_rows = pad_rows(head_rows.transpose(1, 0, 2), ROWS12).reshape(TAPS * ROWS12, -1)
    vec_rows = lanes_of(vectors)
    head_bias = jnp.broadcast_to(pad_rows(vectors[-12:].reshape(12, 1), ROWS12), (ROWS12, C1))
    rows_out, misc = unet_call(
        samples,
        owners,
        peers,
        [
            noisy,
            noise,
            mask_weight,
            time_in,
            stem_blocks,
            head_rows,
            conv1,
            conv1b,
            conv2,
            conv2b,
            skip,
            temb,
            qkv,
            outw,
            vec_rows,
            head_bias,
            same_group(C1),
            same_group(CHANNELS_MID),
            jnp.pad(spread, ((0, 0), (0, 5))),
        ],
    )
    (
        new_matrices,
        new_matrix_moms,
        matrix_copies,
        new_stem,
        new_stem_moms,
        new_head,
        new_head_moms,
        new_vec,
        new_first,
        new_second,
        sums,
    ) = muon_call(
        owners,
        peers,
        [
            rows_out,
            misc,
            matrices,
            matrix_moms,
            pad_rows(stem_weight, 32),
            pad_rows(stem_moms, 32),
            pad_rows(head_turned, ROWS12),
            pad_rows(head_moms.T, ROWS12),
            vec_rows,
            lanes_of(vector_firsts),
            lanes_of(vector_seconds),
        ],
    )
    count = vectors.shape[0]
    new_stem, new_stem_moms = new_stem[:27], new_stem_moms[:27]
    new_head, new_head_moms = new_head[:12].T, new_head_moms[:12].T
    new_vectors = new_vec.reshape(-1)[:count]
    new_firsts = new_first.reshape(-1)[:count]
    new_seconds = new_second.reshape(-1)[:count]
    loss_sum, weight_sum = sums[0, 0], sums[0, 1]
    return (
        loss_sum,
        weight_sum,
        new_matrices,
        new_matrix_moms,
        matrix_copies,
        new_stem,
        new_stem_moms,
        new_stem.astype(LOWTYPE),
        new_head,
        new_head_moms,
        new_head.astype(LOWTYPE),
        new_vectors,
        new_firsts,
        new_seconds,
        new_vectors.astype(LOWTYPE),
    )


def solution(mesh):
    return jax.shard_map(
        shards,
        mesh=mesh,
        in_specs=(
            P(("bucket", "batch"), None, None),
            P(("bucket", "batch"), None),
            P(("bucket", "batch")),
            P(("bucket", "batch"), None, None),
            P("bucket", None),
            P("bucket", None),
            P(),
            P(),
            P(),
            P(),
            P(),
            P(),
            P(),
        ),
        out_specs=(
            P(),
            P(),
            P("bucket", None),
            P("bucket", None),
            P("bucket", None),
            P(),
            P(),
            P(),
            P(),
            P(),
            P(),
            P(),
            P(),
            P(),
            P(),
        ),
        check_vma=False,
    )
```

```python
import functools
import math

import jax
import jax.numpy as jnp
import numpy as np
from jax import lax
from jax.experimental import pallas as pl
from jax.experimental.pallas import tpu as pltpu
from jax.sharding import PartitionSpec as P

C1 = 128
CHANNELS_MID = 256
TEMB = 512
GROUPS = 32
S = 32
TSTEPS = 1000
NS_STEPS = 5
STEP = 10


GN_EPS = 1e-05
NORM_EPS = 1e-12
MOMENTUM = 0.95
LR_MUON = 0.5
DECAY = 0.01
NS_A = 3.4445
NS_B = -4.775
NS_C = 2.0315
BETA_ONE = 0.9
BETA_TWO = 0.999
LR_ADAM = 0.5
ADAM_EPS = 1e-08
EXACT_PRECISION = lax.Precision.HIGHEST
LOWTYPE = jnp.bfloat16


def segment_rows():
    return [
        9 * C1,
        9 * CHANNELS_MID,
        C1,
        TEMB,
        CHANNELS_MID,
        CHANNELS_MID,
        CHANNELS_MID,
        CHANNELS_MID,
    ]


def plan(timesteps):
    frac_t = (timesteps.astype(jnp.float32) / TSTEPS + 0.008) / 1.008
    level = jnp.cos(frac_t * (math.pi / 2)) ** 2
    ratio = level / (1.0 - level)
    return (level, jnp.minimum(1.0, 5.0 / ratio))


def embed(timesteps):
    half_width = TEMB // 2
    freqs = jnp.exp(-math.log(10000.0) * jnp.arange(half_width, dtype=jnp.float32) / half_width)
    angles = timesteps.astype(jnp.float32)[:, None] * freqs[None, :]
    return jnp.concatenate([jnp.sin(angles), jnp.cos(angles)], axis=1)


def swish(values):
    return values * jax.nn.sigmoid(values)


F32 = jnp.float32
PLACES = 256
SIDE = 16
HALO = 288
TAPS = 9
ROWS12 = 16
CHUNK = 64
SMALL_ROWS = 240
VMEM_BYTES = 56 * 1024 * 1024
SEG_OFF = (0, 1152, 3456, 3584, 4096, 4352, 4608, 4864, 5120)


def dot_nn(a, b, precision=None):
    return lax.dot_general(
        a, b, (((1,), (0,)), ((), ())), preferred_element_type=F32, precision=precision
    )


def dot_nt(a, b):
    return lax.dot_general(a, b, (((1,), (1,)), ((), ())), preferred_element_type=F32)


def dot_tn(a, b):
    return lax.dot_general(a, b, (((0,), (0,)), ((), ())), preferred_element_type=F32)


def sigmoid(v):
    return 1.0 / (1.0 + jnp.exp(-v))


def fold8(v):
    rows, chans = v.shape
    return jnp.sum(v.reshape(rows // 8, 8, chans), axis=0)


def shift_lanes(x, di, dj):
    lane = lax.broadcasted_iota(jnp.int32, x.shape, 1)
    row, col = lane // SIDE + di, lane % SIDE + dj
    offset = (-(SIDE * di + dj)) % PLACES
    moved = x if offset == 0 else pltpu.roll(x, offset, 1)
    valid = (row >= 0) & (row < SIDE) & (col >= 0) & (col < SIDE)
    return jnp.where(valid, moved, 0.0)


def tap_offsets():
    return [(di, dj) for di in (-1, 0, 1) for dj in (-1, 0, 1)]


def unet_body(
    group,
    steps,
    owners,
    peers,
    noisy_ref,
    noise_ref,
    maskw_ref,
    time_ref,
    stem_ref,
    head_ref,
    conv1_ref,
    conv1b_ref,
    conv2_ref,
    conv2b_ref,
    skip_ref,
    temb_ref,
    qkv_ref,
    outw_ref,
    vec_ref,
    same128_ref,
    same256_ref,
    spread_ref,
    rows_ref,
    misc_ref,
    acc_ref,
    gstem_ref,
    ghead_ref,
    gvec_ref,
    ghb_ref,
    loss_ref,
    wsum_ref,
    x0,
    hid,
    res,
    outp,
    attn,
    a1,
    a2,
    normed,
    qkv,
    plow,
    attl,
    low0,
    joined,
    patch,
    pad1,
    pad2,
    shiftf,
    dyf,
    dout,
    dq3,
    dpool,
    tproj,
    gtime,
    dtap,
    datt,
    dscore,
    dpool_low,
    stemw_ref,
    headw_ref,
    headb_ref,
    time_low,
    wide_rows,
):
    step = pl.program_id(0)
    mid = CHANNELS_MID
    chunks = range(0, PLACES, CHUNK)
    images = range(group)

    @pl.when(step == 0)
    def _():
        acc_ref[...] = jnp.zeros_like(acc_ref)
        gstem_ref[...] = jnp.zeros_like(gstem_ref)
        ghead_ref[...] = jnp.zeros_like(ghead_ref)
        gvec_ref[...] = jnp.zeros_like(gvec_ref)
        ghb_ref[...] = jnp.zeros_like(ghb_ref)
        loss_ref[...] = jnp.zeros_like(loss_ref)
        wsum_ref[...] = jnp.zeros_like(wsum_ref)
        gtime[...] = jnp.zeros_like(gtime)
        for ref in (a1, a2, pad1, pad2):
            for g in images:
                ref[g, :SIDE, :] = jnp.zeros((SIDE, ref.shape[2]), ref.dtype)
                ref[g, HALO - SIDE :, :] = jnp.zeros((SIDE, ref.shape[2]), ref.dtype)
        shiftf[...] = jnp.zeros_like(shiftf)
        wide_rows[...] = jnp.zeros_like(wide_rows)
        samples = time_ref.shape[0]
        wide_rows[:samples, :TEMB] = time_ref[...]
        time_low[...] = wide_rows[: time_low.shape[0], :TEMB].astype(LOWTYPE)
        tproj[...] = dot_nn(time_low[...], temb_ref[...])
        wide_rows[:27, :C1] = stem_ref[...].astype(LOWTYPE).astype(F32)
        spread_stem = dot_nn(spread_ref[:, :27], wide_rows[:27, :C1], EXACT_PRECISION)
        for piece in range(3):
            low = spread_stem.astype(LOWTYPE)
            stemw_ref[:, piece * C1 : (piece + 1) * C1] = low
            spread_stem = spread_stem - low.astype(F32)
        width = mid + C1
        wide_rows[:ROWS12, :width] = jnp.zeros((ROWS12, width), F32)
        for tap in range(TAPS):
            wide_rows[:12, :width] = head_ref[:, tap * width : (tap + 1) * width]
            headw_ref[tap * ROWS12 : (tap + 1) * ROWS12, :] = wide_rows[:ROWS12, :width].astype(
                LOWTYPE
            )
        row = lax.broadcasted_iota(jnp.int32, (ROWS12, C1), 0)
        lane = lax.broadcasted_iota(jnp.int32, (ROWS12, C1), 1)
        bias = jnp.where(row == lane, vec_ref[23:24, :], 0.0)
        headb_ref[...] = jnp.sum(bias, axis=1, keepdims=True) + jnp.zeros((ROWS12, C1), F32)

    def vec(row, chans=mid):
        if chans == C1:
            return vec_ref[row : row + 1, :]
        row = 2 * row - 3
        return jnp.concatenate([vec_ref[row : row + 1, :], vec_ref[row + 1 : row + 2, :]], axis=1)

    def add_vec(row, value):
        gvec_ref[row : row + 1, : value.shape[1]] += value

    def total(parts):
        return jnp.concatenate([jnp.sum(p, axis=0, keepdims=True) for p in parts], axis=0)

    def grouped(stats, chans):
        same = same128_ref if chans == C1 else same256_ref
        first = stats.astype(LOWTYPE).astype(F32)
        second = (stats - first).astype(LOWTYPE).astype(F32)
        third = stats - first - second
        sums = dot_nn(jnp.concatenate([first, second, third], axis=0).astype(LOWTYPE), same[...])
        return sums[:group] + sums[group : 2 * group] + sums[2 * group :]

    def gn_stats(ref, sums, chans):
        mean = grouped(sums, chans)
        parts = []
        for g in images:
            acc = jnp.zeros((8, chans), F32)
            for r in chunks:
                c = ref[g, r : r + CHUNK, :] - mean[g : g + 1]
                acc += fold8(c * c)
            parts.append(acc)
        return mean, lax.rsqrt(grouped(total(parts), chans) + GN_EPS)

    def edge(chans, left):
        col = lax.broadcasted_iota(jnp.int32, (CHUNK, chans), 0) % SIDE
        return (col > 0) if left else (col < SIDE - 1)

    def act_shift(ref, g, mean, rstd, gain, shift, dest, chans):
        for r in chunks:
            y = (ref[g, r : r + CHUNK, :] - mean[g : g + 1]) * rstd[g : g + 1] * gain + shift
            a = y * sigmoid(y)
            shiftf[g, 8 + r : 8 + r + CHUNK, :chans] = a
            dest[g, SIDE + r : SIDE + r + CHUNK, chans : 2 * chans] = a.astype(LOWTYPE)
        for r in chunks:
            before = shiftf[g, 7 + r : 7 + r + CHUNK, :chans]
            after = shiftf[g, 9 + r : 9 + r + CHUNK, :chans]
            rows = slice(SIDE + r, SIDE + r + CHUNK)
            dest[g, rows, :chans] = jnp.where(edge(chans, True), before, 0.0).astype(LOWTYPE)
            dest[g, rows, 2 * chans :] = jnp.where(edge(chans, False), after, 0.0).astype(LOWTYPE)

    def dy_cat(ref, g, order):
        return jnp.concatenate(
            [ref[g, SIDE * k : SIDE * k + PLACES, :] for k in order], axis=1
        )

    def stack(parts):
        return jnp.concatenate(parts, axis=0) if len(parts) > 1 else parts[0]

    def staged(stages, fillers=()):
        fillers = list(fillers)
        for stage in stages:
            for g in images:
                stage(g)
            if fillers:
                fillers.pop(0)()
        for filler in fillers:
            filler()

    def rows_of(g):
        return slice(g * PLACES, (g + 1) * PLACES)

    sums1 = [None] * group

    def stem_patch(g):
        noisy = noisy_ref[g]
        for tap, (di, dj) in enumerate(tap_offsets()):
            patch[g, tap * ROWS12 : (tap + 1) * ROWS12, :] = shift_lanes(noisy, di, dj).astype(
                LOWTYPE
            )

    def stem_pool(g):
        wide = dot_tn(patch[g], stemw_ref[...])
        acc = jnp.zeros((8, C1), F32)
        for r in chunks:
            w = wide[r : r + CHUNK]
            v = (w[:, :C1] + w[:, C1 : 2 * C1]) + w[:, 2 * C1 :] + vec(0, C1)
            x0[g, r : r + CHUNK, :] = v
            low0[g * PLACES + r : g * PLACES + r + CHUNK, :] = v.astype(LOWTYPE)
            acc += fold8(v)
        sums1[g] = acc

    staged([stem_patch, stem_pool])
    mean1, rstd1 = gn_stats(x0, total(sums1), C1)
    gain1, shift1 = vec(1, C1), vec(2, C1)

    sums2 = [None] * group

    def act_one(g):
        act_shift(x0, g, mean1, rstd1, gain1, shift1, a1, C1)

    def conv_one(g):
        wide = dot_nn(dy_cat(a1, g, (0, 1, 2)), conv1_ref[...])
        bias = vec(3) + vec(4) + tproj[pl.ds(step * group + g, 1), :]
        acc = jnp.zeros((8, mid), F32)
        for r in chunks:
            v = wide[r : r + CHUNK] + bias
            hid[g, r : r + CHUNK, :] = v
            acc += fold8(v)
        sums2[g] = acc

    staged([act_one, conv_one])
    mean2, rstd2 = gn_stats(hid, total(sums2), mid)
    gain2, shift2 = vec(5), vec(6)

    sums3 = [None] * group

    def act_two(g):
        act_shift(hid, g, mean2, rstd2, gain2, shift2, a2, mid)

    def conv_two(g):
        wide = dot_nn(dy_cat(a2, g, (0, 1, 2)), conv2_ref[...])
        wide = wide + dot_nn(low0[rows_of(g), :], skip_ref[...])
        acc = jnp.zeros((8, mid), F32)
        for r in chunks:
            v = wide[r : r + CHUNK] + vec(7)
            res[g, r : r + CHUNK, :] = v
            acc += fold8(v)
        sums3[g] = acc

    staged([act_two, conv_two])
    mean3, rstd3 = gn_stats(res, total(sums3), mid)
    gain3, shift3 = vec(8), vec(9)
    scale = mid ** (-0.5)
    ones3, twos3 = [None] * group, [None] * group

    def norm_three(g):
        for r in chunks:
            xh = (res[g, r : r + CHUNK, :] - mean3[g : g + 1]) * rstd3[g : g + 1]
            y = xh * gain3 + shift3
            normed[g * PLACES + r : g * PLACES + r + CHUNK, :] = y.astype(LOWTYPE)

    def project(g):
        rows = rows_of(g)
        wide = dot_nn(normed[rows, :], qkv_ref[...])
        qkv[rows, :mid] = (wide[:, :mid] + vec(10)).astype(LOWTYPE)
        qkv[rows, mid : 2 * mid] = wide[:, mid : 2 * mid].astype(LOWTYPE)
        qkv[rows, 2 * mid :] = (wide[:, 2 * mid :] + vec(11)).astype(LOWTYPE)

    def weigh(g):
        rows = rows_of(g)
        logits = dot_nt(qkv[rows, :mid], qkv[rows, mid : 2 * mid])
        for r in chunks:
            s = logits[r : r + CHUNK] * scale
            e = jnp.exp(s - jnp.max(s, axis=1, keepdims=True))
            p = e * (1.0 / jnp.sum(e, axis=1, keepdims=True))
            attn[g, r : r + CHUNK, :] = p
            plow[g, r : r + CHUNK, :] = p.astype(LOWTYPE)

    def attend(g):
        attl[rows_of(g), :] = dot_nn(plow[g], qkv[rows_of(g), 2 * mid :]).astype(LOWTYPE)

    def join(g):
        wide = dot_nn(attl[rows_of(g), :], outw_ref[...])
        for r in chunks:
            rows = slice(g * PLACES + r, g * PLACES + r + CHUNK)
            o = res[g, r : r + CHUNK, :] + wide[r : r + CHUNK] + vec(12)
            outp[g, r : r + CHUNK, :] = o
            joined[rows, :mid] = (o * sigmoid(o)).astype(LOWTYPE)
            x = x0[g, r : r + CHUNK, :]
            joined[rows, mid:] = (x * sigmoid(x)).astype(LOWTYPE)

    def head(g):
        taps = dot_nt(headw_ref[...], joined[rows_of(g), :])
        value = headb_ref[:, :1] + jnp.zeros((ROWS12, PLACES), F32)
        for tap, (di, dj) in enumerate(tap_offsets()):
            value = value + shift_lanes(taps[tap * ROWS12 : (tap + 1) * ROWS12, :], di, dj)
        error = value - noise_ref[g]
        masked = maskw_ref[g] * error
        loss_ref[...] += masked * error
        wsum_ref[...] += maskw_ref[g]
        grad = 2.0 * masked
        ghb_ref[...] += grad
        gradl = grad.astype(LOWTYPE).astype(F32)
        for tap, (di, dj) in enumerate(tap_offsets()):
            dtap[g, tap * ROWS12 : (tap + 1) * ROWS12, :] = shift_lanes(gradl, -di, -dj).astype(
                LOWTYPE
            )

    def head_back(g):
        wide = dot_tn(dtap[g], headw_ref[...])
        acc = jnp.zeros((8, mid), F32)
        for r in chunks:
            o = outp[g, r : r + CHUNK, :]
            s = sigmoid(o)
            d = wide[r : r + CHUNK, :mid] * (s * (1.0 + o * (1.0 - s)))
            outp[g, r : r + CHUNK, :] = d
            dout[g * PLACES + r : g * PLACES + r + CHUNK, :] = d.astype(LOWTYPE)
            acc += fold8(d)
            x = x0[g, r : r + CHUNK, :]
            s = sigmoid(x)
            dpool[g, r : r + CHUNK, :] = wide[r : r + CHUNK, mid:] * (s * (1.0 + x * (1.0 - s)))
        add_vec(12, jnp.sum(acc, axis=0, keepdims=True))

    def attend_back(g):
        datt[rows_of(g), :] = dot_nt(dout[rows_of(g), :], outw_ref[...]).astype(LOWTYPE)

    def weigh_back(g):
        rows = rows_of(g)
        gweights = dot_nt(datt[rows, :], qkv[rows, 2 * mid :])
        dval = dot_tn(plow[g], datt[rows, :])
        add_vec(11, jnp.sum(fold8(dval), axis=0, keepdims=True))
        dq3[rows, 2 * mid :] = dval.astype(LOWTYPE)
        for r in chunks:
            p = attn[g, r : r + CHUNK, :]
            gw = gweights[r : r + CHUNK]
            ds = p * (gw - jnp.sum(gw * p, axis=1, keepdims=True))
            dscore[g, r : r + CHUNK, :] = (ds * scale).astype(LOWTYPE)

    def query_back(g):
        rows = rows_of(g)
        dqry = dot_nn(dscore[g], qkv[rows, mid : 2 * mid])
        dkey = dot_tn(dscore[g], qkv[rows, :mid])
        add_vec(10, jnp.sum(fold8(dqry), axis=0, keepdims=True))
        dq3[rows, :mid] = dqry.astype(LOWTYPE)
        dq3[rows, mid : 2 * mid] = dkey.astype(LOWTYPE)

    def project_back(g):
        one, two = jnp.zeros((8, mid), F32), jnp.zeros((8, mid), F32)
        wide = dot_nt(dq3[rows_of(g), :], qkv_ref[...])
        for r in chunks:
            xh = (res[g, r : r + CHUNK, :] - mean3[g : g + 1]) * rstd3[g : g + 1]
            d = wide[r : r + CHUNK]
            res[g, r : r + CHUNK, :] = xh
            dyf[g, r : r + CHUNK, :] = d
            one += fold8(d)
            two += fold8(d * xh)
        ones3[g], twos3[g] = one, two

    staged(
        [
            norm_three,
            project,
            weigh,
            attend,
            join,
            head,
            head_back,
            attend_back,
            weigh_back,
            query_back,
            project_back,
        ]
    )

    ones, twos = total(ones3), total(twos3)
    add_vec(9, jnp.sum(ones, axis=0, keepdims=True))
    add_vec(8, jnp.sum(twos, axis=0, keepdims=True))

    def finish(ref, dest, rstd, gain, m1, m2, chans, extra, g, row):
        r1 = rstd[g : g + 1]
        acc = jnp.zeros((8, chans), F32)
        for r in chunks:
            d = dyf[g, r : r + CHUNK, :chans] * (gain * r1)
            d = d - m1[g : g + 1] * r1 - ref[g, r : r + CHUNK, :] * (m2[g : g + 1] * r1)
            if extra is not None:
                d = d + extra[g, r : r + CHUNK, :]
            acc += fold8(d)
            dest(g, r, d.astype(LOWTYPE))
        acc = jnp.sum(acc, axis=0, keepdims=True)
        add_vec(row, acc)
        return acc

    def to_pad(pad):
        def put(g, r, low):
            pad[g, SIDE + r : SIDE + r + CHUNK, :] = low

        return put

    def turned(parts):
        return stack(parts).T

    def pad_turned(pad):
        return turned([pad[g, SIDE : SIDE + PLACES, :] for g in images])

    def conv_back(pad, weights, g, chans, apply):
        wide = dot_nt(dy_cat(pad, g, (2, 1, 0)), weights)
        shiftf[g, 8 : 8 + PLACES, :chans] = wide[:, :chans]
        dyf[g, :, :chans] = wide[:, chans : 2 * chans]
        for r in chunks:
            after = shiftf[g, 9 + r : 9 + r + CHUNK, :chans]
            dyf[g, r : r + CHUNK, :chans] += jnp.where(edge(chans, False), after, 0.0)
        shiftf[g, 8 : 8 + PLACES, :chans] = wide[:, 2 * chans :]
        for r in chunks:
            before = shiftf[g, 7 + r : 7 + r + CHUNK, :chans]
            apply(r, dyf[g, r : r + CHUNK, :chans] + jnp.where(edge(chans, True), before, 0.0))

    def norm_back(pad, weights, ref, mean, rstd, gain, shift, chans, ones, twos, g):
        sums = [jnp.zeros((8, chans), F32), jnp.zeros((8, chans), F32)]

        def apply(r, da):
            xh = (ref[g, r : r + CHUNK, :] - mean[g : g + 1]) * rstd[g : g + 1]
            y = xh * gain + shift
            s = sigmoid(y)
            d = da * (s * (1.0 + y * (1.0 - s)))
            ref[g, r : r + CHUNK, :] = xh
            dyf[g, r : r + CHUNK, :chans] = d
            sums[0] += fold8(d)
            sums[1] += fold8(d * xh)

        conv_back(pad, weights[...], g, chans, apply)
        ones[g], twos[g] = sums

    def add_product(first, last, left, right):
        acc_ref[:, first:last] += dot_nn(left(), right())

    m1, m2 = grouped(ones * gain3, mid), grouped(twos * gain3, mid)
    ones2, twos2 = [None] * group, [None] * group

    def grad_out():
        add_product(SEG_OFF[7], SEG_OFF[8], lambda: dout[...].T, lambda: attl[...])

    def grad_project(k):
        add_product(
            SEG_OFF[4 + k],
            SEG_OFF[5 + k],
            lambda: dq3[:, k * mid : (k + 1) * mid].T,
            lambda: normed[...],
        )

    def grad_head():
        for g in images:
            ghead_ref[...] += dot_nn(dtap[g], joined[rows_of(g), :])

    staged(
        [
            lambda g: finish(res, to_pad(pad2), rstd3, gain3, m1, m2, mid, outp, g, 7),
            lambda g: norm_back(
                pad2, conv2b_ref, hid, mean2, rstd2, gain2, shift2, mid, ones2, twos2, g
            ),
        ],
        [grad_out, grad_head] + [functools.partial(grad_project, k) for k in range(3)],
    )
    ones, twos = total(ones2), total(twos2)
    add_vec(6, jnp.sum(ones, axis=0, keepdims=True))
    add_vec(5, jnp.sum(twos, axis=0, keepdims=True))

    n1, n2 = grouped(ones * gain2, mid), grouped(twos * gain2, mid)
    ones1, twos1 = [None] * group, [None] * group
    lowt2 = pad_turned(pad2)

    def finish_two(g):
        acc = finish(hid, to_pad(pad1), rstd2, gain2, n1, n2, mid, None, g, 3)
        add_vec(4, acc)
        gtime[pl.ds(step * group + g, 1), :] = acc

    def grad_conv(lowt, act, offset, k):
        width = act.shape[2]
        first = offset + k * width
        add_product(
            first,
            first + width,
            lambda: lowt,
            lambda: stack([act[g, SIDE * k : SIDE * k + PLACES, :] for g in images]),
        )

    def grad_skip():
        add_product(SEG_OFF[2], SEG_OFF[3], lambda: lowt2, lambda: low0[...])
        for g in images:
            dpool[g] += dot_nt(pad2[g, SIDE : SIDE + PLACES, :], skip_ref[...])

    staged(
        [
            finish_two,
            lambda g: norm_back(
                pad1, conv1b_ref, x0, mean1, rstd1, gain1, shift1, C1, ones1, twos1, g
            ),
        ],
        [functools.partial(grad_conv, lowt2, a2, SEG_OFF[1], k) for k in range(3)] + [grad_skip],
    )
    ones, twos = total(ones1), total(twos1)
    add_vec(2, jnp.sum(ones, axis=0, keepdims=True))
    add_vec(1, jnp.sum(twos, axis=0, keepdims=True))

    p1, p2 = grouped(ones * gain1, C1), grouped(twos * gain1, C1)
    lowt1 = pad_turned(pad1)

    def to_pool(g, r, low):
        dpool_low[g, r : r + CHUNK, :] = low

    def grad_stem(g):
        gstem_ref[...] += dot_nn(patch[g], dpool_low[g])

    staged(
        [lambda g: finish(x0, to_pool, rstd1, gain1, p1, p2, C1, dpool, g, 0), grad_stem],
        [functools.partial(grad_conv, lowt1, a1, SEG_OFF[0], k) for k in range(3)],
    )

    @pl.when(step == steps - 1)
    def _():
        acc_ref[:, SEG_OFF[3] : SEG_OFF[4]] = dot_tn(gtime[...].astype(LOWTYPE), time_low[...])
        if rows_ref.shape[0] > 5120 + SMALL_ROWS:
            rows_ref[...] = jnp.zeros_like(rows_ref)
        pieces = gradient_pieces(owners, peers)
        for block in range(0, 5120, C1):
            turned = acc_ref[:, block : block + C1].T
            for source, size, target in pieces:
                low, high = max(source, block), min(source + size, block + C1)
                if low < high:
                    start = target + low - source
                    rows_ref[start : start + high - low, :] = turned[low - block : high - block]
        stem = lax.dot_general(
            spread_ref[...],
            gstem_ref[...],
            (((0,), (0,)), ((), ())),
            preferred_element_type=F32,
            precision=EXACT_PRECISION,
        )
        head = ghead_ref[...]
        none = jnp.zeros((ROWS12, C1), F32)
        tiles = [head[k : k + 16, :mid] for k in range(0, 144, 16)]
        for k in range(0, 80, 16):
            other = head[80 + k : 96 + k, mid:] if k < 64 else none
            tiles.append(jnp.concatenate([head[k : k + 16, mid:], other], axis=1))
        tiles.append(jnp.concatenate([stem[:16], stem[16:]], axis=1))
        for tile, (start, _) in zip(tiles, small_tiles(owners, peers)):
            rows_ref[start : start + 16, :] = tile
        misc_ref[:, :mid] = gvec_ref[...]
        misc_ref[13:14, :mid] = jnp.sum(loss_ref[...], axis=0, keepdims=True)
        misc_ref[14:15, :mid] = jnp.sum(wsum_ref[...], axis=0, keepdims=True)
        misc_ref[:, mid:] = ghb_ref[:, :C1] + ghb_ref[:, C1:]


def chunk_rows(owners, peers):
    share = -(-5120 // (owners * peers))
    return -(-share // 16) * 16, -(-(-(-SMALL_ROWS // peers)) // 16) * 16


def block_rows(owners, peers):
    chunk, small = chunk_rows(owners, peers)
    return owners * chunk + small


def slot_of(peer, peers):
    return peer % 2 * (peers // 2) + peer // 2


def gradient_pieces(owners, peers):
    chunk, _ = chunk_rows(owners, peers)
    block = block_rows(owners, peers)
    pieces = []
    for owner in range(owners):
        packed = 0
        for seg, seg_rows in enumerate(segment_rows()):
            share = seg_rows // owners
            done = 0
            while done < share:
                row = packed + done
                size = min(share - done, chunk - row % chunk)
                target = slot_of(row // chunk, peers) * block + owner * chunk + row % chunk
                pieces.append((SEG_OFF[seg] + owner * share + done, size, target))
                done += size
            packed += share
    return pieces


def small_tiles(owners, peers):
    chunk, small = chunk_rows(owners, peers)
    tiles = []
    for row in range(0, SMALL_ROWS, 16):
        slot = slot_of(row // small, peers)
        tiles.append((slot * block_rows(owners, peers) + owners * chunk + row % small, slot))
    return tiles


def unet_call(samples, owners, peers, operands):
    group = max(k for k in (1, 2, 4) if samples % k == 0)
    steps = samples // group
    time_rows = -(-samples // 16) * 16
    mid = CHANNELS_MID
    places = group * PLACES

    def image_spec():
        return pl.BlockSpec((group, ROWS12, PLACES), lambda i: (i, 0, 0))

    def whole(shape):
        return pl.BlockSpec(shape, lambda i: (0,) * len(shape))

    out_shapes = [(peers * block_rows(owners, peers), mid), (ROWS12, mid + C1)]
    scratch = [
        ((mid, 5120), F32),
        ((TAPS * ROWS12, C1), F32),
        ((TAPS * ROWS12, mid + C1), F32),
        ((ROWS12, mid), F32),
        ((ROWS12, mid), F32),
        ((ROWS12, mid), F32),
        ((ROWS12, mid), F32),
        ((group, PLACES, C1), F32),
        ((group, PLACES, mid), F32),
        ((group, PLACES, mid), F32),
        ((group, PLACES, mid), F32),
        ((group, PLACES, mid), F32),
        ((group, HALO, 3 * C1), LOWTYPE),
        ((group, HALO, 3 * mid), LOWTYPE),
        ((places, mid), LOWTYPE),
        ((places, 3 * mid), LOWTYPE),
        ((group, PLACES, mid), LOWTYPE),
        ((places, mid), LOWTYPE),
        ((places, C1), LOWTYPE),
        ((places, mid + C1), LOWTYPE),
        ((group, TAPS * ROWS12, PLACES), LOWTYPE),
        ((group, HALO, mid), LOWTYPE),
        ((group, HALO, mid), LOWTYPE),
        ((group, PLACES + 16, mid), F32),
        ((group, PLACES, mid), F32),
        ((places, mid), LOWTYPE),
        ((places, 3 * mid), LOWTYPE),
        ((group, PLACES, C1), F32),
        ((time_rows, mid), F32),
        ((time_rows, mid), F32),
        ((group, TAPS * ROWS12, PLACES), LOWTYPE),
        ((places, mid), LOWTYPE),
        ((group, PLACES, mid), LOWTYPE),
        ((group, PLACES, C1), LOWTYPE),
        ((TAPS * ROWS12, 3 * C1), LOWTYPE),
        ((TAPS * ROWS12, mid + C1), LOWTYPE),
        ((ROWS12, C1), F32),
        ((time_rows, TEMB), LOWTYPE),
        ((max(32, time_rows), TEMB), F32),
    ]
    return pl.pallas_call(
        functools.partial(unet_body, group, steps, owners, peers),
        grid=(steps,),
        out_shape=[jax.ShapeDtypeStruct(shape, F32) for shape in out_shapes],
        in_specs=[image_spec()] * 3 + [whole(a.shape) for a in operands[3:]],
        out_specs=[whole(shape) for shape in out_shapes],
        scratch_shapes=[pltpu.VMEM(shape, kind) for shape, kind in scratch],
        compiler_params=pltpu.CompilerParams(vmem_limit_bytes=VMEM_BYTES),
    )(*operands)


TASKS = ((1, 0), (0, 0), (0, 1), (2, 0), (1, 1), (2, 1), (3, 0), (3, 1))
MESH = pl.DeviceIdType.MESH
SMALL_LANES = 9 * (CHANNELS_MID + C1)


def ns_chain(gram, eye):
    product = None
    for step in range(NS_STEPS):
        square = dot_nn(gram, gram, EXACT_PRECISION)
        factor = NS_A * eye + NS_B * gram + NS_C * square
        product = factor if product is None else dot_nn(product, factor, EXACT_PRECISION)
        if step < NS_STEPS - 1:
            gram = dot_nn(factor, dot_nn(gram, factor, EXACT_PRECISION), EXACT_PRECISION)
    return product


def identity(size):
    rows = lax.broadcasted_iota(jnp.int32, (size, size), 0)
    cols = lax.broadcasted_iota(jnp.int32, (size, size), 1)
    return (rows == cols).astype(F32)


def muon_body(
    owners,
    peers,
    rows_ref,
    misc_ref,
    weight_ref,
    moment_ref,
    stem_ref,
    stemm_ref,
    head_ref,
    headm_ref,
    vec_ref,
    first_ref,
    second_ref,
    new_ref,
    newm_ref,
    nstem_ref,
    nstemm_ref,
    nhead_ref,
    nheadm_ref,
    nvec_ref,
    nfirst_ref,
    nsecond_ref,
    sums_ref,
    recv1,
    own2,
    send2,
    recv2,
    send3,
    recv3,
    recvs3,
    gathered,
    misc1,
    misc2,
    misc3,
    direction,
    mine_u,
    gram_part,
    gram_recv,
    gram_all,
    small,
    x_zero,
    x_one,
    flat,
    head_row,
    sem1,
    sem2,
    sem3,
    sems3,
    sema,
    semb,
    semg,
    semh,
    semx,
    semy,
    semm1,
    semm2,
    semm3,
):
    mid = CHANNELS_MID
    chips = peers // 2
    chunk, small_chunk = chunk_rows(owners, peers)
    block = block_rows(owners, peers)
    held = chunk + small_chunk
    own_rows = weight_ref.shape[0]
    z = lax.axis_index("bucket")
    peer = lax.axis_index("batch")
    chip, core = peer // 2, peer % 2
    partner = {"batch": chip * 2 + 1 - core}
    started = []

    def same_core(k):
        return {"batch": lax.rem(chip + k, chips) * 2 + core}

    def along(k):
        return {"bucket": lax.rem(z + k, owners)}

    def send(source, target, sems, slot, device, begin=True):
        copy = pltpu.make_async_remote_copy(
            src_ref=source,
            dst_ref=target,
            send_sem=sems.at[0, slot],
            recv_sem=sems.at[1, slot],
            device_id=device,
            device_id_type=MESH,
        )
        copy.start()
        if begin:
            started.append(copy)
        return copy

    barrier = pltpu.get_barrier_semaphore()
    friends = [partner] + [same_core(k) for k in range(1, chips)]
    friends += [along(k) for k in range(1, owners)]
    for friend in friends:
        pl.semaphore_signal(barrier, inc=1, device_id=friend, device_id_type=MESH)
    pl.semaphore_wait(barrier, len(friends))

    parts = [None] + list(range(1, owners)) + [0]

    def part_rows(part, base=0):
        if part is None:
            return pl.ds(pl.multiple_of(base + owners * chunk, 16), small_chunk)
        start = base + lax.rem(z + part, owners) * chunk
        return pl.ds(pl.multiple_of(start, 16), chunk)

    def base_of(k, other_core):
        owner_core = 1 - core if other_core else core
        return (owner_core * chips + lax.rem(chip + k, chips)) * block

    misc_copy = send(misc_ref, misc1, semm1, 0, partner)
    order = list(range(1, chips)) + [0]
    first = {}
    for number, part in enumerate(parts):
        for k in order:
            first[part, k] = send(
                rows_ref.at[part_rows(part, base_of(k, True)), :],
                recv1.at[k, part_rows(part), :],
                sem1,
                number * chips + k,
                partner,
            )

    misc_copy.wait_recv()
    misc2[chip] = misc_ref[...] + misc1[...]
    misc_copies = [
        send(misc2.at[chip], misc2.at[chip], semm2, k - 1, same_core(k)) for k in range(1, chips)
    ]
    second = {}
    for number, part in enumerate(parts):
        rows = part_rows(part)
        for k in order:
            first[part, k].wait_recv()
            total = rows_ref[part_rows(part, base_of(k, False)), :] + recv1[k, rows, :]
            if k == 0:
                own2[rows, :] = total
            else:
                send2[k - 1, rows, :] = total
                second[part, k] = send(
                    send2.at[k - 1, rows, :],
                    recv2.at[k - 1, rows, :],
                    sem2,
                    number * (chips - 1) + k - 1,
                    same_core(k),
                )

    for copy in misc_copies:
        copy.wait_recv()
    misc3[z] = sum([misc2[k] for k in range(1, chips)], misc2[0])
    misc_copies = [
        send(misc3.at[z], misc3.at[z], semm3, k - 1, along(k)) for k in range(1, owners)
    ]
    third = []
    for part in parts:
        for k in range(1, chips):
            second[part, k].wait_recv()
        rows = part_rows(part)
        total = own2[rows, :]
        for other in range(chips - 1):
            total = total + recv2[other, rows, :]
        if part is None:
            recvs3[z] = total
            third += [
                send(recvs3.at[z], recvs3.at[z], sems3, k - 1, along(k)) for k in range(1, owners)
            ]
        elif part == 0:
            own2[rows, :] = total
        else:
            send3[part - 1] = total
            third.append(
                send(send3.at[part - 1], recv3.at[part - 1], sem3, part - 1, along(part))
            )
    for copy in third:
        copy.wait_recv()
    total = own2[pl.ds(pl.multiple_of(z * chunk, 16), chunk), :]
    for other in range(owners - 1):
        total = total + recv3[other]
    slot = core * chips + chip
    gathered[slot, :chunk, :] = total
    total = recvs3[0]
    for other in range(1, owners):
        total = total + recvs3[other]
    gathered[slot, chunk:, :] = total

    here = gathered.at[slot]
    plane = [send(here, here, sema, k - 1, same_core(k)) for k in range(1, chips)]
    cross = [send(here, here, semb, 0, partner)]

    for copy in misc_copies:
        copy.wait_recv()
    misc = sum([misc3[k] for k in range(1, owners)], misc3[0])
    weight_sum = jnp.sum(misc[14:15, :mid], axis=1, keepdims=True)
    inverse = 1.0 / weight_sum
    loss_sum = jnp.sum(misc[13:14, :mid], axis=1, keepdims=True)
    sums_ref[0:1, :] = loss_sum + jnp.zeros((1, C1), F32)
    sums_ref[1:2, :] = weight_sum + jnp.zeros((1, C1), F32)
    head_bias = jnp.sum(misc[:, mid:].T, axis=0, keepdims=True)
    for row in range(3):
        flat[pl.ds(row * C1, C1)] = misc[row : row + 1, :C1].reshape(C1)
    for row in range(3, 13):
        flat[pl.ds(3 * C1 + (row - 3) * mid, mid)] = misc[row : row + 1, :mid].reshape(mid)
    head_row[...] = jnp.zeros_like(head_row)
    head_row[0:1, :ROWS12] = head_bias
    flat[pl.ds(3 * C1 + 10 * mid, C1)] = head_row[0:1, :].reshape(C1)
    grad = flat[pl.ds(0, vec_ref.shape[0])] * inverse.reshape(1)
    firsts = BETA_ONE * first_ref[...] + (1.0 - BETA_ONE) * grad
    seconds = BETA_TWO * second_ref[...] + (1.0 - BETA_TWO) * grad * grad
    nfirst_ref[...] = firsts
    nsecond_ref[...] = seconds
    change = (
        firsts
        / (1.0 - BETA_ONE**STEP)
        / (jnp.sqrt(seconds / (1.0 - BETA_TWO**STEP)) + ADAM_EPS)
    )
    nvec_ref[...] = vec_ref[...] - LR_ADAM * change

    for k, copy in zip(range(1, chips), plane):
        copy.wait_recv()
        other = gathered.at[core * chips + lax.rem(chip + chips - k, chips)]
        cross.append(send(other, other, semb, k, partner))
    for copy in cross:
        copy.wait_recv()

    for owner_peer in range(peers):
        start = owner_peer * chunk
        size = min(chunk, own_rows - start)
        if size > 0:
            grad = gathered[slot_of(owner_peer, peers), :size, :] * inverse
            rows = slice(start, start + size)
            moment = MOMENTUM * moment_ref[rows, :] + grad
            newm_ref[rows, :] = moment
            direction[rows, :] = grad + MOMENTUM * moment
    shares = [rows // owners for rows in segment_rows()]
    starts = [sum(shares[:k]) for k in range(len(shares))]
    for (task_chip, task_core), share, start in zip(TASKS, shares, starts):

        @pl.when((lax.rem(chip, 4) == task_chip) & (core == task_core))
        def _(share=share, start=start):
            mine_u[:share, :] = direction[start : start + share, :]
            if share < mine_u.shape[0]:
                mine_u[share:, :] = jnp.zeros((mine_u.shape[0] - share, mid), F32)

    mine = mine_u[...]
    gram_part[...] = lax.dot_general(
        mine,
        mine,
        (((0,), (0,)), ((), ())),
        preferred_element_type=F32,
        precision=EXACT_PRECISION,
    )
    part = mid // owners
    copies = []
    for k in range(1, owners):
        start = pl.multiple_of(lax.rem(z + k, owners) * part, 8)
        copies.append(send(gram_part.at[pl.ds(start, part), :], gram_recv.at[z], semg, k - 1, along(k)))
    own_part = pl.ds(pl.multiple_of(z * part, 8), part)
    gram_recv[z] = gram_part[own_part, :]

    chunk_s = small_chunk
    tiles = []
    for tile in range(SMALL_ROWS // 16):
        row = tile * 16
        at = chunk + row % chunk_s
        tiles.append(gathered[slot_of(row // chunk_s, peers), at : at + 16, :] * inverse)
    small[...] = jnp.zeros_like(small)
    for tap in range(TAPS):
        lanes = slice(tap * (mid + C1), tap * (mid + C1) + mid)
        small[:16, lanes] = tiles[tap]
        lanes = slice(tap * (mid + C1) + mid, (tap + 1) * (mid + C1))
        if tap < 5:
            small[:16, lanes] = tiles[9 + tap][:, :C1]
        else:
            small[:16, lanes] = tiles[9 + tap - 5][:, C1:]
    small[32:48, SMALL_LANES:] = tiles[14][:, :C1]
    small[48:, SMALL_LANES:] = tiles[14][:, C1:]
    head_part = (slice(0, 12), slice(0, SMALL_LANES))
    stem_part = (slice(32, 59), slice(SMALL_LANES, SMALL_LANES + C1))
    for part, old_ref, fresh_ref in (
        (head_part, headm_ref, nheadm_ref),
        (stem_part, stemm_ref, nstemm_ref),
    ):
        grad = small[part]
        moment = MOMENTUM * old_ref[...] + grad
        fresh_ref[...] = moment
        turn = grad + MOMENTUM * moment
        small[part] = turn * lax.rsqrt(
            jnp.sum(jnp.sum(turn * turn, axis=1, keepdims=True), axis=0, keepdims=True) + NORM_EPS
        )
    gram = lax.dot_general(
        small[...],
        small[...],
        (((1,), (1,)), ((), ())),
        preferred_element_type=F32,
        precision=EXACT_PRECISION,
    )
    product = ns_chain(gram, identity(64))
    small[...] = dot_nn(product, small[...], EXACT_PRECISION)
    keep = 1.0 - LR_MUON * DECAY
    nhead_ref[...] = head_ref[...] * keep - LR_MUON * small[head_part]
    nstem_ref[...] = stem_ref[...] * keep - LR_MUON * small[stem_part]

    for copy in copies:
        copy.wait_recv()
    gram_all[own_part, :] = sum([gram_recv[k] for k in range(1, owners)], gram_recv[0])
    copies = [
        send(gram_all.at[own_part, :], gram_all.at[own_part, :], semh, k - 1, along(k))
        for k in range(1, owners)
    ]
    for copy in copies:
        copy.wait_recv()
    gram = gram_all[...]
    eye = identity(mid)
    trace = jnp.sum(jnp.sum(gram * eye, axis=1, keepdims=True), axis=0, keepdims=True)
    scale = lax.rsqrt(trace + NORM_EPS)
    product = ns_chain(gram * (scale * scale), eye) * scale
    turned = dot_nn(mine_u[...], product, EXACT_PRECISION)

    place = lax.rem(chip, 4)
    base = chip - place

    def in_group(k):
        return {"batch": (base + lax.rem(place + k, 4)) * 2 + core}

    for task_core, buffer in ((0, x_zero), (1, x_one)):

        @pl.when(core == task_core)
        def _(buffer=buffer, other_buffer=(x_one, x_zero)[task_core]):
            size = buffer.shape[1]
            buffer[place] = turned[:size].astype(LOWTYPE)
            here = buffer.at[place]
            plane = [send(here, here, semx, k - 1, in_group(k), False) for k in range(1, 4)]
            cross = [send(here, here, semy, 0, partner, False)]
            for k in range(1, 4):
                plane[k - 1].wait_recv()
                other = buffer.at[lax.rem(place + 4 - k, 4)]
                cross.append(send(other, other, semy, k, partner, False))
            for k in range(4):
                there = other_buffer.at[lax.rem(place + 4 - k, 4)]
                pltpu.make_async_remote_copy(
                    src_ref=there,
                    dst_ref=there,
                    send_sem=semy.at[0, k],
                    recv_sem=semy.at[1, k],
                    device_id=partner,
                    device_id_type=MESH,
                ).wait_recv()
            for copy in plane + cross:
                copy.wait_send()

    for (task_chip, task_core), share, start in zip(TASKS, shares, starts):
        buffer = (x_zero, x_one)[task_core]
        rows = slice(start, start + share)
        fresh = weight_ref[rows, :] * keep - LR_MUON * buffer[task_chip, :share, :].astype(F32)
        new_ref[rows, :] = fresh
    for copy in started:
        copy.wait_send()


def muon_call(owners, peers, operands):
    mid = CHANNELS_MID
    chips = peers // 2
    chunk, small_chunk = chunk_rows(owners, peers)
    block = block_rows(owners, peers)
    rows = operands[2].shape[0]
    part = mid // owners
    shares = [seg_rows // owners for seg_rows in segment_rows()]
    most = [max(s for s, t in zip(shares, TASKS) if t[1] == core) for core in (0, 1)]
    out_shapes = [
        ((rows, mid), F32),
        ((rows, mid), F32),
        (operands[4].shape, F32),
        (operands[4].shape, F32),
        (operands[6].shape, F32),
        (operands[6].shape, F32),
        (operands[8].shape, F32),
        (operands[8].shape, F32),
        (operands[8].shape, F32),
        ((8, C1), F32),
    ]
    scratch = [
        ((chips, block, mid), F32),
        ((block, mid), F32),
        ((chips - 1, block, mid), F32),
        ((chips - 1, block, mid), F32),
        ((owners - 1, chunk, mid), F32),
        ((owners - 1, chunk, mid), F32),
        ((owners, small_chunk, mid), F32),
        ((peers, chunk + small_chunk, mid), F32),
        (operands[1].shape, F32),
        ((chips,) + operands[1].shape, F32),
        ((owners,) + operands[1].shape, F32),
        ((rows, mid), F32),
        ((max(most), mid), F32),
        ((mid, mid), F32),
        ((owners, part, mid), F32),
        ((mid, mid), F32),
        ((64, SMALL_LANES + C1), F32),
        ((4, most[0], mid), LOWTYPE),
        ((4, most[1], mid), LOWTYPE),
        ((3 * C1 + 10 * mid + C1,), F32),
        ((8, C1), F32),
    ]
    sems = [
        (owners + 1) * chips,
        (owners + 1) * (chips - 1),
        owners - 1,
        owners - 1,
        chips - 1,
        chips,
        owners - 1,
        owners - 1,
        3,
        4,
        1,
        chips - 1,
        owners - 1,
    ]
    vmem = pl.BlockSpec(memory_space=pltpu.VMEM)
    return pl.pallas_call(
        functools.partial(muon_body, owners, peers),
        out_shape=[jax.ShapeDtypeStruct(shape, kind) for shape, kind in out_shapes],
        in_specs=[vmem] * len(operands),
        out_specs=[vmem] * len(out_shapes),
        scratch_shapes=[pltpu.VMEM(shape, kind) for shape, kind in scratch]
        + [pltpu.SemaphoreType.DMA((2, count)) for count in sems],
        compiler_params=pltpu.CompilerParams(
            vmem_limit_bytes=VMEM_BYTES, collective_id=0, has_side_effects=True
        ),
    )(*operands)


def open_body(
    owners,
    peers,
    weight_ref,
    images_ref,
    noise_ref,
    mask_ref,
    image_ref,
    conv1_ref,
    conv1b_ref,
    conv2_ref,
    conv2b_ref,
    skip_ref,
    temb_ref,
    qkv_ref,
    outw_ref,
    noisy_ref,
    planes_ref,
    maskw_ref,
    held,
    left,
    sema,
    semb,
    semc,
):
    mid = CHANNELS_MID
    chips = peers // 2
    chunk, _ = chunk_rows(owners, peers)
    own_rows = weight_ref.shape[0]
    z = lax.axis_index("bucket")
    peer = lax.axis_index("batch")
    chip, core = peer // 2, peer % 2
    partner = {"batch": chip * 2 + 1 - core}
    slot = core * chips + chip
    started = []

    def same_core(k):
        return {"batch": lax.rem(chip + k, chips) * 2 + core}

    def along(k):
        return {"bucket": lax.rem(z + k, owners)}

    def send(source, target, sems, index, device):
        copy = pltpu.make_async_remote_copy(
            src_ref=source,
            dst_ref=target,
            send_sem=sems.at[0, index],
            recv_sem=sems.at[1, index],
            device_id=device,
            device_id_type=MESH,
        )
        copy.start()
        started.append(copy)
        return copy

    barrier = pltpu.get_barrier_semaphore()
    friends = [partner] + [same_core(k) for k in range(1, chips)]
    friends += [along(k) for k in range(1, owners)]
    for friend in friends:
        pl.semaphore_signal(barrier, inc=1, device_id=friend, device_id_type=MESH)

    for other in range(peers):
        start = other * chunk
        size = min(chunk, own_rows - start)
        if size > 0:
            held[z, slot_of(other, peers), :size, :] = weight_ref[start : start + size, :].astype(
                LOWTYPE
            )
        if size < chunk:
            held[z, slot_of(other, peers), max(size, 0) :, :] = jnp.zeros(
                (chunk - max(size, 0), mid), LOWTYPE
            )
    pl.semaphore_wait(barrier, len(friends))

    here = held.at[z, slot]
    first = [send(here, here, sema, k - 1, along(k)) for k in range(1, owners)]

    samples = mask_ref.shape[0]
    left[...] = jnp.zeros_like(left)
    for c in range(3):
        noise = noise_ref[c]
        noisy = image_ref[:, 0:1] * images_ref[c] + image_ref[:, 1:2] * noise
        left[c, :samples, :] = noisy.astype(LOWTYPE)
        one = noise.astype(LOWTYPE)
        rest = noise - one.astype(F32)
        two = rest.astype(LOWTYPE)
        left[3 + c, :samples, :] = one
        left[6 + c, :samples, :] = two
        left[9 + c, :samples, :] = (rest - two.astype(F32)).astype(LOWTYPE)
    left[12, :samples, :] = mask_ref[...].astype(F32).astype(LOWTYPE)
    for ref in (noisy_ref, planes_ref, maskw_ref):
        ref[:, 12:, :] = jnp.zeros((samples, ROWS12 - 12, PLACES), F32)

    def picture(quarter):
        pixel = lax.broadcasted_iota(jnp.int32, (S * S, PLACES), 0)
        lane = lax.broadcasted_iota(jnp.int32, (S * S, PLACES), 1)
        wanted = (
            (lane // SIDE * 2 + quarter // 2) * S + lane % SIDE * 2 + quarter % 2
        )
        pick = jnp.where(pixel == wanted, 1.0, 0.0).astype(LOWTYPE)
        rows = left.shape[1]
        moved = dot_nn(left[...].reshape(13 * rows, S * S), pick)
        maskw = moved[12 * rows : 12 * rows + samples] * image_ref[:, 2:3]
        for c in range(3):
            k = quarter * 3 + c
            noisy_ref[:, k, :] = moved[c * rows : c * rows + samples]
            planes_ref[:, k, :] = sum(
                [moved[(p + c) * rows : (p + c) * rows + samples] for p in (6, 9)],
                moved[(3 + c) * rows : (3 + c) * rows + samples],
            )
            maskw_ref[:, k, :] = maskw

    picture(0)
    second = []
    for k, copy in zip(range(1, owners), first):
        copy.wait_recv()
        there = held.at[lax.rem(z + owners - k, owners), slot]
        second.append(
            [
                send(there, there, semb, (k - 1) * (chips - 1) + j - 1, same_core(j))
                for j in range(1, chips)
            ]
        )
        if k < 4:
            picture(k)
    for k in range(owners, 4):
        picture(k)
    third = []
    for k, copies in zip(range(1, owners), second):
        for copy in copies:
            copy.wait_recv()
        mine = held.at[lax.rem(z + owners - k, owners), pl.ds(core * chips, chips)]
        third.append(send(mine, mine, semc, k - 1, partner))
    for copy in third:
        copy.wait_recv()

    def place(seg, row, values):
        size = values.shape[0]
        if seg < 2:
            whole, side = ((conv1_ref, conv1b_ref), (conv2_ref, conv2b_ref))[seg]
            whole[row : row + size, :] = values
            height = side.shape[0]
            done = 0
            while done < size:
                offset, inner = (row + done) // height, (row + done) % height
                part = min(size - done, height - inner)
                side[inner : inner + part, offset * mid : (offset + 1) * mid] = values[
                    done : done + part
                ]
                done += part
        elif seg in (4, 5, 6):
            qkv_ref[row : row + size, (seg - 4) * mid : (seg - 3) * mid] = values
        else:
            {2: skip_ref, 3: temb_ref, 7: outw_ref}[seg][row : row + size, :] = values

    for owner in range(owners):
        packed = 0
        for seg, seg_rows in enumerate(segment_rows()):
            share = seg_rows // owners
            done = 0
            while done < share:
                row = packed + done
                size = min(share - done, chunk - row % chunk)
                inner = row % chunk
                place(
                    seg,
                    owner * share + done,
                    held[owner, slot_of(row // chunk, peers), inner : inner + size, :],
                )
                done += size
            packed += share
    for copy in started:
        copy.wait_send()


def open_call(owners, peers, operands):
    mid = CHANNELS_MID
    chips = peers // 2
    chunk, _ = chunk_rows(owners, peers)
    samples = operands[3].shape[0]
    rows = -(-samples // 16) * 16
    out_shapes = [
        ((9 * C1, mid), LOWTYPE),
        ((3 * C1, 3 * mid), LOWTYPE),
        ((9 * mid, mid), LOWTYPE),
        ((3 * mid, 3 * mid), LOWTYPE),
        ((C1, mid), LOWTYPE),
        ((TEMB, mid), LOWTYPE),
        ((mid, 3 * mid), LOWTYPE),
        ((mid, mid), LOWTYPE),
        ((samples, ROWS12, PLACES), F32),
        ((samples, ROWS12, PLACES), F32),
        ((samples, ROWS12, PLACES), F32),
    ]
    vmem = pl.BlockSpec(memory_space=pltpu.VMEM)
    return pl.pallas_call(
        functools.partial(open_body, owners, peers),
        out_shape=[jax.ShapeDtypeStruct(shape, kind) for shape, kind in out_shapes],
        in_specs=[vmem] * len(operands),
        out_specs=[vmem] * len(out_shapes),
        scratch_shapes=[
            pltpu.VMEM((owners, peers, chunk, mid), LOWTYPE),
            pltpu.VMEM((13, rows, S * S), LOWTYPE),
            pltpu.SemaphoreType.DMA((2, owners - 1)),
            pltpu.SemaphoreType.DMA((2, (owners - 1) * (chips - 1))),
            pltpu.SemaphoreType.DMA((2, owners - 1)),
        ],
        compiler_params=pltpu.CompilerParams(
            vmem_limit_bytes=VMEM_BYTES, collective_id=1, has_side_effects=True
        ),
    )(*operands)


def close_body(*refs):
    values, outs = refs[:10], refs[10:]
    for source, target in zip(values[:9], outs[:9]):
        target[...] = source[...]
    for source, target in zip((values[0], values[2], values[4]), outs[9:12]):
        target[...] = source[...].astype(LOWTYPE)
    sums = values[9]
    outs[12][...] = sums[0:1, 0:1]
    outs[13][...] = sums[1:2, 0:1]


def close_call(values):
    shapes = [(v.shape, F32) for v in values[:9]]
    shapes += [(values[k].shape, LOWTYPE) for k in (0, 2, 4)] + [((1, 1), F32)] * 2
    vmem = pl.BlockSpec(memory_space=pltpu.VMEM)
    return pl.pallas_call(
        close_body,
        out_shape=[jax.ShapeDtypeStruct(shape, kind) for shape, kind in shapes],
        in_specs=[vmem] * len(values),
        out_specs=[vmem] * len(shapes),
        compiler_params=pltpu.CompilerParams(vmem_limit_bytes=VMEM_BYTES),
    )(*values)


def stem_spread():
    counts = np.zeros((3, 2, 3))
    for block in range(3):
        for inner in range(2):
            for sub in range(2):
                tap = 2 * (block - 1) + inner - sub + 1
                if 0 <= tap <= 2:
                    counts[block, inner, tap] += 1
    full = np.zeros((3, 3, ROWS12, 3, 3, 3))
    both = (np.einsum("ayt,bxu->abyxtu", counts, counts) * 0.25).reshape(3, 3, 4, 3, 3)
    for c in range(3):
        full[:, :, c:12:3, :, :, c] = both
    return jnp.asarray(full.reshape(TAPS * ROWS12, 27), F32)


def lanes_of(vector):
    rows = -(-vector.shape[0] // (8 * C1)) * 8
    return jnp.pad(vector, (0, rows * C1 - vector.shape[0]), constant_values=1.0).reshape(rows, C1)


def same_group(chans):
    group = np.arange(chans) // (chans // GROUPS)
    same = (group[:, None] == group[None, :]) / (PLACES * (chans // GROUPS))
    return jnp.asarray(same, LOWTYPE)


def shards(
    images,
    pixel_mask,
    timesteps,
    noise_field,
    matrices,
    matrix_moms,
    stem_weight,
    stem_moms,
    head_weight,
    head_moms,
    vectors,
    vector_firsts,
    vector_seconds,
):
    owners, peers = lax.axis_size("bucket"), lax.axis_size("batch")
    samples = images.shape[0]
    level, weight = plan(timesteps)
    per_image = jnp.stack([jnp.sqrt(level), jnp.sqrt(1.0 - level), weight], axis=1)
    conv1, conv1b, conv2, conv2b, skip, temb, qkv, outw, noisy, noise, mask_weight = open_call(
        owners,
        peers,
        [
            matrices,
            images.transpose(1, 0, 2),
            noise_field.transpose(1, 0, 2),
            pixel_mask,
            per_image,
        ],
    )
    spread = stem_spread()
    head_turned = head_weight.T
    rows_out, misc = unet_call(
        samples,
        owners,
        peers,
        [
            noisy,
            noise,
            mask_weight,
            swish(embed(timesteps)),
            stem_weight,
            head_turned,
            conv1,
            conv1b,
            conv2,
            conv2b,
            skip,
            temb,
            qkv,
            outw,
            lanes_of(vectors),
            same_group(C1),
            same_group(CHANNELS_MID),
            jnp.pad(spread, ((0, 0), (0, 5))),
        ],
    )
    values = muon_call(
        owners,
        peers,
        [
            rows_out,
            misc,
            matrices,
            matrix_moms,
            stem_weight,
            stem_moms,
            head_turned,
            head_moms.T,
            vectors,
            vector_firsts,
            vector_seconds,
        ],
    )
    (
        new_matrices,
        new_matrix_moms,
        new_stem,
        new_stem_moms,
        new_head,
        new_head_moms,
        new_vectors,
        new_firsts,
        new_seconds,
        matrix_copies,
        stem_copy,
        head_copy,
        loss_sum,
        weight_sum,
    ) = close_call(values)
    loss_sum, weight_sum = loss_sum.reshape(()), weight_sum.reshape(())
    new_head, new_head_moms, head_copy = new_head.T, new_head_moms.T, head_copy.T
    return (
        loss_sum,
        weight_sum,
        new_matrices,
        new_matrix_moms,
        matrix_copies,
        new_stem,
        new_stem_moms,
        stem_copy,
        new_head,
        new_head_moms,
        head_copy,
        new_vectors,
        new_firsts,
        new_seconds,
        new_vectors.astype(LOWTYPE),
    )


def solution(mesh):
    return jax.shard_map(
        shards,
        mesh=mesh,
        in_specs=(
            P(("bucket", "batch"), None, None),
            P(("bucket", "batch"), None),
            P(("bucket", "batch")),
            P(("bucket", "batch"), None, None),
            P("bucket", None),
            P("bucket", None),
            P(),
            P(),
            P(),
            P(),
            P(),
            P(),
            P(),
        ),
        out_specs=(
            P(),
            P(),
            P("bucket", None),
            P("bucket", None),
            P("bucket", None),
            P(),
            P(),
            P(),
            P(),
            P(),
            P(),
            P(),
            P(),
            P(),
            P(),
        ),
        check_vma=False,
    )
```

```python
import functools
import math

import jax
import jax.numpy as jnp
import numpy as np
from jax import lax
from jax.experimental import pallas as pl
from jax.experimental.pallas import tpu as pltpu
from jax.sharding import PartitionSpec as P

C1 = 128
CHANNELS_MID = 256
TEMB = 512
GROUPS = 32
S = 32
TSTEPS = 1000
NS_STEPS = 5
STEP = 10


GN_EPS = 1e-05
NORM_EPS = 1e-12
MOMENTUM = 0.95
LR_MUON = 0.5
DECAY = 0.01
NS_A = 3.4445
NS_B = -4.775
NS_C = 2.0315
BETA_ONE = 0.9
BETA_TWO = 0.999
LR_ADAM = 0.5
ADAM_EPS = 1e-08
EXACT_PRECISION = lax.Precision.HIGHEST
LOWTYPE = jnp.bfloat16


def segment_rows():
    return [
        9 * C1,
        9 * CHANNELS_MID,
        C1,
        TEMB,
        CHANNELS_MID,
        CHANNELS_MID,
        CHANNELS_MID,
        CHANNELS_MID,
    ]


def plan(timesteps):
    frac_t = (timesteps.astype(jnp.float32) / TSTEPS + 0.008) / 1.008
    level = jnp.cos(frac_t * (math.pi / 2)) ** 2
    ratio = level / (1.0 - level)
    return (level, jnp.minimum(1.0, 5.0 / ratio))


def embed(timesteps):
    half_width = TEMB // 2
    freqs = jnp.exp(-math.log(10000.0) * jnp.arange(half_width, dtype=jnp.float32) / half_width)
    angles = timesteps.astype(jnp.float32)[:, None] * freqs[None, :]
    return jnp.concatenate([jnp.sin(angles), jnp.cos(angles)], axis=1)


def swish(values):
    return values * jax.nn.sigmoid(values)


F32 = jnp.float32
PLACES = 256
SIDE = 16
HALO = 288
TAPS = 9
ROWS12 = 16
CHUNK = 64
SMALL_ROWS = 240
VMEM_BYTES = 56 * 1024 * 1024
SEG_OFF = (0, 1152, 3456, 3584, 4096, 4352, 4608, 4864, 5120)


def dot_nn(a, b, precision=None):
    return lax.dot_general(
        a, b, (((1,), (0,)), ((), ())), preferred_element_type=F32, precision=precision
    )


def dot_nt(a, b):
    return lax.dot_general(a, b, (((1,), (1,)), ((), ())), preferred_element_type=F32)


def dot_tn(a, b):
    return lax.dot_general(a, b, (((0,), (0,)), ((), ())), preferred_element_type=F32)


def sigmoid(v):
    return 1.0 / (1.0 + jnp.exp(-v))


def fold8(v):
    rows, chans = v.shape
    return jnp.sum(v.reshape(rows // 8, 8, chans), axis=0)


def shift_lanes(x, di, dj):
    lane = lax.broadcasted_iota(jnp.int32, x.shape, 1)
    row, col = lane // SIDE + di, lane % SIDE + dj
    offset = (-(SIDE * di + dj)) % PLACES
    moved = x if offset == 0 else pltpu.roll(x, offset, 1)
    valid = (row >= 0) & (row < SIDE) & (col >= 0) & (col < SIDE)
    return jnp.where(valid, moved, 0.0)


def tap_offsets():
    return [(di, dj) for di in (-1, 0, 1) for dj in (-1, 0, 1)]


def unet_body(
    group,
    steps,
    owners,
    peers,
    noisy_ref,
    noise_ref,
    maskw_ref,
    time_ref,
    stem_ref,
    head_ref,
    conv1_ref,
    conv1b_ref,
    conv2_ref,
    conv2b_ref,
    skip_ref,
    temb_ref,
    qkv_ref,
    outw_ref,
    vec_ref,
    same128_ref,
    same256_ref,
    spread_ref,
    rows_ref,
    misc_ref,
    acc_ref,
    gstem_ref,
    ghead_ref,
    gvec_ref,
    ghb_ref,
    loss_ref,
    wsum_ref,
    x0,
    hid,
    res,
    outp,
    attn,
    a1,
    a2,
    normed,
    qkv,
    plow,
    attl,
    low0,
    joined,
    patch,
    pad1,
    pad2,
    shiftf,
    dyf,
    dout,
    dq3,
    dpool,
    tproj,
    gtime,
    dtap,
    datt,
    dscore,
    dpool_low,
    stemw_ref,
    headw_ref,
    headb_ref,
    time_low,
    wide_rows,
):
    step = pl.program_id(0)
    mid = CHANNELS_MID
    chunks = range(0, PLACES, CHUNK)
    images = range(group)

    @pl.when(step == 0)
    def _():
        acc_ref[...] = jnp.zeros_like(acc_ref)
        gstem_ref[...] = jnp.zeros_like(gstem_ref)
        ghead_ref[...] = jnp.zeros_like(ghead_ref)
        gvec_ref[...] = jnp.zeros_like(gvec_ref)
        ghb_ref[...] = jnp.zeros_like(ghb_ref)
        loss_ref[...] = jnp.zeros_like(loss_ref)
        wsum_ref[...] = jnp.zeros_like(wsum_ref)
        gtime[...] = jnp.zeros_like(gtime)
        for ref in (a1, a2, pad1, pad2):
            for g in images:
                ref[g, :SIDE, :] = jnp.zeros((SIDE, ref.shape[2]), ref.dtype)
                ref[g, HALO - SIDE :, :] = jnp.zeros((SIDE, ref.shape[2]), ref.dtype)
        shiftf[...] = jnp.zeros_like(shiftf)
        wide_rows[...] = jnp.zeros_like(wide_rows)
        samples = time_ref.shape[0]
        wide_rows[:samples, :TEMB] = time_ref[...]
        time_low[...] = wide_rows[: time_low.shape[0], :TEMB].astype(LOWTYPE)
        tproj[...] = dot_nn(time_low[...], temb_ref[...])
        wide_rows[:27, :C1] = stem_ref[...].astype(LOWTYPE).astype(F32)
        spread_stem = dot_nn(spread_ref[:, :27], wide_rows[:27, :C1], EXACT_PRECISION)
        for piece in range(3):
            low = spread_stem.astype(LOWTYPE)
            stemw_ref[:, piece * C1 : (piece + 1) * C1] = low
            spread_stem = spread_stem - low.astype(F32)
        width = mid + C1
        wide_rows[:ROWS12, :width] = jnp.zeros((ROWS12, width), F32)
        for tap in range(TAPS):
            wide_rows[:12, :width] = head_ref[:, tap * width : (tap + 1) * width]
            headw_ref[tap * ROWS12 : (tap + 1) * ROWS12, :] = wide_rows[:ROWS12, :width].astype(
                LOWTYPE
            )
        row = lax.broadcasted_iota(jnp.int32, (ROWS12, 12), 0)
        lane = lax.broadcasted_iota(jnp.int32, (ROWS12, 12), 1)
        tail = vec_ref[pl.ds(3 * C1 + 10 * mid, 12)].reshape(1, 12)
        bias = jnp.where(row == lane, tail, 0.0)
        headb_ref[...] = jnp.sum(bias, axis=1, keepdims=True) + jnp.zeros((ROWS12, C1), F32)

    def vec(row, chans=mid):
        start = row * C1 if chans == C1 else 3 * C1 + (row - 3) * mid
        return vec_ref[pl.ds(start, chans)].reshape(1, chans)

    def add_vec(row, value):
        gvec_ref[row : row + 1, : value.shape[1]] += value

    def total(parts):
        return jnp.concatenate([jnp.sum(p, axis=0, keepdims=True) for p in parts], axis=0)

    def grouped(stats, chans):
        same = same128_ref if chans == C1 else same256_ref
        first = stats.astype(LOWTYPE).astype(F32)
        second = (stats - first).astype(LOWTYPE).astype(F32)
        third = stats - first - second
        sums = dot_nn(jnp.concatenate([first, second, third], axis=0).astype(LOWTYPE), same[...])
        return sums[:group] + sums[group : 2 * group] + sums[2 * group :]

    def gn_stats(ref, sums, chans):
        mean = grouped(sums, chans)
        parts = []
        for g in images:
            acc = jnp.zeros((8, chans), F32)
            for r in chunks:
                c = ref[g, r : r + CHUNK, :] - mean[g : g + 1]
                acc += fold8(c * c)
            parts.append(acc)
        return mean, lax.rsqrt(grouped(total(parts), chans) + GN_EPS)

    def edge(chans, left):
        col = lax.broadcasted_iota(jnp.int32, (CHUNK, chans), 0) % SIDE
        return (col > 0) if left else (col < SIDE - 1)

    def act_shift(ref, g, mean, rstd, gain, shift, dest, chans):
        for r in chunks:
            y = (ref[g, r : r + CHUNK, :] - mean[g : g + 1]) * rstd[g : g + 1] * gain + shift
            a = y * sigmoid(y)
            shiftf[g, 8 + r : 8 + r + CHUNK, :chans] = a
            dest[g, SIDE + r : SIDE + r + CHUNK, chans : 2 * chans] = a.astype(LOWTYPE)
        for r in chunks:
            before = shiftf[g, 7 + r : 7 + r + CHUNK, :chans]
            after = shiftf[g, 9 + r : 9 + r + CHUNK, :chans]
            rows = slice(SIDE + r, SIDE + r + CHUNK)
            dest[g, rows, :chans] = jnp.where(edge(chans, True), before, 0.0).astype(LOWTYPE)
            dest[g, rows, 2 * chans :] = jnp.where(edge(chans, False), after, 0.0).astype(LOWTYPE)

    def dy_cat(ref, g, order):
        return jnp.concatenate(
            [ref[g, SIDE * k : SIDE * k + PLACES, :] for k in order], axis=1
        )

    def stack(parts):
        return jnp.concatenate(parts, axis=0) if len(parts) > 1 else parts[0]

    def staged(stages, fillers=()):
        fillers = list(fillers)
        for stage in stages:
            for g in images:
                stage(g)
            if fillers:
                fillers.pop(0)()
        for filler in fillers:
            filler()

    def rows_of(g):
        return slice(g * PLACES, (g + 1) * PLACES)

    sums1 = [None] * group

    def stem_patch(g):
        noisy = noisy_ref[g]
        for tap, (di, dj) in enumerate(tap_offsets()):
            patch[g, tap * ROWS12 : (tap + 1) * ROWS12, :] = shift_lanes(noisy, di, dj).astype(
                LOWTYPE
            )

    def stem_pool(g):
        wide = dot_tn(patch[g], stemw_ref[...])
        acc = jnp.zeros((8, C1), F32)
        for r in chunks:
            w = wide[r : r + CHUNK]
            v = (w[:, :C1] + w[:, C1 : 2 * C1]) + w[:, 2 * C1 :] + vec(0, C1)
            x0[g, r : r + CHUNK, :] = v
            low0[g * PLACES + r : g * PLACES + r + CHUNK, :] = v.astype(LOWTYPE)
            acc += fold8(v)
        sums1[g] = acc

    staged([stem_patch, stem_pool])
    mean1, rstd1 = gn_stats(x0, total(sums1), C1)
    gain1, shift1 = vec(1, C1), vec(2, C1)

    sums2 = [None] * group

    def act_one(g):
        act_shift(x0, g, mean1, rstd1, gain1, shift1, a1, C1)

    def conv_one(g):
        wide = dot_nn(dy_cat(a1, g, (0, 1, 2)), conv1_ref[...])
        bias = vec(3) + vec(4) + tproj[pl.ds(step * group + g, 1), :]
        acc = jnp.zeros((8, mid), F32)
        for r in chunks:
            v = wide[r : r + CHUNK] + bias
            hid[g, r : r + CHUNK, :] = v
            acc += fold8(v)
        sums2[g] = acc

    staged([act_one, conv_one])
    mean2, rstd2 = gn_stats(hid, total(sums2), mid)
    gain2, shift2 = vec(5), vec(6)

    sums3 = [None] * group

    def act_two(g):
        act_shift(hid, g, mean2, rstd2, gain2, shift2, a2, mid)

    def conv_two(g):
        wide = dot_nn(dy_cat(a2, g, (0, 1, 2)), conv2_ref[...])
        wide = wide + dot_nn(low0[rows_of(g), :], skip_ref[...])
        acc = jnp.zeros((8, mid), F32)
        for r in chunks:
            v = wide[r : r + CHUNK] + vec(7)
            res[g, r : r + CHUNK, :] = v
            acc += fold8(v)
        sums3[g] = acc

    staged([act_two, conv_two])
    mean3, rstd3 = gn_stats(res, total(sums3), mid)
    gain3, shift3 = vec(8), vec(9)
    scale = mid ** (-0.5)
    ones3, twos3 = [None] * group, [None] * group

    def norm_three(g):
        for r in chunks:
            xh = (res[g, r : r + CHUNK, :] - mean3[g : g + 1]) * rstd3[g : g + 1]
            y = xh * gain3 + shift3
            normed[g * PLACES + r : g * PLACES + r + CHUNK, :] = y.astype(LOWTYPE)

    def project(g):
        rows = rows_of(g)
        wide = dot_nn(normed[rows, :], qkv_ref[...])
        qkv[rows, :mid] = (wide[:, :mid] + vec(10)).astype(LOWTYPE)
        qkv[rows, mid : 2 * mid] = wide[:, mid : 2 * mid].astype(LOWTYPE)
        qkv[rows, 2 * mid :] = (wide[:, 2 * mid :] + vec(11)).astype(LOWTYPE)

    def weigh(g):
        rows = rows_of(g)
        logits = dot_nt(qkv[rows, :mid], qkv[rows, mid : 2 * mid])
        for r in chunks:
            s = logits[r : r + CHUNK] * scale
            e = jnp.exp(s - jnp.max(s, axis=1, keepdims=True))
            p = e * (1.0 / jnp.sum(e, axis=1, keepdims=True))
            attn[g, r : r + CHUNK, :] = p
            plow[g, r : r + CHUNK, :] = p.astype(LOWTYPE)

    def attend(g):
        attl[rows_of(g), :] = dot_nn(plow[g], qkv[rows_of(g), 2 * mid :]).astype(LOWTYPE)

    def join(g):
        wide = dot_nn(attl[rows_of(g), :], outw_ref[...])
        for r in chunks:
            rows = slice(g * PLACES + r, g * PLACES + r + CHUNK)
            o = res[g, r : r + CHUNK, :] + wide[r : r + CHUNK] + vec(12)
            outp[g, r : r + CHUNK, :] = o
            joined[rows, :mid] = (o * sigmoid(o)).astype(LOWTYPE)
            x = x0[g, r : r + CHUNK, :]
            joined[rows, mid:] = (x * sigmoid(x)).astype(LOWTYPE)

    def head(g):
        taps = dot_nt(headw_ref[...], joined[rows_of(g), :])
        value = headb_ref[:, :1] + jnp.zeros((ROWS12, PLACES), F32)
        for tap, (di, dj) in enumerate(tap_offsets()):
            value = value + shift_lanes(taps[tap * ROWS12 : (tap + 1) * ROWS12, :], di, dj)
        error = value - noise_ref[g]
        masked = maskw_ref[g] * error
        loss_ref[...] += masked * error
        wsum_ref[...] += maskw_ref[g]
        grad = 2.0 * masked
        ghb_ref[...] += grad
        gradl = grad.astype(LOWTYPE).astype(F32)
        for tap, (di, dj) in enumerate(tap_offsets()):
            dtap[g, tap * ROWS12 : (tap + 1) * ROWS12, :] = shift_lanes(gradl, -di, -dj).astype(
                LOWTYPE
            )

    def head_back(g):
        wide = dot_tn(dtap[g], headw_ref[...])
        acc = jnp.zeros((8, mid), F32)
        for r in chunks:
            o = outp[g, r : r + CHUNK, :]
            s = sigmoid(o)
            d = wide[r : r + CHUNK, :mid] * (s * (1.0 + o * (1.0 - s)))
            outp[g, r : r + CHUNK, :] = d
            dout[g * PLACES + r : g * PLACES + r + CHUNK, :] = d.astype(LOWTYPE)
            acc += fold8(d)
            x = x0[g, r : r + CHUNK, :]
            s = sigmoid(x)
            dpool[g, r : r + CHUNK, :] = wide[r : r + CHUNK, mid:] * (s * (1.0 + x * (1.0 - s)))
        add_vec(12, jnp.sum(acc, axis=0, keepdims=True))

    def attend_back(g):
        datt[rows_of(g), :] = dot_nt(dout[rows_of(g), :], outw_ref[...]).astype(LOWTYPE)

    def weigh_back(g):
        rows = rows_of(g)
        gweights = dot_nt(datt[rows, :], qkv[rows, 2 * mid :])
        dval = dot_tn(plow[g], datt[rows, :])
        add_vec(11, jnp.sum(fold8(dval), axis=0, keepdims=True))
        dq3[rows, 2 * mid :] = dval.astype(LOWTYPE)
        for r in chunks:
            p = attn[g, r : r + CHUNK, :]
            gw = gweights[r : r + CHUNK]
            ds = p * (gw - jnp.sum(gw * p, axis=1, keepdims=True))
            dscore[g, r : r + CHUNK, :] = (ds * scale).astype(LOWTYPE)

    def query_back(g):
        rows = rows_of(g)
        dqry = dot_nn(dscore[g], qkv[rows, mid : 2 * mid])
        dkey = dot_tn(dscore[g], qkv[rows, :mid])
        add_vec(10, jnp.sum(fold8(dqry), axis=0, keepdims=True))
        dq3[rows, :mid] = dqry.astype(LOWTYPE)
        dq3[rows, mid : 2 * mid] = dkey.astype(LOWTYPE)

    def project_back(g):
        one, two = jnp.zeros((8, mid), F32), jnp.zeros((8, mid), F32)
        wide = dot_nt(dq3[rows_of(g), :], qkv_ref[...])
        for r in chunks:
            xh = (res[g, r : r + CHUNK, :] - mean3[g : g + 1]) * rstd3[g : g + 1]
            d = wide[r : r + CHUNK]
            res[g, r : r + CHUNK, :] = xh
            dyf[g, r : r + CHUNK, :] = d
            one += fold8(d)
            two += fold8(d * xh)
        ones3[g], twos3[g] = one, two

    staged(
        [
            norm_three,
            project,
            weigh,
            attend,
            join,
            head,
            head_back,
            attend_back,
            weigh_back,
            query_back,
            project_back,
        ]
    )

    ones, twos = total(ones3), total(twos3)
    add_vec(9, jnp.sum(ones, axis=0, keepdims=True))
    add_vec(8, jnp.sum(twos, axis=0, keepdims=True))

    def finish(ref, dest, rstd, gain, m1, m2, chans, extra, g, row):
        r1 = rstd[g : g + 1]
        acc = jnp.zeros((8, chans), F32)
        for r in chunks:
            d = dyf[g, r : r + CHUNK, :chans] * (gain * r1)
            d = d - m1[g : g + 1] * r1 - ref[g, r : r + CHUNK, :] * (m2[g : g + 1] * r1)
            if extra is not None:
                d = d + extra[g, r : r + CHUNK, :]
            acc += fold8(d)
            dest(g, r, d.astype(LOWTYPE))
        acc = jnp.sum(acc, axis=0, keepdims=True)
        add_vec(row, acc)
        return acc

    def to_pad(pad):
        def put(g, r, low):
            pad[g, SIDE + r : SIDE + r + CHUNK, :] = low

        return put

    def turned(parts):
        return stack(parts).T

    def pad_turned(pad):
        return turned([pad[g, SIDE : SIDE + PLACES, :] for g in images])

    def conv_back(pad, weights, g, chans, apply):
        wide = dot_nt(dy_cat(pad, g, (2, 1, 0)), weights)
        shiftf[g, 8 : 8 + PLACES, :chans] = wide[:, :chans]
        dyf[g, :, :chans] = wide[:, chans : 2 * chans]
        for r in chunks:
            after = shiftf[g, 9 + r : 9 + r + CHUNK, :chans]
            dyf[g, r : r + CHUNK, :chans] += jnp.where(edge(chans, False), after, 0.0)
        shiftf[g, 8 : 8 + PLACES, :chans] = wide[:, 2 * chans :]
        for r in chunks:
            before = shiftf[g, 7 + r : 7 + r + CHUNK, :chans]
            apply(r, dyf[g, r : r + CHUNK, :chans] + jnp.where(edge(chans, True), before, 0.0))

    def norm_back(pad, weights, ref, mean, rstd, gain, shift, chans, ones, twos, g):
        sums = [jnp.zeros((8, chans), F32), jnp.zeros((8, chans), F32)]

        def apply(r, da):
            xh = (ref[g, r : r + CHUNK, :] - mean[g : g + 1]) * rstd[g : g + 1]
            y = xh * gain + shift
            s = sigmoid(y)
            d = da * (s * (1.0 + y * (1.0 - s)))
            ref[g, r : r + CHUNK, :] = xh
            dyf[g, r : r + CHUNK, :chans] = d
            sums[0] += fold8(d)
            sums[1] += fold8(d * xh)

        conv_back(pad, weights[...], g, chans, apply)
        ones[g], twos[g] = sums

    def add_product(first, last, left, right):
        acc_ref[:, first:last] += dot_nn(left(), right())

    m1, m2 = grouped(ones * gain3, mid), grouped(twos * gain3, mid)
    ones2, twos2 = [None] * group, [None] * group

    def grad_out():
        add_product(SEG_OFF[7], SEG_OFF[8], lambda: dout[...].T, lambda: attl[...])

    def grad_project(k):
        add_product(
            SEG_OFF[4 + k],
            SEG_OFF[5 + k],
            lambda: dq3[:, k * mid : (k + 1) * mid].T,
            lambda: normed[...],
        )

    def grad_head():
        for g in images:
            ghead_ref[...] += dot_nn(dtap[g], joined[rows_of(g), :])

    staged(
        [
            lambda g: finish(res, to_pad(pad2), rstd3, gain3, m1, m2, mid, outp, g, 7),
            lambda g: norm_back(
                pad2, conv2b_ref, hid, mean2, rstd2, gain2, shift2, mid, ones2, twos2, g
            ),
        ],
        [grad_out, grad_head] + [functools.partial(grad_project, k) for k in range(3)],
    )
    ones, twos = total(ones2), total(twos2)
    add_vec(6, jnp.sum(ones, axis=0, keepdims=True))
    add_vec(5, jnp.sum(twos, axis=0, keepdims=True))

    n1, n2 = grouped(ones * gain2, mid), grouped(twos * gain2, mid)
    ones1, twos1 = [None] * group, [None] * group
    lowt2 = pad_turned(pad2)

    def finish_two(g):
        acc = finish(hid, to_pad(pad1), rstd2, gain2, n1, n2, mid, None, g, 3)
        add_vec(4, acc)
        gtime[pl.ds(step * group + g, 1), :] = acc

    def grad_conv(lowt, act, offset, k):
        width = act.shape[2]
        first = offset + k * width
        add_product(
            first,
            first + width,
            lambda: lowt,
            lambda: stack([act[g, SIDE * k : SIDE * k + PLACES, :] for g in images]),
        )

    def grad_skip():
        add_product(SEG_OFF[2], SEG_OFF[3], lambda: lowt2, lambda: low0[...])
        for g in images:
            dpool[g] += dot_nt(pad2[g, SIDE : SIDE + PLACES, :], skip_ref[...])

    staged(
        [
            finish_two,
            lambda g: norm_back(
                pad1, conv1b_ref, x0, mean1, rstd1, gain1, shift1, C1, ones1, twos1, g
            ),
        ],
        [functools.partial(grad_conv, lowt2, a2, SEG_OFF[1], k) for k in range(3)] + [grad_skip],
    )
    ones, twos = total(ones1), total(twos1)
    add_vec(2, jnp.sum(ones, axis=0, keepdims=True))
    add_vec(1, jnp.sum(twos, axis=0, keepdims=True))

    p1, p2 = grouped(ones * gain1, C1), grouped(twos * gain1, C1)
    lowt1 = pad_turned(pad1)

    def to_pool(g, r, low):
        dpool_low[g, r : r + CHUNK, :] = low

    def grad_stem(g):
        gstem_ref[...] += dot_nn(patch[g], dpool_low[g])

    staged(
        [lambda g: finish(x0, to_pool, rstd1, gain1, p1, p2, C1, dpool, g, 0), grad_stem],
        [functools.partial(grad_conv, lowt1, a1, SEG_OFF[0], k) for k in range(3)],
    )

    @pl.when(step == steps - 1)
    def _():
        acc_ref[:, SEG_OFF[3] : SEG_OFF[4]] = dot_tn(gtime[...].astype(LOWTYPE), time_low[...])
        if rows_ref.shape[0] > 5120 + SMALL_ROWS:
            rows_ref[...] = jnp.zeros_like(rows_ref)
        pieces = gradient_pieces(owners, peers)
        for block in range(0, 5120, C1):
            turned = acc_ref[:, block : block + C1].T
            for source, size, target in pieces:
                low, high = max(source, block), min(source + size, block + C1)
                if low < high:
                    start = target + low - source
                    rows_ref[start : start + high - low, :] = turned[low - block : high - block]
        stem = lax.dot_general(
            spread_ref[...],
            gstem_ref[...],
            (((0,), (0,)), ((), ())),
            preferred_element_type=F32,
            precision=EXACT_PRECISION,
        )
        head = ghead_ref[...]
        none = jnp.zeros((ROWS12, C1), F32)
        tiles = [head[k : k + 16, :mid] for k in range(0, 144, 16)]
        for k in range(0, 80, 16):
            other = head[80 + k : 96 + k, mid:] if k < 64 else none
            tiles.append(jnp.concatenate([head[k : k + 16, mid:], other], axis=1))
        tiles.append(jnp.concatenate([stem[:16], stem[16:]], axis=1))
        for tile, (start, _) in zip(tiles, small_tiles(owners, peers)):
            rows_ref[start : start + 16, :] = tile
        misc_ref[:, :mid] = gvec_ref[...]
        misc_ref[13:14, :mid] = jnp.sum(loss_ref[...], axis=0, keepdims=True)
        misc_ref[14:15, :mid] = jnp.sum(wsum_ref[...], axis=0, keepdims=True)
        misc_ref[:, mid:] = ghb_ref[:, :C1] + ghb_ref[:, C1:]


def chunk_rows(owners, peers):
    share = -(-5120 // (owners * peers))
    return -(-share // 16) * 16, -(-(-(-SMALL_ROWS // peers)) // 16) * 16


def block_rows(owners, peers):
    chunk, small = chunk_rows(owners, peers)
    return owners * chunk + small


def slot_of(peer, peers):
    return peer % 2 * (peers // 2) + peer // 2


def gradient_pieces(owners, peers):
    chunk, _ = chunk_rows(owners, peers)
    block = block_rows(owners, peers)
    pieces = []
    for owner in range(owners):
        packed = 0
        for seg, seg_rows in enumerate(segment_rows()):
            share = seg_rows // owners
            done = 0
            while done < share:
                row = packed + done
                size = min(share - done, chunk - row % chunk)
                target = slot_of(row // chunk, peers) * block + owner * chunk + row % chunk
                pieces.append((SEG_OFF[seg] + owner * share + done, size, target))
                done += size
            packed += share
    return pieces


def small_tiles(owners, peers):
    chunk, small = chunk_rows(owners, peers)
    tiles = []
    for row in range(0, SMALL_ROWS, 16):
        slot = slot_of(row // small, peers)
        tiles.append((slot * block_rows(owners, peers) + owners * chunk + row % small, slot))
    return tiles


def unet_call(samples, owners, peers, operands):
    group = max(k for k in (1, 2, 4) if samples % k == 0)
    steps = samples // group
    time_rows = -(-samples // 16) * 16
    mid = CHANNELS_MID
    places = group * PLACES

    def image_spec():
        return pl.BlockSpec((group, ROWS12, PLACES), lambda i: (i, 0, 0))

    def whole(shape):
        return pl.BlockSpec(shape, lambda i: (0,) * len(shape))

    out_shapes = [(peers * block_rows(owners, peers), mid), (ROWS12, mid + C1)]
    scratch = [
        ((mid, 5120), F32),
        ((TAPS * ROWS12, C1), F32),
        ((TAPS * ROWS12, mid + C1), F32),
        ((ROWS12, mid), F32),
        ((ROWS12, mid), F32),
        ((ROWS12, mid), F32),
        ((ROWS12, mid), F32),
        ((group, PLACES, C1), F32),
        ((group, PLACES, mid), F32),
        ((group, PLACES, mid), F32),
        ((group, PLACES, mid), F32),
        ((group, PLACES, mid), F32),
        ((group, HALO, 3 * C1), LOWTYPE),
        ((group, HALO, 3 * mid), LOWTYPE),
        ((places, mid), LOWTYPE),
        ((places, 3 * mid), LOWTYPE),
        ((group, PLACES, mid), LOWTYPE),
        ((places, mid), LOWTYPE),
        ((places, C1), LOWTYPE),
        ((places, mid + C1), LOWTYPE),
        ((group, TAPS * ROWS12, PLACES), LOWTYPE),
        ((group, HALO, mid), LOWTYPE),
        ((group, HALO, mid), LOWTYPE),
        ((group, PLACES + 16, mid), F32),
        ((group, PLACES, mid), F32),
        ((places, mid), LOWTYPE),
        ((places, 3 * mid), LOWTYPE),
        ((group, PLACES, C1), F32),
        ((time_rows, mid), F32),
        ((time_rows, mid), F32),
        ((group, TAPS * ROWS12, PLACES), LOWTYPE),
        ((places, mid), LOWTYPE),
        ((group, PLACES, mid), LOWTYPE),
        ((group, PLACES, C1), LOWTYPE),
        ((TAPS * ROWS12, 3 * C1), LOWTYPE),
        ((TAPS * ROWS12, mid + C1), LOWTYPE),
        ((ROWS12, C1), F32),
        ((time_rows, TEMB), LOWTYPE),
        ((max(32, time_rows), TEMB), F32),
    ]
    return pl.pallas_call(
        functools.partial(unet_body, group, steps, owners, peers),
        grid=(steps,),
        out_shape=[jax.ShapeDtypeStruct(shape, F32) for shape in out_shapes],
        in_specs=[image_spec()] * 3 + [whole(a.shape) for a in operands[3:]],
        out_specs=[whole(shape) for shape in out_shapes],
        scratch_shapes=[pltpu.VMEM(shape, kind) for shape, kind in scratch],
        compiler_params=pltpu.CompilerParams(vmem_limit_bytes=VMEM_BYTES),
    )(*operands)


TASKS = ((1, 0), (0, 0), (0, 1), (2, 0), (1, 1), (2, 1), (3, 0), (3, 1))
MESH = pl.DeviceIdType.MESH
SMALL_LANES = 9 * (CHANNELS_MID + C1)


def ns_chain(gram, eye):
    product = None
    for step in range(NS_STEPS):
        square = dot_nn(gram, gram, EXACT_PRECISION)
        factor = NS_A * eye + NS_B * gram + NS_C * square
        product = factor if product is None else dot_nn(product, factor, EXACT_PRECISION)
        if step < NS_STEPS - 1:
            gram = dot_nn(factor, dot_nn(gram, factor, EXACT_PRECISION), EXACT_PRECISION)
    return product


def identity(size):
    rows = lax.broadcasted_iota(jnp.int32, (size, size), 0)
    cols = lax.broadcasted_iota(jnp.int32, (size, size), 1)
    return (rows == cols).astype(F32)


def muon_body(
    owners,
    peers,
    rows_ref,
    misc_ref,
    weight_hbm,
    moment_hbm,
    stem_ref,
    stemm_ref,
    head_ref,
    headm_ref,
    vec_ref,
    first_ref,
    second_ref,
    new_ref,
    newm_ref,
    nstem_ref,
    nstemm_ref,
    nhead_ref,
    nheadm_ref,
    nvec_ref,
    nfirst_ref,
    nsecond_ref,
    sums_ref,
    recv1,
    own2,
    send2,
    recv2,
    send3,
    recv3,
    recvs3,
    gathered,
    gathered_small,
    misc1,
    misc2,
    misc3,
    direction,
    mine_u,
    gram_part,
    gram_recv,
    gram_all,
    small,
    x_zero,
    x_one,
    flat,
    head_row,
    own_half,
    weight_ref,
    moment_ref,
    sem_load,
    sem1,
    sem2,
    sem3,
    sems3,
    sema,
    semb,
    semg,
    semh,
    semx,
    semy,
    semm1,
    semm2,
    semm3,
    semas,
    sembs,
):
    mid = CHANNELS_MID
    chips = peers // 2
    chunk, small_chunk = chunk_rows(owners, peers)
    block = block_rows(owners, peers)
    own_rows = weight_ref.shape[0]
    z = lax.axis_index("bucket")
    peer = lax.axis_index("batch")
    chip, core = peer // 2, peer % 2
    partner = {"batch": chip * 2 + 1 - core}
    started = []
    half_rows = pl.ds(pl.multiple_of(core * chips * block, 16), chips * block)
    load_half = pltpu.make_async_copy(rows_ref.at[half_rows, :], own_half, sem_load.at[0])
    load_moment = pltpu.make_async_copy(moment_hbm, moment_ref, sem_load.at[1])
    load_weight = pltpu.make_async_copy(weight_hbm, weight_ref, sem_load.at[2])
    for load in (load_half, load_moment, load_weight):
        load.start()

    def same_core(k):
        return {"batch": lax.rem(chip + k, chips) * 2 + core}

    def along(k):
        return {"bucket": lax.rem(z + k, owners)}

    def send(source, target, sems, slot, device, begin=True):
        copy = pltpu.make_async_remote_copy(
            src_ref=source,
            dst_ref=target,
            send_sem=sems.at[0, slot],
            recv_sem=sems.at[1, slot],
            device_id=device,
            device_id_type=MESH,
        )
        copy.start()
        if begin:
            started.append(copy)
        return copy

    barrier = pltpu.get_barrier_semaphore()
    friends = [partner] + [same_core(k) for k in range(1, chips)]
    friends += [along(k) for k in range(1, owners)]
    for friend in friends:
        pl.semaphore_signal(barrier, inc=1, device_id=friend, device_id_type=MESH)
    pl.semaphore_wait(barrier, len(friends))

    parts = [None] + list(range(1, owners)) + [0]

    def part_rows(part, base=0):
        if part is None:
            return pl.ds(pl.multiple_of(base + owners * chunk, 16), small_chunk)
        start = base + lax.rem(z + part, owners) * chunk
        return pl.ds(pl.multiple_of(start, 16), chunk)

    def base_of(k):
        return lax.rem(chip + k, chips) * block

    other_half = (1 - core) * chips * block

    misc_copy = send(misc_ref, misc1, semm1, 0, partner)
    order = list(range(1, chips)) + [0]
    first = {}
    for number, part in enumerate(parts):
        for k in order:
            first[part, k] = send(
                rows_ref.at[part_rows(part, other_half + base_of(k)), :],
                recv1.at[k, part_rows(part), :],
                sem1,
                number * chips + k,
                partner,
            )

    misc_copy.wait_recv()
    misc2[chip] = misc_ref[...] + misc1[...]
    misc_copies = [
        send(misc2.at[chip], misc2.at[chip], semm2, k - 1, same_core(k)) for k in range(1, chips)
    ]
    load_half.wait()
    second = {}
    for number, part in enumerate(parts):
        rows = part_rows(part)
        for k in order:
            first[part, k].wait_recv()
            total = own_half[part_rows(part, base_of(k)), :] + recv1[k, rows, :]
            if k == 0:
                own2[rows, :] = total
            else:
                send2[k - 1, rows, :] = total
                second[part, k] = send(
                    send2.at[k - 1, rows, :],
                    recv2.at[k - 1, rows, :],
                    sem2,
                    number * (chips - 1) + k - 1,
                    same_core(k),
                )

    for copy in misc_copies:
        copy.wait_recv()
    misc3[z] = sum([misc2[k] for k in range(1, chips)], misc2[0])
    misc_copies = [
        send(misc3.at[z], misc3.at[z], semm3, k - 1, along(k)) for k in range(1, owners)
    ]
    third = []
    for part in parts:
        for k in range(1, chips):
            second[part, k].wait_recv()
        rows = part_rows(part)
        total = own2[rows, :]
        for other in range(chips - 1):
            total = total + recv2[other, rows, :]
        if part is None:
            recvs3[z] = total
            third += [
                send(recvs3.at[z], recvs3.at[z], sems3, k - 1, along(k)) for k in range(1, owners)
            ]
        elif part == 0:
            own2[rows, :] = total
        else:
            send3[part - 1] = total
            third.append(
                send(send3.at[part - 1], recv3.at[part - 1], sem3, part - 1, along(part))
            )
    for copy in third:
        copy.wait_recv()
    total = own2[pl.ds(pl.multiple_of(z * chunk, 16), chunk), :]
    for other in range(owners - 1):
        total = total + recv3[other]
    slot = core * chips + chip
    gathered[slot] = total
    total = recvs3[0]
    for other in range(1, owners):
        total = total + recvs3[other]
    gathered_small[slot] = total

    here = gathered.at[slot]
    plane = [send(here, here, sema, k - 1, same_core(k)) for k in range(1, chips)]
    cross = [send(here, here, semb, 0, partner)]
    here = gathered_small.at[slot]
    plane_small = [send(here, here, semas, k - 1, same_core(k)) for k in range(1, chips)]
    cross_small = [send(here, here, sembs, 0, partner)]

    for copy in misc_copies:
        copy.wait_recv()
    misc = sum([misc3[k] for k in range(1, owners)], misc3[0])
    weight_sum = jnp.sum(misc[14:15, :mid], axis=1, keepdims=True)
    inverse = 1.0 / weight_sum
    loss_sum = jnp.sum(misc[13:14, :mid], axis=1, keepdims=True)
    sums_ref[0:1, :] = loss_sum + jnp.zeros((1, C1), F32)
    sums_ref[1:2, :] = weight_sum + jnp.zeros((1, C1), F32)
    head_bias = jnp.sum(misc[:, mid:].T, axis=0, keepdims=True)
    for row in range(3):
        flat[pl.ds(row * C1, C1)] = misc[row : row + 1, :C1].reshape(C1)
    for row in range(3, 13):
        flat[pl.ds(3 * C1 + (row - 3) * mid, mid)] = misc[row : row + 1, :mid].reshape(mid)
    head_row[...] = jnp.zeros_like(head_row)
    head_row[0:1, :ROWS12] = head_bias
    flat[pl.ds(3 * C1 + 10 * mid, C1)] = head_row[0:1, :].reshape(C1)
    grad = flat[pl.ds(0, vec_ref.shape[0])] * inverse.reshape(1)
    firsts = BETA_ONE * first_ref[...] + (1.0 - BETA_ONE) * grad
    seconds = BETA_TWO * second_ref[...] + (1.0 - BETA_TWO) * grad * grad
    nfirst_ref[...] = firsts
    nsecond_ref[...] = seconds
    change = (
        firsts
        / (1.0 - BETA_ONE**STEP)
        / (jnp.sqrt(seconds / (1.0 - BETA_TWO**STEP)) + ADAM_EPS)
    )
    nvec_ref[...] = vec_ref[...] - LR_ADAM * change

    for k, copy in zip(range(1, chips), plane):
        copy.wait_recv()
        other = gathered.at[core * chips + lax.rem(chip + chips - k, chips)]
        cross.append(send(other, other, semb, k, partner))
    for copy in cross:
        copy.wait_recv()

    load_moment.wait()

    for owner_peer in range(peers):
        start = owner_peer * chunk
        size = min(chunk, own_rows - start)
        if size > 0:
            grad = gathered[slot_of(owner_peer, peers), :size, :] * inverse
            rows = slice(start, start + size)
            moment = MOMENTUM * moment_ref[rows, :] + grad
            newm_ref[rows, :] = moment
            direction[rows, :] = grad + MOMENTUM * moment
    shares = [rows // owners for rows in segment_rows()]
    starts = [sum(shares[:k]) for k in range(len(shares))]
    for (task_chip, task_core), share, start in zip(TASKS, shares, starts):

        @pl.when((lax.rem(chip, 4) == task_chip) & (core == task_core))
        def _(share=share, start=start):
            mine_u[:share, :] = direction[start : start + share, :]
            if share < mine_u.shape[0]:
                mine_u[share:, :] = jnp.zeros((mine_u.shape[0] - share, mid), F32)

    mine = mine_u[...]
    gram = lax.dot_general(
        mine,
        mine,
        (((0,), (0,)), ((), ())),
        preferred_element_type=F32,
        precision=EXACT_PRECISION,
    )
    gram_part[:C1, :] = gram[:C1, :]
    gram_part[C1:, :C1] = gram[C1 : C1 + 64, C1:]
    gram_part[C1:, C1:] = gram[C1 + 64 :, C1:]
    part = gram_part.shape[0] // owners
    copies = []
    for k in range(1, owners):
        start = pl.multiple_of(lax.rem(z + k, owners) * part, 8)
        copies.append(send(gram_part.at[pl.ds(start, part), :], gram_recv.at[z], semg, k - 1, along(k)))
    own_part = pl.ds(pl.multiple_of(z * part, 8), part)
    gram_recv[z] = gram_part[own_part, :]

    for k, copy in zip(range(1, chips), plane_small):
        copy.wait_recv()
        other = gathered_small.at[core * chips + lax.rem(chip + chips - k, chips)]
        cross_small.append(send(other, other, sembs, k, partner))
    for copy in cross_small:
        copy.wait_recv()
    tiles = []
    for row in range(0, SMALL_ROWS, 16):
        at = row % small_chunk
        tile = gathered_small[slot_of(row // small_chunk, peers), at : at + 16, :]
        tiles.append(tile * inverse)
    small[...] = jnp.zeros_like(small)
    for tap in range(TAPS):
        lanes = slice(tap * (mid + C1), tap * (mid + C1) + mid)
        small[:16, lanes] = tiles[tap]
        lanes = slice(tap * (mid + C1) + mid, (tap + 1) * (mid + C1))
        if tap < 5:
            small[:16, lanes] = tiles[9 + tap][:, :C1]
        else:
            small[:16, lanes] = tiles[9 + tap - 5][:, C1:]
    small[32:48, SMALL_LANES:] = tiles[14][:, :C1]
    small[48:, SMALL_LANES:] = tiles[14][:, C1:]
    head_part = (slice(0, 12), slice(0, SMALL_LANES))
    stem_part = (slice(32, 59), slice(SMALL_LANES, SMALL_LANES + C1))
    for part, old_ref, fresh_ref in (
        (head_part, headm_ref, nheadm_ref),
        (stem_part, stemm_ref, nstemm_ref),
    ):
        grad = small[part]
        moment = MOMENTUM * old_ref[...] + grad
        fresh_ref[...] = moment
        turn = grad + MOMENTUM * moment
        small[part] = turn * lax.rsqrt(
            jnp.sum(jnp.sum(turn * turn, axis=1, keepdims=True), axis=0, keepdims=True) + NORM_EPS
        )
    gram = lax.dot_general(
        small[...],
        small[...],
        (((1,), (1,)), ((), ())),
        preferred_element_type=F32,
        precision=EXACT_PRECISION,
    )
    product = ns_chain(gram, identity(64))
    small[...] = dot_nn(product, small[...], EXACT_PRECISION)
    keep = 1.0 - LR_MUON * DECAY
    nhead_ref[...] = head_ref[...] * keep - LR_MUON * small[head_part]
    nstem_ref[...] = stem_ref[...] * keep - LR_MUON * small[stem_part]

    for copy in copies:
        copy.wait_recv()
    gram_all[own_part, :] = sum([gram_recv[k] for k in range(1, owners)], gram_recv[0])
    copies = [
        send(gram_all.at[own_part, :], gram_all.at[own_part, :], semh, k - 1, along(k))
        for k in range(1, owners)
    ]
    for copy in copies:
        copy.wait_recv()
    upper, corner = gram_all[:C1, :], gram_all[C1:, :]
    gram = jnp.concatenate(
        [
            upper,
            jnp.concatenate(
                [upper[:, C1:].T, jnp.concatenate([corner[:, :C1], corner[:, C1:]], axis=0)],
                axis=1,
            ),
        ],
        axis=0,
    )
    eye = identity(mid)
    trace = jnp.sum(jnp.sum(gram * eye, axis=1, keepdims=True), axis=0, keepdims=True)
    scale = lax.rsqrt(trace + NORM_EPS)
    product = ns_chain(gram * (scale * scale), eye) * scale
    turned = dot_nn(mine_u[...], product, EXACT_PRECISION)

    place = lax.rem(chip, 4)
    base = chip - place

    def in_group(k):
        return {"batch": (base + lax.rem(place + k, 4)) * 2 + core}

    for task_core, buffer in ((0, x_zero), (1, x_one)):

        @pl.when(core == task_core)
        def _(buffer=buffer, other_buffer=(x_one, x_zero)[task_core]):
            size = buffer.shape[1]
            buffer[place] = turned[:size].astype(LOWTYPE)
            here = buffer.at[place]
            plane = [send(here, here, semx, k - 1, in_group(k), False) for k in range(1, 4)]
            cross = [send(here, here, semy, 0, partner, False)]
            for k in range(1, 4):
                plane[k - 1].wait_recv()
                other = buffer.at[lax.rem(place + 4 - k, 4)]
                cross.append(send(other, other, semy, k, partner, False))
            for k in range(4):
                there = other_buffer.at[lax.rem(place + 4 - k, 4)]
                pltpu.make_async_remote_copy(
                    src_ref=there,
                    dst_ref=there,
                    send_sem=semy.at[0, k],
                    recv_sem=semy.at[1, k],
                    device_id=partner,
                    device_id_type=MESH,
                ).wait_recv()
            for copy in plane + cross:
                copy.wait_send()

    load_weight.wait()
    for (task_chip, task_core), share, start in zip(TASKS, shares, starts):
        buffer = (x_zero, x_one)[task_core]
        rows = slice(start, start + share)
        fresh = weight_ref[rows, :] * keep - LR_MUON * buffer[task_chip, :share, :].astype(F32)
        new_ref[rows, :] = fresh
    for copy in started:
        copy.wait_send()


def muon_call(owners, peers, operands):
    mid = CHANNELS_MID
    chips = peers // 2
    chunk, small_chunk = chunk_rows(owners, peers)
    block = block_rows(owners, peers)
    rows = operands[2].shape[0]
    part = 192 // owners
    shares = [seg_rows // owners for seg_rows in segment_rows()]
    most = [max(s for s, t in zip(shares, TASKS) if t[1] == core) for core in (0, 1)]
    out_shapes = [
        ((rows, mid), F32),
        ((rows, mid), F32),
        (operands[4].shape, F32),
        (operands[4].shape, F32),
        (operands[6].shape, F32),
        (operands[6].shape, F32),
        (operands[8].shape, F32),
        (operands[8].shape, F32),
        (operands[8].shape, F32),
        ((8, C1), F32),
    ]
    scratch = [
        ((chips, block, mid), F32),
        ((block, mid), F32),
        ((chips - 1, block, mid), F32),
        ((chips - 1, block, mid), F32),
        ((owners - 1, chunk, mid), F32),
        ((owners - 1, chunk, mid), F32),
        ((owners, small_chunk, mid), F32),
        ((peers, chunk, mid), F32),
        ((peers, small_chunk, mid), F32),
        (operands[1].shape, F32),
        ((chips,) + operands[1].shape, F32),
        ((owners,) + operands[1].shape, F32),
        ((rows, mid), F32),
        ((max(most), mid), F32),
        ((192, mid), F32),
        ((owners, part, mid), F32),
        ((192, mid), F32),
        ((64, SMALL_LANES + C1), F32),
        ((4, most[0], mid), LOWTYPE),
        ((4, most[1], mid), LOWTYPE),
        ((3 * C1 + 10 * mid + C1,), F32),
        ((8, C1), F32),
        ((chips * block, mid), F32),
        ((rows, mid), F32),
        ((rows, mid), F32),
    ]
    sems = [
        (owners + 1) * chips,
        (owners + 1) * (chips - 1),
        owners - 1,
        owners - 1,
        chips - 1,
        chips,
        owners - 1,
        owners - 1,
        3,
        4,
        1,
        chips - 1,
        owners - 1,
        chips - 1,
        chips,
    ]
    hbm = pl.BlockSpec(memory_space=pl.ANY)
    vmem = pl.BlockSpec(memory_space=pltpu.VMEM)
    return pl.pallas_call(
        functools.partial(muon_body, owners, peers),
        out_shape=[jax.ShapeDtypeStruct(shape, kind) for shape, kind in out_shapes],
        in_specs=[hbm, vmem, hbm, hbm] + [vmem] * (len(operands) - 4),
        out_specs=[vmem] * len(out_shapes),
        scratch_shapes=[pltpu.VMEM(shape, kind) for shape, kind in scratch]
        + [pltpu.SemaphoreType.DMA((3,))]
        + [pltpu.SemaphoreType.DMA((2, count)) for count in sems],
        compiler_params=pltpu.CompilerParams(
            vmem_limit_bytes=VMEM_BYTES, collective_id=0, has_side_effects=True
        ),
    )(*operands)


def open_body(
    owners,
    peers,
    weight_ref,
    images_ref,
    noise_ref,
    mask_ref,
    image_ref,
    conv1_ref,
    conv1b_ref,
    conv2_ref,
    conv2b_ref,
    skip_ref,
    temb_ref,
    qkv_ref,
    outw_ref,
    noisy_ref,
    planes_ref,
    maskw_ref,
    held,
    left,
    sema,
    semb,
    semc,
):
    mid = CHANNELS_MID
    chips = peers // 2
    chunk, _ = chunk_rows(owners, peers)
    own_rows = weight_ref.shape[0]
    z = lax.axis_index("bucket")
    peer = lax.axis_index("batch")
    chip, core = peer // 2, peer % 2
    partner = {"batch": chip * 2 + 1 - core}
    slot = core * chips + chip
    started = []

    def same_core(k):
        return {"batch": lax.rem(chip + k, chips) * 2 + core}

    def along(k):
        return {"bucket": lax.rem(z + k, owners)}

    def send(source, target, sems, index, device):
        copy = pltpu.make_async_remote_copy(
            src_ref=source,
            dst_ref=target,
            send_sem=sems.at[0, index],
            recv_sem=sems.at[1, index],
            device_id=device,
            device_id_type=MESH,
        )
        copy.start()
        started.append(copy)
        return copy

    barrier = pltpu.get_barrier_semaphore()
    friends = [partner] + [same_core(k) for k in range(1, chips)]
    friends += [along(k) for k in range(1, owners)]
    for friend in friends:
        pl.semaphore_signal(barrier, inc=1, device_id=friend, device_id_type=MESH)

    for other in range(peers):
        start = other * chunk
        size = min(chunk, own_rows - start)
        if size > 0:
            held[z, slot_of(other, peers), :size, :] = weight_ref[start : start + size, :].astype(
                LOWTYPE
            )
        if size < chunk:
            held[z, slot_of(other, peers), max(size, 0) :, :] = jnp.zeros(
                (chunk - max(size, 0), mid), LOWTYPE
            )
    pl.semaphore_wait(barrier, len(friends))

    here = held.at[z, slot]
    first = [send(here, here, sema, k - 1, along(k)) for k in range(1, owners)]

    samples = mask_ref.shape[0]
    row = lax.broadcasted_iota(jnp.int32, (samples, samples), 0)
    lane = lax.broadcasted_iota(jnp.int32, (samples, samples), 1)

    def column(k):
        return jnp.sum(jnp.where(row == lane, image_ref[k : k + 1, :], 0.0), axis=1, keepdims=True)

    keep, spread, weight = column(0), column(1), column(2)
    left[...] = jnp.zeros_like(left)
    for c in range(3):
        noise = noise_ref[c]
        noisy = keep * images_ref[c] + spread * noise
        left[c, :samples, :] = noisy.astype(LOWTYPE)
        one = noise.astype(LOWTYPE)
        rest = noise - one.astype(F32)
        two = rest.astype(LOWTYPE)
        left[3 + c, :samples, :] = one
        left[6 + c, :samples, :] = two
        left[9 + c, :samples, :] = (rest - two.astype(F32)).astype(LOWTYPE)
    left[12, :samples, :] = mask_ref[...].astype(F32).astype(LOWTYPE)
    for ref in (noisy_ref, planes_ref, maskw_ref):
        ref[:, 12:, :] = jnp.zeros((samples, ROWS12 - 12, PLACES), F32)

    def picture(quarter):
        pixel = lax.broadcasted_iota(jnp.int32, (S * S, PLACES), 0)
        lane = lax.broadcasted_iota(jnp.int32, (S * S, PLACES), 1)
        wanted = (
            (lane // SIDE * 2 + quarter // 2) * S + lane % SIDE * 2 + quarter % 2
        )
        pick = jnp.where(pixel == wanted, 1.0, 0.0).astype(LOWTYPE)
        rows = left.shape[1]
        moved = dot_nn(left[...].reshape(13 * rows, S * S), pick)
        maskw = moved[12 * rows : 12 * rows + samples] * weight
        for c in range(3):
            k = quarter * 3 + c
            noisy_ref[:, k, :] = moved[c * rows : c * rows + samples]
            planes_ref[:, k, :] = sum(
                [moved[(p + c) * rows : (p + c) * rows + samples] for p in (6, 9)],
                moved[(3 + c) * rows : (3 + c) * rows + samples],
            )
            maskw_ref[:, k, :] = maskw

    picture(0)
    second = []
    for k, copy in zip(range(1, owners), first):
        copy.wait_recv()
        there = held.at[lax.rem(z + owners - k, owners), slot]
        second.append(
            [
                send(there, there, semb, (k - 1) * (chips - 1) + j - 1, same_core(j))
                for j in range(1, chips)
            ]
        )
        if k < 4:
            picture(k)
    for k in range(owners, 4):
        picture(k)
    third = []
    for k, copies in zip(range(1, owners), second):
        for copy in copies:
            copy.wait_recv()
        mine = held.at[lax.rem(z + owners - k, owners), pl.ds(core * chips, chips)]
        third.append(send(mine, mine, semc, k - 1, partner))
    for copy in third:
        copy.wait_recv()

    def place(seg, row, values):
        size = values.shape[0]
        if seg < 2:
            whole, side = ((conv1_ref, conv1b_ref), (conv2_ref, conv2b_ref))[seg]
            whole[row : row + size, :] = values
            height = side.shape[0]
            done = 0
            while done < size:
                offset, inner = (row + done) // height, (row + done) % height
                part = min(size - done, height - inner)
                side[inner : inner + part, offset * mid : (offset + 1) * mid] = values[
                    done : done + part
                ]
                done += part
        elif seg in (4, 5, 6):
            qkv_ref[row : row + size, (seg - 4) * mid : (seg - 3) * mid] = values
        else:
            {2: skip_ref, 3: temb_ref, 7: outw_ref}[seg][row : row + size, :] = values

    for owner in range(owners):
        packed = 0
        for seg, seg_rows in enumerate(segment_rows()):
            share = seg_rows // owners
            done = 0
            while done < share:
                row = packed + done
                size = min(share - done, chunk - row % chunk)
                inner = row % chunk
                place(
                    seg,
                    owner * share + done,
                    held[owner, slot_of(row // chunk, peers), inner : inner + size, :],
                )
                done += size
            packed += share
    for copy in started:
        copy.wait_send()


def open_call(owners, peers, operands):
    mid = CHANNELS_MID
    chips = peers // 2
    chunk, _ = chunk_rows(owners, peers)
    samples = operands[3].shape[0]
    rows = -(-samples // 16) * 16
    out_shapes = [
        ((9 * C1, mid), LOWTYPE),
        ((3 * C1, 3 * mid), LOWTYPE),
        ((9 * mid, mid), LOWTYPE),
        ((3 * mid, 3 * mid), LOWTYPE),
        ((C1, mid), LOWTYPE),
        ((TEMB, mid), LOWTYPE),
        ((mid, 3 * mid), LOWTYPE),
        ((mid, mid), LOWTYPE),
        ((samples, ROWS12, PLACES), F32),
        ((samples, ROWS12, PLACES), F32),
        ((samples, ROWS12, PLACES), F32),
    ]
    vmem = pl.BlockSpec(memory_space=pltpu.VMEM)
    return pl.pallas_call(
        functools.partial(open_body, owners, peers),
        out_shape=[jax.ShapeDtypeStruct(shape, kind) for shape, kind in out_shapes],
        in_specs=[vmem] * len(operands),
        out_specs=[vmem] * len(out_shapes),
        scratch_shapes=[
            pltpu.VMEM((owners, peers, chunk, mid), LOWTYPE),
            pltpu.VMEM((13, rows, S * S), LOWTYPE),
            pltpu.SemaphoreType.DMA((2, owners - 1)),
            pltpu.SemaphoreType.DMA((2, (owners - 1) * (chips - 1))),
            pltpu.SemaphoreType.DMA((2, owners - 1)),
        ],
        compiler_params=pltpu.CompilerParams(
            vmem_limit_bytes=VMEM_BYTES, collective_id=1, has_side_effects=True
        ),
    )(*operands)


def close_body(*refs):
    values, outs = refs[:10], refs[10:]
    for source, target in zip(values[:9], outs[:9]):
        target[...] = source[...]
    for source, target in zip((values[0], values[2], values[4], values[6]), outs[9:13]):
        target[...] = source[...].astype(LOWTYPE)
    sums = values[9]
    outs[13][...] = sums[0:1, 0:1]
    outs[14][...] = sums[1:2, 0:1]


def close_call(values):
    shapes = [(v.shape, F32) for v in values[:9]]
    shapes += [(values[k].shape, LOWTYPE) for k in (0, 2, 4, 6)] + [((1, 1), F32)] * 2
    vmem = pl.BlockSpec(memory_space=pltpu.VMEM)
    return pl.pallas_call(
        close_body,
        out_shape=[jax.ShapeDtypeStruct(shape, kind) for shape, kind in shapes],
        in_specs=[vmem] * len(values),
        out_specs=[vmem] * len(shapes),
        compiler_params=pltpu.CompilerParams(vmem_limit_bytes=VMEM_BYTES),
    )(*values)


def stem_spread():
    counts = np.zeros((3, 2, 3))
    for block in range(3):
        for inner in range(2):
            for sub in range(2):
                tap = 2 * (block - 1) + inner - sub + 1
                if 0 <= tap <= 2:
                    counts[block, inner, tap] += 1
    full = np.zeros((3, 3, ROWS12, 3, 3, 3))
    both = (np.einsum("ayt,bxu->abyxtu", counts, counts) * 0.25).reshape(3, 3, 4, 3, 3)
    for c in range(3):
        full[:, :, c:12:3, :, :, c] = both
    return np.pad(full.reshape(TAPS * ROWS12, 27), ((0, 0), (0, 5))).astype(np.float32)


def same_group(chans):
    group = np.arange(chans) // (chans // GROUPS)
    same = (group[:, None] == group[None, :]) / (PLACES * (chans // GROUPS))
    return same.astype(LOWTYPE)


def shards(
    images,
    pixel_mask,
    timesteps,
    noise_field,
    matrices,
    matrix_moms,
    stem_weight,
    stem_moms,
    head_weight,
    head_moms,
    vectors,
    vector_firsts,
    vector_seconds,
):
    owners, peers = lax.axis_size("bucket"), lax.axis_size("batch")
    samples = images.shape[0]
    level, weight = plan(timesteps)
    per_image = jnp.stack([jnp.sqrt(level), jnp.sqrt(1.0 - level), weight], axis=0)
    conv1, conv1b, conv2, conv2b, skip, temb, qkv, outw, noisy, noise, mask_weight = open_call(
        owners,
        peers,
        [
            matrices,
            images.transpose(1, 0, 2),
            noise_field.transpose(1, 0, 2),
            pixel_mask,
            per_image,
        ],
    )
    head_turned = head_weight.T
    rows_out, misc = unet_call(
        samples,
        owners,
        peers,
        [
            noisy,
            noise,
            mask_weight,
            swish(embed(timesteps)),
            stem_weight,
            head_turned,
            conv1,
            conv1b,
            conv2,
            conv2b,
            skip,
            temb,
            qkv,
            outw,
            vectors,
            same_group(C1),
            same_group(CHANNELS_MID),
            stem_spread(),
        ],
    )
    values = muon_call(
        owners,
        peers,
        [
            rows_out,
            misc,
            matrices,
            matrix_moms,
            stem_weight,
            stem_moms,
            head_turned,
            head_moms.T,
            vectors,
            vector_firsts,
            vector_seconds,
        ],
    )
    (
        new_matrices,
        new_matrix_moms,
        new_stem,
        new_stem_moms,
        new_head,
        new_head_moms,
        new_vectors,
        new_firsts,
        new_seconds,
        matrix_copies,
        stem_copy,
        head_copy,
        vector_copy,
        loss_sum,
        weight_sum,
    ) = close_call(values)
    loss_sum, weight_sum = loss_sum.reshape(()), weight_sum.reshape(())
    new_head, new_head_moms, head_copy = new_head.T, new_head_moms.T, head_copy.T
    return (
        loss_sum,
        weight_sum,
        new_matrices,
        new_matrix_moms,
        matrix_copies,
        new_stem,
        new_stem_moms,
        stem_copy,
        new_head,
        new_head_moms,
        head_copy,
        new_vectors,
        new_firsts,
        new_seconds,
        vector_copy,
    )


def solution(mesh):
    return jax.shard_map(
        shards,
        mesh=mesh,
        in_specs=(
            P(("bucket", "batch"), None, None),
            P(("bucket", "batch"), None),
            P(("bucket", "batch")),
            P(("bucket", "batch"), None, None),
            P("bucket", None),
            P("bucket", None),
            P(),
            P(),
            P(),
            P(),
            P(),
            P(),
            P(),
        ),
        out_specs=(
            P(),
            P(),
            P("bucket", None),
            P("bucket", None),
            P("bucket", None),
            P(),
            P(),
            P(),
            P(),
            P(),
            P(),
            P(),
            P(),
            P(),
            P(),
        ),
        check_vma=False,
    )
```

```python
import functools
import math

import jax
import jax.numpy as jnp
import numpy as np
from jax import lax
from jax.experimental import pallas as pl
from jax.experimental.pallas import tpu as pltpu
from jax.sharding import PartitionSpec as P

C1 = 128
CHANNELS_MID = 256
TEMB = 512
GROUPS = 32
S = 32
TSTEPS = 1000
NS_STEPS = 5
STEP = 10


GN_EPS = 1e-05
NORM_EPS = 1e-12
MOMENTUM = 0.95
LR_MUON = 0.5
DECAY = 0.01
NS_A = 3.4445
NS_B = -4.775
NS_C = 2.0315
BETA_ONE = 0.9
BETA_TWO = 0.999
LR_ADAM = 0.5
ADAM_EPS = 1e-08
EXACT_PRECISION = lax.Precision.HIGHEST
LOWTYPE = jnp.bfloat16


def segment_rows():
    return [
        9 * C1,
        9 * CHANNELS_MID,
        C1,
        TEMB,
        CHANNELS_MID,
        CHANNELS_MID,
        CHANNELS_MID,
        CHANNELS_MID,
    ]


def plan(timesteps):
    frac_t = (timesteps.astype(jnp.float32) / TSTEPS + 0.008) / 1.008
    level = jnp.cos(frac_t * (math.pi / 2)) ** 2
    ratio = level / (1.0 - level)
    return (level, jnp.minimum(1.0, 5.0 / ratio))


def embed(timesteps):
    half_width = TEMB // 2
    freqs = jnp.exp(-math.log(10000.0) * jnp.arange(half_width, dtype=jnp.float32) / half_width)
    angles = timesteps.astype(jnp.float32)[:, None] * freqs[None, :]
    return jnp.concatenate([jnp.sin(angles), jnp.cos(angles)], axis=1)


def swish(values):
    return values * jax.nn.sigmoid(values)


F32 = jnp.float32
PLACES = 256
SIDE = 16
HALO = 288
TAPS = 9
ROWS12 = 16
CHUNK = 64
SMALL_ROWS = 240
VMEM_BYTES = 56 * 1024 * 1024
SEG_OFF = (0, 1152, 3456, 3584, 4096, 4352, 4608, 4864, 5120)


def dot_nn(a, b, precision=None):
    return lax.dot_general(
        a, b, (((1,), (0,)), ((), ())), preferred_element_type=F32, precision=precision
    )


def dot_nt(a, b):
    return lax.dot_general(a, b, (((1,), (1,)), ((), ())), preferred_element_type=F32)


def dot_tn(a, b):
    return lax.dot_general(a, b, (((0,), (0,)), ((), ())), preferred_element_type=F32)


def sigmoid(v):
    return 1.0 / (1.0 + jnp.exp(-v))


def fold8(v):
    rows, chans = v.shape
    return jnp.sum(v.reshape(rows // 8, 8, chans), axis=0)


def shift_lanes(x, di, dj):
    lane = lax.broadcasted_iota(jnp.int32, x.shape, 1)
    row, col = lane // SIDE + di, lane % SIDE + dj
    offset = (-(SIDE * di + dj)) % PLACES
    moved = x if offset == 0 else pltpu.roll(x, offset, 1)
    valid = (row >= 0) & (row < SIDE) & (col >= 0) & (col < SIDE)
    return jnp.where(valid, moved, 0.0)


def tap_offsets():
    return [(di, dj) for di in (-1, 0, 1) for dj in (-1, 0, 1)]


def unet_body(
    group,
    steps,
    owners,
    peers,
    noisy_ref,
    noise_ref,
    maskw_ref,
    time_ref,
    stem_ref,
    head_ref,
    conv1_ref,
    conv1b_ref,
    conv2_ref,
    conv2b_ref,
    skip_ref,
    temb_ref,
    qkv_ref,
    outw_ref,
    vec_ref,
    same128_ref,
    same256_ref,
    spread_ref,
    rows_ref,
    misc_ref,
    acc_ref,
    gstem_ref,
    ghead_ref,
    gvec_ref,
    ghb_ref,
    loss_ref,
    wsum_ref,
    x0,
    hid,
    res,
    outp,
    attn,
    a1,
    a2,
    normed,
    qkv,
    plow,
    attl,
    low0,
    joined,
    patch,
    pad1,
    pad2,
    shiftf,
    dyf,
    dout,
    dq3,
    dpool,
    tproj,
    gtime,
    dtap,
    datt,
    dscore,
    dpool_low,
    stemw_ref,
    headw_ref,
    headb_ref,
    time_low,
    wide_rows,
):
    step = pl.program_id(0)
    mid = CHANNELS_MID
    chunks = range(0, PLACES, CHUNK)
    images = range(group)

    @pl.when(step == 0)
    def _():
        acc_ref[...] = jnp.zeros_like(acc_ref)
        gstem_ref[...] = jnp.zeros_like(gstem_ref)
        ghead_ref[...] = jnp.zeros_like(ghead_ref)
        gvec_ref[...] = jnp.zeros_like(gvec_ref)
        ghb_ref[...] = jnp.zeros_like(ghb_ref)
        loss_ref[...] = jnp.zeros_like(loss_ref)
        wsum_ref[...] = jnp.zeros_like(wsum_ref)
        gtime[...] = jnp.zeros_like(gtime)
        for ref in (a1, a2, pad1, pad2):
            for g in images:
                ref[g, :SIDE, :] = jnp.zeros((SIDE, ref.shape[2]), ref.dtype)
                ref[g, HALO - SIDE :, :] = jnp.zeros((SIDE, ref.shape[2]), ref.dtype)
        shiftf[...] = jnp.zeros_like(shiftf)
        wide_rows[...] = jnp.zeros_like(wide_rows)
        samples = time_ref.shape[0]
        wide_rows[:samples, :TEMB] = time_ref[...]
        time_low[...] = wide_rows[: time_low.shape[0], :TEMB].astype(LOWTYPE)
        tproj[...] = dot_nn(time_low[...], temb_ref[...])
        wide_rows[:27, :C1] = stem_ref[...].astype(LOWTYPE).astype(F32)
        spread_stem = dot_nn(spread_ref[:, :27], wide_rows[:27, :C1], EXACT_PRECISION)
        for piece in range(3):
            low = spread_stem.astype(LOWTYPE)
            stemw_ref[:, piece * C1 : (piece + 1) * C1] = low
            spread_stem = spread_stem - low.astype(F32)
        width = mid + C1
        wide_rows[:ROWS12, :width] = jnp.zeros((ROWS12, width), F32)
        for tap in range(TAPS):
            wide_rows[:12, :width] = head_ref[:, tap * width : (tap + 1) * width]
            headw_ref[tap * ROWS12 : (tap + 1) * ROWS12, :] = wide_rows[:ROWS12, :width].astype(
                LOWTYPE
            )
        row = lax.broadcasted_iota(jnp.int32, (ROWS12, 12), 0)
        lane = lax.broadcasted_iota(jnp.int32, (ROWS12, 12), 1)
        tail = vec_ref[pl.ds(3 * C1 + 10 * mid, 12)].reshape(1, 12)
        bias = jnp.where(row == lane, tail, 0.0)
        headb_ref[...] = jnp.sum(bias, axis=1, keepdims=True) + jnp.zeros((ROWS12, C1), F32)

    def vec(row, chans=mid):
        start = row * C1 if chans == C1 else 3 * C1 + (row - 3) * mid
        return vec_ref[pl.ds(start, chans)].reshape(1, chans)

    def add_vec(row, value):
        gvec_ref[row : row + 1, : value.shape[1]] += value

    def total(parts):
        return jnp.concatenate([jnp.sum(p, axis=0, keepdims=True) for p in parts], axis=0)

    def grouped(stats, chans):
        same = same128_ref if chans == C1 else same256_ref
        first = stats.astype(LOWTYPE).astype(F32)
        second = (stats - first).astype(LOWTYPE).astype(F32)
        third = stats - first - second
        sums = dot_nn(jnp.concatenate([first, second, third], axis=0).astype(LOWTYPE), same[...])
        return sums[:group] + sums[group : 2 * group] + sums[2 * group :]

    def gn_stats(ref, sums, chans):
        mean = grouped(sums, chans)
        parts = []
        for g in images:
            acc = jnp.zeros((8, chans), F32)
            for r in chunks:
                c = ref[g, r : r + CHUNK, :] - mean[g : g + 1]
                acc += fold8(c * c)
            parts.append(acc)
        return mean, lax.rsqrt(grouped(total(parts), chans) + GN_EPS)

    def edge(chans, left):
        col = lax.broadcasted_iota(jnp.int32, (CHUNK, chans), 0) % SIDE
        return (col > 0) if left else (col < SIDE - 1)

    def act_shift(ref, g, mean, rstd, gain, shift, dest, chans):
        for r in chunks:
            y = (ref[g, r : r + CHUNK, :] - mean[g : g + 1]) * rstd[g : g + 1] * gain + shift
            a = y * sigmoid(y)
            shiftf[g, 8 + r : 8 + r + CHUNK, :chans] = a
            dest[g, SIDE + r : SIDE + r + CHUNK, chans : 2 * chans] = a.astype(LOWTYPE)
        for r in chunks:
            before = shiftf[g, 7 + r : 7 + r + CHUNK, :chans]
            after = shiftf[g, 9 + r : 9 + r + CHUNK, :chans]
            rows = slice(SIDE + r, SIDE + r + CHUNK)
            dest[g, rows, :chans] = jnp.where(edge(chans, True), before, 0.0).astype(LOWTYPE)
            dest[g, rows, 2 * chans :] = jnp.where(edge(chans, False), after, 0.0).astype(LOWTYPE)

    def dy_cat(ref, g, order):
        return jnp.concatenate(
            [ref[g, SIDE * k : SIDE * k + PLACES, :] for k in order], axis=1
        )

    def stack(parts):
        return jnp.concatenate(parts, axis=0) if len(parts) > 1 else parts[0]

    def staged(stages, fillers=()):
        fillers = list(fillers)
        for stage in stages:
            for g in images:
                stage(g)
            if fillers:
                fillers.pop(0)()
        for filler in fillers:
            filler()

    def rows_of(g):
        return slice(g * PLACES, (g + 1) * PLACES)

    sums1 = [None] * group

    def stem_patch(g):
        noisy = noisy_ref[g]
        for tap, (di, dj) in enumerate(tap_offsets()):
            patch[g, tap * ROWS12 : (tap + 1) * ROWS12, :] = shift_lanes(noisy, di, dj).astype(
                LOWTYPE
            )

    def stem_pool(g):
        wide = dot_tn(patch[g], stemw_ref[...])
        acc = jnp.zeros((8, C1), F32)
        for r in chunks:
            w = wide[r : r + CHUNK]
            v = (w[:, :C1] + w[:, C1 : 2 * C1]) + w[:, 2 * C1 :] + vec(0, C1)
            x0[g, r : r + CHUNK, :] = v
            low0[g * PLACES + r : g * PLACES + r + CHUNK, :] = v.astype(LOWTYPE)
            acc += fold8(v)
        sums1[g] = acc

    staged([stem_patch, stem_pool])
    mean1, rstd1 = gn_stats(x0, total(sums1), C1)
    gain1, shift1 = vec(1, C1), vec(2, C1)

    sums2 = [None] * group

    def act_one(g):
        act_shift(x0, g, mean1, rstd1, gain1, shift1, a1, C1)

    def conv_one(g):
        wide = dot_nn(dy_cat(a1, g, (0, 1, 2)), conv1_ref[...])
        bias = vec(3) + vec(4) + tproj[pl.ds(step * group + g, 1), :]
        acc = jnp.zeros((8, mid), F32)
        for r in chunks:
            v = wide[r : r + CHUNK] + bias
            hid[g, r : r + CHUNK, :] = v
            acc += fold8(v)
        sums2[g] = acc

    staged([act_one, conv_one])
    mean2, rstd2 = gn_stats(hid, total(sums2), mid)
    gain2, shift2 = vec(5), vec(6)

    sums3 = [None] * group

    def act_two(g):
        act_shift(hid, g, mean2, rstd2, gain2, shift2, a2, mid)

    def conv_two(g):
        wide = dot_nn(dy_cat(a2, g, (0, 1, 2)), conv2_ref[...])
        wide = wide + dot_nn(low0[rows_of(g), :], skip_ref[...])
        acc = jnp.zeros((8, mid), F32)
        for r in chunks:
            v = wide[r : r + CHUNK] + vec(7)
            res[g, r : r + CHUNK, :] = v
            acc += fold8(v)
        sums3[g] = acc

    staged([act_two, conv_two])
    mean3, rstd3 = gn_stats(res, total(sums3), mid)
    gain3, shift3 = vec(8), vec(9)
    scale = mid ** (-0.5)
    ones3, twos3 = [None] * group, [None] * group

    def norm_three(g):
        for r in chunks:
            xh = (res[g, r : r + CHUNK, :] - mean3[g : g + 1]) * rstd3[g : g + 1]
            y = xh * gain3 + shift3
            normed[g * PLACES + r : g * PLACES + r + CHUNK, :] = y.astype(LOWTYPE)

    def project(g):
        rows = rows_of(g)
        wide = dot_nn(normed[rows, :], qkv_ref[...])
        qkv[rows, :mid] = (wide[:, :mid] + vec(10)).astype(LOWTYPE)
        qkv[rows, mid : 2 * mid] = wide[:, mid : 2 * mid].astype(LOWTYPE)
        qkv[rows, 2 * mid :] = (wide[:, 2 * mid :] + vec(11)).astype(LOWTYPE)

    def weigh(g):
        rows = rows_of(g)
        logits = dot_nt(qkv[rows, :mid], qkv[rows, mid : 2 * mid])
        for r in chunks:
            s = logits[r : r + CHUNK] * scale
            e = jnp.exp(s - jnp.max(s, axis=1, keepdims=True))
            p = e * (1.0 / jnp.sum(e, axis=1, keepdims=True))
            attn[g, r : r + CHUNK, :] = p
            plow[g, r : r + CHUNK, :] = p.astype(LOWTYPE)

    def attend(g):
        attl[rows_of(g), :] = dot_nn(plow[g], qkv[rows_of(g), 2 * mid :]).astype(LOWTYPE)

    def join(g):
        wide = dot_nn(attl[rows_of(g), :], outw_ref[...])
        for r in chunks:
            rows = slice(g * PLACES + r, g * PLACES + r + CHUNK)
            o = res[g, r : r + CHUNK, :] + wide[r : r + CHUNK] + vec(12)
            outp[g, r : r + CHUNK, :] = o
            joined[rows, :mid] = (o * sigmoid(o)).astype(LOWTYPE)
            x = x0[g, r : r + CHUNK, :]
            joined[rows, mid:] = (x * sigmoid(x)).astype(LOWTYPE)

    def head(g):
        taps = dot_nt(headw_ref[...], joined[rows_of(g), :])
        value = headb_ref[:, :1] + jnp.zeros((ROWS12, PLACES), F32)
        for tap, (di, dj) in enumerate(tap_offsets()):
            value = value + shift_lanes(taps[tap * ROWS12 : (tap + 1) * ROWS12, :], di, dj)
        error = value - noise_ref[g]
        masked = maskw_ref[g] * error
        loss_ref[...] += masked * error
        wsum_ref[...] += maskw_ref[g]
        grad = 2.0 * masked
        ghb_ref[...] += grad
        gradl = grad.astype(LOWTYPE).astype(F32)
        for tap, (di, dj) in enumerate(tap_offsets()):
            dtap[g, tap * ROWS12 : (tap + 1) * ROWS12, :] = shift_lanes(gradl, -di, -dj).astype(
                LOWTYPE
            )

    def head_back(g):
        wide = dot_tn(dtap[g], headw_ref[...])
        acc = jnp.zeros((8, mid), F32)
        for r in chunks:
            o = outp[g, r : r + CHUNK, :]
            s = sigmoid(o)
            d = wide[r : r + CHUNK, :mid] * (s * (1.0 + o * (1.0 - s)))
            outp[g, r : r + CHUNK, :] = d
            dout[g * PLACES + r : g * PLACES + r + CHUNK, :] = d.astype(LOWTYPE)
            acc += fold8(d)
            x = x0[g, r : r + CHUNK, :]
            s = sigmoid(x)
            dpool[g, r : r + CHUNK, :] = wide[r : r + CHUNK, mid:] * (s * (1.0 + x * (1.0 - s)))
        add_vec(12, jnp.sum(acc, axis=0, keepdims=True))

    def attend_back(g):
        datt[rows_of(g), :] = dot_nt(dout[rows_of(g), :], outw_ref[...]).astype(LOWTYPE)

    def weigh_back(g):
        rows = rows_of(g)
        gweights = dot_nt(datt[rows, :], qkv[rows, 2 * mid :])
        dval = dot_tn(plow[g], datt[rows, :])
        add_vec(11, jnp.sum(fold8(dval), axis=0, keepdims=True))
        dq3[rows, 2 * mid :] = dval.astype(LOWTYPE)
        for r in chunks:
            p = attn[g, r : r + CHUNK, :]
            gw = gweights[r : r + CHUNK]
            ds = p * (gw - jnp.sum(gw * p, axis=1, keepdims=True))
            dscore[g, r : r + CHUNK, :] = (ds * scale).astype(LOWTYPE)

    def query_back(g):
        rows = rows_of(g)
        dqry = dot_nn(dscore[g], qkv[rows, mid : 2 * mid])
        dkey = dot_tn(dscore[g], qkv[rows, :mid])
        add_vec(10, jnp.sum(fold8(dqry), axis=0, keepdims=True))
        dq3[rows, :mid] = dqry.astype(LOWTYPE)
        dq3[rows, mid : 2 * mid] = dkey.astype(LOWTYPE)

    def project_back(g):
        one, two = jnp.zeros((8, mid), F32), jnp.zeros((8, mid), F32)
        wide = dot_nt(dq3[rows_of(g), :], qkv_ref[...])
        for r in chunks:
            xh = (res[g, r : r + CHUNK, :] - mean3[g : g + 1]) * rstd3[g : g + 1]
            d = wide[r : r + CHUNK]
            res[g, r : r + CHUNK, :] = xh
            dyf[g, r : r + CHUNK, :] = d
            one += fold8(d)
            two += fold8(d * xh)
        ones3[g], twos3[g] = one, two

    staged(
        [
            norm_three,
            project,
            weigh,
            attend,
            join,
            head,
            head_back,
            attend_back,
            weigh_back,
            query_back,
            project_back,
        ]
    )

    ones, twos = total(ones3), total(twos3)
    add_vec(9, jnp.sum(ones, axis=0, keepdims=True))
    add_vec(8, jnp.sum(twos, axis=0, keepdims=True))

    def finish(ref, dest, rstd, gain, m1, m2, chans, extra, g, row):
        r1 = rstd[g : g + 1]
        acc = jnp.zeros((8, chans), F32)
        for r in chunks:
            d = dyf[g, r : r + CHUNK, :chans] * (gain * r1)
            d = d - m1[g : g + 1] * r1 - ref[g, r : r + CHUNK, :] * (m2[g : g + 1] * r1)
            if extra is not None:
                d = d + extra[g, r : r + CHUNK, :]
            acc += fold8(d)
            dest(g, r, d.astype(LOWTYPE))
        acc = jnp.sum(acc, axis=0, keepdims=True)
        add_vec(row, acc)
        return acc

    def to_pad(pad):
        def put(g, r, low):
            pad[g, SIDE + r : SIDE + r + CHUNK, :] = low

        return put

    def turned(parts):
        return stack(parts).T

    def pad_turned(pad):
        return turned([pad[g, SIDE : SIDE + PLACES, :] for g in images])

    def conv_back(pad, weights, g, chans, apply):
        wide = dot_nt(dy_cat(pad, g, (2, 1, 0)), weights)
        shiftf[g, 8 : 8 + PLACES, :chans] = wide[:, :chans]
        dyf[g, :, :chans] = wide[:, chans : 2 * chans]
        for r in chunks:
            after = shiftf[g, 9 + r : 9 + r + CHUNK, :chans]
            dyf[g, r : r + CHUNK, :chans] += jnp.where(edge(chans, False), after, 0.0)
        shiftf[g, 8 : 8 + PLACES, :chans] = wide[:, 2 * chans :]
        for r in chunks:
            before = shiftf[g, 7 + r : 7 + r + CHUNK, :chans]
            apply(r, dyf[g, r : r + CHUNK, :chans] + jnp.where(edge(chans, True), before, 0.0))

    def norm_back(pad, weights, ref, mean, rstd, gain, shift, chans, ones, twos, g):
        sums = [jnp.zeros((8, chans), F32), jnp.zeros((8, chans), F32)]

        def apply(r, da):
            xh = (ref[g, r : r + CHUNK, :] - mean[g : g + 1]) * rstd[g : g + 1]
            y = xh * gain + shift
            s = sigmoid(y)
            d = da * (s * (1.0 + y * (1.0 - s)))
            ref[g, r : r + CHUNK, :] = xh
            dyf[g, r : r + CHUNK, :chans] = d
            sums[0] += fold8(d)
            sums[1] += fold8(d * xh)

        conv_back(pad, weights[...], g, chans, apply)
        ones[g], twos[g] = sums

    def add_product(first, last, left, right):
        acc_ref[:, first:last] += dot_nn(left(), right())

    m1, m2 = grouped(ones * gain3, mid), grouped(twos * gain3, mid)
    ones2, twos2 = [None] * group, [None] * group

    def grad_out():
        add_product(SEG_OFF[7], SEG_OFF[8], lambda: dout[...].T, lambda: attl[...])

    def grad_project(k):
        add_product(
            SEG_OFF[4 + k],
            SEG_OFF[5 + k],
            lambda: dq3[:, k * mid : (k + 1) * mid].T,
            lambda: normed[...],
        )

    def grad_head():
        for g in images:
            ghead_ref[...] += dot_nn(dtap[g], joined[rows_of(g), :])

    staged(
        [
            lambda g: finish(res, to_pad(pad2), rstd3, gain3, m1, m2, mid, outp, g, 7),
            lambda g: norm_back(
                pad2, conv2b_ref, hid, mean2, rstd2, gain2, shift2, mid, ones2, twos2, g
            ),
        ],
        [grad_out, grad_head] + [functools.partial(grad_project, k) for k in range(3)],
    )
    ones, twos = total(ones2), total(twos2)
    add_vec(6, jnp.sum(ones, axis=0, keepdims=True))
    add_vec(5, jnp.sum(twos, axis=0, keepdims=True))

    n1, n2 = grouped(ones * gain2, mid), grouped(twos * gain2, mid)
    ones1, twos1 = [None] * group, [None] * group
    lowt2 = pad_turned(pad2)

    def finish_two(g):
        acc = finish(hid, to_pad(pad1), rstd2, gain2, n1, n2, mid, None, g, 3)
        add_vec(4, acc)
        gtime[pl.ds(step * group + g, 1), :] = acc

    def grad_conv(lowt, act, offset, k):
        width = act.shape[2]
        first = offset + k * width
        add_product(
            first,
            first + width,
            lambda: lowt,
            lambda: stack([act[g, SIDE * k : SIDE * k + PLACES, :] for g in images]),
        )

    def grad_skip():
        add_product(SEG_OFF[2], SEG_OFF[3], lambda: lowt2, lambda: low0[...])
        for g in images:
            dpool[g] += dot_nt(pad2[g, SIDE : SIDE + PLACES, :], skip_ref[...])

    staged(
        [
            finish_two,
            lambda g: norm_back(
                pad1, conv1b_ref, x0, mean1, rstd1, gain1, shift1, C1, ones1, twos1, g
            ),
        ],
        [functools.partial(grad_conv, lowt2, a2, SEG_OFF[1], k) for k in range(3)] + [grad_skip],
    )
    ones, twos = total(ones1), total(twos1)
    add_vec(2, jnp.sum(ones, axis=0, keepdims=True))
    add_vec(1, jnp.sum(twos, axis=0, keepdims=True))

    p1, p2 = grouped(ones * gain1, C1), grouped(twos * gain1, C1)
    lowt1 = pad_turned(pad1)

    def to_pool(g, r, low):
        dpool_low[g, r : r + CHUNK, :] = low

    def grad_stem(g):
        gstem_ref[...] += dot_nn(patch[g], dpool_low[g])

    staged(
        [lambda g: finish(x0, to_pool, rstd1, gain1, p1, p2, C1, dpool, g, 0), grad_stem],
        [functools.partial(grad_conv, lowt1, a1, SEG_OFF[0], k) for k in range(3)],
    )

    @pl.when(step == steps - 1)
    def _():
        acc_ref[:, SEG_OFF[3] : SEG_OFF[4]] = dot_tn(gtime[...].astype(LOWTYPE), time_low[...])
        if rows_ref.shape[0] > 5120 + SMALL_ROWS:
            rows_ref[...] = jnp.zeros_like(rows_ref)
        pieces = gradient_pieces(owners, peers)
        for block in range(0, 5120, C1):
            turned = acc_ref[:, block : block + C1].T
            for source, size, target in pieces:
                low, high = max(source, block), min(source + size, block + C1)
                if low < high:
                    start = target + low - source
                    rows_ref[start : start + high - low, :] = turned[low - block : high - block]
        stem = lax.dot_general(
            spread_ref[...],
            gstem_ref[...],
            (((0,), (0,)), ((), ())),
            preferred_element_type=F32,
            precision=EXACT_PRECISION,
        )
        head = ghead_ref[...]
        none = jnp.zeros((ROWS12, C1), F32)
        tiles = [head[k : k + 16, :mid] for k in range(0, 144, 16)]
        for k in range(0, 80, 16):
            other = head[80 + k : 96 + k, mid:] if k < 64 else none
            tiles.append(jnp.concatenate([head[k : k + 16, mid:], other], axis=1))
        tiles.append(jnp.concatenate([stem[:16], stem[16:]], axis=1))
        for tile, (start, _) in zip(tiles, small_tiles(owners, peers)):
            rows_ref[start : start + 16, :] = tile
        misc_ref[:, :mid] = gvec_ref[...]
        misc_ref[13:14, :mid] = jnp.sum(loss_ref[...], axis=0, keepdims=True)
        misc_ref[14:15, :mid] = jnp.sum(wsum_ref[...], axis=0, keepdims=True)
        misc_ref[:, mid:] = ghb_ref[:, :C1] + ghb_ref[:, C1:]


def chunk_rows(owners, peers):
    share = -(-5120 // (owners * peers))
    return -(-share // 16) * 16, -(-(-(-SMALL_ROWS // peers)) // 16) * 16


def block_rows(owners, peers):
    chunk, small = chunk_rows(owners, peers)
    return owners * chunk + small


def slot_of(peer, peers):
    return peer % 2 * (peers // 2) + peer // 2


def gradient_pieces(owners, peers):
    chunk, _ = chunk_rows(owners, peers)
    block = block_rows(owners, peers)
    pieces = []
    for owner in range(owners):
        packed = 0
        for seg, seg_rows in enumerate(segment_rows()):
            share = seg_rows // owners
            done = 0
            while done < share:
                row = packed + done
                size = min(share - done, chunk - row % chunk)
                target = slot_of(row // chunk, peers) * block + owner * chunk + row % chunk
                pieces.append((SEG_OFF[seg] + owner * share + done, size, target))
                done += size
            packed += share
    return pieces


def small_tiles(owners, peers):
    chunk, small = chunk_rows(owners, peers)
    tiles = []
    for row in range(0, SMALL_ROWS, 16):
        slot = slot_of(row // small, peers)
        tiles.append((slot * block_rows(owners, peers) + owners * chunk + row % small, slot))
    return tiles


def unet_call(samples, owners, peers, operands):
    group = max(k for k in (1, 2, 4) if samples % k == 0)
    steps = samples // group
    time_rows = -(-samples // 16) * 16
    mid = CHANNELS_MID
    places = group * PLACES

    def image_spec():
        return pl.BlockSpec((group, ROWS12, PLACES), lambda i: (i, 0, 0))

    def whole(shape):
        return pl.BlockSpec(shape, lambda i: (0,) * len(shape))

    out_shapes = [(peers * block_rows(owners, peers), mid), (ROWS12, mid + C1)]
    scratch = [
        ((mid, 5120), F32),
        ((TAPS * ROWS12, C1), F32),
        ((TAPS * ROWS12, mid + C1), F32),
        ((ROWS12, mid), F32),
        ((ROWS12, mid), F32),
        ((ROWS12, mid), F32),
        ((ROWS12, mid), F32),
        ((group, PLACES, C1), F32),
        ((group, PLACES, mid), F32),
        ((group, PLACES, mid), F32),
        ((group, PLACES, mid), F32),
        ((group, PLACES, mid), F32),
        ((group, HALO, 3 * C1), LOWTYPE),
        ((group, HALO, 3 * mid), LOWTYPE),
        ((places, mid), LOWTYPE),
        ((places, 3 * mid), LOWTYPE),
        ((group, PLACES, mid), LOWTYPE),
        ((places, mid), LOWTYPE),
        ((places, C1), LOWTYPE),
        ((places, mid + C1), LOWTYPE),
        ((group, TAPS * ROWS12, PLACES), LOWTYPE),
        ((group, HALO, mid), LOWTYPE),
        ((group, HALO, mid), LOWTYPE),
        ((group, PLACES + 16, mid), F32),
        ((group, PLACES, mid), F32),
        ((places, mid), LOWTYPE),
        ((places, 3 * mid), LOWTYPE),
        ((group, PLACES, C1), F32),
        ((time_rows, mid), F32),
        ((time_rows, mid), F32),
        ((group, TAPS * ROWS12, PLACES), LOWTYPE),
        ((places, mid), LOWTYPE),
        ((group, PLACES, mid), LOWTYPE),
        ((group, PLACES, C1), LOWTYPE),
        ((TAPS * ROWS12, 3 * C1), LOWTYPE),
        ((TAPS * ROWS12, mid + C1), LOWTYPE),
        ((ROWS12, C1), F32),
        ((time_rows, TEMB), LOWTYPE),
        ((max(32, time_rows), TEMB), F32),
    ]
    return pl.pallas_call(
        functools.partial(unet_body, group, steps, owners, peers),
        grid=(steps,),
        out_shape=[jax.ShapeDtypeStruct(shape, F32) for shape in out_shapes],
        in_specs=[image_spec()] * 3 + [whole(a.shape) for a in operands[3:]],
        out_specs=[whole(shape) for shape in out_shapes],
        scratch_shapes=[pltpu.VMEM(shape, kind) for shape, kind in scratch],
        compiler_params=pltpu.CompilerParams(vmem_limit_bytes=VMEM_BYTES),
    )(*operands)


TASKS = ((1, 0), (0, 0), (0, 1), (2, 0), (1, 1), (2, 1), (3, 0), (3, 1))
MESH = pl.DeviceIdType.MESH
SMALL_LANES = 9 * (CHANNELS_MID + C1)


def ns_chain(gram, eye):
    product = None
    for step in range(NS_STEPS):
        square = dot_nn(gram, gram, EXACT_PRECISION)
        factor = NS_A * eye + NS_B * gram + NS_C * square
        product = factor if product is None else dot_nn(product, factor, EXACT_PRECISION)
        if step < NS_STEPS - 1:
            gram = dot_nn(factor, dot_nn(gram, factor, EXACT_PRECISION), EXACT_PRECISION)
    return product


def identity(size):
    rows = lax.broadcasted_iota(jnp.int32, (size, size), 0)
    cols = lax.broadcasted_iota(jnp.int32, (size, size), 1)
    return (rows == cols).astype(F32)


def task_pieces(owners, peers):
    chunk, _ = chunk_rows(owners, peers)
    pieces = []
    packed = 0
    for seg, seg_rows in enumerate(segment_rows()):
        share = seg_rows // owners
        done, number = 0, 0
        while done < share:
            row = packed + done
            size = min(share - done, chunk - row % chunk)
            pieces.append((seg, number, row // chunk, row % chunk, size, done))
            done += size
            number += 1
        packed += share
    return pieces


def task_peers(seg, peers):
    chip, core = TASKS[seg]
    return [(base + chip) * 2 + core for base in range(0, peers // 2, 4)]


def muon_body(
    owners,
    peers,
    rows_ref,
    misc_ref,
    weight_hbm,
    moment_hbm,
    stem_ref,
    stemm_ref,
    head_ref,
    headm_ref,
    vec_ref,
    first_ref,
    second_ref,
    new_ref,
    newm_ref,
    nstem_ref,
    nstemm_ref,
    nhead_ref,
    nheadm_ref,
    nvec_ref,
    nfirst_ref,
    nsecond_ref,
    sums_ref,
    recv1,
    own2,
    send2,
    recv2,
    send3,
    recv3,
    recvs3,
    gathered,
    gathered_small,
    misc1,
    misc2,
    misc3,
    mine_g,
    mine_u,
    gram_part,
    gram_recv,
    gram_all,
    small,
    x_zero,
    x_one,
    flat,
    head_row,
    own_half,
    weight_ref,
    moment_ref,
    sem_load,
    sem1,
    sem2,
    sem3,
    sems3,
    sema,
    semb,
    semg,
    semh,
    semx,
    semy,
    semm1,
    semm2,
    semm3,
    semas,
    sembs,
    semp,
):
    mid = CHANNELS_MID
    chips = peers // 2
    chunk, small_chunk = chunk_rows(owners, peers)
    block = block_rows(owners, peers)
    own_rows = weight_ref.shape[0]
    z = lax.axis_index("bucket")
    peer = lax.axis_index("batch")
    chip, core = peer // 2, peer % 2
    partner = {"batch": chip * 2 + 1 - core}
    started = []
    half_rows = pl.ds(pl.multiple_of(core * chips * block, 16), chips * block)
    load_half = pltpu.make_async_copy(rows_ref.at[half_rows, :], own_half, sem_load.at[0])
    load_moment = pltpu.make_async_copy(moment_hbm, moment_ref, sem_load.at[1])
    load_weight = pltpu.make_async_copy(weight_hbm, weight_ref, sem_load.at[2])
    for load in (load_half, load_moment, load_weight):
        load.start()

    def same_core(k):
        return {"batch": lax.rem(chip + k, chips) * 2 + core}

    def along(k):
        return {"bucket": lax.rem(z + k, owners)}

    def send(source, target, sems, slot, device, begin=True):
        copy = pltpu.make_async_remote_copy(
            src_ref=source,
            dst_ref=target,
            send_sem=sems.at[0, slot],
            recv_sem=sems.at[1, slot],
            device_id=device,
            device_id_type=MESH,
        )
        copy.start()
        if begin:
            started.append(copy)
        return copy

    barrier = pltpu.get_barrier_semaphore()
    friends = [{"batch": lax.rem(peer + k, peers)} for k in range(1, peers)]
    friends += [along(k) for k in range(1, owners)]
    for friend in friends:
        pl.semaphore_signal(barrier, inc=1, device_id=friend, device_id_type=MESH)
    pl.semaphore_wait(barrier, len(friends))

    parts = [None] + list(range(1, owners)) + [0]

    def part_rows(part, base=0):
        if part is None:
            return pl.ds(pl.multiple_of(base + owners * chunk, 16), small_chunk)
        start = base + lax.rem(z + part, owners) * chunk
        return pl.ds(pl.multiple_of(start, 16), chunk)

    def base_of(k):
        return lax.rem(chip + k, chips) * block

    other_half = (1 - core) * chips * block

    misc_copy = send(misc_ref, misc1, semm1, 0, partner)
    order = list(range(1, chips)) + [0]
    first = {}
    for number, part in enumerate(parts):
        for k in order:
            first[part, k] = send(
                rows_ref.at[part_rows(part, other_half + base_of(k)), :],
                recv1.at[k, part_rows(part), :],
                sem1,
                number * chips + k,
                partner,
            )

    misc_copy.wait_recv()
    misc2[chip] = misc_ref[...] + misc1[...]
    misc_copies = [
        send(misc2.at[chip], misc2.at[chip], semm2, k - 1, same_core(k)) for k in range(1, chips)
    ]
    load_half.wait()
    second = {}
    for number, part in enumerate(parts):
        rows = part_rows(part)
        for k in order:
            first[part, k].wait_recv()
            total = own_half[part_rows(part, base_of(k)), :] + recv1[k, rows, :]
            if k == 0:
                own2[rows, :] = total
            else:
                send2[k - 1, rows, :] = total
                second[part, k] = send(
                    send2.at[k - 1, rows, :],
                    recv2.at[k - 1, rows, :],
                    sem2,
                    number * (chips - 1) + k - 1,
                    same_core(k),
                )

    for copy in misc_copies:
        copy.wait_recv()
    misc3[z] = sum([misc2[k] for k in range(1, chips)], misc2[0])
    misc_copies = [
        send(misc3.at[z], misc3.at[z], semm3, k - 1, along(k)) for k in range(1, owners)
    ]
    third = []
    for part in parts:
        for k in range(1, chips):
            second[part, k].wait_recv()
        rows = part_rows(part)
        total = own2[rows, :]
        for other in range(chips - 1):
            total = total + recv2[other, rows, :]
        if part is None:
            recvs3[z] = total
            third += [
                send(recvs3.at[z], recvs3.at[z], sems3, k - 1, along(k)) for k in range(1, owners)
            ]
        elif part == 0:
            own2[rows, :] = total
        else:
            send3[part - 1] = total
            third.append(
                send(send3.at[part - 1], recv3.at[part - 1], sem3, part - 1, along(part))
            )
    for copy in third:
        copy.wait_recv()
    total = own2[pl.ds(pl.multiple_of(z * chunk, 16), chunk), :]
    for other in range(owners - 1):
        total = total + recv3[other]
    slot = core * chips + chip
    gathered[slot] = total
    total = recvs3[0]
    for other in range(1, owners):
        total = total + recvs3[other]
    gathered_small[slot] = total

    pieces = task_pieces(owners, peers)

    def piece_copy(piece, index, target):
        seg, number, source, row, size, place = piece
        return pltpu.make_async_remote_copy(
            src_ref=gathered.at[slot_of(source, peers), pl.ds(row, size), :],
            dst_ref=mine_g.at[pl.ds(place, size), :],
            send_sem=semp.at[0, index],
            recv_sem=semp.at[1, number],
            device_id={"batch": target},
            device_id_type=MESH,
        )

    def from_peer(source):
        copies = []
        for piece in pieces:
            if piece[2] == source:
                for target in task_peers(piece[0], peers):
                    if target != source:
                        copies.append(piece_copy(piece, len(copies), target))
        return copies

    for source in range(peers):

        @pl.when(peer == source)
        def _(source=source):
            for copy in from_peer(source):
                copy.start()

    for copy in misc_copies:
        copy.wait_recv()
    misc = sum([misc3[k] for k in range(1, owners)], misc3[0])
    weight_sum = jnp.sum(misc[14:15, :mid], axis=1, keepdims=True)
    inverse = 1.0 / weight_sum
    loss_sum = jnp.sum(misc[13:14, :mid], axis=1, keepdims=True)
    sums_ref[0:1, :] = loss_sum + jnp.zeros((1, C1), F32)
    sums_ref[1:2, :] = weight_sum + jnp.zeros((1, C1), F32)
    head_bias = jnp.sum(misc[:, mid:].T, axis=0, keepdims=True)
    for row in range(3):
        flat[pl.ds(row * C1, C1)] = misc[row : row + 1, :C1].reshape(C1)
    for row in range(3, 13):
        flat[pl.ds(3 * C1 + (row - 3) * mid, mid)] = misc[row : row + 1, :mid].reshape(mid)
    head_row[...] = jnp.zeros_like(head_row)
    head_row[0:1, :ROWS12] = head_bias
    flat[pl.ds(3 * C1 + 10 * mid, C1)] = head_row[0:1, :].reshape(C1)
    grad = flat[pl.ds(0, vec_ref.shape[0])] * inverse.reshape(1)
    firsts = BETA_ONE * first_ref[...] + (1.0 - BETA_ONE) * grad
    seconds = BETA_TWO * second_ref[...] + (1.0 - BETA_TWO) * grad * grad
    nfirst_ref[...] = firsts
    nsecond_ref[...] = seconds
    change = (
        firsts
        / (1.0 - BETA_ONE**STEP)
        / (jnp.sqrt(seconds / (1.0 - BETA_TWO**STEP)) + ADAM_EPS)
    )
    nvec_ref[...] = vec_ref[...] - LR_ADAM * change

    load_moment.wait()
    for target in range(peers):

        @pl.when(peer == target)
        def _(target=target):
            for piece in pieces:
                seg, number, source, row, size, place = piece
                if target in task_peers(seg, peers):
                    if source == target:
                        mine_g[place : place + size, :] = gathered[
                            slot_of(source, peers), row : row + size, :
                        ]
                    else:
                        piece_copy(piece, 0, target).wait_recv()

    shares = [rows // owners for rows in segment_rows()]
    starts = [sum(shares[:k]) for k in range(len(shares))]
    for (task_chip, task_core), share, start in zip(TASKS, shares, starts):

        @pl.when((lax.rem(chip, 4) == task_chip) & (core == task_core))
        def _(share=share, start=start):
            grad = mine_g[:share, :] * inverse
            moment = MOMENTUM * moment_ref[start : start + share, :] + grad
            mine_u[:share, :] = grad + MOMENTUM * moment
            if share < mine_u.shape[0]:
                mine_u[share:, :] = jnp.zeros((mine_u.shape[0] - share, mid), F32)

    mine = mine_u[...]
    gram = lax.dot_general(
        mine,
        mine,
        (((0,), (0,)), ((), ())),
        preferred_element_type=F32,
        precision=EXACT_PRECISION,
    )
    gram_part[:C1, :] = gram[:C1, :]
    gram_part[C1:, :C1] = gram[C1 : C1 + 64, C1:]
    gram_part[C1:, C1:] = gram[C1 + 64 :, C1:]
    part = gram_part.shape[0] // owners
    copies = []
    for k in range(1, owners):
        start = pl.multiple_of(lax.rem(z + k, owners) * part, 8)
        copies.append(send(gram_part.at[pl.ds(start, part), :], gram_recv.at[z], semg, k - 1, along(k)))
    own_part = pl.ds(pl.multiple_of(z * part, 8), part)
    gram_recv[z] = gram_part[own_part, :]

    here = gathered.at[slot]
    plane = [send(here, here, sema, k - 1, same_core(k)) for k in range(1, chips)]
    cross = [send(here, here, semb, 0, partner)]
    here = gathered_small.at[slot]
    plane_small = [send(here, here, semas, k - 1, same_core(k)) for k in range(1, chips)]
    cross_small = [send(here, here, sembs, 0, partner)]

    for copy in copies:
        copy.wait_recv()
    gram_all[own_part, :] = sum([gram_recv[k] for k in range(1, owners)], gram_recv[0])
    copies = [
        send(gram_all.at[own_part, :], gram_all.at[own_part, :], semh, k - 1, along(k))
        for k in range(1, owners)
    ]
    for copy in copies:
        copy.wait_recv()
    upper, corner = gram_all[:C1, :], gram_all[C1:, :]
    gram = jnp.concatenate(
        [
            upper,
            jnp.concatenate(
                [upper[:, C1:].T, jnp.concatenate([corner[:, :C1], corner[:, C1:]], axis=0)],
                axis=1,
            ),
        ],
        axis=0,
    )
    eye = identity(mid)
    trace = jnp.sum(jnp.sum(gram * eye, axis=1, keepdims=True), axis=0, keepdims=True)
    scale = lax.rsqrt(trace + NORM_EPS)
    product = ns_chain(gram * (scale * scale), eye) * scale
    for k, copy in zip(range(1, chips), plane):
        copy.wait_recv()
        other = gathered.at[core * chips + lax.rem(chip + chips - k, chips)]
        cross.append(send(other, other, semb, k, partner))
    for k, copy in zip(range(1, chips), plane_small):
        copy.wait_recv()
        other = gathered_small.at[core * chips + lax.rem(chip + chips - k, chips)]
        cross_small.append(send(other, other, sembs, k, partner))
    turned = dot_nn(mine_u[...], product, EXACT_PRECISION)

    place = lax.rem(chip, 4)
    base = chip - place

    def in_group(k):
        return {"batch": (base + lax.rem(place + k, 4)) * 2 + core}

    buffers = (x_zero, x_one)

    def step_copy(buffer, index, sems, slot, device):
        there = buffer.at[index]
        return pltpu.make_async_remote_copy(
            src_ref=there,
            dst_ref=there,
            send_sem=sems.at[0, slot],
            recv_sem=sems.at[1, slot],
            device_id=device,
            device_id_type=MESH,
        )

    def step_copies(buffer):
        copies = [step_copy(buffer, place, semx, k - 1, in_group(k)) for k in range(1, 4)]
        return copies, step_copy(buffer, place, semy, 0, partner)

    for task_core, buffer in enumerate(buffers):

        @pl.when(core == task_core)
        def _(buffer=buffer):
            buffer[place] = turned[: buffer.shape[1]].astype(LOWTYPE)
            copies, own = step_copies(buffer)
            for copy in copies:
                copy.start()
            own.start()

    for copy in cross:
        copy.wait_recv()
    for owner_peer in range(peers):
        start = owner_peer * chunk
        size = min(chunk, own_rows - start)
        if size > 0:
            grad = gathered[slot_of(owner_peer, peers), :size, :] * inverse
            rows = slice(start, start + size)
            newm_ref[rows, :] = MOMENTUM * moment_ref[rows, :] + grad
    for copy in cross_small:
        copy.wait_recv()
    tiles = []
    for row in range(0, SMALL_ROWS, 16):
        at = row % small_chunk
        tile = gathered_small[slot_of(row // small_chunk, peers), at : at + 16, :]
        tiles.append(tile * inverse)
    small[...] = jnp.zeros_like(small)
    for tap in range(TAPS):
        lanes = slice(tap * (mid + C1), tap * (mid + C1) + mid)
        small[:16, lanes] = tiles[tap]
        lanes = slice(tap * (mid + C1) + mid, (tap + 1) * (mid + C1))
        if tap < 5:
            small[:16, lanes] = tiles[9 + tap][:, :C1]
        else:
            small[:16, lanes] = tiles[9 + tap - 5][:, C1:]
    small[32:48, SMALL_LANES:] = tiles[14][:, :C1]
    small[48:, SMALL_LANES:] = tiles[14][:, C1:]
    head_part = (slice(0, 12), slice(0, SMALL_LANES))
    stem_part = (slice(32, 59), slice(SMALL_LANES, SMALL_LANES + C1))
    for part, old_ref, fresh_ref in (
        (head_part, headm_ref, nheadm_ref),
        (stem_part, stemm_ref, nstemm_ref),
    ):
        grad = small[part]
        moment = MOMENTUM * old_ref[...] + grad
        fresh_ref[...] = moment
        turn = grad + MOMENTUM * moment
        small[part] = turn * lax.rsqrt(
            jnp.sum(jnp.sum(turn * turn, axis=1, keepdims=True), axis=0, keepdims=True) + NORM_EPS
        )
    gram = lax.dot_general(
        small[...],
        small[...],
        (((1,), (1,)), ((), ())),
        preferred_element_type=F32,
        precision=EXACT_PRECISION,
    )
    product = ns_chain(gram, identity(64))
    small[...] = dot_nn(product, small[...], EXACT_PRECISION)
    keep = 1.0 - LR_MUON * DECAY
    nhead_ref[...] = head_ref[...] * keep - LR_MUON * small[head_part]
    nstem_ref[...] = stem_ref[...] * keep - LR_MUON * small[stem_part]


    for task_core, buffer in enumerate(buffers):

        @pl.when(core == task_core)
        def _(buffer=buffer, other_buffer=buffers[1 - task_core]):
            copies, own = step_copies(buffer)
            forwards = [own]
            for k in range(1, 4):
                copies[k - 1].wait_recv()
                forwards.append(
                    step_copy(buffer, lax.rem(place + 4 - k, 4), semy, k, partner)
                )
                forwards[-1].start()
            for k in range(4):
                step_copy(other_buffer, lax.rem(place + 4 - k, 4), semy, k, partner).wait_recv()
            for copy in copies + forwards:
                copy.wait_send()

    load_weight.wait()
    for (task_chip, task_core), share, start in zip(TASKS, shares, starts):
        buffer = (x_zero, x_one)[task_core]
        rows = slice(start, start + share)
        fresh = weight_ref[rows, :] * keep - LR_MUON * buffer[task_chip, :share, :].astype(F32)
        new_ref[rows, :] = fresh
    for copy in started:
        copy.wait_send()
    for source in range(peers):

        @pl.when(peer == source)
        def _(source=source):
            for copy in from_peer(source):
                copy.wait_send()


def muon_call(owners, peers, operands):
    mid = CHANNELS_MID
    chips = peers // 2
    chunk, small_chunk = chunk_rows(owners, peers)
    block = block_rows(owners, peers)
    rows = operands[2].shape[0]
    part = 192 // owners
    pieces = task_pieces(owners, peers)
    shares = [seg_rows // owners for seg_rows in segment_rows()]
    most = [max(s for s, t in zip(shares, TASKS) if t[1] == core) for core in (0, 1)]
    out_shapes = [
        ((rows, mid), F32),
        ((rows, mid), F32),
        (operands[4].shape, F32),
        (operands[4].shape, F32),
        (operands[6].shape, F32),
        (operands[6].shape, F32),
        (operands[8].shape, F32),
        (operands[8].shape, F32),
        (operands[8].shape, F32),
        ((8, C1), F32),
    ]
    scratch = [
        ((chips, block, mid), F32),
        ((block, mid), F32),
        ((chips - 1, block, mid), F32),
        ((chips - 1, block, mid), F32),
        ((owners - 1, chunk, mid), F32),
        ((owners - 1, chunk, mid), F32),
        ((owners, small_chunk, mid), F32),
        ((peers, chunk, mid), F32),
        ((peers, small_chunk, mid), F32),
        (operands[1].shape, F32),
        ((chips,) + operands[1].shape, F32),
        ((owners,) + operands[1].shape, F32),
        ((max(most), mid), F32),
        ((max(most), mid), F32),
        ((192, mid), F32),
        ((owners, part, mid), F32),
        ((192, mid), F32),
        ((64, SMALL_LANES + C1), F32),
        ((4, most[0], mid), LOWTYPE),
        ((4, most[1], mid), LOWTYPE),
        ((3 * C1 + 10 * mid + C1,), F32),
        ((8, C1), F32),
        ((chips * block, mid), F32),
        ((rows, mid), F32),
        ((rows, mid), F32),
    ]
    sems = [
        (owners + 1) * chips,
        (owners + 1) * (chips - 1),
        owners - 1,
        owners - 1,
        chips - 1,
        chips,
        owners - 1,
        owners - 1,
        3,
        4,
        1,
        chips - 1,
        owners - 1,
        chips - 1,
        chips,
        len(pieces) * (peers // 8),
    ]
    hbm = pl.BlockSpec(memory_space=pl.ANY)
    vmem = pl.BlockSpec(memory_space=pltpu.VMEM)
    return pl.pallas_call(
        functools.partial(muon_body, owners, peers),
        out_shape=[jax.ShapeDtypeStruct(shape, kind) for shape, kind in out_shapes],
        in_specs=[hbm, vmem, hbm, hbm] + [vmem] * (len(operands) - 4),
        out_specs=[vmem] * len(out_shapes),
        scratch_shapes=[pltpu.VMEM(shape, kind) for shape, kind in scratch]
        + [pltpu.SemaphoreType.DMA((3,))]
        + [pltpu.SemaphoreType.DMA((2, count)) for count in sems],
        compiler_params=pltpu.CompilerParams(
            vmem_limit_bytes=VMEM_BYTES, collective_id=0, has_side_effects=True
        ),
    )(*operands)


def open_body(
    owners,
    peers,
    weight_ref,
    images_ref,
    noise_ref,
    mask_ref,
    image_ref,
    conv1_ref,
    conv1b_ref,
    conv2_ref,
    conv2b_ref,
    skip_ref,
    temb_ref,
    qkv_ref,
    outw_ref,
    noisy_ref,
    planes_ref,
    maskw_ref,
    held,
    left,
    sema,
    semb,
    semc,
):
    mid = CHANNELS_MID
    chips = peers // 2
    chunk, _ = chunk_rows(owners, peers)
    own_rows = weight_ref.shape[0]
    z = lax.axis_index("bucket")
    peer = lax.axis_index("batch")
    chip, core = peer // 2, peer % 2
    partner = {"batch": chip * 2 + 1 - core}
    slot = core * chips + chip
    started = []

    def same_core(k):
        return {"batch": lax.rem(chip + k, chips) * 2 + core}

    def along(k):
        return {"bucket": lax.rem(z + k, owners)}

    def send(source, target, sems, index, device):
        copy = pltpu.make_async_remote_copy(
            src_ref=source,
            dst_ref=target,
            send_sem=sems.at[0, index],
            recv_sem=sems.at[1, index],
            device_id=device,
            device_id_type=MESH,
        )
        copy.start()
        started.append(copy)
        return copy

    barrier = pltpu.get_barrier_semaphore()
    friends = [partner] + [same_core(k) for k in range(1, chips)]
    friends += [along(k) for k in range(1, owners)]
    for friend in friends:
        pl.semaphore_signal(barrier, inc=1, device_id=friend, device_id_type=MESH)

    for other in range(peers):
        start = other * chunk
        size = min(chunk, own_rows - start)
        if size > 0:
            held[z, slot_of(other, peers), :size, :] = weight_ref[start : start + size, :].astype(
                LOWTYPE
            )
        if size < chunk:
            held[z, slot_of(other, peers), max(size, 0) :, :] = jnp.zeros(
                (chunk - max(size, 0), mid), LOWTYPE
            )
    pl.semaphore_wait(barrier, len(friends))

    here = held.at[z, slot]
    first = [send(here, here, sema, k - 1, along(k)) for k in range(1, owners)]

    samples = mask_ref.shape[0]
    row = lax.broadcasted_iota(jnp.int32, (samples, samples), 0)
    lane = lax.broadcasted_iota(jnp.int32, (samples, samples), 1)

    def column(k):
        return jnp.sum(jnp.where(row == lane, image_ref[k : k + 1, :], 0.0), axis=1, keepdims=True)

    keep, spread, weight = column(0), column(1), column(2)
    left[...] = jnp.zeros_like(left)
    for c in range(3):
        noise = noise_ref[c]
        noisy = keep * images_ref[c] + spread * noise
        left[c, :samples, :] = noisy.astype(LOWTYPE)
        one = noise.astype(LOWTYPE)
        rest = noise - one.astype(F32)
        two = rest.astype(LOWTYPE)
        left[3 + c, :samples, :] = one
        left[6 + c, :samples, :] = two
        left[9 + c, :samples, :] = (rest - two.astype(F32)).astype(LOWTYPE)
    left[12, :samples, :] = mask_ref[...].astype(F32).astype(LOWTYPE)
    for ref in (noisy_ref, planes_ref, maskw_ref):
        ref[:, 12:, :] = jnp.zeros((samples, ROWS12 - 12, PLACES), F32)

    def picture(quarter):
        pixel = lax.broadcasted_iota(jnp.int32, (S * S, PLACES), 0)
        lane = lax.broadcasted_iota(jnp.int32, (S * S, PLACES), 1)
        wanted = (
            (lane // SIDE * 2 + quarter // 2) * S + lane % SIDE * 2 + quarter % 2
        )
        pick = jnp.where(pixel == wanted, 1.0, 0.0).astype(LOWTYPE)
        rows = left.shape[1]
        moved = dot_nn(left[...].reshape(13 * rows, S * S), pick)
        maskw = moved[12 * rows : 12 * rows + samples] * weight
        for c in range(3):
            k = quarter * 3 + c
            noisy_ref[:, k, :] = moved[c * rows : c * rows + samples]
            planes_ref[:, k, :] = sum(
                [moved[(p + c) * rows : (p + c) * rows + samples] for p in (6, 9)],
                moved[(3 + c) * rows : (3 + c) * rows + samples],
            )
            maskw_ref[:, k, :] = maskw

    picture(0)
    second = []
    for k, copy in zip(range(1, owners), first):
        copy.wait_recv()
        there = held.at[lax.rem(z + owners - k, owners), slot]
        second.append(
            [
                send(there, there, semb, (k - 1) * (chips - 1) + j - 1, same_core(j))
                for j in range(1, chips)
            ]
        )
        if k < 4:
            picture(k)
    for k in range(owners, 4):
        picture(k)
    third = []
    for k, copies in zip(range(1, owners), second):
        for copy in copies:
            copy.wait_recv()
        mine = held.at[lax.rem(z + owners - k, owners), pl.ds(core * chips, chips)]
        third.append(send(mine, mine, semc, k - 1, partner))
    for copy in third:
        copy.wait_recv()

    def place(seg, row, values):
        size = values.shape[0]
        if seg < 2:
            whole, side = ((conv1_ref, conv1b_ref), (conv2_ref, conv2b_ref))[seg]
            whole[row : row + size, :] = values
            height = side.shape[0]
            done = 0
            while done < size:
                offset, inner = (row + done) // height, (row + done) % height
                part = min(size - done, height - inner)
                side[inner : inner + part, offset * mid : (offset + 1) * mid] = values[
                    done : done + part
                ]
                done += part
        elif seg in (4, 5, 6):
            qkv_ref[row : row + size, (seg - 4) * mid : (seg - 3) * mid] = values
        else:
            {2: skip_ref, 3: temb_ref, 7: outw_ref}[seg][row : row + size, :] = values

    for owner in range(owners):
        packed = 0
        for seg, seg_rows in enumerate(segment_rows()):
            share = seg_rows // owners
            done = 0
            while done < share:
                row = packed + done
                size = min(share - done, chunk - row % chunk)
                inner = row % chunk
                place(
                    seg,
                    owner * share + done,
                    held[owner, slot_of(row // chunk, peers), inner : inner + size, :],
                )
                done += size
            packed += share
    for copy in started:
        copy.wait_send()


def open_call(owners, peers, operands):
    mid = CHANNELS_MID
    chips = peers // 2
    chunk, _ = chunk_rows(owners, peers)
    samples = operands[3].shape[0]
    rows = -(-samples // 16) * 16
    out_shapes = [
        ((9 * C1, mid), LOWTYPE),
        ((3 * C1, 3 * mid), LOWTYPE),
        ((9 * mid, mid), LOWTYPE),
        ((3 * mid, 3 * mid), LOWTYPE),
        ((C1, mid), LOWTYPE),
        ((TEMB, mid), LOWTYPE),
        ((mid, 3 * mid), LOWTYPE),
        ((mid, mid), LOWTYPE),
        ((samples, ROWS12, PLACES), F32),
        ((samples, ROWS12, PLACES), F32),
        ((samples, ROWS12, PLACES), F32),
    ]
    vmem = pl.BlockSpec(memory_space=pltpu.VMEM)
    return pl.pallas_call(
        functools.partial(open_body, owners, peers),
        out_shape=[jax.ShapeDtypeStruct(shape, kind) for shape, kind in out_shapes],
        in_specs=[vmem] * len(operands),
        out_specs=[vmem] * len(out_shapes),
        scratch_shapes=[
            pltpu.VMEM((owners, peers, chunk, mid), LOWTYPE),
            pltpu.VMEM((13, rows, S * S), LOWTYPE),
            pltpu.SemaphoreType.DMA((2, owners - 1)),
            pltpu.SemaphoreType.DMA((2, (owners - 1) * (chips - 1))),
            pltpu.SemaphoreType.DMA((2, owners - 1)),
        ],
        compiler_params=pltpu.CompilerParams(
            vmem_limit_bytes=VMEM_BYTES, collective_id=1, has_side_effects=True
        ),
    )(*operands)


def close_body(*refs):
    values, outs = refs[:10], refs[10:]
    for source, target in zip(values[:9], outs[:9]):
        target[...] = source[...]
    for source, target in zip((values[0], values[2], values[4], values[6]), outs[9:13]):
        target[...] = source[...].astype(LOWTYPE)
    sums = values[9]
    outs[13][...] = sums[0:1, 0:1]
    outs[14][...] = sums[1:2, 0:1]


def close_call(values):
    shapes = [(v.shape, F32) for v in values[:9]]
    shapes += [(values[k].shape, LOWTYPE) for k in (0, 2, 4, 6)] + [((1, 1), F32)] * 2
    vmem = pl.BlockSpec(memory_space=pltpu.VMEM)
    return pl.pallas_call(
        close_body,
        out_shape=[jax.ShapeDtypeStruct(shape, kind) for shape, kind in shapes],
        in_specs=[vmem] * len(values),
        out_specs=[vmem] * len(shapes),
        compiler_params=pltpu.CompilerParams(vmem_limit_bytes=VMEM_BYTES),
    )(*values)


def stem_spread():
    counts = np.zeros((3, 2, 3))
    for block in range(3):
        for inner in range(2):
            for sub in range(2):
                tap = 2 * (block - 1) + inner - sub + 1
                if 0 <= tap <= 2:
                    counts[block, inner, tap] += 1
    full = np.zeros((3, 3, ROWS12, 3, 3, 3))
    both = (np.einsum("ayt,bxu->abyxtu", counts, counts) * 0.25).reshape(3, 3, 4, 3, 3)
    for c in range(3):
        full[:, :, c:12:3, :, :, c] = both
    return np.pad(full.reshape(TAPS * ROWS12, 27), ((0, 0), (0, 5))).astype(np.float32)


def same_group(chans):
    group = np.arange(chans) // (chans // GROUPS)
    same = (group[:, None] == group[None, :]) / (PLACES * (chans // GROUPS))
    return same.astype(LOWTYPE)


def shards(
    images,
    pixel_mask,
    timesteps,
    noise_field,
    matrices,
    matrix_moms,
    stem_weight,
    stem_moms,
    head_weight,
    head_moms,
    vectors,
    vector_firsts,
    vector_seconds,
):
    owners, peers = lax.axis_size("bucket"), lax.axis_size("batch")
    samples = images.shape[0]
    level, weight = plan(timesteps)
    per_image = jnp.stack([jnp.sqrt(level), jnp.sqrt(1.0 - level), weight], axis=0)
    conv1, conv1b, conv2, conv2b, skip, temb, qkv, outw, noisy, noise, mask_weight = open_call(
        owners,
        peers,
        [
            matrices,
            images.transpose(1, 0, 2),
            noise_field.transpose(1, 0, 2),
            pixel_mask,
            per_image,
        ],
    )
    head_turned = head_weight.T
    rows_out, misc = unet_call(
        samples,
        owners,
        peers,
        [
            noisy,
            noise,
            mask_weight,
            swish(embed(timesteps)),
            stem_weight,
            head_turned,
            conv1,
            conv1b,
            conv2,
            conv2b,
            skip,
            temb,
            qkv,
            outw,
            vectors,
            same_group(C1),
            same_group(CHANNELS_MID),
            stem_spread(),
        ],
    )
    values = muon_call(
        owners,
        peers,
        [
            rows_out,
            misc,
            matrices,
            matrix_moms,
            stem_weight,
            stem_moms,
            head_turned,
            head_moms.T,
            vectors,
            vector_firsts,
            vector_seconds,
        ],
    )
    (
        new_matrices,
        new_matrix_moms,
        new_stem,
        new_stem_moms,
        new_head,
        new_head_moms,
        new_vectors,
        new_firsts,
        new_seconds,
        matrix_copies,
        stem_copy,
        head_copy,
        vector_copy,
        loss_sum,
        weight_sum,
    ) = close_call(values)
    loss_sum, weight_sum = loss_sum.reshape(()), weight_sum.reshape(())
    new_head, new_head_moms, head_copy = new_head.T, new_head_moms.T, head_copy.T
    return (
        loss_sum,
        weight_sum,
        new_matrices,
        new_matrix_moms,
        matrix_copies,
        new_stem,
        new_stem_moms,
        stem_copy,
        new_head,
        new_head_moms,
        head_copy,
        new_vectors,
        new_firsts,
        new_seconds,
        vector_copy,
    )


def solution(mesh):
    return jax.shard_map(
        shards,
        mesh=mesh,
        in_specs=(
            P(("bucket", "batch"), None, None),
            P(("bucket", "batch"), None),
            P(("bucket", "batch")),
            P(("bucket", "batch"), None, None),
            P("bucket", None),
            P("bucket", None),
            P(),
            P(),
            P(),
            P(),
            P(),
            P(),
            P(),
        ),
        out_specs=(
            P(),
            P(),
            P("bucket", None),
            P("bucket", None),
            P("bucket", None),
            P(),
            P(),
            P(),
            P(),
            P(),
            P(),
            P(),
            P(),
            P(),
            P(),
        ),
        check_vma=False,
    )
```

```python
import functools
import math

import jax
import jax.numpy as jnp
import numpy as np
from jax import lax
from jax.experimental import pallas as pl
from jax.experimental.pallas import tpu as pltpu
from jax.sharding import PartitionSpec as P

C1 = 128
CHANNELS_MID = 256
TEMB = 512
GROUPS = 32
S = 32
TSTEPS = 1000
NS_STEPS = 5
STEP = 10


GN_EPS = 1e-05
NORM_EPS = 1e-12
MOMENTUM = 0.95
LR_MUON = 0.5
DECAY = 0.01
NS_A = 3.4445
NS_B = -4.775
NS_C = 2.0315
BETA_ONE = 0.9
BETA_TWO = 0.999
LR_ADAM = 0.5
ADAM_EPS = 1e-08
EXACT_PRECISION = lax.Precision.HIGHEST
LOWTYPE = jnp.bfloat16


def segment_rows():
    return [
        9 * C1,
        9 * CHANNELS_MID,
        C1,
        TEMB,
        CHANNELS_MID,
        CHANNELS_MID,
        CHANNELS_MID,
        CHANNELS_MID,
    ]


def plan(timesteps):
    frac_t = (timesteps.astype(jnp.float32) / TSTEPS + 0.008) / 1.008
    level = jnp.cos(frac_t * (math.pi / 2)) ** 2
    ratio = level / (1.0 - level)
    return (level, jnp.minimum(1.0, 5.0 / ratio))


def embed(timesteps):
    half_width = TEMB // 2
    freqs = jnp.exp(-math.log(10000.0) * jnp.arange(half_width, dtype=jnp.float32) / half_width)
    angles = timesteps.astype(jnp.float32)[:, None] * freqs[None, :]
    return jnp.concatenate([jnp.sin(angles), jnp.cos(angles)], axis=1)


def swish(values):
    return values * jax.nn.sigmoid(values)


F32 = jnp.float32
PLACES = 256
SIDE = 16
HALO = 288
TAPS = 9
ROWS12 = 16
CHUNK = 64
SMALL_ROWS = 240
VMEM_BYTES = 56 * 1024 * 1024
SEG_OFF = (0, 1152, 3456, 3584, 4096, 4352, 4608, 4864, 5120)


def dot_nn(a, b, precision=None):
    return lax.dot_general(
        a, b, (((1,), (0,)), ((), ())), preferred_element_type=F32, precision=precision
    )


def dot_nt(a, b):
    return lax.dot_general(a, b, (((1,), (1,)), ((), ())), preferred_element_type=F32)


def dot_tn(a, b):
    return lax.dot_general(a, b, (((0,), (0,)), ((), ())), preferred_element_type=F32)


def sigmoid(v):
    return 1.0 / (1.0 + jnp.exp(-v))


def fold8(v):
    rows, chans = v.shape
    return jnp.sum(v.reshape(rows // 8, 8, chans), axis=0)


def shift_lanes(x, di, dj):
    lane = lax.broadcasted_iota(jnp.int32, x.shape, 1)
    row, col = lane // SIDE + di, lane % SIDE + dj
    offset = (-(SIDE * di + dj)) % PLACES
    moved = x if offset == 0 else pltpu.roll(x, offset, 1)
    valid = (row >= 0) & (row < SIDE) & (col >= 0) & (col < SIDE)
    return jnp.where(valid, moved, 0.0)


def tap_offsets():
    return [(di, dj) for di in (-1, 0, 1) for dj in (-1, 0, 1)]


def unet_body(
    group,
    steps,
    owners,
    peers,
    noisy_ref,
    noise_ref,
    maskw_ref,
    time_ref,
    stem_ref,
    head_ref,
    conv1_ref,
    conv1b_ref,
    conv2_ref,
    conv2b_ref,
    skip_ref,
    temb_ref,
    qkv_ref,
    outw_ref,
    vec_ref,
    spread_ref,
    rows_ref,
    misc_ref,
    acc_ref,
    gstem_ref,
    ghead_ref,
    gvec_ref,
    ghb_ref,
    loss_ref,
    wsum_ref,
    x0,
    hid,
    res,
    outp,
    attn,
    a1,
    a2,
    normed,
    qkv,
    plow,
    attl,
    low0,
    joined,
    patch,
    pad1,
    pad2,
    shiftf,
    dyf,
    dout,
    dq3,
    dpool,
    tproj,
    gtime,
    dtap,
    datt,
    dscore,
    dpool_low,
    stemw_ref,
    headw_ref,
    headb_ref,
    time_low,
    wide_rows,
    same128_ref,
    same256_ref,
):
    step = pl.program_id(0)
    mid = CHANNELS_MID
    chunks = range(0, PLACES, CHUNK)
    images = range(group)

    @pl.when(step == 0)
    def _():
        acc_ref[...] = jnp.zeros_like(acc_ref)
        gstem_ref[...] = jnp.zeros_like(gstem_ref)
        ghead_ref[...] = jnp.zeros_like(ghead_ref)
        gvec_ref[...] = jnp.zeros_like(gvec_ref)
        ghb_ref[...] = jnp.zeros_like(ghb_ref)
        loss_ref[...] = jnp.zeros_like(loss_ref)
        wsum_ref[...] = jnp.zeros_like(wsum_ref)
        gtime[...] = jnp.zeros_like(gtime)
        for ref in (a1, a2, pad1, pad2):
            for g in images:
                ref[g, :SIDE, :] = jnp.zeros((SIDE, ref.shape[2]), ref.dtype)
                ref[g, HALO - SIDE :, :] = jnp.zeros((SIDE, ref.shape[2]), ref.dtype)
        shiftf[...] = jnp.zeros_like(shiftf)
        for ref in (same128_ref, same256_ref):
            width = ref.shape[0] // GROUPS
            row = lax.broadcasted_iota(jnp.int32, ref.shape, 0) // width
            lane = lax.broadcasted_iota(jnp.int32, ref.shape, 1) // width
            ref[...] = jnp.where(row == lane, 1.0 / (PLACES * width), 0.0).astype(LOWTYPE)
        wide_rows[...] = jnp.zeros_like(wide_rows)
        samples = time_ref.shape[0]
        wide_rows[:samples, :TEMB] = time_ref[:, :TEMB]
        time_low[...] = wide_rows[: time_low.shape[0], :TEMB].astype(LOWTYPE)
        tproj[...] = dot_nn(time_low[...], temb_ref[...])
        wide_rows[:27, :C1] = stem_ref[...].astype(LOWTYPE).astype(F32)
        spread_stem = dot_nn(spread_ref[:, :27], wide_rows[:27, :C1], EXACT_PRECISION)
        for piece in range(3):
            low = spread_stem.astype(LOWTYPE)
            stemw_ref[:, piece * C1 : (piece + 1) * C1] = low
            spread_stem = spread_stem - low.astype(F32)
        width = mid + C1
        wide_rows[:ROWS12, :width] = jnp.zeros((ROWS12, width), F32)
        for tap in range(TAPS):
            wide_rows[:12, :width] = head_ref[:, tap * width : (tap + 1) * width]
            headw_ref[tap * ROWS12 : (tap + 1) * ROWS12, :] = wide_rows[:ROWS12, :width].astype(
                LOWTYPE
            )
        row = lax.broadcasted_iota(jnp.int32, (ROWS12, 12), 0)
        lane = lax.broadcasted_iota(jnp.int32, (ROWS12, 12), 1)
        tail = vec_ref[pl.ds(3 * C1 + 10 * mid, 12)].reshape(1, 12)
        bias = jnp.where(row == lane, tail, 0.0)
        headb_ref[...] = jnp.sum(bias, axis=1, keepdims=True) + jnp.zeros((ROWS12, C1), F32)

    def vec(row, chans=mid):
        start = row * C1 if chans == C1 else 3 * C1 + (row - 3) * mid
        return vec_ref[pl.ds(start, chans)].reshape(1, chans)

    def add_vec(row, value):
        gvec_ref[row : row + 1, : value.shape[1]] += value

    def total(parts):
        return jnp.concatenate([jnp.sum(p, axis=0, keepdims=True) for p in parts], axis=0)

    def grouped(stats, chans):
        same = same128_ref if chans == C1 else same256_ref
        first = stats.astype(LOWTYPE).astype(F32)
        second = (stats - first).astype(LOWTYPE).astype(F32)
        third = stats - first - second
        sums = dot_nn(jnp.concatenate([first, second, third], axis=0).astype(LOWTYPE), same[...])
        return sums[:group] + sums[group : 2 * group] + sums[2 * group :]

    def gn_stats(ref, sums, chans):
        mean = grouped(sums, chans)
        parts = []
        for g in images:
            acc = jnp.zeros((8, chans), F32)
            for r in chunks:
                c = ref[g, r : r + CHUNK, :] - mean[g : g + 1]
                acc += fold8(c * c)
            parts.append(acc)
        return mean, lax.rsqrt(grouped(total(parts), chans) + GN_EPS)

    def edge(chans, left):
        col = lax.broadcasted_iota(jnp.int32, (CHUNK, chans), 0) % SIDE
        return (col > 0) if left else (col < SIDE - 1)

    def act_shift(ref, g, mean, rstd, gain, shift, dest, chans):
        for r in chunks:
            y = (ref[g, r : r + CHUNK, :] - mean[g : g + 1]) * rstd[g : g + 1] * gain + shift
            a = y * sigmoid(y)
            shiftf[g, 8 + r : 8 + r + CHUNK, :chans] = a
            dest[g, SIDE + r : SIDE + r + CHUNK, chans : 2 * chans] = a.astype(LOWTYPE)
        for r in chunks:
            before = shiftf[g, 7 + r : 7 + r + CHUNK, :chans]
            after = shiftf[g, 9 + r : 9 + r + CHUNK, :chans]
            rows = slice(SIDE + r, SIDE + r + CHUNK)
            dest[g, rows, :chans] = jnp.where(edge(chans, True), before, 0.0).astype(LOWTYPE)
            dest[g, rows, 2 * chans :] = jnp.where(edge(chans, False), after, 0.0).astype(LOWTYPE)

    def dy_cat(ref, g, order):
        return jnp.concatenate(
            [ref[g, SIDE * k : SIDE * k + PLACES, :] for k in order], axis=1
        )

    def stack(parts):
        return jnp.concatenate(parts, axis=0) if len(parts) > 1 else parts[0]

    def staged(stages, fillers=()):
        fillers = list(fillers)
        for stage in stages:
            for g in images:
                stage(g)
            if fillers:
                fillers.pop(0)()
        for filler in fillers:
            filler()

    def rows_of(g):
        return slice(g * PLACES, (g + 1) * PLACES)

    sums1 = [None] * group

    def stem_patch(g):
        noisy = noisy_ref[g]
        for tap, (di, dj) in enumerate(tap_offsets()):
            patch[g, tap * ROWS12 : (tap + 1) * ROWS12, :] = shift_lanes(noisy, di, dj).astype(
                LOWTYPE
            )

    def stem_pool(g):
        wide = dot_tn(patch[g], stemw_ref[...])
        acc = jnp.zeros((8, C1), F32)
        for r in chunks:
            w = wide[r : r + CHUNK]
            v = (w[:, :C1] + w[:, C1 : 2 * C1]) + w[:, 2 * C1 :] + vec(0, C1)
            x0[g, r : r + CHUNK, :] = v
            low0[g * PLACES + r : g * PLACES + r + CHUNK, :] = v.astype(LOWTYPE)
            acc += fold8(v)
        sums1[g] = acc

    staged([stem_patch, stem_pool])
    mean1, rstd1 = gn_stats(x0, total(sums1), C1)
    gain1, shift1 = vec(1, C1), vec(2, C1)

    sums2 = [None] * group

    def act_one(g):
        act_shift(x0, g, mean1, rstd1, gain1, shift1, a1, C1)

    def conv_one(g):
        wide = dot_nn(dy_cat(a1, g, (0, 1, 2)), conv1_ref[...])
        bias = vec(3) + vec(4) + tproj[pl.ds(step * group + g, 1), :]
        acc = jnp.zeros((8, mid), F32)
        for r in chunks:
            v = wide[r : r + CHUNK] + bias
            hid[g, r : r + CHUNK, :] = v
            acc += fold8(v)
        sums2[g] = acc

    staged([act_one, conv_one])
    mean2, rstd2 = gn_stats(hid, total(sums2), mid)
    gain2, shift2 = vec(5), vec(6)

    sums3 = [None] * group

    def act_two(g):
        act_shift(hid, g, mean2, rstd2, gain2, shift2, a2, mid)

    def conv_two(g):
        wide = dot_nn(dy_cat(a2, g, (0, 1, 2)), conv2_ref[...])
        wide = wide + dot_nn(low0[rows_of(g), :], skip_ref[...])
        acc = jnp.zeros((8, mid), F32)
        for r in chunks:
            v = wide[r : r + CHUNK] + vec(7)
            res[g, r : r + CHUNK, :] = v
            acc += fold8(v)
        sums3[g] = acc

    staged([act_two, conv_two])
    mean3, rstd3 = gn_stats(res, total(sums3), mid)
    gain3, shift3 = vec(8), vec(9)
    scale = mid ** (-0.5)
    ones3, twos3 = [None] * group, [None] * group

    def norm_three(g):
        for r in chunks:
            xh = (res[g, r : r + CHUNK, :] - mean3[g : g + 1]) * rstd3[g : g + 1]
            y = xh * gain3 + shift3
            normed[g * PLACES + r : g * PLACES + r + CHUNK, :] = y.astype(LOWTYPE)

    def project(g):
        rows = rows_of(g)
        wide = dot_nn(normed[rows, :], qkv_ref[...])
        qkv[rows, :mid] = (wide[:, :mid] + vec(10)).astype(LOWTYPE)
        qkv[rows, mid : 2 * mid] = wide[:, mid : 2 * mid].astype(LOWTYPE)
        qkv[rows, 2 * mid :] = (wide[:, 2 * mid :] + vec(11)).astype(LOWTYPE)

    def weigh(g):
        rows = rows_of(g)
        logits = dot_nt(qkv[rows, :mid], qkv[rows, mid : 2 * mid])
        for r in chunks:
            s = logits[r : r + CHUNK] * scale
            e = jnp.exp(s - jnp.max(s, axis=1, keepdims=True))
            p = e * (1.0 / jnp.sum(e, axis=1, keepdims=True))
            attn[g, r : r + CHUNK, :] = p
            plow[g, r : r + CHUNK, :] = p.astype(LOWTYPE)

    def attend(g):
        attl[rows_of(g), :] = dot_nn(plow[g], qkv[rows_of(g), 2 * mid :]).astype(LOWTYPE)

    def join(g):
        wide = dot_nn(attl[rows_of(g), :], outw_ref[...])
        for r in chunks:
            rows = slice(g * PLACES + r, g * PLACES + r + CHUNK)
            o = res[g, r : r + CHUNK, :] + wide[r : r + CHUNK] + vec(12)
            outp[g, r : r + CHUNK, :] = o
            joined[rows, :mid] = (o * sigmoid(o)).astype(LOWTYPE)
            x = x0[g, r : r + CHUNK, :]
            joined[rows, mid:] = (x * sigmoid(x)).astype(LOWTYPE)

    def head(g):
        taps = dot_nt(headw_ref[...], joined[rows_of(g), :])
        value = headb_ref[:, :1] + jnp.zeros((ROWS12, PLACES), F32)
        for tap, (di, dj) in enumerate(tap_offsets()):
            value = value + shift_lanes(taps[tap * ROWS12 : (tap + 1) * ROWS12, :], di, dj)
        error = value - noise_ref[g]
        masked = maskw_ref[g] * error
        loss_ref[...] += masked * error
        wsum_ref[...] += maskw_ref[g]
        grad = 2.0 * masked
        ghb_ref[...] += grad
        gradl = grad.astype(LOWTYPE).astype(F32)
        for tap, (di, dj) in enumerate(tap_offsets()):
            dtap[g, tap * ROWS12 : (tap + 1) * ROWS12, :] = shift_lanes(gradl, -di, -dj).astype(
                LOWTYPE
            )

    def head_back(g):
        wide = dot_tn(dtap[g], headw_ref[...])
        acc = jnp.zeros((8, mid), F32)
        for r in chunks:
            o = outp[g, r : r + CHUNK, :]
            s = sigmoid(o)
            d = wide[r : r + CHUNK, :mid] * (s * (1.0 + o * (1.0 - s)))
            outp[g, r : r + CHUNK, :] = d
            dout[g * PLACES + r : g * PLACES + r + CHUNK, :] = d.astype(LOWTYPE)
            acc += fold8(d)
            x = x0[g, r : r + CHUNK, :]
            s = sigmoid(x)
            dpool[g, r : r + CHUNK, :] = wide[r : r + CHUNK, mid:] * (s * (1.0 + x * (1.0 - s)))
        add_vec(12, jnp.sum(acc, axis=0, keepdims=True))

    def attend_back(g):
        datt[rows_of(g), :] = dot_nt(dout[rows_of(g), :], outw_ref[...]).astype(LOWTYPE)

    def weigh_back(g):
        rows = rows_of(g)
        gweights = dot_nt(datt[rows, :], qkv[rows, 2 * mid :])
        dval = dot_tn(plow[g], datt[rows, :])
        add_vec(11, jnp.sum(fold8(dval), axis=0, keepdims=True))
        dq3[rows, 2 * mid :] = dval.astype(LOWTYPE)
        for r in chunks:
            p = attn[g, r : r + CHUNK, :]
            gw = gweights[r : r + CHUNK]
            ds = p * (gw - jnp.sum(gw * p, axis=1, keepdims=True))
            dscore[g, r : r + CHUNK, :] = (ds * scale).astype(LOWTYPE)

    def query_back(g):
        rows = rows_of(g)
        dqry = dot_nn(dscore[g], qkv[rows, mid : 2 * mid])
        dkey = dot_tn(dscore[g], qkv[rows, :mid])
        add_vec(10, jnp.sum(fold8(dqry), axis=0, keepdims=True))
        dq3[rows, :mid] = dqry.astype(LOWTYPE)
        dq3[rows, mid : 2 * mid] = dkey.astype(LOWTYPE)

    def project_back(g):
        one, two = jnp.zeros((8, mid), F32), jnp.zeros((8, mid), F32)
        wide = dot_nt(dq3[rows_of(g), :], qkv_ref[...])
        for r in chunks:
            xh = (res[g, r : r + CHUNK, :] - mean3[g : g + 1]) * rstd3[g : g + 1]
            d = wide[r : r + CHUNK]
            res[g, r : r + CHUNK, :] = xh
            dyf[g, r : r + CHUNK, :] = d
            one += fold8(d)
            two += fold8(d * xh)
        ones3[g], twos3[g] = one, two

    staged(
        [
            norm_three,
            project,
            weigh,
            attend,
            join,
            head,
            head_back,
            attend_back,
            weigh_back,
            query_back,
            project_back,
        ]
    )

    ones, twos = total(ones3), total(twos3)
    add_vec(9, jnp.sum(ones, axis=0, keepdims=True))
    add_vec(8, jnp.sum(twos, axis=0, keepdims=True))

    def finish(ref, dest, rstd, gain, m1, m2, chans, extra, g, row):
        r1 = rstd[g : g + 1]
        acc = jnp.zeros((8, chans), F32)
        for r in chunks:
            d = dyf[g, r : r + CHUNK, :chans] * (gain * r1)
            d = d - m1[g : g + 1] * r1 - ref[g, r : r + CHUNK, :] * (m2[g : g + 1] * r1)
            if extra is not None:
                d = d + extra[g, r : r + CHUNK, :]
            acc += fold8(d)
            dest(g, r, d.astype(LOWTYPE))
        acc = jnp.sum(acc, axis=0, keepdims=True)
        add_vec(row, acc)
        return acc

    def to_pad(pad):
        def put(g, r, low):
            pad[g, SIDE + r : SIDE + r + CHUNK, :] = low

        return put

    def turned(parts):
        return stack(parts).T

    def pad_turned(pad):
        return turned([pad[g, SIDE : SIDE + PLACES, :] for g in images])

    def conv_back(pad, weights, g, chans, apply):
        wide = dot_nt(dy_cat(pad, g, (2, 1, 0)), weights)
        shiftf[g, 8 : 8 + PLACES, :chans] = wide[:, :chans]
        dyf[g, :, :chans] = wide[:, chans : 2 * chans]
        for r in chunks:
            after = shiftf[g, 9 + r : 9 + r + CHUNK, :chans]
            dyf[g, r : r + CHUNK, :chans] += jnp.where(edge(chans, False), after, 0.0)
        shiftf[g, 8 : 8 + PLACES, :chans] = wide[:, 2 * chans :]
        for r in chunks:
            before = shiftf[g, 7 + r : 7 + r + CHUNK, :chans]
            apply(r, dyf[g, r : r + CHUNK, :chans] + jnp.where(edge(chans, True), before, 0.0))

    def norm_back(pad, weights, ref, mean, rstd, gain, shift, chans, ones, twos, g):
        sums = [jnp.zeros((8, chans), F32), jnp.zeros((8, chans), F32)]

        def apply(r, da):
            xh = (ref[g, r : r + CHUNK, :] - mean[g : g + 1]) * rstd[g : g + 1]
            y = xh * gain + shift
            s = sigmoid(y)
            d = da * (s * (1.0 + y * (1.0 - s)))
            ref[g, r : r + CHUNK, :] = xh
            dyf[g, r : r + CHUNK, :chans] = d
            sums[0] += fold8(d)
            sums[1] += fold8(d * xh)

        conv_back(pad, weights[...], g, chans, apply)
        ones[g], twos[g] = sums

    def add_product(first, last, left, right):
        acc_ref[:, first:last] += dot_nn(left(), right())

    m1, m2 = grouped(ones * gain3, mid), grouped(twos * gain3, mid)
    ones2, twos2 = [None] * group, [None] * group

    def grad_out():
        add_product(SEG_OFF[7], SEG_OFF[8], lambda: dout[...].T, lambda: attl[...])

    def grad_project(k):
        add_product(
            SEG_OFF[4 + k],
            SEG_OFF[5 + k],
            lambda: dq3[:, k * mid : (k + 1) * mid].T,
            lambda: normed[...],
        )

    def grad_head():
        for g in images:
            ghead_ref[...] += dot_nn(dtap[g], joined[rows_of(g), :])

    staged(
        [
            lambda g: finish(res, to_pad(pad2), rstd3, gain3, m1, m2, mid, outp, g, 7),
            lambda g: norm_back(
                pad2, conv2b_ref, hid, mean2, rstd2, gain2, shift2, mid, ones2, twos2, g
            ),
        ],
        [grad_out, grad_head] + [functools.partial(grad_project, k) for k in range(3)],
    )
    ones, twos = total(ones2), total(twos2)
    add_vec(6, jnp.sum(ones, axis=0, keepdims=True))
    add_vec(5, jnp.sum(twos, axis=0, keepdims=True))

    n1, n2 = grouped(ones * gain2, mid), grouped(twos * gain2, mid)
    ones1, twos1 = [None] * group, [None] * group
    lowt2 = pad_turned(pad2)

    def finish_two(g):
        acc = finish(hid, to_pad(pad1), rstd2, gain2, n1, n2, mid, None, g, 3)
        add_vec(4, acc)
        gtime[pl.ds(step * group + g, 1), :] = acc

    def grad_conv(lowt, act, offset, k):
        width = act.shape[2]
        first = offset + k * width
        add_product(
            first,
            first + width,
            lambda: lowt,
            lambda: stack([act[g, SIDE * k : SIDE * k + PLACES, :] for g in images]),
        )

    def grad_skip():
        add_product(SEG_OFF[2], SEG_OFF[3], lambda: lowt2, lambda: low0[...])
        for g in images:
            dpool[g] += dot_nt(pad2[g, SIDE : SIDE + PLACES, :], skip_ref[...])

    staged(
        [
            finish_two,
            lambda g: norm_back(
                pad1, conv1b_ref, x0, mean1, rstd1, gain1, shift1, C1, ones1, twos1, g
            ),
        ],
        [functools.partial(grad_conv, lowt2, a2, SEG_OFF[1], k) for k in range(3)] + [grad_skip],
    )
    ones, twos = total(ones1), total(twos1)
    add_vec(2, jnp.sum(ones, axis=0, keepdims=True))
    add_vec(1, jnp.sum(twos, axis=0, keepdims=True))

    p1, p2 = grouped(ones * gain1, C1), grouped(twos * gain1, C1)
    lowt1 = pad_turned(pad1)

    def to_pool(g, r, low):
        dpool_low[g, r : r + CHUNK, :] = low

    def grad_stem(g):
        gstem_ref[...] += dot_nn(patch[g], dpool_low[g])

    staged(
        [lambda g: finish(x0, to_pool, rstd1, gain1, p1, p2, C1, dpool, g, 0), grad_stem],
        [functools.partial(grad_conv, lowt1, a1, SEG_OFF[0], k) for k in range(3)],
    )

    @pl.when(step == steps - 1)
    def _():
        acc_ref[:, SEG_OFF[3] : SEG_OFF[4]] = dot_tn(gtime[...].astype(LOWTYPE), time_low[...])
        if rows_ref.shape[0] > 5120 + SMALL_ROWS:
            rows_ref[...] = jnp.zeros_like(rows_ref)
        pieces = gradient_pieces(owners, peers)
        for block in range(0, 5120, C1):
            turned = acc_ref[:, block : block + C1].T
            for source, size, target in pieces:
                low, high = max(source, block), min(source + size, block + C1)
                if low < high:
                    start = target + low - source
                    rows_ref[start : start + high - low, :] = turned[low - block : high - block]
        stem = lax.dot_general(
            spread_ref[...],
            gstem_ref[...],
            (((0,), (0,)), ((), ())),
            preferred_element_type=F32,
            precision=EXACT_PRECISION,
        )
        head = ghead_ref[...]
        none = jnp.zeros((ROWS12, C1), F32)
        tiles = [head[k : k + 16, :mid] for k in range(0, 144, 16)]
        for k in range(0, 80, 16):
            other = head[80 + k : 96 + k, mid:] if k < 64 else none
            tiles.append(jnp.concatenate([head[k : k + 16, mid:], other], axis=1))
        tiles.append(jnp.concatenate([stem[:16], stem[16:]], axis=1))
        for tile, (start, _) in zip(tiles, small_tiles(owners, peers)):
            rows_ref[start : start + 16, :] = tile
        misc_ref[:, :mid] = gvec_ref[...]
        misc_ref[13:14, :mid] = jnp.sum(loss_ref[...], axis=0, keepdims=True)
        misc_ref[14:15, :mid] = jnp.sum(wsum_ref[...], axis=0, keepdims=True)
        misc_ref[:, mid:] = ghb_ref[:, :C1] + ghb_ref[:, C1:]


def chunk_rows(owners, peers):
    share = -(-5120 // (owners * peers))
    return -(-share // 16) * 16, -(-(-(-SMALL_ROWS // peers)) // 16) * 16


def block_rows(owners, peers):
    chunk, small = chunk_rows(owners, peers)
    return owners * chunk + small


def slot_of(peer, peers):
    return peer % 2 * (peers // 2) + peer // 2


def gradient_pieces(owners, peers):
    chunk, _ = chunk_rows(owners, peers)
    block = block_rows(owners, peers)
    pieces = []
    for owner in range(owners):
        packed = 0
        for seg, seg_rows in enumerate(segment_rows()):
            share = seg_rows // owners
            done = 0
            while done < share:
                row = packed + done
                size = min(share - done, chunk - row % chunk)
                target = slot_of(row // chunk, peers) * block + owner * chunk + row % chunk
                pieces.append((SEG_OFF[seg] + owner * share + done, size, target))
                done += size
            packed += share
    return pieces


def small_tiles(owners, peers):
    chunk, small = chunk_rows(owners, peers)
    tiles = []
    for row in range(0, SMALL_ROWS, 16):
        slot = slot_of(row // small, peers)
        tiles.append((slot * block_rows(owners, peers) + owners * chunk + row % small, slot))
    return tiles


def unet_call(samples, owners, peers, operands):
    group = max(k for k in (1, 2, 4) if samples % k == 0)
    steps = samples // group
    time_rows = -(-samples // 16) * 16
    mid = CHANNELS_MID
    places = group * PLACES

    def image_spec():
        return pl.BlockSpec((group, ROWS12, PLACES), lambda i: (i, 0, 0))

    def whole(shape):
        return pl.BlockSpec(shape, lambda i: (0,) * len(shape))

    out_shapes = [(peers * block_rows(owners, peers), mid), (ROWS12, mid + C1)]
    scratch = [
        ((mid, 5120), F32),
        ((TAPS * ROWS12, C1), F32),
        ((TAPS * ROWS12, mid + C1), F32),
        ((ROWS12, mid), F32),
        ((ROWS12, mid), F32),
        ((ROWS12, mid), F32),
        ((ROWS12, mid), F32),
        ((group, PLACES, C1), F32),
        ((group, PLACES, mid), F32),
        ((group, PLACES, mid), F32),
        ((group, PLACES, mid), F32),
        ((group, PLACES, mid), F32),
        ((group, HALO, 3 * C1), LOWTYPE),
        ((group, HALO, 3 * mid), LOWTYPE),
        ((places, mid), LOWTYPE),
        ((places, 3 * mid), LOWTYPE),
        ((group, PLACES, mid), LOWTYPE),
        ((places, mid), LOWTYPE),
        ((places, C1), LOWTYPE),
        ((places, mid + C1), LOWTYPE),
        ((group, TAPS * ROWS12, PLACES), LOWTYPE),
        ((group, HALO, mid), LOWTYPE),
        ((group, HALO, mid), LOWTYPE),
        ((group, PLACES + 16, mid), F32),
        ((group, PLACES, mid), F32),
        ((places, mid), LOWTYPE),
        ((places, 3 * mid), LOWTYPE),
        ((group, PLACES, C1), F32),
        ((time_rows, mid), F32),
        ((time_rows, mid), F32),
        ((group, TAPS * ROWS12, PLACES), LOWTYPE),
        ((places, mid), LOWTYPE),
        ((group, PLACES, mid), LOWTYPE),
        ((group, PLACES, C1), LOWTYPE),
        ((TAPS * ROWS12, 3 * C1), LOWTYPE),
        ((TAPS * ROWS12, mid + C1), LOWTYPE),
        ((ROWS12, C1), F32),
        ((time_rows, TEMB), LOWTYPE),
        ((max(32, time_rows), TEMB), F32),
        ((C1, C1), LOWTYPE),
        ((mid, mid), LOWTYPE),
    ]
    return pl.pallas_call(
        functools.partial(unet_body, group, steps, owners, peers),
        grid=(steps,),
        out_shape=[jax.ShapeDtypeStruct(shape, F32) for shape in out_shapes],
        in_specs=[image_spec()] * 3 + [whole(a.shape) for a in operands[3:]],
        out_specs=[whole(shape) for shape in out_shapes],
        scratch_shapes=[pltpu.VMEM(shape, kind) for shape, kind in scratch],
        compiler_params=pltpu.CompilerParams(vmem_limit_bytes=VMEM_BYTES),
    )(*operands)


TASKS = ((1, 0), (0, 0), (0, 1), (2, 0), (1, 1), (2, 1), (3, 0), (3, 1))
MESH = pl.DeviceIdType.MESH
LEAD = 2
SMALL_LANES = 9 * (CHANNELS_MID + C1)


def ns_chain(gram, eye):
    product = None
    for step in range(NS_STEPS):
        square = dot_nn(gram, gram, EXACT_PRECISION)
        factor = NS_A * eye + NS_B * gram + NS_C * square
        product = factor if product is None else dot_nn(product, factor, EXACT_PRECISION)
        if step < NS_STEPS - 1:
            gram = dot_nn(factor, dot_nn(gram, factor, EXACT_PRECISION), EXACT_PRECISION)
    return product


def identity(size):
    rows = lax.broadcasted_iota(jnp.int32, (size, size), 0)
    cols = lax.broadcasted_iota(jnp.int32, (size, size), 1)
    return (rows == cols).astype(F32)


def task_pieces(owners, peers):
    chunk, _ = chunk_rows(owners, peers)
    pieces = []
    packed = 0
    for seg, seg_rows in enumerate(segment_rows()):
        share = seg_rows // owners
        done, number = 0, 0
        while done < share:
            row = packed + done
            size = min(share - done, chunk - row % chunk)
            pieces.append((seg, number, row // chunk, row % chunk, size, done))
            done += size
            number += 1
        packed += share
    return pieces


def task_peers(seg, peers):
    chip, core = TASKS[seg]
    return [(base + chip) * 2 + core for base in range(0, peers // 2, 4)]


def muon_body(
    owners,
    peers,
    rows_ref,
    misc_ref,
    weight_hbm,
    moment_hbm,
    stem_ref,
    stemm_ref,
    head_ref,
    headm_ref,
    vec_ref,
    first_ref,
    second_ref,
    new_ref,
    newm_ref,
    nstem_ref,
    nstemm_ref,
    nhead_ref,
    nheadm_ref,
    nvec_ref,
    nfirst_ref,
    nsecond_ref,
    sums_ref,
    recv1,
    own2,
    passed,
    send2,
    recv2,
    send3,
    recv3,
    recvs3,
    gathered,
    gathered_small,
    misc1,
    misc2,
    misc3,
    mine_g,
    mine_u,
    gram_part,
    gram_recv,
    gram_all,
    small,
    x_zero,
    x_one,
    flat,
    head_row,
    own_half,
    weight_ref,
    moment_ref,
    sem_load,
    sem1,
    sem2,
    sem3,
    sems3,
    sema,
    semb,
    semg,
    semh,
    semx,
    semy,
    semm1,
    semm2,
    semm3,
    semas,
    sembs,
    semp,
):
    mid = CHANNELS_MID
    chips = peers // 2
    chunk, small_chunk = chunk_rows(owners, peers)
    block = block_rows(owners, peers)
    own_rows = weight_ref.shape[0]
    z = lax.axis_index("bucket")
    peer = lax.axis_index("batch")
    chip, core = peer // 2, peer % 2
    partner = {"batch": chip * 2 + 1 - core}
    started = []
    half_rows = pl.ds(pl.multiple_of(core * chips * block, 16), chips * block)
    load_half = pltpu.make_async_copy(rows_ref.at[half_rows, :], own_half, sem_load.at[0])
    load_moment = pltpu.make_async_copy(moment_hbm, moment_ref, sem_load.at[1])
    load_weight = pltpu.make_async_copy(weight_hbm, weight_ref, sem_load.at[2])
    for load in (load_half, load_moment, load_weight):
        load.start()

    def same_core(k):
        return {"batch": lax.rem(chip + k, chips) * 2 + core}

    def along(k):
        return {"bucket": lax.rem(z + k, owners)}

    def send(source, target, sems, slot, device, begin=True):
        copy = pltpu.make_async_remote_copy(
            src_ref=source,
            dst_ref=target,
            send_sem=sems.at[0, slot],
            recv_sem=sems.at[1, slot],
            device_id=device,
            device_id_type=MESH,
        )
        copy.start()
        if begin:
            started.append(copy)
        return copy

    barrier = pltpu.get_barrier_semaphore()
    friends = [{"batch": lax.rem(peer + k, peers)} for k in range(1, peers)]
    friends += [along(k) for k in range(1, owners)]
    for friend in friends:
        pl.semaphore_signal(barrier, inc=1, device_id=friend, device_id_type=MESH)
    pl.semaphore_wait(barrier, len(friends))

    parts = [None] + list(range(1, owners)) + [0]

    def part_rows(part, base=0, half=None):
        start = base + (owners * chunk if part is None else lax.rem(z + part, owners) * chunk)
        size = small_chunk if part is None else chunk
        if half is not None:
            size = size // 2
            start = start + half * size
        return pl.ds(pl.multiple_of(start, 8), size)

    square = chips == 4
    across_x = chip + 1 - 2 * lax.rem(chip, 2)
    across_y = lax.rem(chip + 2, 4)

    def near(k):
        if not square:
            return lax.rem(chip + k, chips)
        return (chip, across_x, across_y, lax.rem(across_x + 2, 4))[k]

    def at_chip(k):
        return {"batch": near(k) * 2 + core}

    def base_of(k):
        return near(k) * block

    other_half = (1 - core) * chips * block

    misc_copy = send(misc_ref, misc1, semm1, 0, partner)
    order = list(range(1, chips)) + [0]
    first = {}
    for number, part in enumerate(parts):
        for k in order:
            first[part, k] = send(
                rows_ref.at[part_rows(part, other_half + base_of(k)), :],
                recv1.at[k, part_rows(part), :],
                sem1,
                number * chips + k,
                partner,
            )

    misc_copy.wait_recv()
    misc2[chip] = misc_ref[...] + misc1[...]
    misc_copies = [
        send(misc2.at[chip], misc2.at[chip], semm2, k - 1, same_core(k)) for k in range(1, chips)
    ]
    load_half.wait()
    second = {}
    third = []

    def add_cores(number):
        part = parts[number]
        rows = part_rows(part)
        for k in order:
            first[part, k].wait_recv()
            total = own_half[part_rows(part, base_of(k)), :] + recv1[k, rows, :]
            if k == 0:
                own2[rows, :] = total
                continue
            send2[k - 1, rows, :] = total
            if not square:
                second[part, k] = send(
                    send2.at[k - 1, rows, :],
                    recv2.at[k - 1, rows, :],
                    sem2,
                    number * (chips - 1) + k - 1,
                    at_chip(k),
                )
        if square:
            for index, (half, source, into, target) in enumerate(
                ((0, 2, 1, 1), (1, 2, 1, 2), (0, 0, 0, 1), (1, 1, 0, 2))
            ):
                rows = part_rows(part, 0, half)
                second[part, index] = send(
                    send2.at[source, rows, :],
                    recv2.at[into, rows, :],
                    sem2,
                    number * 6 + index,
                    at_chip(target),
                )

    def pass_on(number):
        part = parts[number]
        for half, source, target in ((0, 1, 2), (1, 0, 1)):
            second[part, half].wait_recv()
            rows = part_rows(part, 0, half)
            passed[rows, :] = send2[source, rows, :] + recv2[1, rows, :]
            second[part, 4 + half] = send(
                passed.at[rows, :], recv2.at[2, rows, :], sem2, number * 6 + 4 + half, at_chip(target)
            )

    def add_chips(number):
        part = parts[number]
        for k in (2, 3, 4, 5) if square else range(1, chips):
            second[part, k].wait_recv()
        rows = part_rows(part)
        total = own2[rows, :]
        for other in (0, 2) if square else range(chips - 1):
            total = total + recv2[other, rows, :]
        if part is None:
            recvs3[z] = total
            third.extend(
                send(recvs3.at[z], recvs3.at[z], sems3, k - 1, along(k)) for k in range(1, owners)
            )
        elif part == 0:
            own2[rows, :] = total
        else:
            send3[part - 1] = total
            third.append(
                send(send3.at[part - 1], recv3.at[part - 1], sem3, part - 1, along(part))
            )

    lead = LEAD if square else len(parts)
    for turn in range(len(parts) + lead):
        if turn < len(parts):
            add_cores(turn)
        if square and 0 <= turn - 1 < len(parts):
            pass_on(turn - 1)
        if turn == min(2, len(parts)):
            for copy in misc_copies:
                copy.wait_recv()
            misc3[z] = sum([misc2[k] for k in range(1, chips)], misc2[0])
            misc_copies = [
                send(misc3.at[z], misc3.at[z], semm3, k - 1, along(k)) for k in range(1, owners)
            ]
        if 0 <= turn - lead < len(parts):
            add_chips(turn - lead)
    for copy in third:
        copy.wait_recv()
    total = own2[pl.ds(pl.multiple_of(z * chunk, 16), chunk), :]
    for other in range(owners - 1):
        total = total + recv3[other]
    slot = core * chips + chip
    gathered[slot] = total
    total = recvs3[0]
    for other in range(1, owners):
        total = total + recvs3[other]
    gathered_small[slot] = total

    pieces = task_pieces(owners, peers)

    def piece_copy(piece, index, target):
        seg, number, source, row, size, place = piece
        return pltpu.make_async_remote_copy(
            src_ref=gathered.at[slot_of(source, peers), pl.ds(row, size), :],
            dst_ref=mine_g.at[pl.ds(place, size), :],
            send_sem=semp.at[0, index],
            recv_sem=semp.at[1, number],
            device_id={"batch": target},
            device_id_type=MESH,
        )

    def from_peer(source):
        copies = []
        for piece in pieces:
            if piece[2] == source:
                for target in task_peers(piece[0], peers):
                    if target != source:
                        copies.append(piece_copy(piece, len(copies), target))
        return copies

    for source in range(peers):

        @pl.when(peer == source)
        def _(source=source):
            for copy in from_peer(source):
                copy.start()

    for copy in misc_copies:
        copy.wait_recv()
    misc = sum([misc3[k] for k in range(1, owners)], misc3[0])
    weight_sum = jnp.sum(misc[14:15, :mid], axis=1, keepdims=True)
    inverse = 1.0 / weight_sum
    loss_sum = jnp.sum(misc[13:14, :mid], axis=1, keepdims=True)
    sums_ref[0:1, :] = loss_sum + jnp.zeros((1, C1), F32)
    sums_ref[1:2, :] = weight_sum + jnp.zeros((1, C1), F32)
    head_bias = jnp.sum(misc[:, mid:].T, axis=0, keepdims=True)
    for row in range(3):
        flat[pl.ds(row * C1, C1)] = misc[row : row + 1, :C1].reshape(C1)
    for row in range(3, 13):
        flat[pl.ds(3 * C1 + (row - 3) * mid, mid)] = misc[row : row + 1, :mid].reshape(mid)
    head_row[...] = jnp.zeros_like(head_row)
    head_row[0:1, :ROWS12] = head_bias
    flat[pl.ds(3 * C1 + 10 * mid, C1)] = head_row[0:1, :].reshape(C1)
    grad = flat[pl.ds(0, vec_ref.shape[0])] * inverse.reshape(1)
    firsts = BETA_ONE * first_ref[...] + (1.0 - BETA_ONE) * grad
    seconds = BETA_TWO * second_ref[...] + (1.0 - BETA_TWO) * grad * grad
    nfirst_ref[...] = firsts
    nsecond_ref[...] = seconds
    change = (
        firsts
        / (1.0 - BETA_ONE**STEP)
        / (jnp.sqrt(seconds / (1.0 - BETA_TWO**STEP)) + ADAM_EPS)
    )
    nvec_ref[...] = vec_ref[...] - LR_ADAM * change

    load_moment.wait()
    for target in range(peers):

        @pl.when(peer == target)
        def _(target=target):
            for piece in pieces:
                seg, number, source, row, size, place = piece
                if target in task_peers(seg, peers):
                    if source == target:
                        mine_g[place : place + size, :] = gathered[
                            slot_of(source, peers), row : row + size, :
                        ]
                    else:
                        piece_copy(piece, 0, target).wait_recv()

    shares = [rows // owners for rows in segment_rows()]
    starts = [sum(shares[:k]) for k in range(len(shares))]
    for (task_chip, task_core), share, start in zip(TASKS, shares, starts):

        @pl.when((lax.rem(chip, 4) == task_chip) & (core == task_core))
        def _(share=share, start=start):
            grad = mine_g[:share, :] * inverse
            moment = MOMENTUM * moment_ref[start : start + share, :] + grad
            mine_u[:share, :] = grad + MOMENTUM * moment
            if share < mine_u.shape[0]:
                mine_u[share:, :] = jnp.zeros((mine_u.shape[0] - share, mid), F32)

    mine = mine_u[...]
    gram = lax.dot_general(
        mine,
        mine,
        (((0,), (0,)), ((), ())),
        preferred_element_type=F32,
        precision=EXACT_PRECISION,
    )
    gram_part[:C1, :] = gram[:C1, :]
    gram_part[C1:, :C1] = gram[C1 : C1 + 64, C1:]
    gram_part[C1:, C1:] = gram[C1 + 64 :, C1:]
    part = gram_part.shape[0] // owners
    copies = []
    for k in range(1, owners):
        start = pl.multiple_of(lax.rem(z + k, owners) * part, 8)
        copies.append(send(gram_part.at[pl.ds(start, part), :], gram_recv.at[z], semg, k - 1, along(k)))
    own_part = pl.ds(pl.multiple_of(z * part, 8), part)
    gram_recv[z] = gram_part[own_part, :]

    here = gathered.at[slot]
    plane = [send(here, here, sema, k - 1, same_core(k)) for k in range(1, chips)]
    cross = [send(here, here, semb, 0, partner)]
    here = gathered_small.at[slot]
    plane_small = [send(here, here, semas, k - 1, same_core(k)) for k in range(1, chips)]
    cross_small = [send(here, here, sembs, 0, partner)]

    for copy in copies:
        copy.wait_recv()
    gram_all[own_part, :] = sum([gram_recv[k] for k in range(1, owners)], gram_recv[0])
    copies = [
        send(gram_all.at[own_part, :], gram_all.at[own_part, :], semh, k - 1, along(k))
        for k in range(1, owners)
    ]
    for copy in copies:
        copy.wait_recv()
    upper, corner = gram_all[:C1, :], gram_all[C1:, :]
    gram = jnp.concatenate(
        [
            upper,
            jnp.concatenate(
                [upper[:, C1:].T, jnp.concatenate([corner[:, :C1], corner[:, C1:]], axis=0)],
                axis=1,
            ),
        ],
        axis=0,
    )
    eye = identity(mid)
    trace = jnp.sum(jnp.sum(gram * eye, axis=1, keepdims=True), axis=0, keepdims=True)
    scale = lax.rsqrt(trace + NORM_EPS)
    product = ns_chain(gram * (scale * scale), eye) * scale
    for k, copy in zip(range(1, chips), plane):
        copy.wait_recv()
        other = gathered.at[core * chips + lax.rem(chip + chips - k, chips)]
        cross.append(send(other, other, semb, k, partner))
    for k, copy in zip(range(1, chips), plane_small):
        copy.wait_recv()
        other = gathered_small.at[core * chips + lax.rem(chip + chips - k, chips)]
        cross_small.append(send(other, other, sembs, k, partner))
    turned = dot_nn(mine_u[...], product, EXACT_PRECISION)

    place = lax.rem(chip, 4)
    base = chip - place

    def in_group(k):
        return {"batch": (base + lax.rem(place + k, 4)) * 2 + core}

    buffers = (x_zero, x_one)

    def step_copy(buffer, index, sems, slot, device):
        there = buffer.at[index]
        return pltpu.make_async_remote_copy(
            src_ref=there,
            dst_ref=there,
            send_sem=sems.at[0, slot],
            recv_sem=sems.at[1, slot],
            device_id=device,
            device_id_type=MESH,
        )

    def step_copies(buffer):
        copies = [step_copy(buffer, place, semx, k - 1, in_group(k)) for k in range(1, 4)]
        return copies, step_copy(buffer, place, semy, 0, partner)

    for task_core, buffer in enumerate(buffers):

        @pl.when(core == task_core)
        def _(buffer=buffer):
            buffer[place] = turned[: buffer.shape[1]].astype(LOWTYPE)
            copies, own = step_copies(buffer)
            for copy in copies:
                copy.start()
            own.start()

    for copy in cross:
        copy.wait_recv()
    for owner_peer in range(peers):
        start = owner_peer * chunk
        size = min(chunk, own_rows - start)
        if size > 0:
            grad = gathered[slot_of(owner_peer, peers), :size, :] * inverse
            rows = slice(start, start + size)
            newm_ref[rows, :] = MOMENTUM * moment_ref[rows, :] + grad
    for copy in cross_small:
        copy.wait_recv()
    tiles = []
    for row in range(0, SMALL_ROWS, 16):
        at = row % small_chunk
        tile = gathered_small[slot_of(row // small_chunk, peers), at : at + 16, :]
        tiles.append(tile * inverse)
    small[...] = jnp.zeros_like(small)
    for tap in range(TAPS):
        lanes = slice(tap * (mid + C1), tap * (mid + C1) + mid)
        small[:16, lanes] = tiles[tap]
        lanes = slice(tap * (mid + C1) + mid, (tap + 1) * (mid + C1))
        if tap < 5:
            small[:16, lanes] = tiles[9 + tap][:, :C1]
        else:
            small[:16, lanes] = tiles[9 + tap - 5][:, C1:]
    small[32:48, SMALL_LANES:] = tiles[14][:, :C1]
    small[48:, SMALL_LANES:] = tiles[14][:, C1:]
    head_part = (slice(0, 12), slice(0, SMALL_LANES))
    stem_part = (slice(32, 59), slice(SMALL_LANES, SMALL_LANES + C1))
    for part, old_ref, fresh_ref in (
        (head_part, headm_ref, nheadm_ref),
        (stem_part, stemm_ref, nstemm_ref),
    ):
        grad = small[part]
        moment = MOMENTUM * old_ref[...] + grad
        fresh_ref[...] = moment
        turn = grad + MOMENTUM * moment
        small[part] = turn * lax.rsqrt(
            jnp.sum(jnp.sum(turn * turn, axis=1, keepdims=True), axis=0, keepdims=True) + NORM_EPS
        )
    gram = lax.dot_general(
        small[...],
        small[...],
        (((1,), (1,)), ((), ())),
        preferred_element_type=F32,
        precision=EXACT_PRECISION,
    )
    product = ns_chain(gram, identity(64))
    small[...] = dot_nn(product, small[...], EXACT_PRECISION)
    keep = 1.0 - LR_MUON * DECAY
    nhead_ref[...] = head_ref[...] * keep - LR_MUON * small[head_part]
    nstem_ref[...] = stem_ref[...] * keep - LR_MUON * small[stem_part]


    for task_core, buffer in enumerate(buffers):

        @pl.when(core == task_core)
        def _(buffer=buffer, other_buffer=buffers[1 - task_core]):
            copies, own = step_copies(buffer)
            forwards = [own]
            for k in range(1, 4):
                copies[k - 1].wait_recv()
                forwards.append(
                    step_copy(buffer, lax.rem(place + 4 - k, 4), semy, k, partner)
                )
                forwards[-1].start()
            for k in range(4):
                step_copy(other_buffer, lax.rem(place + 4 - k, 4), semy, k, partner).wait_recv()
            for copy in copies + forwards:
                copy.wait_send()

    load_weight.wait()
    for (task_chip, task_core), share, start in zip(TASKS, shares, starts):
        buffer = (x_zero, x_one)[task_core]
        rows = slice(start, start + share)
        fresh = weight_ref[rows, :] * keep - LR_MUON * buffer[task_chip, :share, :].astype(F32)
        new_ref[rows, :] = fresh
    for copy in started:
        copy.wait_send()
    for source in range(peers):

        @pl.when(peer == source)
        def _(source=source):
            for copy in from_peer(source):
                copy.wait_send()


def muon_call(owners, peers, operands):
    mid = CHANNELS_MID
    chips = peers // 2
    chunk, small_chunk = chunk_rows(owners, peers)
    block = block_rows(owners, peers)
    rows = operands[2].shape[0]
    part = 192 // owners
    pieces = task_pieces(owners, peers)
    shares = [seg_rows // owners for seg_rows in segment_rows()]
    most = [max(s for s, t in zip(shares, TASKS) if t[1] == core) for core in (0, 1)]
    out_shapes = [
        ((rows, mid), F32),
        ((rows, mid), F32),
        (operands[4].shape, F32),
        (operands[4].shape, F32),
        (operands[6].shape, F32),
        (operands[6].shape, F32),
        (operands[8].shape, F32),
        (operands[8].shape, F32),
        (operands[8].shape, F32),
        ((8, C1), F32),
    ]
    scratch = [
        ((chips, block, mid), F32),
        ((block, mid), F32),
        ((block, mid), F32),
        ((chips - 1, block, mid), F32),
        ((chips - 1, block, mid), F32),
        ((owners - 1, chunk, mid), F32),
        ((owners - 1, chunk, mid), F32),
        ((owners, small_chunk, mid), F32),
        ((peers, chunk, mid), F32),
        ((peers, small_chunk, mid), F32),
        (operands[1].shape, F32),
        ((chips,) + operands[1].shape, F32),
        ((owners,) + operands[1].shape, F32),
        ((max(most), mid), F32),
        ((max(most), mid), F32),
        ((192, mid), F32),
        ((owners, part, mid), F32),
        ((192, mid), F32),
        ((64, SMALL_LANES + C1), F32),
        ((4, most[0], mid), LOWTYPE),
        ((4, most[1], mid), LOWTYPE),
        ((3 * C1 + 10 * mid + C1,), F32),
        ((8, C1), F32),
        ((chips * block, mid), F32),
        ((rows, mid), F32),
        ((rows, mid), F32),
    ]
    sems = [
        (owners + 1) * chips,
        (owners + 1) * max(6, chips - 1),
        owners - 1,
        owners - 1,
        chips - 1,
        chips,
        owners - 1,
        owners - 1,
        3,
        4,
        1,
        chips - 1,
        owners - 1,
        chips - 1,
        chips,
        len(pieces) * (peers // 8),
    ]
    hbm = pl.BlockSpec(memory_space=pl.ANY)
    vmem = pl.BlockSpec(memory_space=pltpu.VMEM)
    return pl.pallas_call(
        functools.partial(muon_body, owners, peers),
        out_shape=[jax.ShapeDtypeStruct(shape, kind) for shape, kind in out_shapes],
        in_specs=[hbm, vmem, hbm, hbm] + [vmem] * (len(operands) - 4),
        out_specs=[vmem] * len(out_shapes),
        scratch_shapes=[pltpu.VMEM(shape, kind) for shape, kind in scratch]
        + [pltpu.SemaphoreType.DMA((3,))]
        + [pltpu.SemaphoreType.DMA((2, count)) for count in sems],
        compiler_params=pltpu.CompilerParams(
            vmem_limit_bytes=VMEM_BYTES, collective_id=0, has_side_effects=True
        ),
    )(*operands)


def open_body(
    owners,
    peers,
    weight_ref,
    images_ref,
    noise_ref,
    mask_ref,
    image_ref,
    conv1_ref,
    conv1b_ref,
    conv2_ref,
    conv2b_ref,
    skip_ref,
    temb_ref,
    qkv_ref,
    outw_ref,
    noisy_ref,
    planes_ref,
    maskw_ref,
    held,
    left,
    sema,
    semb,
    semc,
):
    mid = CHANNELS_MID
    chips = peers // 2
    chunk, _ = chunk_rows(owners, peers)
    own_rows = weight_ref.shape[0]
    z = lax.axis_index("bucket")
    peer = lax.axis_index("batch")
    chip, core = peer // 2, peer % 2
    partner = {"batch": chip * 2 + 1 - core}
    slot = core * chips + chip
    started = []

    def same_core(k):
        return {"batch": lax.rem(chip + k, chips) * 2 + core}

    def along(k):
        return {"bucket": lax.rem(z + k, owners)}

    def send(source, target, sems, index, device):
        copy = pltpu.make_async_remote_copy(
            src_ref=source,
            dst_ref=target,
            send_sem=sems.at[0, index],
            recv_sem=sems.at[1, index],
            device_id=device,
            device_id_type=MESH,
        )
        copy.start()
        started.append(copy)
        return copy

    barrier = pltpu.get_barrier_semaphore()
    friends = [partner] + [same_core(k) for k in range(1, chips)]
    friends += [along(k) for k in range(1, owners)]
    for friend in friends:
        pl.semaphore_signal(barrier, inc=1, device_id=friend, device_id_type=MESH)

    for other in range(peers):
        start = other * chunk
        size = min(chunk, own_rows - start)
        if size > 0:
            held[z, slot_of(other, peers), :size, :] = weight_ref[start : start + size, :].astype(
                LOWTYPE
            )
        if size < chunk:
            held[z, slot_of(other, peers), max(size, 0) :, :] = jnp.zeros(
                (chunk - max(size, 0), mid), LOWTYPE
            )
    pl.semaphore_wait(barrier, len(friends))

    here = held.at[z, slot]
    first = [send(here, here, sema, k - 1, along(k)) for k in range(1, owners)]

    samples = mask_ref.shape[0]
    keep = image_ref[:, TEMB : TEMB + 1]
    spread = image_ref[:, TEMB + 1 : TEMB + 2]
    weight = image_ref[:, TEMB + 2 : TEMB + 3]
    left[...] = jnp.zeros_like(left)
    for c in range(3):
        noise = noise_ref[c]
        noisy = keep * images_ref[c] + spread * noise
        left[c, :samples, :] = noisy.astype(LOWTYPE)
        one = noise.astype(LOWTYPE)
        rest = noise - one.astype(F32)
        two = rest.astype(LOWTYPE)
        left[3 + c, :samples, :] = one
        left[6 + c, :samples, :] = two
        left[9 + c, :samples, :] = (rest - two.astype(F32)).astype(LOWTYPE)
    left[12, :samples, :] = mask_ref[...].astype(F32).astype(LOWTYPE)
    for ref in (noisy_ref, planes_ref, maskw_ref):
        ref[:, 12:, :] = jnp.zeros((samples, ROWS12 - 12, PLACES), F32)

    def picture(quarter):
        pixel = lax.broadcasted_iota(jnp.int32, (S * S, PLACES), 0)
        lane = lax.broadcasted_iota(jnp.int32, (S * S, PLACES), 1)
        wanted = (
            (lane // SIDE * 2 + quarter // 2) * S + lane % SIDE * 2 + quarter % 2
        )
        pick = jnp.where(pixel == wanted, 1.0, 0.0).astype(LOWTYPE)
        rows = left.shape[1]
        moved = dot_nn(left[...].reshape(13 * rows, S * S), pick)
        maskw = moved[12 * rows : 12 * rows + samples] * weight
        for c in range(3):
            k = quarter * 3 + c
            noisy_ref[:, k, :] = moved[c * rows : c * rows + samples]
            planes_ref[:, k, :] = sum(
                [moved[(p + c) * rows : (p + c) * rows + samples] for p in (6, 9)],
                moved[(3 + c) * rows : (3 + c) * rows + samples],
            )
            maskw_ref[:, k, :] = maskw

    picture(0)
    second = []
    for k, copy in zip(range(1, owners), first):
        copy.wait_recv()
        there = held.at[lax.rem(z + owners - k, owners), slot]
        second.append(
            [
                send(there, there, semb, (k - 1) * (chips - 1) + j - 1, same_core(j))
                for j in range(1, chips)
            ]
        )
        if k < 4:
            picture(k)
    for k in range(owners, 4):
        picture(k)
    third = []
    for k, copies in zip(range(1, owners), second):
        for copy in copies:
            copy.wait_recv()
        mine = held.at[lax.rem(z + owners - k, owners), pl.ds(core * chips, chips)]
        third.append(send(mine, mine, semc, k - 1, partner))
    for copy in third:
        copy.wait_recv()

    def place(seg, row, values):
        size = values.shape[0]
        if seg < 2:
            whole, side = ((conv1_ref, conv1b_ref), (conv2_ref, conv2b_ref))[seg]
            whole[row : row + size, :] = values
            height = side.shape[0]
            done = 0
            while done < size:
                offset, inner = (row + done) // height, (row + done) % height
                part = min(size - done, height - inner)
                side[inner : inner + part, offset * mid : (offset + 1) * mid] = values[
                    done : done + part
                ]
                done += part
        elif seg in (4, 5, 6):
            qkv_ref[row : row + size, (seg - 4) * mid : (seg - 3) * mid] = values
        else:
            {2: skip_ref, 3: temb_ref, 7: outw_ref}[seg][row : row + size, :] = values

    for owner in range(owners):
        packed = 0
        for seg, seg_rows in enumerate(segment_rows()):
            share = seg_rows // owners
            done = 0
            while done < share:
                row = packed + done
                size = min(share - done, chunk - row % chunk)
                inner = row % chunk
                place(
                    seg,
                    owner * share + done,
                    held[owner, slot_of(row // chunk, peers), inner : inner + size, :],
                )
                done += size
            packed += share
    for copy in started:
        copy.wait_send()


def open_call(owners, peers, operands):
    mid = CHANNELS_MID
    chips = peers // 2
    chunk, _ = chunk_rows(owners, peers)
    samples = operands[3].shape[0]
    rows = -(-samples // 16) * 16
    out_shapes = [
        ((9 * C1, mid), LOWTYPE),
        ((3 * C1, 3 * mid), LOWTYPE),
        ((9 * mid, mid), LOWTYPE),
        ((3 * mid, 3 * mid), LOWTYPE),
        ((C1, mid), LOWTYPE),
        ((TEMB, mid), LOWTYPE),
        ((mid, 3 * mid), LOWTYPE),
        ((mid, mid), LOWTYPE),
        ((samples, ROWS12, PLACES), F32),
        ((samples, ROWS12, PLACES), F32),
        ((samples, ROWS12, PLACES), F32),
    ]
    vmem = pl.BlockSpec(memory_space=pltpu.VMEM)
    return pl.pallas_call(
        functools.partial(open_body, owners, peers),
        out_shape=[jax.ShapeDtypeStruct(shape, kind) for shape, kind in out_shapes],
        in_specs=[vmem] * len(operands),
        out_specs=[vmem] * len(out_shapes),
        scratch_shapes=[
            pltpu.VMEM((owners, peers, chunk, mid), LOWTYPE),
            pltpu.VMEM((13, rows, S * S), LOWTYPE),
            pltpu.SemaphoreType.DMA((2, owners - 1)),
            pltpu.SemaphoreType.DMA((2, (owners - 1) * (chips - 1))),
            pltpu.SemaphoreType.DMA((2, owners - 1)),
        ],
        compiler_params=pltpu.CompilerParams(
            vmem_limit_bytes=VMEM_BYTES, collective_id=1, has_side_effects=True
        ),
    )(*operands)


def close_body(*refs):
    values, outs = refs[:10], refs[10:]
    for source, target in zip(values[:9], outs[:9]):
        target[...] = source[...]
    for source, target in zip((values[0], values[2], values[4], values[6]), outs[9:13]):
        target[...] = source[...].astype(LOWTYPE)
    sums = values[9]
    outs[13][...] = sums[0:1, 0:1]
    outs[14][...] = sums[1:2, 0:1]


def close_call(values):
    shapes = [(v.shape, F32) for v in values[:9]]
    shapes += [(values[k].shape, LOWTYPE) for k in (0, 2, 4, 6)] + [((1, 1), F32)] * 2
    vmem = pl.BlockSpec(memory_space=pltpu.VMEM)
    return pl.pallas_call(
        close_body,
        out_shape=[jax.ShapeDtypeStruct(shape, kind) for shape, kind in shapes],
        in_specs=[vmem] * len(values),
        out_specs=[vmem] * len(shapes),
        compiler_params=pltpu.CompilerParams(vmem_limit_bytes=VMEM_BYTES),
    )(*values)


def stem_spread():
    counts = np.zeros((3, 2, 3))
    for block in range(3):
        for inner in range(2):
            for sub in range(2):
                tap = 2 * (block - 1) + inner - sub + 1
                if 0 <= tap <= 2:
                    counts[block, inner, tap] += 1
    full = np.zeros((3, 3, ROWS12, 3, 3, 3))
    both = (np.einsum("ayt,bxu->abyxtu", counts, counts) * 0.25).reshape(3, 3, 4, 3, 3)
    for c in range(3):
        full[:, :, c:12:3, :, :, c] = both
    return np.pad(full.reshape(TAPS * ROWS12, 27), ((0, 0), (0, 5))).astype(np.float32)


def shards(
    images,
    pixel_mask,
    timesteps,
    noise_field,
    matrices,
    matrix_moms,
    stem_weight,
    stem_moms,
    head_weight,
    head_moms,
    vectors,
    vector_firsts,
    vector_seconds,
):
    owners, peers = lax.axis_size("bucket"), lax.axis_size("batch")
    samples = images.shape[0]
    level, weight = plan(timesteps)
    lone = [v[:, None] for v in (jnp.sqrt(level), jnp.sqrt(1.0 - level), weight)]
    per_image = jnp.concatenate([swish(embed(timesteps))] + lone, axis=1)
    conv1, conv1b, conv2, conv2b, skip, temb, qkv, outw, noisy, noise, mask_weight = open_call(
        owners,
        peers,
        [
            matrices,
            images.transpose(1, 0, 2),
            noise_field.transpose(1, 0, 2),
            pixel_mask,
            per_image,
        ],
    )
    head_turned = head_weight.T
    rows_out, misc = unet_call(
        samples,
        owners,
        peers,
        [
            noisy,
            noise,
            mask_weight,
            per_image,
            stem_weight,
            head_turned,
            conv1,
            conv1b,
            conv2,
            conv2b,
            skip,
            temb,
            qkv,
            outw,
            vectors,
            stem_spread(),
        ],
    )
    values = muon_call(
        owners,
        peers,
        [
            rows_out,
            misc,
            matrices,
            matrix_moms,
            stem_weight,
            stem_moms,
            head_turned,
            head_moms.T,
            vectors,
            vector_firsts,
            vector_seconds,
        ],
    )
    (
        new_matrices,
        new_matrix_moms,
        new_stem,
        new_stem_moms,
        new_head,
        new_head_moms,
        new_vectors,
        new_firsts,
        new_seconds,
        matrix_copies,
        stem_copy,
        head_copy,
        vector_copy,
        loss_sum,
        weight_sum,
    ) = close_call(values)
    loss_sum, weight_sum = loss_sum.reshape(()), weight_sum.reshape(())
    new_head, new_head_moms, head_copy = new_head.T, new_head_moms.T, head_copy.T
    return (
        loss_sum,
        weight_sum,
        new_matrices,
        new_matrix_moms,
        matrix_copies,
        new_stem,
        new_stem_moms,
        stem_copy,
        new_head,
        new_head_moms,
        head_copy,
        new_vectors,
        new_firsts,
        new_seconds,
        vector_copy,
    )


def solution(mesh):
    return jax.shard_map(
        shards,
        mesh=mesh,
        in_specs=(
            P(("bucket", "batch"), None, None),
            P(("bucket", "batch"), None),
            P(("bucket", "batch")),
            P(("bucket", "batch"), None, None),
            P("bucket", None),
            P("bucket", None),
            P(),
            P(),
            P(),
            P(),
            P(),
            P(),
            P(),
        ),
        out_specs=(
            P(),
            P(),
            P("bucket", None),
            P("bucket", None),
            P("bucket", None),
            P(),
            P(),
            P(),
            P(),
            P(),
            P(),
            P(),
            P(),
            P(),
            P(),
        ),
        check_vma=False,
    )
```

```python
import functools
import math

import jax
import jax.numpy as jnp
import numpy as np
from jax import lax
from jax.experimental import pallas as pl
from jax.experimental.pallas import tpu as pltpu
from jax.sharding import PartitionSpec as P

C1 = 128
CHANNELS_MID = 256
TEMB = 512
GROUPS = 32
S = 32
TSTEPS = 1000
NS_STEPS = 5
STEP = 10


GN_EPS = 1e-05
NORM_EPS = 1e-12
MOMENTUM = 0.95
LR_MUON = 0.5
DECAY = 0.01
NS_A = 3.4445
NS_B = -4.775
NS_C = 2.0315
BETA_ONE = 0.9
BETA_TWO = 0.999
LR_ADAM = 0.5
ADAM_EPS = 1e-08
EXACT_PRECISION = lax.Precision.HIGHEST
LOWTYPE = jnp.bfloat16


def segment_rows():
    return [
        9 * C1,
        9 * CHANNELS_MID,
        C1,
        TEMB,
        CHANNELS_MID,
        CHANNELS_MID,
        CHANNELS_MID,
        CHANNELS_MID,
    ]


def plan(timesteps):
    frac_t = (timesteps.astype(jnp.float32) / TSTEPS + 0.008) / 1.008
    level = jnp.cos(frac_t * (math.pi / 2)) ** 2
    ratio = level / (1.0 - level)
    return (level, jnp.minimum(1.0, 5.0 / ratio))


def embed(timesteps):
    half_width = TEMB // 2
    freqs = jnp.exp(-math.log(10000.0) * jnp.arange(half_width, dtype=jnp.float32) / half_width)
    angles = timesteps.astype(jnp.float32)[:, None] * freqs[None, :]
    return jnp.concatenate([jnp.sin(angles), jnp.cos(angles)], axis=1)


def swish(values):
    return values * jax.nn.sigmoid(values)


F32 = jnp.float32
PLACES = 256
SIDE = 16
HALO = 288
TAPS = 9
ROWS12 = 16
CHUNK = 64
SMALL_ROWS = 240
VMEM_BYTES = 56 * 1024 * 1024
SEG_OFF = (0, 1152, 3456, 3584, 4096, 4352, 4608, 4864, 5120)


def dot_nn(a, b, precision=None):
    return lax.dot_general(
        a, b, (((1,), (0,)), ((), ())), preferred_element_type=F32, precision=precision
    )


def dot_nt(a, b):
    return lax.dot_general(a, b, (((1,), (1,)), ((), ())), preferred_element_type=F32)


def dot_tn(a, b):
    return lax.dot_general(a, b, (((0,), (0,)), ((), ())), preferred_element_type=F32)


def sigmoid(v):
    return 1.0 / (1.0 + jnp.exp(-v))


def fold8(v):
    rows, chans = v.shape
    return jnp.sum(v.reshape(rows // 8, 8, chans), axis=0)


def shift_lanes(x, di, dj):
    lane = lax.broadcasted_iota(jnp.int32, x.shape, 1)
    row, col = lane // SIDE + di, lane % SIDE + dj
    offset = (-(SIDE * di + dj)) % PLACES
    moved = x if offset == 0 else pltpu.roll(x, offset, 1)
    valid = (row >= 0) & (row < SIDE) & (col >= 0) & (col < SIDE)
    return jnp.where(valid, moved, 0.0)


def tap_offsets():
    return [(di, dj) for di in (-1, 0, 1) for dj in (-1, 0, 1)]


def unet_body(
    group,
    steps,
    owners,
    peers,
    noisy_ref,
    noise_ref,
    maskw_ref,
    time_ref,
    stem_ref,
    head_ref,
    conv1_ref,
    conv1b_ref,
    conv2_ref,
    conv2b_ref,
    skip_ref,
    temb_ref,
    qkv_ref,
    outw_ref,
    vec_ref,
    spread_ref,
    rows_ref,
    misc_ref,
    acc_ref,
    gstem_ref,
    ghead_ref,
    gvec_ref,
    ghb_ref,
    loss_ref,
    wsum_ref,
    x0,
    hid,
    res,
    outp,
    attn,
    a1,
    a2,
    normed,
    qkv,
    plow,
    attl,
    low0,
    joined,
    patch,
    pad1,
    pad2,
    shiftf,
    dyf,
    dout,
    dq3,
    dpool,
    tproj,
    gtime,
    dtap,
    datt,
    dscore,
    dpool_low,
    stemw_ref,
    headw_ref,
    headb_ref,
    time_low,
    wide_rows,
    same128_ref,
    same256_ref,
):
    step = pl.program_id(0)
    mid = CHANNELS_MID
    chunks = range(0, PLACES, CHUNK)
    images = range(group)

    @pl.when(step == 0)
    def _():
        acc_ref[...] = jnp.zeros_like(acc_ref)
        gstem_ref[...] = jnp.zeros_like(gstem_ref)
        ghead_ref[...] = jnp.zeros_like(ghead_ref)
        gvec_ref[...] = jnp.zeros_like(gvec_ref)
        ghb_ref[...] = jnp.zeros_like(ghb_ref)
        loss_ref[...] = jnp.zeros_like(loss_ref)
        wsum_ref[...] = jnp.zeros_like(wsum_ref)
        gtime[...] = jnp.zeros_like(gtime)
        for ref in (a1, a2, pad1, pad2):
            for g in images:
                ref[g, :SIDE, :] = jnp.zeros((SIDE, ref.shape[2]), ref.dtype)
                ref[g, HALO - SIDE :, :] = jnp.zeros((SIDE, ref.shape[2]), ref.dtype)
        shiftf[...] = jnp.zeros_like(shiftf)
        for ref in (same128_ref, same256_ref):
            width = ref.shape[0] // GROUPS
            row = lax.broadcasted_iota(jnp.int32, ref.shape, 0) // width
            lane = lax.broadcasted_iota(jnp.int32, ref.shape, 1) // width
            ref[...] = jnp.where(row == lane, 1.0 / (PLACES * width), 0.0).astype(LOWTYPE)
        wide_rows[...] = jnp.zeros_like(wide_rows)
        samples = time_ref.shape[0]
        wide_rows[:samples, :TEMB] = time_ref[:, :TEMB]
        time_low[...] = wide_rows[: time_low.shape[0], :TEMB].astype(LOWTYPE)
        tproj[...] = dot_nn(time_low[...], temb_ref[...])
        wide_rows[:27, :C1] = stem_ref[...].astype(LOWTYPE).astype(F32)
        spread_stem = dot_nn(spread_ref[:, :27], wide_rows[:27, :C1], EXACT_PRECISION)
        for piece in range(3):
            low = spread_stem.astype(LOWTYPE)
            stemw_ref[:, piece * C1 : (piece + 1) * C1] = low
            spread_stem = spread_stem - low.astype(F32)
        width = mid + C1
        wide_rows[:ROWS12, :width] = jnp.zeros((ROWS12, width), F32)
        for tap in range(TAPS):
            wide_rows[:12, :width] = head_ref[:, tap * width : (tap + 1) * width]
            headw_ref[tap * ROWS12 : (tap + 1) * ROWS12, :] = wide_rows[:ROWS12, :width].astype(
                LOWTYPE
            )
        row = lax.broadcasted_iota(jnp.int32, (ROWS12, 12), 0)
        lane = lax.broadcasted_iota(jnp.int32, (ROWS12, 12), 1)
        tail = vec_ref[pl.ds(3 * C1 + 10 * mid, 12)].reshape(1, 12)
        bias = jnp.where(row == lane, tail, 0.0)
        headb_ref[...] = jnp.sum(bias, axis=1, keepdims=True) + jnp.zeros((ROWS12, C1), F32)

    def vec(row, chans=mid):
        start = row * C1 if chans == C1 else 3 * C1 + (row - 3) * mid
        return vec_ref[pl.ds(start, chans)].reshape(1, chans)

    def add_vec(row, value):
        gvec_ref[row : row + 1, : value.shape[1]] += value

    def total(parts):
        return jnp.concatenate([jnp.sum(p, axis=0, keepdims=True) for p in parts], axis=0)

    def grouped(stats, chans):
        same = same128_ref if chans == C1 else same256_ref
        first = stats.astype(LOWTYPE).astype(F32)
        second = (stats - first).astype(LOWTYPE).astype(F32)
        third = stats - first - second
        sums = dot_nn(jnp.concatenate([first, second, third], axis=0).astype(LOWTYPE), same[...])
        return sums[:group] + sums[group : 2 * group] + sums[2 * group :]

    def gn_stats(ref, sums, chans):
        mean = grouped(sums, chans)
        parts = []
        for g in images:
            acc = jnp.zeros((8, chans), F32)
            for r in chunks:
                c = ref[g, r : r + CHUNK, :] - mean[g : g + 1]
                acc += fold8(c * c)
            parts.append(acc)
        return mean, lax.rsqrt(grouped(total(parts), chans) + GN_EPS)

    def edge(chans, left):
        col = lax.broadcasted_iota(jnp.int32, (CHUNK, chans), 0) % SIDE
        return (col > 0) if left else (col < SIDE - 1)

    def act_shift(ref, g, mean, rstd, gain, shift, dest, chans):
        for r in chunks:
            y = (ref[g, r : r + CHUNK, :] - mean[g : g + 1]) * rstd[g : g + 1] * gain + shift
            a = y * sigmoid(y)
            shiftf[g, 8 + r : 8 + r + CHUNK, :chans] = a
            dest[g, SIDE + r : SIDE + r + CHUNK, chans : 2 * chans] = a.astype(LOWTYPE)
        for r in chunks:
            before = shiftf[g, 7 + r : 7 + r + CHUNK, :chans]
            after = shiftf[g, 9 + r : 9 + r + CHUNK, :chans]
            rows = slice(SIDE + r, SIDE + r + CHUNK)
            dest[g, rows, :chans] = jnp.where(edge(chans, True), before, 0.0).astype(LOWTYPE)
            dest[g, rows, 2 * chans :] = jnp.where(edge(chans, False), after, 0.0).astype(LOWTYPE)

    def dy_cat(ref, g, order):
        return jnp.concatenate(
            [ref[g, SIDE * k : SIDE * k + PLACES, :] for k in order], axis=1
        )

    def stack(parts):
        return jnp.concatenate(parts, axis=0) if len(parts) > 1 else parts[0]

    def staged(stages, fillers=()):
        fillers = list(fillers)
        for stage in stages:
            for g in images:
                stage(g)
            if fillers:
                fillers.pop(0)()
        for filler in fillers:
            filler()

    def rows_of(g):
        return slice(g * PLACES, (g + 1) * PLACES)

    sums1 = [None] * group

    def stem_patch(g):
        noisy = noisy_ref[g]
        for tap, (di, dj) in enumerate(tap_offsets()):
            patch[g, tap * ROWS12 : (tap + 1) * ROWS12, :] = shift_lanes(noisy, di, dj).astype(
                LOWTYPE
            )

    def stem_pool(g):
        wide = dot_tn(patch[g], stemw_ref[...])
        acc = jnp.zeros((8, C1), F32)
        for r in chunks:
            w = wide[r : r + CHUNK]
            v = (w[:, :C1] + w[:, C1 : 2 * C1]) + w[:, 2 * C1 :] + vec(0, C1)
            x0[g, r : r + CHUNK, :] = v
            low0[g * PLACES + r : g * PLACES + r + CHUNK, :] = v.astype(LOWTYPE)
            acc += fold8(v)
        sums1[g] = acc

    staged([stem_patch, stem_pool])
    mean1, rstd1 = gn_stats(x0, total(sums1), C1)
    gain1, shift1 = vec(1, C1), vec(2, C1)

    sums2 = [None] * group

    def act_one(g):
        act_shift(x0, g, mean1, rstd1, gain1, shift1, a1, C1)

    def conv_one(g):
        wide = dot_nn(dy_cat(a1, g, (0, 1, 2)), conv1_ref[...])
        bias = vec(3) + vec(4) + tproj[pl.ds(step * group + g, 1), :]
        acc = jnp.zeros((8, mid), F32)
        for r in chunks:
            v = wide[r : r + CHUNK] + bias
            hid[g, r : r + CHUNK, :] = v
            acc += fold8(v)
        sums2[g] = acc

    staged([act_one, conv_one])
    mean2, rstd2 = gn_stats(hid, total(sums2), mid)
    gain2, shift2 = vec(5), vec(6)

    sums3 = [None] * group

    def act_two(g):
        act_shift(hid, g, mean2, rstd2, gain2, shift2, a2, mid)

    def conv_two(g):
        wide = dot_nn(dy_cat(a2, g, (0, 1, 2)), conv2_ref[...])
        wide = wide + dot_nn(low0[rows_of(g), :], skip_ref[...])
        acc = jnp.zeros((8, mid), F32)
        for r in chunks:
            v = wide[r : r + CHUNK] + vec(7)
            res[g, r : r + CHUNK, :] = v
            acc += fold8(v)
        sums3[g] = acc

    staged([act_two, conv_two])
    mean3, rstd3 = gn_stats(res, total(sums3), mid)
    gain3, shift3 = vec(8), vec(9)
    scale = mid ** (-0.5)
    ones3, twos3 = [None] * group, [None] * group

    def norm_three(g):
        for r in chunks:
            xh = (res[g, r : r + CHUNK, :] - mean3[g : g + 1]) * rstd3[g : g + 1]
            y = xh * gain3 + shift3
            normed[g * PLACES + r : g * PLACES + r + CHUNK, :] = y.astype(LOWTYPE)

    def project(g):
        rows = rows_of(g)
        wide = dot_nn(normed[rows, :], qkv_ref[...])
        qkv[rows, :mid] = (wide[:, :mid] + vec(10)).astype(LOWTYPE)
        qkv[rows, mid : 2 * mid] = wide[:, mid : 2 * mid].astype(LOWTYPE)
        qkv[rows, 2 * mid :] = (wide[:, 2 * mid :] + vec(11)).astype(LOWTYPE)

    def weigh(g):
        rows = rows_of(g)
        logits = dot_nt(qkv[rows, :mid], qkv[rows, mid : 2 * mid])
        for r in chunks:
            s = logits[r : r + CHUNK] * scale
            e = jnp.exp(s - jnp.max(s, axis=1, keepdims=True))
            p = e * (1.0 / jnp.sum(e, axis=1, keepdims=True))
            attn[g, r : r + CHUNK, :] = p
            plow[g, r : r + CHUNK, :] = p.astype(LOWTYPE)

    def attend(g):
        attl[rows_of(g), :] = dot_nn(plow[g], qkv[rows_of(g), 2 * mid :]).astype(LOWTYPE)

    def join(g):
        wide = dot_nn(attl[rows_of(g), :], outw_ref[...])
        for r in chunks:
            rows = slice(g * PLACES + r, g * PLACES + r + CHUNK)
            o = res[g, r : r + CHUNK, :] + wide[r : r + CHUNK] + vec(12)
            outp[g, r : r + CHUNK, :] = o
            joined[rows, :mid] = (o * sigmoid(o)).astype(LOWTYPE)
            x = x0[g, r : r + CHUNK, :]
            joined[rows, mid:] = (x * sigmoid(x)).astype(LOWTYPE)

    def head(g):
        taps = dot_nt(headw_ref[...], joined[rows_of(g), :])
        value = headb_ref[:, :1] + jnp.zeros((ROWS12, PLACES), F32)
        for tap, (di, dj) in enumerate(tap_offsets()):
            value = value + shift_lanes(taps[tap * ROWS12 : (tap + 1) * ROWS12, :], di, dj)
        error = value - noise_ref[g]
        masked = maskw_ref[g] * error
        loss_ref[...] += masked * error
        wsum_ref[...] += maskw_ref[g]
        grad = 2.0 * masked
        ghb_ref[...] += grad
        gradl = grad.astype(LOWTYPE).astype(F32)
        for tap, (di, dj) in enumerate(tap_offsets()):
            dtap[g, tap * ROWS12 : (tap + 1) * ROWS12, :] = shift_lanes(gradl, -di, -dj).astype(
                LOWTYPE
            )

    def head_back(g):
        wide = dot_tn(dtap[g], headw_ref[...])
        acc = jnp.zeros((8, mid), F32)
        for r in chunks:
            o = outp[g, r : r + CHUNK, :]
            s = sigmoid(o)
            d = wide[r : r + CHUNK, :mid] * (s * (1.0 + o * (1.0 - s)))
            outp[g, r : r + CHUNK, :] = d
            dout[g * PLACES + r : g * PLACES + r + CHUNK, :] = d.astype(LOWTYPE)
            acc += fold8(d)
            x = x0[g, r : r + CHUNK, :]
            s = sigmoid(x)
            dpool[g, r : r + CHUNK, :] = wide[r : r + CHUNK, mid:] * (s * (1.0 + x * (1.0 - s)))
        add_vec(12, jnp.sum(acc, axis=0, keepdims=True))

    def attend_back(g):
        datt[rows_of(g), :] = dot_nt(dout[rows_of(g), :], outw_ref[...]).astype(LOWTYPE)

    def weigh_back(g):
        rows = rows_of(g)
        gweights = dot_nt(datt[rows, :], qkv[rows, 2 * mid :])
        dval = dot_tn(plow[g], datt[rows, :])
        add_vec(11, jnp.sum(fold8(dval), axis=0, keepdims=True))
        dq3[rows, 2 * mid :] = dval.astype(LOWTYPE)
        for r in chunks:
            p = attn[g, r : r + CHUNK, :]
            gw = gweights[r : r + CHUNK]
            ds = p * (gw - jnp.sum(gw * p, axis=1, keepdims=True))
            dscore[g, r : r + CHUNK, :] = (ds * scale).astype(LOWTYPE)

    def query_back(g):
        rows = rows_of(g)
        dqry = dot_nn(dscore[g], qkv[rows, mid : 2 * mid])
        dkey = dot_tn(dscore[g], qkv[rows, :mid])
        add_vec(10, jnp.sum(fold8(dqry), axis=0, keepdims=True))
        dq3[rows, :mid] = dqry.astype(LOWTYPE)
        dq3[rows, mid : 2 * mid] = dkey.astype(LOWTYPE)

    def project_back(g):
        one, two = jnp.zeros((8, mid), F32), jnp.zeros((8, mid), F32)
        wide = dot_nt(dq3[rows_of(g), :], qkv_ref[...])
        for r in chunks:
            xh = (res[g, r : r + CHUNK, :] - mean3[g : g + 1]) * rstd3[g : g + 1]
            d = wide[r : r + CHUNK]
            res[g, r : r + CHUNK, :] = xh
            dyf[g, r : r + CHUNK, :] = d
            one += fold8(d)
            two += fold8(d * xh)
        ones3[g], twos3[g] = one, two

    staged(
        [
            norm_three,
            project,
            weigh,
            attend,
            join,
            head,
            head_back,
            attend_back,
            weigh_back,
            query_back,
            project_back,
        ]
    )

    ones, twos = total(ones3), total(twos3)
    add_vec(9, jnp.sum(ones, axis=0, keepdims=True))
    add_vec(8, jnp.sum(twos, axis=0, keepdims=True))

    def finish(ref, dest, rstd, gain, m1, m2, chans, extra, g, row):
        r1 = rstd[g : g + 1]
        acc = jnp.zeros((8, chans), F32)
        for r in chunks:
            d = dyf[g, r : r + CHUNK, :chans] * (gain * r1)
            d = d - m1[g : g + 1] * r1 - ref[g, r : r + CHUNK, :] * (m2[g : g + 1] * r1)
            if extra is not None:
                d = d + extra[g, r : r + CHUNK, :]
            acc += fold8(d)
            dest(g, r, d.astype(LOWTYPE))
        acc = jnp.sum(acc, axis=0, keepdims=True)
        add_vec(row, acc)
        return acc

    def to_pad(pad):
        def put(g, r, low):
            pad[g, SIDE + r : SIDE + r + CHUNK, :] = low

        return put

    def turned(parts):
        return stack(parts).T

    def pad_turned(pad):
        return turned([pad[g, SIDE : SIDE + PLACES, :] for g in images])

    def conv_back(pad, weights, g, chans, apply):
        wide = dot_nt(dy_cat(pad, g, (2, 1, 0)), weights)
        shiftf[g, 8 : 8 + PLACES, :chans] = wide[:, :chans]
        dyf[g, :, :chans] = wide[:, chans : 2 * chans]
        for r in chunks:
            after = shiftf[g, 9 + r : 9 + r + CHUNK, :chans]
            dyf[g, r : r + CHUNK, :chans] += jnp.where(edge(chans, False), after, 0.0)
        shiftf[g, 8 : 8 + PLACES, :chans] = wide[:, 2 * chans :]
        for r in chunks:
            before = shiftf[g, 7 + r : 7 + r + CHUNK, :chans]
            apply(r, dyf[g, r : r + CHUNK, :chans] + jnp.where(edge(chans, True), before, 0.0))

    def norm_back(pad, weights, ref, mean, rstd, gain, shift, chans, ones, twos, g):
        sums = [jnp.zeros((8, chans), F32), jnp.zeros((8, chans), F32)]

        def apply(r, da):
            xh = (ref[g, r : r + CHUNK, :] - mean[g : g + 1]) * rstd[g : g + 1]
            y = xh * gain + shift
            s = sigmoid(y)
            d = da * (s * (1.0 + y * (1.0 - s)))
            ref[g, r : r + CHUNK, :] = xh
            dyf[g, r : r + CHUNK, :chans] = d
            sums[0] += fold8(d)
            sums[1] += fold8(d * xh)

        conv_back(pad, weights[...], g, chans, apply)
        ones[g], twos[g] = sums

    def add_product(first, last, left, right):
        acc_ref[:, first:last] += dot_nn(left(), right())

    m1, m2 = grouped(ones * gain3, mid), grouped(twos * gain3, mid)
    ones2, twos2 = [None] * group, [None] * group

    def grad_out():
        add_product(SEG_OFF[7], SEG_OFF[8], lambda: dout[...].T, lambda: attl[...])

    def grad_project(k):
        add_product(
            SEG_OFF[4 + k],
            SEG_OFF[5 + k],
            lambda: dq3[:, k * mid : (k + 1) * mid].T,
            lambda: normed[...],
        )

    def grad_head():
        for g in images:
            ghead_ref[...] += dot_nn(dtap[g], joined[rows_of(g), :])

    staged(
        [
            lambda g: finish(res, to_pad(pad2), rstd3, gain3, m1, m2, mid, outp, g, 7),
            lambda g: norm_back(
                pad2, conv2b_ref, hid, mean2, rstd2, gain2, shift2, mid, ones2, twos2, g
            ),
        ],
        [grad_out, grad_head] + [functools.partial(grad_project, k) for k in range(3)],
    )
    ones, twos = total(ones2), total(twos2)
    add_vec(6, jnp.sum(ones, axis=0, keepdims=True))
    add_vec(5, jnp.sum(twos, axis=0, keepdims=True))

    n1, n2 = grouped(ones * gain2, mid), grouped(twos * gain2, mid)
    ones1, twos1 = [None] * group, [None] * group
    lowt2 = pad_turned(pad2)

    def finish_two(g):
        acc = finish(hid, to_pad(pad1), rstd2, gain2, n1, n2, mid, None, g, 3)
        add_vec(4, acc)
        gtime[pl.ds(step * group + g, 1), :] = acc

    def grad_conv(lowt, act, offset, k):
        width = act.shape[2]
        first = offset + k * width
        add_product(
            first,
            first + width,
            lambda: lowt,
            lambda: stack([act[g, SIDE * k : SIDE * k + PLACES, :] for g in images]),
        )

    def grad_skip():
        add_product(SEG_OFF[2], SEG_OFF[3], lambda: lowt2, lambda: low0[...])
        for g in images:
            dpool[g] += dot_nt(pad2[g, SIDE : SIDE + PLACES, :], skip_ref[...])

    staged(
        [
            finish_two,
            lambda g: norm_back(
                pad1, conv1b_ref, x0, mean1, rstd1, gain1, shift1, C1, ones1, twos1, g
            ),
        ],
        [functools.partial(grad_conv, lowt2, a2, SEG_OFF[1], k) for k in range(3)] + [grad_skip],
    )
    ones, twos = total(ones1), total(twos1)
    add_vec(2, jnp.sum(ones, axis=0, keepdims=True))
    add_vec(1, jnp.sum(twos, axis=0, keepdims=True))

    p1, p2 = grouped(ones * gain1, C1), grouped(twos * gain1, C1)
    lowt1 = pad_turned(pad1)

    def to_pool(g, r, low):
        dpool_low[g, r : r + CHUNK, :] = low

    def grad_stem(g):
        gstem_ref[...] += dot_nn(patch[g], dpool_low[g])

    staged(
        [lambda g: finish(x0, to_pool, rstd1, gain1, p1, p2, C1, dpool, g, 0), grad_stem],
        [functools.partial(grad_conv, lowt1, a1, SEG_OFF[0], k) for k in range(3)],
    )

    @pl.when(step == steps - 1)
    def _():
        acc_ref[:, SEG_OFF[3] : SEG_OFF[4]] = dot_tn(gtime[...].astype(LOWTYPE), time_low[...])
        if rows_ref.shape[0] > 5120 + SMALL_ROWS:
            rows_ref[...] = jnp.zeros_like(rows_ref)
        pieces = gradient_pieces(owners, peers)
        for block in range(0, 5120, C1):
            turned = acc_ref[:, block : block + C1].T
            for source, size, target in pieces:
                low, high = max(source, block), min(source + size, block + C1)
                if low < high:
                    start = target + low - source
                    rows_ref[start : start + high - low, :] = turned[low - block : high - block]
        stem = lax.dot_general(
            spread_ref[...],
            gstem_ref[...],
            (((0,), (0,)), ((), ())),
            preferred_element_type=F32,
            precision=EXACT_PRECISION,
        )
        head = ghead_ref[...]
        none = jnp.zeros((ROWS12, C1), F32)
        tiles = [head[k : k + 16, :mid] for k in range(0, 144, 16)]
        for k in range(0, 80, 16):
            other = head[80 + k : 96 + k, mid:] if k < 64 else none
            tiles.append(jnp.concatenate([head[k : k + 16, mid:], other], axis=1))
        tiles.append(jnp.concatenate([stem[:16], stem[16:]], axis=1))
        for tile, (start, _) in zip(tiles, small_tiles(owners, peers)):
            rows_ref[start : start + 16, :] = tile
        misc_ref[:, :mid] = gvec_ref[...]
        misc_ref[13:14, :mid] = jnp.sum(loss_ref[...], axis=0, keepdims=True)
        misc_ref[14:15, :mid] = jnp.sum(wsum_ref[...], axis=0, keepdims=True)
        misc_ref[:, mid:] = ghb_ref[:, :C1] + ghb_ref[:, C1:]


def chunk_rows(owners, peers):
    share = -(-5120 // (owners * peers))
    return -(-share // 16) * 16, -(-(-(-SMALL_ROWS // peers)) // 16) * 16


def block_rows(owners, peers):
    chunk, small = chunk_rows(owners, peers)
    return owners * chunk + small


def slot_of(peer, peers):
    return peer % 2 * (peers // 2) + peer // 2


def gradient_pieces(owners, peers):
    chunk, _ = chunk_rows(owners, peers)
    block = block_rows(owners, peers)
    pieces = []
    for owner in range(owners):
        packed = 0
        for seg, seg_rows in enumerate(segment_rows()):
            share = seg_rows // owners
            done = 0
            while done < share:
                row = packed + done
                size = min(share - done, chunk - row % chunk)
                target = slot_of(row // chunk, peers) * block + owner * chunk + row % chunk
                pieces.append((SEG_OFF[seg] + owner * share + done, size, target))
                done += size
            packed += share
    return pieces


def small_tiles(owners, peers):
    chunk, small = chunk_rows(owners, peers)
    tiles = []
    for row in range(0, SMALL_ROWS, 16):
        slot = slot_of(row // small, peers)
        tiles.append((slot * block_rows(owners, peers) + owners * chunk + row % small, slot))
    return tiles


def unet_call(samples, owners, peers, operands):
    group = max(k for k in (1, 2, 4) if samples % k == 0)
    steps = samples // group
    time_rows = -(-samples // 16) * 16
    mid = CHANNELS_MID
    places = group * PLACES

    def image_spec():
        return pl.BlockSpec((group, ROWS12, PLACES), lambda i: (i, 0, 0))

    def whole(shape):
        return pl.BlockSpec(shape, lambda i: (0,) * len(shape))

    out_shapes = [(peers * block_rows(owners, peers), mid), (ROWS12, mid + C1)]
    scratch = [
        ((mid, 5120), F32),
        ((TAPS * ROWS12, C1), F32),
        ((TAPS * ROWS12, mid + C1), F32),
        ((ROWS12, mid), F32),
        ((ROWS12, mid), F32),
        ((ROWS12, mid), F32),
        ((ROWS12, mid), F32),
        ((group, PLACES, C1), F32),
        ((group, PLACES, mid), F32),
        ((group, PLACES, mid), F32),
        ((group, PLACES, mid), F32),
        ((group, PLACES, mid), F32),
        ((group, HALO, 3 * C1), LOWTYPE),
        ((group, HALO, 3 * mid), LOWTYPE),
        ((places, mid), LOWTYPE),
        ((places, 3 * mid), LOWTYPE),
        ((group, PLACES, mid), LOWTYPE),
        ((places, mid), LOWTYPE),
        ((places, C1), LOWTYPE),
        ((places, mid + C1), LOWTYPE),
        ((group, TAPS * ROWS12, PLACES), LOWTYPE),
        ((group, HALO, mid), LOWTYPE),
        ((group, HALO, mid), LOWTYPE),
        ((group, PLACES + 16, mid), F32),
        ((group, PLACES, mid), F32),
        ((places, mid), LOWTYPE),
        ((places, 3 * mid), LOWTYPE),
        ((group, PLACES, C1), F32),
        ((time_rows, mid), F32),
        ((time_rows, mid), F32),
        ((group, TAPS * ROWS12, PLACES), LOWTYPE),
        ((places, mid), LOWTYPE),
        ((group, PLACES, mid), LOWTYPE),
        ((group, PLACES, C1), LOWTYPE),
        ((TAPS * ROWS12, 3 * C1), LOWTYPE),
        ((TAPS * ROWS12, mid + C1), LOWTYPE),
        ((ROWS12, C1), F32),
        ((time_rows, TEMB), LOWTYPE),
        ((max(32, time_rows), TEMB), F32),
        ((C1, C1), LOWTYPE),
        ((mid, mid), LOWTYPE),
    ]
    return pl.pallas_call(
        functools.partial(unet_body, group, steps, owners, peers),
        grid=(steps,),
        out_shape=[jax.ShapeDtypeStruct(shape, F32) for shape in out_shapes],
        in_specs=[image_spec()] * 3 + [whole(a.shape) for a in operands[3:]],
        out_specs=[whole(shape) for shape in out_shapes],
        scratch_shapes=[pltpu.VMEM(shape, kind) for shape, kind in scratch],
        compiler_params=pltpu.CompilerParams(vmem_limit_bytes=VMEM_BYTES),
    )(*operands)


TASKS = ((1, 0), (0, 0), (0, 1), (2, 0), (1, 1), (2, 1), (3, 0), (3, 1))
MESH = pl.DeviceIdType.MESH
LEAD = 2
SMALL_LANES = 9 * (CHANNELS_MID + C1)


def ns_chain(gram, eye):
    product = None
    for step in range(NS_STEPS):
        square = dot_nn(gram, gram, EXACT_PRECISION)
        factor = NS_A * eye + NS_B * gram + NS_C * square
        product = factor if product is None else dot_nn(product, factor, EXACT_PRECISION)
        if step < NS_STEPS - 1:
            gram = dot_nn(factor, dot_nn(gram, factor, EXACT_PRECISION), EXACT_PRECISION)
    return product


def identity(size):
    rows = lax.broadcasted_iota(jnp.int32, (size, size), 0)
    cols = lax.broadcasted_iota(jnp.int32, (size, size), 1)
    return (rows == cols).astype(F32)


def task_pieces(owners, peers):
    chunk, _ = chunk_rows(owners, peers)
    pieces = []
    packed = 0
    for seg, seg_rows in enumerate(segment_rows()):
        share = seg_rows // owners
        done, number = 0, 0
        while done < share:
            row = packed + done
            size = min(share - done, chunk - row % chunk)
            pieces.append((seg, number, row // chunk, row % chunk, size, done))
            done += size
            number += 1
        packed += share
    return pieces


def task_peers(seg, peers):
    chip, core = TASKS[seg]
    return [(base + chip) * 2 + core for base in range(0, peers // 2, 4)]


def muon_body(
    owners,
    peers,
    rows_ref,
    misc_ref,
    weight_hbm,
    moment_hbm,
    stem_ref,
    stemm_ref,
    head_ref,
    headm_ref,
    vec_ref,
    first_ref,
    second_ref,
    new_ref,
    newm_ref,
    nstem_ref,
    nstemm_ref,
    nhead_ref,
    nheadm_ref,
    nvec_ref,
    nfirst_ref,
    nsecond_ref,
    sums_ref,
    recv1,
    own2,
    passed,
    send2,
    recv2,
    send3,
    recv3,
    recvs3,
    gathered,
    gathered_small,
    misc1,
    misc2,
    misc3,
    mine_g,
    mine_u,
    gram_part,
    gram_recv,
    gram_all,
    small,
    x_zero,
    x_one,
    flat,
    head_row,
    own_half,
    weight_ref,
    moment_ref,
    sem_load,
    sem1,
    sem2,
    sem3,
    sems3,
    sema,
    semb,
    semg,
    semh,
    semx,
    semy,
    semm1,
    semm2,
    semm3,
    semas,
    sembs,
    semp,
):
    mid = CHANNELS_MID
    chips = peers // 2
    chunk, small_chunk = chunk_rows(owners, peers)
    block = block_rows(owners, peers)
    own_rows = weight_ref.shape[0]
    z = lax.axis_index("bucket")
    peer = lax.axis_index("batch")
    chip, core = peer // 2, peer % 2
    partner = {"batch": chip * 2 + 1 - core}
    started = []
    half_rows = pl.ds(pl.multiple_of(core * chips * block, 16), chips * block)
    load_half = pltpu.make_async_copy(rows_ref.at[half_rows, :], own_half, sem_load.at[0])
    load_moment = pltpu.make_async_copy(moment_hbm, moment_ref, sem_load.at[1])
    load_weight = pltpu.make_async_copy(weight_hbm, weight_ref, sem_load.at[2])
    for load in (load_half, load_moment, load_weight):
        load.start()

    def same_core(k):
        return {"batch": lax.rem(chip + k, chips) * 2 + core}

    def along(k):
        return {"bucket": lax.rem(z + k, owners)}

    def send(source, target, sems, slot, device, begin=True):
        copy = pltpu.make_async_remote_copy(
            src_ref=source,
            dst_ref=target,
            send_sem=sems.at[0, slot],
            recv_sem=sems.at[1, slot],
            device_id=device,
            device_id_type=MESH,
        )
        copy.start()
        if begin:
            started.append(copy)
        return copy

    barrier = pltpu.get_barrier_semaphore()
    friends = [{"batch": lax.rem(peer + k, peers)} for k in range(1, peers)]
    friends += [along(k) for k in range(1, owners)]
    for friend in friends:
        pl.semaphore_signal(barrier, inc=1, device_id=friend, device_id_type=MESH)
    pl.semaphore_wait(barrier, len(friends))

    parts = [None] + list(range(1, owners)) + [0]

    def part_rows(part, base=0, half=None):
        start = base + (owners * chunk if part is None else lax.rem(z + part, owners) * chunk)
        size = small_chunk if part is None else chunk
        if half is not None:
            size = size // 2
            start = start + half * size
        return pl.ds(pl.multiple_of(start, 8), size)

    square = chips == 4
    across_x = chip + 1 - 2 * lax.rem(chip, 2)
    across_y = lax.rem(chip + 2, 4)

    def near(k):
        if not square:
            return lax.rem(chip + k, chips)
        return (chip, across_x, across_y, lax.rem(across_x + 2, 4))[k]

    def at_chip(k):
        return {"batch": near(k) * 2 + core}

    def base_of(k):
        return near(k) * block

    other_half = (1 - core) * chips * block

    misc_copy = send(misc_ref, misc1, semm1, 0, partner)
    order = list(range(1, chips)) + [0]
    first = {}
    for number, part in enumerate(parts):
        for k in order:
            first[part, k] = send(
                rows_ref.at[part_rows(part, other_half + base_of(k)), :],
                recv1.at[k, part_rows(part), :],
                sem1,
                number * chips + k,
                partner,
            )

    misc_copy.wait_recv()
    misc2[chip] = misc_ref[...] + misc1[...]
    misc_copies = [
        send(misc2.at[chip], misc2.at[chip], semm2, k - 1, same_core(k)) for k in range(1, chips)
    ]
    load_half.wait()
    second = {}
    third = []

    def add_cores(number):
        part = parts[number]
        rows = part_rows(part)
        for k in order:
            first[part, k].wait_recv()
            total = own_half[part_rows(part, base_of(k)), :] + recv1[k, rows, :]
            if k == 0:
                own2[rows, :] = total
                continue
            send2[k - 1, rows, :] = total
            if not square:
                second[part, k] = send(
                    send2.at[k - 1, rows, :],
                    recv2.at[k - 1, rows, :],
                    sem2,
                    number * (chips - 1) + k - 1,
                    at_chip(k),
                )
        if square:
            for index, (half, source, into, target) in enumerate(
                ((0, 2, 1, 1), (1, 2, 1, 2), (0, 0, 0, 1), (1, 1, 0, 2))
            ):
                rows = part_rows(part, 0, half)
                second[part, index] = send(
                    send2.at[source, rows, :],
                    recv2.at[into, rows, :],
                    sem2,
                    number * 6 + index,
                    at_chip(target),
                )

    def pass_on(number):
        part = parts[number]
        for half, source, target in ((0, 1, 2), (1, 0, 1)):
            second[part, half].wait_recv()
            rows = part_rows(part, 0, half)
            passed[rows, :] = send2[source, rows, :] + recv2[1, rows, :]
            second[part, 4 + half] = send(
                passed.at[rows, :], recv2.at[2, rows, :], sem2, number * 6 + 4 + half, at_chip(target)
            )

    def add_chips(number):
        part = parts[number]
        for k in (2, 3, 4, 5) if square else range(1, chips):
            second[part, k].wait_recv()
        rows = part_rows(part)
        total = own2[rows, :]
        for other in (0, 2) if square else range(chips - 1):
            total = total + recv2[other, rows, :]
        if part is None:
            recvs3[z] = total
            third.extend(
                send(recvs3.at[z], recvs3.at[z], sems3, k - 1, along(k)) for k in range(1, owners)
            )
        elif part == 0:
            own2[rows, :] = total
        else:
            send3[part - 1] = total
            third.append(
                send(send3.at[part - 1], recv3.at[part - 1], sem3, part - 1, along(part))
            )

    lead = LEAD if square else len(parts)
    for turn in range(len(parts) + lead):
        if turn < len(parts):
            add_cores(turn)
        if square and 0 <= turn - 1 < len(parts):
            pass_on(turn - 1)
        if turn == min(2, len(parts)):
            for copy in misc_copies:
                copy.wait_recv()
            misc3[z] = sum([misc2[k] for k in range(1, chips)], misc2[0])
            misc_copies = [
                send(misc3.at[z], misc3.at[z], semm3, k - 1, along(k)) for k in range(1, owners)
            ]
        if 0 <= turn - lead < len(parts):
            add_chips(turn - lead)
    for copy in third:
        copy.wait_recv()
    total = own2[pl.ds(pl.multiple_of(z * chunk, 16), chunk), :]
    for other in range(owners - 1):
        total = total + recv3[other]
    slot = core * chips + chip
    gathered[slot] = total
    total = recvs3[0]
    for other in range(1, owners):
        total = total + recvs3[other]
    gathered_small[slot] = total

    pieces = task_pieces(owners, peers)

    def piece_copy(piece, index, target):
        seg, number, source, row, size, place = piece
        return pltpu.make_async_remote_copy(
            src_ref=gathered.at[slot_of(source, peers), pl.ds(row, size), :],
            dst_ref=mine_g.at[pl.ds(place, size), :],
            send_sem=semp.at[0, index],
            recv_sem=semp.at[1, number],
            device_id={"batch": target},
            device_id_type=MESH,
        )

    def from_peer(source):
        copies = []
        for piece in pieces:
            if piece[2] == source:
                for target in task_peers(piece[0], peers):
                    if target != source:
                        copies.append(piece_copy(piece, len(copies), target))
        return copies

    for source in range(peers):

        @pl.when(peer == source)
        def _(source=source):
            for copy in from_peer(source):
                copy.start()

    for copy in misc_copies:
        copy.wait_recv()
    misc = sum([misc3[k] for k in range(1, owners)], misc3[0])
    weight_sum = jnp.sum(misc[14:15, :mid], axis=1, keepdims=True)
    inverse = 1.0 / weight_sum
    loss_sum = jnp.sum(misc[13:14, :mid], axis=1, keepdims=True)
    sums_ref[0:1, :] = loss_sum + jnp.zeros((1, C1), F32)
    sums_ref[1:2, :] = weight_sum + jnp.zeros((1, C1), F32)
    head_bias = jnp.sum(misc[:, mid:].T, axis=0, keepdims=True)
    for row in range(3):
        flat[pl.ds(row * C1, C1)] = misc[row : row + 1, :C1].reshape(C1)
    for row in range(3, 13):
        flat[pl.ds(3 * C1 + (row - 3) * mid, mid)] = misc[row : row + 1, :mid].reshape(mid)
    head_row[...] = jnp.zeros_like(head_row)
    head_row[0:1, :ROWS12] = head_bias
    flat[pl.ds(3 * C1 + 10 * mid, C1)] = head_row[0:1, :].reshape(C1)
    grad = flat[pl.ds(0, vec_ref.shape[0])] * inverse.reshape(1)
    firsts = BETA_ONE * first_ref[...] + (1.0 - BETA_ONE) * grad
    seconds = BETA_TWO * second_ref[...] + (1.0 - BETA_TWO) * grad * grad
    nfirst_ref[...] = firsts
    nsecond_ref[...] = seconds
    change = (
        firsts
        / (1.0 - BETA_ONE**STEP)
        / (jnp.sqrt(seconds / (1.0 - BETA_TWO**STEP)) + ADAM_EPS)
    )
    nvec_ref[...] = vec_ref[...] - LR_ADAM * change

    load_moment.wait()
    for target in range(peers):

        @pl.when(peer == target)
        def _(target=target):
            for piece in pieces:
                seg, number, source, row, size, place = piece
                if target in task_peers(seg, peers):
                    if source == target:
                        mine_g[place : place + size, :] = gathered[
                            slot_of(source, peers), row : row + size, :
                        ]
                    else:
                        piece_copy(piece, 0, target).wait_recv()

    shares = [rows // owners for rows in segment_rows()]
    starts = [sum(shares[:k]) for k in range(len(shares))]
    for (task_chip, task_core), share, start in zip(TASKS, shares, starts):

        @pl.when((lax.rem(chip, 4) == task_chip) & (core == task_core))
        def _(share=share, start=start):
            grad = mine_g[:share, :] * inverse
            moment = MOMENTUM * moment_ref[start : start + share, :] + grad
            mine_u[:share, :] = grad + MOMENTUM * moment
            if share < mine_u.shape[0]:
                mine_u[share:, :] = jnp.zeros((mine_u.shape[0] - share, mid), F32)

    mine = mine_u[...]
    gram = lax.dot_general(
        mine,
        mine,
        (((0,), (0,)), ((), ())),
        preferred_element_type=F32,
        precision=EXACT_PRECISION,
    )
    gram_part[:C1, :] = gram[:C1, :]
    gram_part[C1:, :C1] = gram[C1 : C1 + 64, C1:]
    gram_part[C1:, C1:] = gram[C1 + 64 :, C1:]
    part = gram_part.shape[0] // owners
    copies = []
    for k in range(1, owners):
        start = pl.multiple_of(lax.rem(z + k, owners) * part, 8)
        copies.append(send(gram_part.at[pl.ds(start, part), :], gram_recv.at[z], semg, k - 1, along(k)))
    own_part = pl.ds(pl.multiple_of(z * part, 8), part)
    gram_recv[z] = gram_part[own_part, :]

    here = gathered.at[slot]
    plane = [send(here, here, sema, k - 1, same_core(k)) for k in range(1, chips)]
    cross = [send(here, here, semb, 0, partner)]
    here = gathered_small.at[slot]
    plane_small = [send(here, here, semas, k - 1, same_core(k)) for k in range(1, chips)]
    cross_small = [send(here, here, sembs, 0, partner)]

    for copy in copies:
        copy.wait_recv()
    gram_all[own_part, :] = sum([gram_recv[k] for k in range(1, owners)], gram_recv[0])
    copies = [
        send(gram_all.at[own_part, :], gram_all.at[own_part, :], semh, k - 1, along(k))
        for k in range(1, owners)
    ]
    for copy in copies:
        copy.wait_recv()
    upper, corner = gram_all[:C1, :], gram_all[C1:, :]
    gram = jnp.concatenate(
        [
            upper,
            jnp.concatenate(
                [upper[:, C1:].T, jnp.concatenate([corner[:, :C1], corner[:, C1:]], axis=0)],
                axis=1,
            ),
        ],
        axis=0,
    )
    eye = identity(mid)
    trace = jnp.sum(jnp.sum(gram * eye, axis=1, keepdims=True), axis=0, keepdims=True)
    scale = lax.rsqrt(trace + NORM_EPS)
    product = ns_chain(gram * (scale * scale), eye) * scale
    for k, copy in zip(range(1, chips), plane):
        copy.wait_recv()
        other = gathered.at[core * chips + lax.rem(chip + chips - k, chips)]
        cross.append(send(other, other, semb, k, partner))
    for k, copy in zip(range(1, chips), plane_small):
        copy.wait_recv()
        other = gathered_small.at[core * chips + lax.rem(chip + chips - k, chips)]
        cross_small.append(send(other, other, sembs, k, partner))
    turned = dot_nn(mine_u[...], product, EXACT_PRECISION)

    place = lax.rem(chip, 4)
    base = chip - place

    def in_group(k):
        return {"batch": (base + lax.rem(place + k, 4)) * 2 + core}

    buffers = (x_zero, x_one)

    def step_copy(buffer, index, sems, slot, device):
        there = buffer.at[index]
        return pltpu.make_async_remote_copy(
            src_ref=there,
            dst_ref=there,
            send_sem=sems.at[0, slot],
            recv_sem=sems.at[1, slot],
            device_id=device,
            device_id_type=MESH,
        )

    def step_copies(buffer):
        copies = [step_copy(buffer, place, semx, k - 1, in_group(k)) for k in range(1, 4)]
        return copies, step_copy(buffer, place, semy, 0, partner)

    for task_core, buffer in enumerate(buffers):

        @pl.when(core == task_core)
        def _(buffer=buffer):
            buffer[place] = turned[: buffer.shape[1]].astype(LOWTYPE)
            copies, own = step_copies(buffer)
            for copy in copies:
                copy.start()
            own.start()

    for copy in cross:
        copy.wait_recv()
    for owner_peer in range(peers):
        start = owner_peer * chunk
        size = min(chunk, own_rows - start)
        if size > 0:
            grad = gathered[slot_of(owner_peer, peers), :size, :] * inverse
            rows = slice(start, start + size)
            newm_ref[rows, :] = MOMENTUM * moment_ref[rows, :] + grad
    for copy in cross_small:
        copy.wait_recv()
    tiles = []
    for row in range(0, SMALL_ROWS, 16):
        at = row % small_chunk
        tile = gathered_small[slot_of(row // small_chunk, peers), at : at + 16, :]
        tiles.append(tile * inverse)
    small[...] = jnp.zeros_like(small)
    for tap in range(TAPS):
        lanes = slice(tap * (mid + C1), tap * (mid + C1) + mid)
        small[:16, lanes] = tiles[tap]
        lanes = slice(tap * (mid + C1) + mid, (tap + 1) * (mid + C1))
        if tap < 5:
            small[:16, lanes] = tiles[9 + tap][:, :C1]
        else:
            small[:16, lanes] = tiles[9 + tap - 5][:, C1:]
    small[32:48, SMALL_LANES:] = tiles[14][:, :C1]
    small[48:, SMALL_LANES:] = tiles[14][:, C1:]
    head_part = (slice(0, 12), slice(0, SMALL_LANES))
    stem_part = (slice(32, 59), slice(SMALL_LANES, SMALL_LANES + C1))
    for part, old_ref, fresh_ref in (
        (head_part, headm_ref, nheadm_ref),
        (stem_part, stemm_ref, nstemm_ref),
    ):
        grad = small[part]
        moment = MOMENTUM * old_ref[...] + grad
        fresh_ref[...] = moment
        turn = grad + MOMENTUM * moment
        small[part] = turn * lax.rsqrt(
            jnp.sum(jnp.sum(turn * turn, axis=1, keepdims=True), axis=0, keepdims=True) + NORM_EPS
        )
    gram = lax.dot_general(
        small[...],
        small[...],
        (((1,), (1,)), ((), ())),
        preferred_element_type=F32,
        precision=EXACT_PRECISION,
    )
    product = ns_chain(gram, identity(64))
    small[...] = dot_nn(product, small[...], EXACT_PRECISION)
    keep = 1.0 - LR_MUON * DECAY
    nhead_ref[...] = head_ref[...] * keep - LR_MUON * small[head_part]
    nstem_ref[...] = stem_ref[...] * keep - LR_MUON * small[stem_part]


    for task_core, buffer in enumerate(buffers):

        @pl.when(core == task_core)
        def _(buffer=buffer, other_buffer=buffers[1 - task_core]):
            copies, own = step_copies(buffer)
            forwards = [own]
            for k in range(1, 4):
                copies[k - 1].wait_recv()
                forwards.append(
                    step_copy(buffer, lax.rem(place + 4 - k, 4), semy, k, partner)
                )
                forwards[-1].start()
            for k in range(4):
                step_copy(other_buffer, lax.rem(place + 4 - k, 4), semy, k, partner).wait_recv()
            for copy in copies + forwards:
                copy.wait_send()

    load_weight.wait()
    for (task_chip, task_core), share, start in zip(TASKS, shares, starts):
        buffer = (x_zero, x_one)[task_core]
        rows = slice(start, start + share)
        fresh = weight_ref[rows, :] * keep - LR_MUON * buffer[task_chip, :share, :].astype(F32)
        new_ref[rows, :] = fresh
    for copy in started:
        copy.wait_send()
    for source in range(peers):

        @pl.when(peer == source)
        def _(source=source):
            for copy in from_peer(source):
                copy.wait_send()


def muon_call(owners, peers, operands):
    mid = CHANNELS_MID
    chips = peers // 2
    chunk, small_chunk = chunk_rows(owners, peers)
    block = block_rows(owners, peers)
    rows = operands[2].shape[0]
    part = 192 // owners
    pieces = task_pieces(owners, peers)
    shares = [seg_rows // owners for seg_rows in segment_rows()]
    most = [max(s for s, t in zip(shares, TASKS) if t[1] == core) for core in (0, 1)]
    out_shapes = [
        ((rows, mid), F32),
        ((rows, mid), F32),
        (operands[4].shape, F32),
        (operands[4].shape, F32),
        (operands[6].shape, F32),
        (operands[6].shape, F32),
        (operands[8].shape, F32),
        (operands[8].shape, F32),
        (operands[8].shape, F32),
        ((8, C1), F32),
    ]
    scratch = [
        ((chips, block, mid), F32),
        ((block, mid), F32),
        ((block, mid), F32),
        ((chips - 1, block, mid), F32),
        ((chips - 1, block, mid), F32),
        ((owners - 1, chunk, mid), F32),
        ((owners - 1, chunk, mid), F32),
        ((owners, small_chunk, mid), F32),
        ((peers, chunk, mid), F32),
        ((peers, small_chunk, mid), F32),
        (operands[1].shape, F32),
        ((chips,) + operands[1].shape, F32),
        ((owners,) + operands[1].shape, F32),
        ((max(most), mid), F32),
        ((max(most), mid), F32),
        ((192, mid), F32),
        ((owners, part, mid), F32),
        ((192, mid), F32),
        ((64, SMALL_LANES + C1), F32),
        ((4, most[0], mid), LOWTYPE),
        ((4, most[1], mid), LOWTYPE),
        ((3 * C1 + 10 * mid + C1,), F32),
        ((8, C1), F32),
        ((chips * block, mid), F32),
        ((rows, mid), F32),
        ((rows, mid), F32),
    ]
    sems = [
        (owners + 1) * chips,
        (owners + 1) * max(6, chips - 1),
        owners - 1,
        owners - 1,
        chips - 1,
        chips,
        owners - 1,
        owners - 1,
        3,
        4,
        1,
        chips - 1,
        owners - 1,
        chips - 1,
        chips,
        len(pieces) * (peers // 8),
    ]
    hbm = pl.BlockSpec(memory_space=pl.ANY)
    vmem = pl.BlockSpec(memory_space=pltpu.VMEM)
    return pl.pallas_call(
        functools.partial(muon_body, owners, peers),
        out_shape=[jax.ShapeDtypeStruct(shape, kind) for shape, kind in out_shapes],
        in_specs=[hbm, vmem, hbm, hbm] + [vmem] * (len(operands) - 4),
        out_specs=[vmem] * len(out_shapes),
        scratch_shapes=[pltpu.VMEM(shape, kind) for shape, kind in scratch]
        + [pltpu.SemaphoreType.DMA((3,))]
        + [pltpu.SemaphoreType.DMA((2, count)) for count in sems],
        compiler_params=pltpu.CompilerParams(
            vmem_limit_bytes=VMEM_BYTES, collective_id=0, has_side_effects=True
        ),
    )(*operands)


def open_body(
    owners,
    peers,
    weight_ref,
    images_ref,
    noise_ref,
    mask_ref,
    image_ref,
    conv1_ref,
    conv1b_ref,
    conv2_ref,
    conv2b_ref,
    skip_ref,
    temb_ref,
    qkv_ref,
    outw_ref,
    noisy_ref,
    planes_ref,
    maskw_ref,
    held,
    left,
    sema,
    semb,
    semc,
):
    mid = CHANNELS_MID
    chips = peers // 2
    chunk, _ = chunk_rows(owners, peers)
    own_rows = weight_ref.shape[0]
    z = lax.axis_index("bucket")
    peer = lax.axis_index("batch")
    chip, core = peer // 2, peer % 2
    partner = {"batch": chip * 2 + 1 - core}
    slot = core * chips + chip
    started = []

    def same_core(k):
        return {"batch": lax.rem(chip + k, chips) * 2 + core}

    def along(k):
        return {"bucket": lax.rem(z + k, owners)}

    def send(source, target, sems, index, device):
        copy = pltpu.make_async_remote_copy(
            src_ref=source,
            dst_ref=target,
            send_sem=sems.at[0, index],
            recv_sem=sems.at[1, index],
            device_id=device,
            device_id_type=MESH,
        )
        copy.start()
        started.append(copy)
        return copy

    barrier = pltpu.get_barrier_semaphore()
    friends = [partner] + [same_core(k) for k in range(1, chips)]
    friends += [along(k) for k in range(1, owners)]
    for friend in friends:
        pl.semaphore_signal(barrier, inc=1, device_id=friend, device_id_type=MESH)

    for other in range(peers):
        start = other * chunk
        size = min(chunk, own_rows - start)
        if size > 0:
            held[z, slot_of(other, peers), :size, :] = weight_ref[start : start + size, :].astype(
                LOWTYPE
            )
        if size < chunk:
            held[z, slot_of(other, peers), max(size, 0) :, :] = jnp.zeros(
                (chunk - max(size, 0), mid), LOWTYPE
            )
    pl.semaphore_wait(barrier, len(friends))

    here = held.at[z, slot]
    first = [send(here, here, sema, k - 1, along(k)) for k in range(1, owners)]

    samples = mask_ref.shape[0]
    keep = image_ref[:, TEMB : TEMB + 1]
    spread = image_ref[:, TEMB + 1 : TEMB + 2]
    weight = image_ref[:, TEMB + 2 : TEMB + 3]
    left[...] = jnp.zeros_like(left)
    for c in range(3):
        noise = noise_ref[c]
        noisy = keep * images_ref[c] + spread * noise
        left[c, :samples, :] = noisy.astype(LOWTYPE)
        one = noise.astype(LOWTYPE)
        rest = noise - one.astype(F32)
        two = rest.astype(LOWTYPE)
        left[3 + c, :samples, :] = one
        left[6 + c, :samples, :] = two
        left[9 + c, :samples, :] = (rest - two.astype(F32)).astype(LOWTYPE)
    left[12, :samples, :] = mask_ref[...].astype(F32).astype(LOWTYPE)
    for ref in (noisy_ref, planes_ref, maskw_ref):
        ref[:, 12:, :] = jnp.zeros((samples, ROWS12 - 12, PLACES), F32)

    def picture(quarter):
        pixel = lax.broadcasted_iota(jnp.int32, (S * S, PLACES), 0)
        lane = lax.broadcasted_iota(jnp.int32, (S * S, PLACES), 1)
        wanted = (
            (lane // SIDE * 2 + quarter // 2) * S + lane % SIDE * 2 + quarter % 2
        )
        pick = jnp.where(pixel == wanted, 1.0, 0.0).astype(LOWTYPE)
        rows = left.shape[1]
        moved = dot_nn(left[...].reshape(13 * rows, S * S), pick)
        maskw = moved[12 * rows : 12 * rows + samples] * weight
        for c in range(3):
            k = quarter * 3 + c
            noisy_ref[:, k, :] = moved[c * rows : c * rows + samples]
            planes_ref[:, k, :] = sum(
                [moved[(p + c) * rows : (p + c) * rows + samples] for p in (6, 9)],
                moved[(3 + c) * rows : (3 + c) * rows + samples],
            )
            maskw_ref[:, k, :] = maskw

    picture(0)
    second = []
    for k, copy in zip(range(1, owners), first):
        copy.wait_recv()
        there = held.at[lax.rem(z + owners - k, owners), slot]
        second.append(
            [
                send(there, there, semb, (k - 1) * (chips - 1) + j - 1, same_core(j))
                for j in range(1, chips)
            ]
        )
        if k < 4:
            picture(k)
    for k in range(owners, 4):
        picture(k)
    third = []
    for k, copies in zip(range(1, owners), second):
        for copy in copies:
            copy.wait_recv()
        mine = held.at[lax.rem(z + owners - k, owners), pl.ds(core * chips, chips)]
        third.append(send(mine, mine, semc, k - 1, partner))
    for copy in third:
        copy.wait_recv()

    def place(seg, row, values):
        size = values.shape[0]
        if seg < 2:
            whole, side = ((conv1_ref, conv1b_ref), (conv2_ref, conv2b_ref))[seg]
            whole[row : row + size, :] = values
            height = side.shape[0]
            done = 0
            while done < size:
                offset, inner = (row + done) // height, (row + done) % height
                part = min(size - done, height - inner)
                side[inner : inner + part, offset * mid : (offset + 1) * mid] = values[
                    done : done + part
                ]
                done += part
        elif seg in (4, 5, 6):
            qkv_ref[row : row + size, (seg - 4) * mid : (seg - 3) * mid] = values
        else:
            {2: skip_ref, 3: temb_ref, 7: outw_ref}[seg][row : row + size, :] = values

    for owner in range(owners):
        packed = 0
        for seg, seg_rows in enumerate(segment_rows()):
            share = seg_rows // owners
            done = 0
            while done < share:
                row = packed + done
                size = min(share - done, chunk - row % chunk)
                inner = row % chunk
                place(
                    seg,
                    owner * share + done,
                    held[owner, slot_of(row // chunk, peers), inner : inner + size, :],
                )
                done += size
            packed += share
    for copy in started:
        copy.wait_send()


def open_call(owners, peers, operands):
    mid = CHANNELS_MID
    chips = peers // 2
    chunk, _ = chunk_rows(owners, peers)
    samples = operands[3].shape[0]
    rows = -(-samples // 16) * 16
    out_shapes = [
        ((9 * C1, mid), LOWTYPE),
        ((3 * C1, 3 * mid), LOWTYPE),
        ((9 * mid, mid), LOWTYPE),
        ((3 * mid, 3 * mid), LOWTYPE),
        ((C1, mid), LOWTYPE),
        ((TEMB, mid), LOWTYPE),
        ((mid, 3 * mid), LOWTYPE),
        ((mid, mid), LOWTYPE),
        ((samples, ROWS12, PLACES), F32),
        ((samples, ROWS12, PLACES), F32),
        ((samples, ROWS12, PLACES), F32),
    ]
    vmem = pl.BlockSpec(memory_space=pltpu.VMEM)
    return pl.pallas_call(
        functools.partial(open_body, owners, peers),
        out_shape=[jax.ShapeDtypeStruct(shape, kind) for shape, kind in out_shapes],
        in_specs=[vmem] * len(operands),
        out_specs=[vmem] * len(out_shapes),
        scratch_shapes=[
            pltpu.VMEM((owners, peers, chunk, mid), LOWTYPE),
            pltpu.VMEM((13, rows, S * S), LOWTYPE),
            pltpu.SemaphoreType.DMA((2, owners - 1)),
            pltpu.SemaphoreType.DMA((2, (owners - 1) * (chips - 1))),
            pltpu.SemaphoreType.DMA((2, owners - 1)),
        ],
        compiler_params=pltpu.CompilerParams(
            vmem_limit_bytes=VMEM_BYTES, collective_id=1, has_side_effects=True
        ),
    )(*operands)


def close_body(*refs):
    large, values, outs, sems = refs[:2], refs[2:12], refs[12:-1], refs[-1]
    copies = [pltpu.make_async_copy(large[k], outs[k], sems.at[k]) for k in range(2)]
    for copy in copies:
        copy.start()
    for source, target in zip(values[2:9], outs[2:9]):
        target[...] = source[...]
    for source, target in zip((values[0], values[2], values[4], values[6]), outs[9:13]):
        target[...] = source[...].astype(LOWTYPE)
    sums = values[9]
    outs[13][...] = sums[0:1, 0:1]
    outs[14][...] = sums[1:2, 0:1]
    for copy in copies:
        copy.wait()


def close_call(values):
    shapes = [(v.shape, F32) for v in values[:9]]
    shapes += [(values[k].shape, LOWTYPE) for k in (0, 2, 4, 6)] + [((1, 1), F32)] * 2
    hbm = pl.BlockSpec(memory_space=pl.ANY)
    vmem = pl.BlockSpec(memory_space=pltpu.VMEM)
    return pl.pallas_call(
        close_body,
        out_shape=[jax.ShapeDtypeStruct(shape, kind) for shape, kind in shapes],
        in_specs=[hbm, hbm, vmem, hbm] + [vmem] * (len(values) - 2),
        out_specs=[hbm, hbm] + [vmem] * (len(shapes) - 2),
        scratch_shapes=[pltpu.SemaphoreType.DMA((2,))],
        compiler_params=pltpu.CompilerParams(vmem_limit_bytes=VMEM_BYTES),
    )(values[0], values[1], *values)


def stem_spread():
    counts = np.zeros((3, 2, 3))
    for block in range(3):
        for inner in range(2):
            for sub in range(2):
                tap = 2 * (block - 1) + inner - sub + 1
                if 0 <= tap <= 2:
                    counts[block, inner, tap] += 1
    full = np.zeros((3, 3, ROWS12, 3, 3, 3))
    both = (np.einsum("ayt,bxu->abyxtu", counts, counts) * 0.25).reshape(3, 3, 4, 3, 3)
    for c in range(3):
        full[:, :, c:12:3, :, :, c] = both
    return np.pad(full.reshape(TAPS * ROWS12, 27), ((0, 0), (0, 5))).astype(np.float32)


def shards(
    images,
    pixel_mask,
    timesteps,
    noise_field,
    matrices,
    matrix_moms,
    stem_weight,
    stem_moms,
    head_weight,
    head_moms,
    vectors,
    vector_firsts,
    vector_seconds,
):
    owners, peers = lax.axis_size("bucket"), lax.axis_size("batch")
    samples = images.shape[0]
    level, weight = plan(timesteps)
    lone = [v[:, None] for v in (jnp.sqrt(level), jnp.sqrt(1.0 - level), weight)]
    per_image = jnp.concatenate([swish(embed(timesteps))] + lone, axis=1)
    conv1, conv1b, conv2, conv2b, skip, temb, qkv, outw, noisy, noise, mask_weight = open_call(
        owners,
        peers,
        [
            matrices,
            images.transpose(1, 0, 2),
            noise_field.transpose(1, 0, 2),
            pixel_mask,
            per_image,
        ],
    )
    head_turned = head_weight.T
    rows_out, misc = unet_call(
        samples,
        owners,
        peers,
        [
            noisy,
            noise,
            mask_weight,
            per_image,
            stem_weight,
            head_turned,
            conv1,
            conv1b,
            conv2,
            conv2b,
            skip,
            temb,
            qkv,
            outw,
            vectors,
            stem_spread(),
        ],
    )
    values = muon_call(
        owners,
        peers,
        [
            rows_out,
            misc,
            matrices,
            matrix_moms,
            stem_weight,
            stem_moms,
            head_turned,
            head_moms.T,
            vectors,
            vector_firsts,
            vector_seconds,
        ],
    )
    (
        new_matrices,
        new_matrix_moms,
        new_stem,
        new_stem_moms,
        new_head,
        new_head_moms,
        new_vectors,
        new_firsts,
        new_seconds,
        matrix_copies,
        stem_copy,
        head_copy,
        vector_copy,
        loss_sum,
        weight_sum,
    ) = close_call(values)
    loss_sum, weight_sum = loss_sum.reshape(()), weight_sum.reshape(())
    new_head, new_head_moms, head_copy = new_head.T, new_head_moms.T, head_copy.T
    return (
        loss_sum,
        weight_sum,
        new_matrices,
        new_matrix_moms,
        matrix_copies,
        new_stem,
        new_stem_moms,
        stem_copy,
        new_head,
        new_head_moms,
        head_copy,
        new_vectors,
        new_firsts,
        new_seconds,
        vector_copy,
    )


def solution(mesh):
    return jax.shard_map(
        shards,
        mesh=mesh,
        in_specs=(
            P(("bucket", "batch"), None, None),
            P(("bucket", "batch"), None),
            P(("bucket", "batch")),
            P(("bucket", "batch"), None, None),
            P("bucket", None),
            P("bucket", None),
            P(),
            P(),
            P(),
            P(),
            P(),
            P(),
            P(),
        ),
        out_specs=(
            P(),
            P(),
            P("bucket", None),
            P("bucket", None),
            P("bucket", None),
            P(),
            P(),
            P(),
            P(),
            P(),
            P(),
            P(),
            P(),
            P(),
            P(),
        ),
        check_vma=False,
    )
```
